32 devices in a mesh: dp: 8 (over z, y), head: 4 (over x, core).
Axes of the slice: x: 2, y: 2, z: 4, core: 2. Of those that a mesh axis runs over, the one named last changes fastest.
Arguments:
- block_in: bfloat16 [4096, 2304], P(('dp', 'head')), may hold values from -6 to 6
- cotangent: bfloat16 [4096, 2304], P(('dp', 'head')), may hold values from -6 to 6
- seq_ids: int32 [4096], P(('dp', 'head')), may hold values from 0 to 3, as said below
- weights: float32 [2304, 132, 256], P('dp', 'head')
- momentum: float32 [2304, 132, 256], P('dp', 'head')
- gains: float32 [2, 2304], replicated, may hold values from 0.5 to 1.5
- gain_first: float32 [2, 2304], replicated
- gain_second: float32 [2, 2304], replicated, as said below
Outputs:
- block_out: bfloat16 [4096, 2304], P(('dp', 'head'))
- grad_input: float32 [4096, 2304], P(('dp', 'head'))
- weight_grads: float32 [2304, 132, 256], P('dp', 'head')
- new_momentum: float32 [2304, 132, 256], P('dp', 'head')
- new_weights: float32 [2304, 132, 256], P('dp', 'head')
- gain_grads: float32 [2, 2304], replicated
- new_gain_first: float32 [2, 2304], replicated
- new_gain_second: float32 [2, 2304], replicated
- new_gains: float32 [2, 2304], replicated
The draws below stay inside these ranges and needn't reach their ends.
Inputs may be any that keep to these rules, and one draw needn't show every extreme that they name: seq_ids never fall along the tokens; no sequence is longer than 4096 tokens; sequence 0 is shorter than 512 tokens; sequences 1 to 1 are the long ones, and each boundary between two of them lies between a quarter and a half of 512 tokens after a multiple of 4096; the last two sequences together are shorter than 512 tokens. `gain_second`: positive.
All inputs are finite; a program needn't handle non-finite values.
Results may differ from the reference program's by a relative error of at most 0.02.
The reference program's roundings to bfloat16 on the way count: a program that leaves them out, or rounds other values in their place, can miss the bound.
Values may be sent and summed in bfloat16 or wider, within the bound.
No kernel may reach another device: no remote copies, remote signals or barrier semaphores. Data moves between devices by JAX's collectives and lax.ppermute only.
A program may use at most 448 MiB of HBM per device.

```python
import math
from functools import partial
import jax
import jax.numpy as jnp
from jax import lax

D = 2304
H = 8
KV = 4
HD = 256
FF = 9216
NEWTON_STEPS = 5
UPDATE_STEP = 10
GROUP_TOK = 512
TOKENS = 4096
SEQ = 4096
QG = 2
KG = 1
FG = 9
BG = 33
BLOCKS = 132
N_HEAD = 4


def kind_scales(query_scale, key_scale, value_scale, out_scale, gate_scale, down_scale):
    per_group = jnp.concatenate([jnp.full((QG,), query_scale, jnp.float32), jnp.full((KG,), key_scale, jnp.float32), jnp.full((KG,), value_scale, jnp.float32), jnp.full((QG,), out_scale, jnp.float32), jnp.full((2 * FG,), gate_scale, jnp.float32), jnp.full((FG,), down_scale, jnp.float32)])
    return jnp.tile(per_group, BLOCKS // BG)


def draw_seq_ids(key, part):
    key = jax.random.fold_in(key, 11)
    shift_key, head_key, tail_key, split_key = jax.random.split(key, 4)
    long_count = TOKENS // SEQ
    shift = jax.random.randint(shift_key, (), GROUP_TOK // 4, GROUP_TOK // 2 + 1)
    head_length = shift + jax.random.randint(head_key, (), 0, GROUP_TOK // 4 + 1)
    tail_length = jax.random.randint(tail_key, (), 2, GROUP_TOK // 4 + 3)
    split_length = jax.random.randint(split_key, (), 1, tail_length)
    positions = jnp.arange(TOKENS, dtype=jnp.int32)
    inner = jnp.clip((positions - shift) // SEQ, 0, long_count - 1).astype(jnp.int32)
    ids_head = (positions >= head_length).astype(jnp.int32)
    ids_tail = (positions >= TOKENS - tail_length).astype(jnp.int32)
    ids_split = (positions >= TOKENS - tail_length + split_length).astype(jnp.int32)
    return ids_head + inner + ids_tail + ids_split


def draw_weights(key, part):
    key = jax.random.fold_in(key, 12)
    spread = kind_scales(1.6 / math.sqrt(D), 1.6 / math.sqrt(D), 1.0 / math.sqrt(D), 4.0 / math.sqrt(H * HD), 1.0 / math.sqrt(D), 1.0 / math.sqrt(FF))
    noise = jax.random.truncated_normal(key, -4.0, 4.0, (D, BLOCKS, HD), jnp.float32)
    return noise * spread[None, :, None]


def draw_momentum(key, part):
    key = jax.random.fold_in(key, 13)
    root = math.sqrt(TOKENS)
    spread = kind_scales(0.5 * root, 0.5 * root, root, 0.25 * root, 0.3 * root, 0.6 * root)
    noise = jax.random.truncated_normal(key, -4.0, 4.0, (D, BLOCKS, HD), jnp.float32)
    return noise * spread[None, :, None]


def draw_gain_first(key, part):
    key = jax.random.fold_in(key, 14)
    row_scale = jnp.array([0.6, 1.0], jnp.float32) * math.sqrt(TOKENS)
    noise = jax.random.truncated_normal(key, -4.0, 4.0, (2, D), jnp.float32)
    return noise * row_scale[:, None]


def draw_gain_second(key, part):
    key = jax.random.fold_in(key, 15)
    lowest = jnp.array([0.5, 1.0], jnp.float32) * TOKENS * 1.2
    exponent = jax.random.uniform(key, (2, D), jnp.float32, 0.0, math.log(4.0))
    return lowest[:, None] * jnp.exp(exponent)


def steps_of(stream_key, dims, cuts, least, largest):
    level = 1.0
    for dim, blocks in cuts:
        steps = jax.random.uniform(jax.random.fold_in(jax.random.fold_in(stream_key, 6), dim), (blocks,), jnp.float32, least / len(cuts), largest / len(cuts))
        level = level * jnp.repeat(jnp.exp(steps), dims[dim] // blocks).reshape((-1,) + (1,) * (len(dims) - 1 - dim))
    return level


def centred(rng, extent, deviation, bound, pieces=(), kind=jnp.bfloat16):
    entries = jax.random.normal(rng, extent, jnp.float32) * deviation
    if len(pieces) > 0:
        entries = steps_of(rng, extent, pieces, -0.22, 0.18) * entries
    return jnp.clip(entries, min=-bound, max=bound).astype(kind)


def setup_inputs(seed: int = 0) -> dict:
    splits = jax.random.split(jax.random.key(seed), 9)
    return {
        "block_in": centred(splits[0], (TOKENS, D), 1.0, 6.0, ((0, 32),)),
        "cotangent": centred(splits[1], (TOKENS, D), 1.0, 6.0, ((0, 32),)),
        "seq_ids": draw_seq_ids(jax.random.fold_in(splits[8], 71), 0),
        "weights": draw_weights(jax.random.fold_in(splits[8], 71), 0),
        "momentum": draw_momentum(jax.random.fold_in(splits[8], 71), 0),
        "gains": jnp.clip(1.0 + 0.1 * jax.random.normal(splits[5], (2, D), jnp.float32), 0.5, 1.5),
        "gain_first": draw_gain_first(jax.random.fold_in(splits[8], 71), 0),
        "gain_second": draw_gain_second(jax.random.fold_in(splits[8], 71), 0),
    }


NORM_EPS = 1e-06
SOFT_CAP = 50.0
NEG_FILL = -1e+30
MUON_RATE = 0.2
MUON_DECAY = 0.01
MUON_BETA = 0.95
ADAM_RATE = 0.3
BETA_ONE = 0.9
BETA_TWO = 0.95
ADAM_EPS = 1e-08
NEWTON_LINEAR = 3.4445
NEWTON_SQUARE = -4.775
NEWTON_CUBIC = 2.0315
TOP_PRECISION = lax.Precision.HIGHEST

@jax.custom_vjp
def low(v):
    return lax.optimization_barrier(v.astype(jnp.bfloat16)).astype(jnp.float32)

@jax.custom_vjp
def low_back(v):
    return v

def low_keep(v):
    return (low(v), None)

def low_pass(kept, grad):
    return (grad,)

def back_keep(v):
    return (v, None)

def back_low(kept, grad):
    return (low(grad),)
low.defvjp(low_keep, low_pass)
low_back.defvjp(back_keep, back_low)

def rms_scale(rows, gain):
    inverse = lax.rsqrt(lax.optimization_barrier(jnp.mean(rows * rows, axis=-1, keepdims=True)) + NORM_EPS)
    return rows * inverse * gain

def gelu_tanh(values):
    return jax.nn.gelu(values, approximate=True)

def orthogonal(blocks):
    frob_norm = jnp.sqrt(lax.optimization_barrier(jnp.sum(blocks * blocks, axis=(0, 2), keepdims=True)))
    current = blocks / (frob_norm + 1e-07)
    for sweep in range(NEWTON_STEPS):
        gram_matrix = jnp.einsum('dke,dkf->kef', current, current, precision=TOP_PRECISION)
        poly_term = NEWTON_SQUARE * gram_matrix + NEWTON_CUBIC * jnp.einsum('kef,kfg->keg', gram_matrix, gram_matrix, precision=TOP_PRECISION)
        current = NEWTON_LINEAR * current + jnp.einsum('dke,kef->dkf', current, poly_term, precision=TOP_PRECISION)
    factor = math.sqrt(max(1.0, blocks.shape[0] / blocks.shape[2]))
    return current * factor

def attend(queries, keys, values, seq_ids):
    total_rows = queries.shape[0]
    block_rows = min(512, total_rows)
    repeat = H // KV
    query_heads = queries.reshape(total_rows, KV, repeat, HD)
    key_heads = keys.reshape(total_rows, KV, HD)
    value_heads = values.reshape(total_rows, KV, HD)
    key_pos = jnp.arange(total_rows, dtype=jnp.int32)

    def one_block(block_index):
        start_row = block_index * block_rows
        query_block = lax.dynamic_slice_in_dim(query_heads, start_row, block_rows, 0)
        id_block = lax.dynamic_slice_in_dim(seq_ids, start_row, block_rows, 0)
        query_pos = start_row + jnp.arange(block_rows, dtype=jnp.int32)
        raw_scores = low_back(jnp.einsum('qkre,pke->krqp', query_block, key_heads, precision=TOP_PRECISION) * HD ** (-0.5))
        soft = SOFT_CAP * jnp.tanh(raw_scores / SOFT_CAP)
        allowed = (id_block[:, None] == seq_ids[None, :]) & (query_pos[:, None] >= key_pos[None, :])
        soft_probs = jax.nn.softmax(jnp.where(allowed, soft, NEG_FILL), axis=-1)
        mixed = jnp.einsum('krqp,pke->qkre', low(soft_probs), value_heads, precision=TOP_PRECISION)
        return mixed.reshape(block_rows, H * HD)
    block_count = total_rows // block_rows
    outputs = lax.map(jax.checkpoint(one_block), jnp.arange(block_count, dtype=jnp.int32))
    return outputs.reshape(total_rows, H * HD)

def block_forward(seq_ids, inputs, master, gain_rows):
    used_weights = low(master)
    grouped = used_weights.reshape(D, N_HEAD, BG, HD)
    key_mark = QG
    value_mark = QG + KG
    out_mark = QG + 2 * KG
    gate_mark = 2 * QG + 2 * KG
    up_mark = gate_mark + FG
    down_mark = up_mark + FG
    query_matrix = grouped[:, :, :key_mark].reshape(D, H * HD)
    key_matrix = grouped[:, :, key_mark:value_mark].reshape(D, KV * HD)
    value_matrix = grouped[:, :, value_mark:out_mark].reshape(D, KV * HD)
    out_matrix = grouped[:, :, out_mark:gate_mark].reshape(D, H * HD)
    gate_matrix = grouped[:, :, gate_mark:up_mark].reshape(D, FF)
    up_matrix = grouped[:, :, up_mark:down_mark].reshape(D, FF)
    down_matrix = grouped[:, :, down_mark:].reshape(D, FF)
    attn_input = low(rms_scale(inputs, gain_rows[0]))
    queries = low_back(low(jnp.dot(attn_input, query_matrix, precision=TOP_PRECISION)))
    keys = low_back(low(jnp.dot(attn_input, key_matrix, precision=TOP_PRECISION)))
    values = low_back(low(jnp.dot(attn_input, value_matrix, precision=TOP_PRECISION)))
    mixed = low_back(low(attend(queries, keys, values, seq_ids)))
    attn_add = low_back(jnp.dot(mixed, out_matrix.T, precision=TOP_PRECISION))
    residual = inputs + attn_add
    ffn_input = low(rms_scale(residual, gain_rows[1]))
    gate_proj = low_back(jnp.dot(ffn_input, gate_matrix, precision=TOP_PRECISION))
    up_proj = low_back(jnp.dot(ffn_input, up_matrix, precision=TOP_PRECISION))
    hidden = low(gelu_tanh(gate_proj) * up_proj)
    return residual + jnp.dot(hidden, down_matrix.T, precision=TOP_PRECISION)

def reference(block_in, cotangent, seq_ids, weights, momentum, gains, gain_first, gain_second):
    inputs = block_in.astype(jnp.float32)
    result, pullback = jax.vjp(partial(block_forward, seq_ids), inputs, weights, gains)
    grad_input, weight_grads, gain_grads = pullback(cotangent.astype(jnp.float32))
    block_out = result.astype(jnp.bfloat16)
    new_momentum = MUON_BETA * momentum + weight_grads
    orthonormal = orthogonal(new_momentum)
    new_weights = weights * (1.0 - MUON_RATE * MUON_DECAY) - MUON_RATE * orthonormal
    new_gain_first = BETA_ONE * gain_first + (1.0 - BETA_ONE) * gain_grads
    new_gain_second = BETA_TWO * gain_second + (1.0 - BETA_TWO) * gain_grads * gain_grads
    first_hat = new_gain_first / (1.0 - BETA_ONE ** UPDATE_STEP)
    second_hat = new_gain_second / (1.0 - BETA_TWO ** UPDATE_STEP)
    new_gains = gains - ADAM_RATE * first_hat / (jnp.sqrt(second_hat) + ADAM_EPS)
    return (block_out, grad_input, weight_grads, new_momentum, new_weights, gain_grads, new_gain_first, new_gain_second, new_gains)
```

```python
import functools
import math

import jax
import jax.numpy as jnp
from jax import lax
from jax.experimental import pallas as pl
from jax.experimental.pallas import tpu as pltpu
from jax.sharding import PartitionSpec as P

H = 8
KV = 4
FF = 9216
NEWTON_STEPS = 5
UPDATE_STEP = 10

NORM_EPS = 1e-06
SOFT_CAP = 50.0
MUON_RATE = 0.2
MUON_DECAY = 0.01
MUON_BETA = 0.95
ADAM_RATE = 0.3
BETA_ONE = 0.9
BETA_TWO = 0.95
ADAM_EPS = 1e-08
NEWTON_LINEAR = 3.4445
NEWTON_SQUARE = -4.775
NEWTON_CUBIC = 2.0315
TOP_PRECISION = lax.Precision.HIGHEST

BF16 = jnp.bfloat16
F32 = jnp.float32
VMEM_LIMIT = 62 * 1024 * 1024
NN = (((1,), (0,)), ((), ()))
NT = (((1,), (1,)), ((), ()))
TN = (((0,), (0,)), ((), ()))


def mm(a, b, dims):
    return lax.dot_general(a, b, dims, preferred_element_type=F32)


def rms_scale(rows, gain):
    inverse = lax.rsqrt(jnp.mean(rows * rows, axis=-1, keepdims=True) + NORM_EPS)
    return rows * inverse * gain


def swap(value, axis, mask):
    size = lax.axis_size(axis)
    return lax.ppermute(value, axis, [(i, i ^ mask) for i in range(size)])


def head_gather(rows):
    pair = jnp.stack([rows, swap(rows, "head", 2)], axis=0)
    quad = jnp.stack([pair, swap(pair, "head", 1)], axis=1)
    return quad.reshape((4 * rows.shape[0],) + rows.shape[1:])


def wide_gather(rows):
    both = jnp.stack([rows, swap(rows, "dp", 2)], axis=0)
    pair = jnp.stack([both, swap(both, "head", 2)], axis=1)
    quad = jnp.stack([pair, swap(pair, "head", 1)], axis=2)
    return quad.reshape((8 * rows.shape[0],) + rows.shape[1:])


def head_scatter(part):
    rows = part.shape[0] // 4
    quad = part.reshape(2, 2, rows, -1)
    other = swap(quad[:, 1], "head", 1)
    pair = (quad[:, 0].astype(F32) + other.astype(F32)).astype(BF16)
    other = swap(pair[1], "head", 2)
    return pair[0].astype(F32) + other.astype(F32)


def wide_scatter(part):
    rows = part.shape[0] // 8
    octet = part.reshape(2, 2, 2, rows, -1)
    other = swap(octet[:, :, 1], "head", 1)
    quad = (octet[:, :, 0].astype(F32) + other.astype(F32)).astype(BF16)
    other = swap(quad[:, 1], "head", 2)
    pair = (quad[:, 0].astype(F32) + other.astype(F32)).astype(BF16)
    other = swap(pair[1], "dp", 2)
    return pair[0].astype(F32) + other.astype(F32)


class Ring:
    def __init__(self):
        size = lax.axis_size("dp")
        order = list(range(0, size, 2)) + list(range(size - 1, 0, -2))
        place = [order.index(i) for i in range(size)]
        self.size = size
        self.order = jnp.array(order, jnp.int32)
        self.place = jnp.array(place, jnp.int32)[lax.axis_index("dp")]
        self.up = [(order[k], order[(k + 1) % size]) for k in range(size)]
        self.down = [(order[(k + 1) % size], order[k]) for k in range(size)]

    def index(self, offset):
        return self.order[(self.place + offset + self.size) % self.size]

    def gather(self, value):
        half = self.size // 2
        mid = value.shape[0] // 2
        pieces = {0: value}
        ahead, back = value, value
        for step in range(1, half):
            ahead = lax.ppermute(ahead, "dp", self.up)
            back = lax.ppermute(back, "dp", self.down)
            pieces[-step] = ahead
            pieces[step] = back
        first = lax.ppermute(ahead[:mid], "dp", self.up)
        second = lax.ppermute(back[mid:], "dp", self.down)
        out = jnp.zeros((self.size,) + value.shape, value.dtype)
        for offset, piece in pieces.items():
            out = lax.dynamic_update_index_in_dim(out, piece, self.index(offset), 0)
        far = self.index(half)
        zeros = (0,) * (value.ndim - 1)
        out = lax.dynamic_update_slice(out, first[None], (far, 0) + zeros)
        return lax.dynamic_update_slice(out, second[None], (far, mid) + zeros)

    def scatter(self, take):
        half = self.size // 2
        far = take(self.index(half))
        kind = far.dtype
        mid = far.shape[0] // 2
        up = lax.ppermute(far[:mid], "dp", self.up)
        down = lax.ppermute(far[mid:], "dp", self.down)
        for step in range(half - 1, 0, -1):
            part = take(self.index(step)).astype(F32)
            send = jnp.concatenate([part[:mid] + up[:mid], part[mid:]]) if step == half - 1 else part + up
            up = lax.ppermute(send.astype(kind), "dp", self.up)
            part = take(self.index(-step)).astype(F32)
            send = jnp.concatenate([part[:mid], part[mid:] + down]) if step == half - 1 else part + down
            down = lax.ppermute(send.astype(kind), "dp", self.down)
        return take(self.index(0)).astype(F32) + up.astype(F32) + down.astype(F32)


def params(**more):
    return pltpu.CompilerParams(vmem_limit_bytes=VMEM_LIMIT, **more)


def block_project(rows, blocks):
    t, d = rows.shape
    count, _, c = blocks.shape

    def body(x_ref, w_ref, o_ref):
        o_ref[...] = mm(x_ref[...], w_ref[...], NN).astype(BF16)

    return pl.pallas_call(
        body,
        grid=(count,),
        in_specs=[
            pl.BlockSpec((t, d), lambda b: (0, 0)),
            pl.BlockSpec((None, d, c), lambda b: (b, 0, 0)),
        ],
        out_specs=pl.BlockSpec((None, t, c), lambda b: (b, 0, 0)),
        out_shape=jax.ShapeDtypeStruct((count, t, c), BF16),
        compiler_params=params(),
        cost_estimate=pl.CostEstimate(
            flops=2 * count * t * d * c, bytes_accessed=2 * (t * d + count * (d * c + t * c)), transcendentals=0
        ),
    )(rows, blocks)


def block_back(cols, blocks):
    count, t, c = cols.shape
    d = blocks.shape[1]

    def body(x_ref, w_ref, o_ref, acc_ref):
        b = pl.program_id(0)

        @pl.when(b == 0)
        def _():
            acc_ref[...] = jnp.zeros_like(acc_ref)

        acc_ref[...] += mm(x_ref[...], w_ref[...], NT)

        @pl.when(b == count - 1)
        def _():
            o_ref[...] = acc_ref[...].astype(BF16)

    return pl.pallas_call(
        body,
        grid=(count,),
        in_specs=[
            pl.BlockSpec((None, t, c), lambda b: (b, 0, 0)),
            pl.BlockSpec((None, d, c), lambda b: (b, 0, 0)),
        ],
        out_specs=pl.BlockSpec((t, d), lambda b: (0, 0)),
        out_shape=jax.ShapeDtypeStruct((t, d), BF16),
        scratch_shapes=[pltpu.VMEM((t, d), F32)],
        compiler_params=params(),
        cost_estimate=pl.CostEstimate(
            flops=2 * count * t * d * c, bytes_accessed=2 * (t * d + count * (d * c + t * c)), transcendentals=0
        ),
    )(cols, blocks)


def block_outer(rows, cols):
    t, d = rows.shape
    count, _, c = cols.shape

    def body(x_ref, y_ref, o_ref, xt_ref):
        @pl.when(pl.program_id(0) == 0)
        def _():
            xt_ref[...] = x_ref[...].T

        o_ref[...] = mm(xt_ref[...], y_ref[...], NN).astype(BF16)

    return pl.pallas_call(
        body,
        grid=(count,),
        in_specs=[
            pl.BlockSpec((t, d), lambda b: (0, 0)),
            pl.BlockSpec((None, t, c), lambda b: (b, 0, 0)),
        ],
        out_specs=pl.BlockSpec((None, d, c), lambda b: (b, 0, 0)),
        out_shape=jax.ShapeDtypeStruct((count, d, c), BF16),
        scratch_shapes=[pltpu.VMEM((d, t), BF16)],
        compiler_params=params(),
        cost_estimate=pl.CostEstimate(
            flops=2 * count * t * d * c, bytes_accessed=2 * (t * d + count * (d * c + t * c)), transcendentals=0
        ),
    )(rows, cols)


def key_position(block, width, head_shift, shape, axis):
    local = lax.broadcasted_iota(jnp.int32, shape, axis)
    return block * width + jnp.bitwise_xor(local, head_shift)


def attend(place, queries, keys_values, query_pos, first_pos, scale):
    m, e = queries.shape
    n, _, p, _ = keys_values.shape
    step = 256

    def body(place_ref, q_ref, kv_ref, pos_ref, first_ref, low_ref, full_ref, sum_ref, acc_ref, tot_ref):
        j = pl.program_id(0)

        @pl.when(j == 0)
        def _():
            acc_ref[...] = jnp.zeros_like(acc_ref)
            tot_ref[...] = jnp.zeros_like(tot_ref)

        @pl.when(j <= place_ref[0])
        def _():
            key_pos = key_position(j, p, place_ref[1], (1, p), 1)
            for r in range(0, m, step):
                rows = pl.ds(r, step)
                raw = mm(q_ref[rows, :], kv_ref[0], NT)
                soft = SOFT_CAP * jnp.tanh(raw * (scale / SOFT_CAP))
                seen = (key_pos >= first_ref[rows, :]) & (key_pos <= pos_ref[rows, :])
                terms = jnp.where(seen, jnp.exp(soft), 0.0)
                tot_ref[rows, :] += jnp.sum(terms, axis=1, keepdims=True)
                acc_ref[rows, :] += mm(terms.astype(BF16), kv_ref[1], NN)

        @pl.when(j == n - 1)
        def _():
            total = tot_ref[...]
            mixed = acc_ref[...] / total
            full_ref[...] = mixed
            low_ref[...] = mixed.astype(BF16)
            sum_ref[...] = total

    whole = lambda shape: pl.BlockSpec(shape, lambda j, s: (0, 0))
    return pl.pallas_call(
        body,
        grid_spec=pltpu.PrefetchScalarGridSpec(
            num_scalar_prefetch=1,
            grid=(n,),
            in_specs=[
                whole((m, e)),
                pl.BlockSpec((None, 2, p, e), lambda j, s: (jnp.minimum(j, s[0]), 0, 0, 0)),
                whole((m, 1)),
                whole((m, 1)),
            ],
            out_specs=[whole((m, e)), whole((m, e)), whole((m, 1))],
            scratch_shapes=[pltpu.VMEM((m, e), F32), pltpu.VMEM((m, 1), F32)],
        ),
        out_shape=[
            jax.ShapeDtypeStruct((m, e), BF16),
            jax.ShapeDtypeStruct((m, e), F32),
            jax.ShapeDtypeStruct((m, 1), F32),
        ],
        compiler_params=params(),
        cost_estimate=pl.CostEstimate(
            flops=4 * m * n * p * e, bytes_accessed=4 * n * p * e, transcendentals=2 * m * n * p
        ),
    )(place, queries, keys_values, query_pos, first_pos)


def attend_back(place, queries, grads, keys_values, inverse, delta, query_pos, first_pos, scale):
    m, e = queries.shape
    n, _, p, _ = keys_values.shape
    step = 256

    def body(
        place_ref, q_ref, g_ref, kv_ref, inv_ref, delta_ref, pos_ref, first_ref, dq_ref, dkv_ref, acc_ref, dk_ref, dv_ref
    ):
        j = pl.program_id(0)

        @pl.when(j == 0)
        def _():
            acc_ref[...] = jnp.zeros_like(acc_ref)

        @pl.when(j <= place_ref[0])
        def _():
            key_pos = key_position(j, p, place_ref[1], (p, 1), 0)
            for r in range(0, m, step):
                rows = pl.ds(r, step)
                raw = mm(kv_ref[0], q_ref[rows, :], NT)
                capped = jnp.tanh(raw * (scale / SOFT_CAP))
                seen = (key_pos >= first_ref[:, rows]) & (key_pos <= pos_ref[:, rows])
                probs = jnp.where(seen, jnp.exp(SOFT_CAP * capped), 0.0) * inv_ref[:, rows]
                grad_probs = mm(kv_ref[1], g_ref[rows, :], NT)
                grad_raw = probs * (grad_probs - delta_ref[:, rows]) * (1.0 - capped * capped)
                grad_low = grad_raw.astype(BF16)
                value_part = mm(probs.astype(BF16), g_ref[rows, :], NN)
                key_part = mm(grad_low, q_ref[rows, :], NN)
                if r == 0:
                    dv_ref[...] = value_part
                    dk_ref[...] = key_part
                else:
                    dv_ref[...] += value_part
                    dk_ref[...] += key_part
                acc_ref[rows, :] += mm(grad_low, kv_ref[0], TN)
            dkv_ref[0] = dk_ref[...].astype(BF16)
            dkv_ref[1] = dv_ref[...].astype(BF16)

        @pl.when(j > place_ref[0])
        def _():
            dkv_ref[...] = jnp.zeros_like(dkv_ref)

        @pl.when(j == n - 1)
        def _():
            dq_ref[...] = (acc_ref[...] * scale).astype(BF16)

    whole = lambda shape: pl.BlockSpec(shape, lambda j, s: (0, 0))
    return pl.pallas_call(
        body,
        grid_spec=pltpu.PrefetchScalarGridSpec(
            num_scalar_prefetch=1,
            grid=(n,),
            in_specs=[
                whole((m, e)),
                whole((m, e)),
                pl.BlockSpec((None, 2, p, e), lambda j, s: (jnp.minimum(j, s[0]), 0, 0, 0)),
                whole((1, m)),
                whole((1, m)),
                whole((1, m)),
                whole((1, m)),
            ],
            out_specs=[whole((m, e)), pl.BlockSpec((None, 2, p, e), lambda j, s: (j, 0, 0, 0))],
            scratch_shapes=[pltpu.VMEM((m, e), F32), pltpu.VMEM((p, e), F32), pltpu.VMEM((p, e), F32)],
        ),
        out_shape=[jax.ShapeDtypeStruct((m, e), BF16), jax.ShapeDtypeStruct((n, 2, p, e), BF16)],
        compiler_params=params(),
        cost_estimate=pl.CostEstimate(
            flops=10 * m * n * p * e, bytes_accessed=8 * n * p * e, transcendentals=2 * m * n * p
        ),
    )(place, queries, grads, keys_values, inverse, delta, query_pos, first_pos)


def gelu_pair(gate):
    outer = math.sqrt(2.0 / math.pi)
    square = gate * gate
    bent = jnp.tanh(outer * gate * (1.0 + 0.044715 * square))
    half = 0.5 * (1.0 + bent)
    slope = half + 0.5 * gate * (1.0 - bent * bent) * outer * (1.0 + 3.0 * 0.044715 * square)
    return gate * half, slope


def feed_forward(rows, cots, blocks):
    t, d = rows.shape
    count, _, c = blocks.shape
    full = (count - 2) // 3
    half = c // 2
    step = 256
    tokens = t // step
    widths = d // step

    def body(x_ref, y_ref, g_ref, u_ref, w_ref, out_ref, dx_ref, dg_ref, du_ref, dw_ref, xt, yt, acc, dacc, hid, gg, gu):
        f = pl.program_id(0)

        @pl.when(f == 0)
        def _():
            acc[...] = jnp.zeros_like(acc)
            dacc[...] = jnp.zeros_like(dacc)

            @pl.loop(0, widths)
            def _(k):
                cols = pl.ds(pl.multiple_of(k * step, step), step)
                xt[cols, :] = x_ref[:, cols].T
                yt[cols, :] = y_ref[:, cols].T

        @pl.when(f < full)
        def _():
            @pl.loop(0, tokens)
            def _(i):
                part = pl.ds(pl.multiple_of(i * step, step), step)
                gate = mm(x_ref[part, :], g_ref[...], NN)
                up = mm(x_ref[part, :], u_ref[...], NN)
                grad = mm(y_ref[part, :], w_ref[...], NN)
                active, slope = gelu_pair(gate)
                hidden = (active * up).astype(BF16)
                grad_gate = (grad * up * slope).astype(BF16)
                grad_up = (grad * active).astype(BF16)
                hid[part, :] = hidden
                gg[part, :] = grad_gate
                gu[part, :] = grad_up
                acc[part, :] += mm(hidden, w_ref[...], NT)
                dacc[part, :] += mm(grad_gate, g_ref[...], NT) + mm(grad_up, u_ref[...], NT)

            @pl.loop(0, widths)
            def _(k):
                cols = pl.ds(pl.multiple_of(k * step, step), step)
                dg_ref[cols, :] = mm(xt[cols, :], gg[...], NN).astype(BF16)
                du_ref[cols, :] = mm(xt[cols, :], gu[...], NN).astype(BF16)
                dw_ref[cols, :] = mm(yt[cols, :], hid[...], NN).astype(BF16)

        @pl.when(f == full)
        def _():
            @pl.loop(0, tokens)
            def _(i):
                part = pl.ds(pl.multiple_of(i * step, step), step)
                both = mm(x_ref[part, :], g_ref[...], NN)
                gate, up = both[:, :half], both[:, half:]
                grad = mm(y_ref[part, :], w_ref[:, :half], NN)
                active, slope = gelu_pair(gate)
                hidden = (active * up).astype(BF16)
                hid[part, :half] = hidden
                gg[part, :half] = (grad * up * slope).astype(BF16)
                gg[part, half:] = (grad * active).astype(BF16)
                acc[part, :] += mm(hidden, w_ref[:, :half], NT)
                dacc[part, :] += mm(gg[part, :], g_ref[...], NT)

            @pl.loop(0, widths)
            def _(k):
                cols = pl.ds(pl.multiple_of(k * step, step), step)
                dg_ref[cols, :] = mm(xt[cols, :], gg[...], NN).astype(BF16)
                dw_ref[cols, :half] = mm(yt[cols, :], hid[:, :half], NN).astype(BF16)
                dw_ref[cols, half:] = jnp.zeros((step, half), BF16)

            out_ref[...] = acc[...].astype(BF16)
            dx_ref[...] = dacc[...].astype(BF16)

    once = pl.Buffered(1)
    gate_at = lambda f: (jnp.where(f < full, f, 3 * full), 0, 0)
    up_at = lambda f: (jnp.where(f < full, full + f, 2 * full - 1), 0, 0)
    down_at = lambda f: (jnp.where(f < full, 2 * full + f, 3 * full + 1), 0, 0)
    block = (None, d, c)
    whole = pl.BlockSpec((t, d), lambda f: (0, 0), pipeline_mode=once)
    gate_out = lambda f: (f, 0, 0)
    up_out = lambda f: (jnp.minimum(f, full - 1), 0, 0)
    return pl.pallas_call(
        body,
        grid=(full + 1,),
        in_specs=[
            whole,
            whole,
            pl.BlockSpec(block, gate_at),
            pl.BlockSpec(block, up_at),
            pl.BlockSpec(block, down_at),
        ],
        out_specs=[
            whole,
            whole,
            pl.BlockSpec(block, gate_out),
            pl.BlockSpec(block, up_out),
            pl.BlockSpec(block, gate_out),
        ],
        out_shape=[
            jax.ShapeDtypeStruct((t, d), BF16),
            jax.ShapeDtypeStruct((t, d), BF16),
            jax.ShapeDtypeStruct((full + 1, d, c), BF16),
            jax.ShapeDtypeStruct((full, d, c), BF16),
            jax.ShapeDtypeStruct((full + 1, d, c), BF16),
        ],
        scratch_shapes=[
            pltpu.VMEM((d, t), BF16),
            pltpu.VMEM((d, t), BF16),
            pltpu.VMEM((t, d), F32),
            pltpu.VMEM((t, d), F32),
            pltpu.VMEM((t, c), BF16),
            pltpu.VMEM((t, c), BF16),
            pltpu.VMEM((t, c), BF16),
        ],
        compiler_params=params(),
        cost_estimate=pl.CostEstimate(
            flops=6 * count * t * d * c, bytes_accessed=4 * count * d * c + 8 * t * d, transcendentals=t * c * full
        ),
    )(rows, cots, blocks, blocks, blocks)


def top(spec, a, b):
    return jnp.einsum(spec, a, b, precision=TOP_PRECISION)


def newton_factor(grams, growth):
    size = grams.shape[-1]
    eye = jnp.eye(size, dtype=F32)
    norm = jnp.sqrt(jnp.sum(grams * eye, axis=(1, 2), keepdims=True))
    inverse = 1.0 / (norm + 1e-07)
    gram = grams * (inverse * inverse)
    factor = None
    for sweep in range(NEWTON_STEPS):
        square = top("bij,bjk->bik", gram, gram)
        poly = NEWTON_LINEAR * eye + NEWTON_SQUARE * gram + NEWTON_CUBIC * square
        factor = poly if sweep == 0 else top("bij,bjk->bik", factor, poly)
        if sweep < NEWTON_STEPS - 1:
            gram = top("bij,bjk->bik", top("bij,bjk->bik", gram, poly), poly)
    return factor * (growth * inverse)


def muon_factors(ring, momentum, growth):
    count, _, c = momentum.shape
    size = ring.size
    cap = -(-count // size)
    grams = top("bre,brf->bef", momentum, momentum)
    grams = jnp.pad(grams, ((0, cap * size - count), (0, 0), (0, 0))).reshape(size, cap * c, c)
    mine = ring.scatter(lambda i: lax.dynamic_index_in_dim(grams, i, 0, keepdims=False))
    factor = newton_factor(mine.reshape(cap, c, c), growth).astype(BF16)
    return ring.gather(factor.reshape(cap * c, c)).reshape(size * cap, c, c)[:count]


def on_device(block_in, cotangent, seq_ids, weights, momentum, gains, gain_first, gain_second):
    tok_rows, model_width = block_in.shape
    rows_dp, group_blocks, head_dim = weights.shape
    head_count = lax.axis_size("head")
    data_count = lax.axis_size("dp")
    group_rows = tok_rows * head_count
    key_heads = KV // head_count
    query_heads = H // head_count
    ffn_blocks = FF // (head_dim * head_count)
    out_mark = query_heads + 2 * key_heads
    gate_mark = out_mark + query_heads
    half_dim = head_dim // 2
    full = ffn_blocks // 2
    scale = head_dim ** (-0.5)
    growth = math.sqrt(max(1.0, model_width / head_dim))
    data_index = lax.axis_index("dp")
    head_index = lax.axis_index("head")
    parity = (data_index >> 1) & 1
    planes = data_count // 2
    ring = Ring()

    weights = jnp.transpose(weights, (1, 0, 2))
    momentum = jnp.transpose(momentum, (1, 0, 2))
    attn_low = weights[:gate_mark].astype(BF16)

    gathered = ring.gather(attn_low[:out_mark])
    qkv_blocks = jnp.transpose(gathered, (1, 0, 2, 3)).reshape(out_mark, model_width, head_dim)
    gathered = ring.gather(attn_low[out_mark:])
    out_blocks = jnp.transpose(gathered, (1, 0, 2, 3)).reshape(query_heads, model_width, head_dim)

    inputs = block_in.astype(F32)
    normed_one, norm_one_back = jax.vjp(rms_scale, inputs, gains[0])
    group_in = head_gather(normed_one.astype(BF16))
    group_cot = wide_gather(cotangent)

    def pack(kinds, side):
        lanes = slice(side * half_dim, (side + 1) * half_dim)
        whole = [kind[side * full : (side + 1) * full] for kind in kinds]
        gate, up, down = (kind[2 * full : 2 * full + 1, :, lanes] for kind in kinds)
        mixed = jnp.concatenate([gate, up], axis=2)
        alone = jnp.concatenate([down, jnp.zeros_like(down)], axis=2)
        return jnp.concatenate(whole + [mixed, alone], axis=0).astype(BF16)

    ffn_weights = weights[gate_mark:]
    kinds = [ffn_weights[k * ffn_blocks : (k + 1) * ffn_blocks] for k in range(3)]
    sides = (pack(kinds, 0), pack(kinds, 1))
    mine = jnp.where(parity == 1, sides[1], sides[0])
    other = jnp.where(parity == 1, sides[0], sides[1])
    pack_count = 3 * full + 2
    ffn_full = jnp.zeros((pack_count, data_count, rows_dp, head_dim), BF16)
    for plane in range(planes):
        send = other if plane & 1 else mine
        piece = mine if plane == 0 else swap(send, "dp", plane << 1)
        far = swap(piece, "dp", 1)
        spot = data_index ^ (plane << 1)
        ffn_full = lax.dynamic_update_index_in_dim(ffn_full, piece, spot, 1)
        ffn_full = lax.dynamic_update_index_in_dim(ffn_full, far, spot ^ 1, 1)
    ffn_full = ffn_full.reshape(pack_count, model_width, head_dim)

    projected = block_project(group_in, qkv_blocks)
    queries = projected[:query_heads].reshape(query_heads * group_rows, head_dim)
    keys_values = ring.gather(projected[query_heads:])
    all_ids = lax.all_gather(seq_ids, ("dp", "head"), axis=0, tiled=True)
    local = jnp.arange(group_rows, dtype=jnp.int32) ^ (head_index * tok_rows)
    query_pos = data_index * group_rows + local
    query_ids = all_ids[query_pos]
    first_pos = jnp.sum((all_ids[None, :] < query_ids[:, None]).astype(jnp.int32), axis=1)
    query_pos = jnp.tile(query_pos, query_heads)
    first_pos = jnp.tile(first_pos, query_heads)
    place = jnp.stack([data_index, head_index * tok_rows]).astype(jnp.int32)
    mixed_low, mixed_full, totals = attend(
        place, queries, keys_values, query_pos[:, None], first_pos[:, None], scale
    )
    mixed_heads = mixed_low.reshape(query_heads, group_rows, head_dim)
    attn_add = head_scatter(block_back(mixed_heads, out_blocks))
    residual = inputs + attn_add
    normed_two, norm_two_back = jax.vjp(rms_scale, residual, gains[1])
    wide_ffn = wide_gather(normed_two.astype(BF16))

    down_part, grad_part, grad_gate, grad_up, grad_down = feed_forward(wide_ffn, group_cot, ffn_full)
    grad_normed_two = wide_scatter(grad_part)
    block_out = (residual + wide_scatter(down_part)).astype(BF16)
    grad_residual_norm, grad_gain_two = norm_two_back(grad_normed_two)
    grad_residual = cotangent.astype(F32) + grad_residual_norm
    group_grad = head_gather(grad_residual.astype(BF16))

    def cut(array):
        return array.reshape(array.shape[0], data_count, rows_dp, head_dim)

    grads = [cut(grad_gate[:full]), cut(grad_up), cut(grad_down[:full]), cut(grad_gate[full:]), cut(grad_down[full:])]

    def rows_of(index):
        return jnp.concatenate(
            [lax.dynamic_index_in_dim(grad, index, 1, keepdims=False) for grad in grads], axis=0
        )

    own_side = None
    other_side = None
    for plane in range(planes - 1, -1, -1):
        spot = data_index ^ (plane << 1)
        arrived = swap(rows_of(spot ^ 1), "dp", 1)
        total = rows_of(spot).astype(F32) + arrived.astype(F32)
        if plane:
            total = swap(total.astype(BF16), "dp", plane << 1).astype(F32)
        if plane & 1:
            other_side = total if other_side is None else other_side + total
        else:
            own_side = total if own_side is None else own_side + total
    low_side = jnp.where(parity == 1, other_side, own_side)
    high_side = jnp.where(parity == 1, own_side, other_side)

    def unpack(kind):
        if kind < 2:
            rest = [side[3 * full, :, kind * half_dim : (kind + 1) * half_dim] for side in (low_side, high_side)]
        else:
            rest = [side[3 * full + 1, :, :half_dim] for side in (low_side, high_side)]
        last = jnp.concatenate(rest, axis=1)[None]
        whole = [side[kind * full : (kind + 1) * full] for side in (low_side, high_side)]
        return jnp.concatenate(whole + [last], axis=0)

    ffn_grads = jnp.concatenate([unpack(0), unpack(1), unpack(2)], axis=0)
    late = 2
    ffn_momentum = MUON_BETA * momentum[gate_mark:] + ffn_grads
    ffn_factors = muon_factors(ring, ffn_momentum[:-late], growth)

    grad_heads = block_project(group_grad, out_blocks)
    grad_mixed = grad_heads.reshape(query_heads * group_rows, head_dim)
    delta = jnp.sum(grad_mixed.astype(F32) * mixed_full, axis=1)
    grad_queries, grad_keys_values = attend_back(
        place,
        queries,
        grad_mixed,
        keys_values,
        1.0 / totals.reshape(1, -1),
        delta[None, :],
        query_pos[None, :],
        first_pos[None, :],
        scale,
    )
    key_value_sums = ring.scatter(lambda i: lax.dynamic_index_in_dim(grad_keys_values, i, 0, keepdims=False))
    grad_projected = jnp.concatenate(
        [
            grad_queries.reshape(query_heads, group_rows, head_dim),
            (key_value_sums[:key_heads] * scale).astype(BF16),
            key_value_sums[key_heads:].astype(BF16),
        ],
        axis=0,
    )
    out_part = block_outer(group_grad, mixed_heads)
    qkv_part = block_outer(group_in, grad_projected)
    out_part = out_part.reshape(query_heads, data_count, rows_dp, head_dim)
    qkv_part = qkv_part.reshape(out_mark, data_count, rows_dp, head_dim)
    qkv_grads = ring.scatter(lambda i: lax.dynamic_index_in_dim(qkv_part, i, 1, keepdims=False))
    out_grads = ring.scatter(lambda i: lax.dynamic_index_in_dim(out_part, i, 1, keepdims=False))
    attn_grads = jnp.concatenate([qkv_grads, out_grads], axis=0)
    attn_momentum = MUON_BETA * momentum[:gate_mark] + attn_grads
    late_momentum = jnp.concatenate([attn_momentum, ffn_momentum[-late:]], axis=0)
    late_factors = muon_factors(ring, late_momentum, growth)

    grad_normed_one = head_scatter(block_back(grad_projected, qkv_blocks))
    grad_input_norm, grad_gain_one = norm_one_back(grad_normed_one)
    grad_input = grad_residual + grad_input_norm
    gain_grads = lax.psum(jnp.stack([grad_gain_one, grad_gain_two]), ("dp", "head"))

    weight_grads = jnp.concatenate([attn_grads, ffn_grads], axis=0)
    new_momentum = jnp.concatenate([attn_momentum, ffn_momentum], axis=0)
    factors = jnp.concatenate([late_factors[:gate_mark], ffn_factors, late_factors[gate_mark:]], axis=0)
    update = jnp.einsum("bre,bef->brf", new_momentum.astype(BF16), factors, preferred_element_type=F32)
    new_weights = weights * (1.0 - MUON_RATE * MUON_DECAY) - MUON_RATE * update

    new_gain_first = BETA_ONE * gain_first + (1.0 - BETA_ONE) * gain_grads
    new_gain_second = BETA_TWO * gain_second + (1.0 - BETA_TWO) * gain_grads * gain_grads
    first_hat = new_gain_first / (1.0 - BETA_ONE**UPDATE_STEP)
    second_hat = new_gain_second / (1.0 - BETA_TWO**UPDATE_STEP)
    new_gains = gains - ADAM_RATE * first_hat / (jnp.sqrt(second_hat) + ADAM_EPS)
    back = lambda array: jnp.transpose(array, (1, 0, 2))
    return (
        block_out,
        grad_input,
        back(weight_grads),
        back(new_momentum),
        back(new_weights),
        gain_grads,
        new_gain_first,
        new_gain_second,
        new_gains,
    )


def solution(mesh):
    return jax.shard_map(
        on_device,
        mesh=mesh,
        in_specs=(
            P(("dp", "head"), None),
            P(("dp", "head"), None),
            P(("dp", "head")),
            P("dp", "head", None),
            P("dp", "head", None),
            P(),
            P(),
            P(),
        ),
        out_specs=(
            P(("dp", "head"), None),
            P(("dp", "head"), None),
            P("dp", "head", None),
            P("dp", "head", None),
            P("dp", "head", None),
            P(),
            P(),
            P(),
            P(),
        ),
        check_vma=False,
    )
```

```python
import functools
import math

import jax
import jax.numpy as jnp
from jax import lax
from jax.experimental import pallas as pl
from jax.experimental.pallas import tpu as pltpu
from jax.sharding import PartitionSpec as P

H = 8
KV = 4
FF = 9216
NEWTON_STEPS = 5
UPDATE_STEP = 10

NORM_EPS = 1e-06
SOFT_CAP = 50.0
MUON_RATE = 0.2
MUON_DECAY = 0.01
MUON_BETA = 0.95
ADAM_RATE = 0.3
BETA_ONE = 0.9
BETA_TWO = 0.95
ADAM_EPS = 1e-08
NEWTON_LINEAR = 3.4445
NEWTON_SQUARE = -4.775
NEWTON_CUBIC = 2.0315
TOP_PRECISION = lax.Precision.HIGHEST

BF16 = jnp.bfloat16
F32 = jnp.float32
VMEM_LIMIT = 62 * 1024 * 1024
NN = (((1,), (0,)), ((), ()))
NT = (((1,), (1,)), ((), ()))
TN = (((0,), (0,)), ((), ()))


def mm(a, b, dims):
    return lax.dot_general(a, b, dims, preferred_element_type=F32)


def rms_scale(rows, gain):
    inverse = lax.rsqrt(jnp.mean(rows * rows, axis=-1, keepdims=True) + NORM_EPS)
    return rows * inverse * gain


class Flow:
    def __init__(self, steps):
        self.steps = steps
        self.value = None
        self.sends = None
        self.advance(None)

    def advance(self, arrived):
        try:
            self.sends = self.steps.send(arrived)
        except StopIteration as stop:
            self.sends = None
            self.value = stop.value


def stage(flows, extra=(), idle=()):
    flows = [flow for flow in flows if flow.sends is not None]
    idle = [flow for flow in idle if flow.sends is not None and flow not in flows]
    arrived = [[lax.ppermute(*send) for send in flow.sends] for flow in flows]
    held = [[send[0] for send in flow.sends] for flow in idle]
    arrived, held, extra = lax.optimization_barrier((arrived, held, list(extra)))
    for flow, got in zip(flows, arrived):
        flow.advance(got)
    for flow, kept in zip(idle, held):
        flow.sends = [(value,) + send[1:] for value, send in zip(kept, flow.sends)]
    return extra


def finish(*flows):
    while any(flow.sends is not None for flow in flows):
        stage(flows)


def swap(value, axis, mask):
    size = lax.axis_size(axis)
    return (value, axis, [(i, i ^ mask) for i in range(size)])


def head_gather(rows):
    (other,) = yield [swap(rows, "head", 2)]
    pair = jnp.stack([rows, other], axis=0)
    (other,) = yield [swap(pair, "head", 1)]
    quad = jnp.stack([pair, other], axis=1)
    return quad.reshape((4 * rows.shape[0],) + rows.shape[1:])


def wide_gather(rows):
    (other,) = yield [swap(rows, "dp", 2)]
    both = jnp.stack([rows, other], axis=0)
    (other,) = yield [swap(both, "head", 2)]
    pair = jnp.stack([both, other], axis=1)
    (other,) = yield [swap(pair, "head", 1)]
    quad = jnp.stack([pair, other], axis=2)
    return quad.reshape((8 * rows.shape[0],) + rows.shape[1:])


def add_low(kept, other):
    return (kept.astype(F32) + other.astype(F32)).astype(BF16)


def head_scatter(part):
    rows = part.shape[0] // 4
    quad = part.reshape(2, 2, rows, -1)
    (other,) = yield [swap(quad[:, 1].astype(BF16), "head", 1)]
    pair = add_low(quad[:, 0], other)
    (other,) = yield [swap(pair[1], "head", 2)]
    return pair[0].astype(F32) + other.astype(F32)


def wide_scatter(part):
    rows = part.shape[0] // 8
    octet = part.reshape(2, 2, 2, rows, -1)
    (other,) = yield [swap(octet[:, :, 1].astype(BF16), "head", 1)]
    quad = add_low(octet[:, :, 0], other)
    (other,) = yield [swap(quad[:, 1], "head", 2)]
    pair = add_low(quad[:, 0], other)
    (other,) = yield [swap(pair[1], "dp", 2)]
    return pair[0].astype(F32) + other.astype(F32)


def total_sum(value):
    for axis in ("head", "dp"):
        mask = 1
        while mask < lax.axis_size(axis):
            (other,) = yield [swap(value, axis, mask)]
            value = value + other
            mask *= 2
    return value


class Ring:
    def __init__(self):
        size = lax.axis_size("dp")
        order = list(range(0, size, 2)) + list(range(size - 1, 0, -2))
        around = [[order[(order.index(i) + offset) % size] for offset in range(size)] for i in range(size)]
        self.size = size
        self.around = jnp.array(around, jnp.int32)[lax.axis_index("dp")]
        self.up = [(order[k], order[(k + 1) % size]) for k in range(size)]
        self.down = [(order[(k + 1) % size], order[k]) for k in range(size)]

    def index(self, offset):
        return self.around[offset % self.size]

    def gather(self, value, mid):
        half = self.size // 2
        zeros = (0,) * (value.ndim - 1)
        out = jnp.zeros((self.size,) + value.shape, value.dtype)
        out = lax.dynamic_update_index_in_dim(out, value, self.index(0), 0)
        ahead, back = value, value
        for step in range(1, half):
            ahead, back = yield [(ahead, "dp", self.up), (back, "dp", self.down)]
            out = lax.dynamic_update_index_in_dim(out, ahead, self.index(-step), 0)
            out = lax.dynamic_update_index_in_dim(out, back, self.index(step), 0)
        first, second = yield [(ahead[:mid], "dp", self.up), (back[mid:], "dp", self.down)]
        far = self.index(half)
        out = lax.dynamic_update_slice(out, first[None], (far, 0) + zeros)
        return lax.dynamic_update_slice(out, second[None], (far, mid) + zeros)

    def scatter(self, take, mid):
        half = self.size // 2
        far = take(self.index(half))
        kind = far.dtype
        up, down = yield [(far[:mid], "dp", self.up), (far[mid:], "dp", self.down)]
        for step in range(half - 1, 0, -1):
            part = take(self.index(step)).astype(F32)
            ahead = jnp.concatenate([part[:mid] + up, part[mid:]]) if step == half - 1 else part + up
            part = take(self.index(-step)).astype(F32)
            back = jnp.concatenate([part[:mid], part[mid:] + down]) if step == half - 1 else part + down
            up, down = yield [(ahead.astype(kind), "dp", self.up), (back.astype(kind), "dp", self.down)]
        return take(self.index(0)).astype(F32) + up.astype(F32) + down.astype(F32)


def plane_groups():
    planes = lax.axis_size("dp") // 2
    offsets = list(range(planes - 1, 0, -2)) + list(range(planes - 2, -1, -2))
    return [offsets[k : k + 2] for k in range(0, planes, 2)]


def spread_blocks(mine, other):
    me = lax.axis_index("dp")
    size = lax.axis_size("dp")
    count, rows, c = mine.shape
    out = jnp.zeros((count, size, rows, c), mine.dtype)
    ready = [(0, mine)]
    for group in plane_groups():
        offsets = [offset for offset in group if offset]
        sends = [swap(other if offset & 1 else mine, "dp", offset << 1) for offset in offsets]
        arrived = yield sends + [swap(piece, "dp", 1) for _, piece in ready]
        for (offset, piece), far in zip(ready, arrived[len(sends) :]):
            out = lax.dynamic_update_index_in_dim(out, piece, me ^ (offset << 1), 1)
            out = lax.dynamic_update_index_in_dim(out, far, me ^ (offset << 1) ^ 1, 1)
        ready = list(zip(offsets, arrived))
    arrived = yield [swap(piece, "dp", 1) for _, piece in ready]
    for (offset, piece), far in zip(ready, arrived):
        out = lax.dynamic_update_index_in_dim(out, piece, me ^ (offset << 1), 1)
        out = lax.dynamic_update_index_in_dim(out, far, me ^ (offset << 1) ^ 1, 1)
    return out.reshape(count, size * rows, c)


def reduce_blocks(take):
    me = lax.axis_index("dp")
    sums = [None, None]
    ready = []
    for group in plane_groups() + [[]]:
        sends = [swap(take(me ^ (offset << 1) ^ 1), "dp", 1) for offset in group]
        moves = [(offset, total) for offset, total in ready if offset]
        arrived = yield sends + [swap(total.astype(BF16), "dp", offset << 1) for offset, total in moves]
        for offset, total in [(0, total) for offset, total in ready if not offset] + [
            (offset, got) for (offset, _), got in zip(moves, arrived[len(sends) :])
        ]:
            side = offset & 1
            total = total.astype(F32)
            sums[side] = total if sums[side] is None else sums[side] + total
        ready = [
            (offset, take(me ^ (offset << 1)).astype(F32) + got.astype(F32)) for offset, got in zip(group, arrived)
        ]
    return sums


def params(**more):
    return pltpu.CompilerParams(vmem_limit_bytes=VMEM_LIMIT, **more)


def block_project(rows, blocks):
    t = rows.shape[0]
    count, d, c = blocks.shape

    def body(x_ref, w_ref, o_ref):
        o_ref[...] = mm(x_ref[...], w_ref[...], NN).astype(BF16)

    return pl.pallas_call(
        body,
        grid=(count,),
        in_specs=[
            pl.BlockSpec((t, d), lambda b: (0, 0)),
            pl.BlockSpec((None, d, c), lambda b: (b, 0, 0)),
        ],
        out_specs=pl.BlockSpec((None, t, c), lambda b: (b, 0, 0)),
        out_shape=jax.ShapeDtypeStruct((count, t, c), BF16),
        compiler_params=params(),
        cost_estimate=pl.CostEstimate(
            flops=2 * count * t * d * c, bytes_accessed=2 * (t * d + count * (d * c + t * c)), transcendentals=0
        ),
    )(rows, blocks)


def block_back(cols, blocks):
    count, t, c = cols.shape
    d = blocks.shape[1]

    def body(x_ref, w_ref, o_ref, acc_ref):
        b = pl.program_id(0)

        @pl.when(b == 0)
        def _():
            acc_ref[...] = jnp.zeros_like(acc_ref)

        acc_ref[...] += mm(x_ref[...], w_ref[...], NT)

        @pl.when(b == count - 1)
        def _():
            o_ref[...] = acc_ref[...].astype(BF16)

    return pl.pallas_call(
        body,
        grid=(count,),
        in_specs=[
            pl.BlockSpec((None, t, c), lambda b: (b, 0, 0)),
            pl.BlockSpec((None, d, c), lambda b: (b, 0, 0)),
        ],
        out_specs=pl.BlockSpec((t, d), lambda b: (0, 0)),
        out_shape=jax.ShapeDtypeStruct((t, d), BF16),
        scratch_shapes=[pltpu.VMEM((t, d), F32)],
        compiler_params=params(),
        cost_estimate=pl.CostEstimate(
            flops=2 * count * t * d * c, bytes_accessed=2 * (t * d + count * (d * c + t * c)), transcendentals=0
        ),
    )(cols, blocks)


def block_outer(rows, cols, d):
    t = rows.shape[0]
    count, _, c = cols.shape

    def body(x_ref, y_ref, o_ref, xt_ref):
        @pl.when(pl.program_id(0) == 0)
        def _():
            xt_ref[...] = x_ref[...].T

        o_ref[...] = mm(xt_ref[...], y_ref[...], NN).astype(BF16)

    return pl.pallas_call(
        body,
        grid=(count,),
        in_specs=[
            pl.BlockSpec((t, d), lambda b: (0, 0)),
            pl.BlockSpec((None, t, c), lambda b: (b, 0, 0)),
        ],
        out_specs=pl.BlockSpec((None, d, c), lambda b: (b, 0, 0)),
        out_shape=jax.ShapeDtypeStruct((count, d, c), BF16),
        scratch_shapes=[pltpu.VMEM((d, t), BF16)],
        compiler_params=params(),
        cost_estimate=pl.CostEstimate(
            flops=2 * count * t * d * c, bytes_accessed=2 * (t * d + count * (d * c + t * c)), transcendentals=0
        ),
    )(rows, cols)


def key_position(block, width, head_shift, shape, axis):
    local = lax.broadcasted_iota(jnp.int32, shape, axis)
    return block * width + jnp.bitwise_xor(local, head_shift)


def attend(place, queries, keys_values, query_pos, first_pos, scale, p):
    m, e = queries.shape
    n = keys_values.shape[0]
    step = 256

    def body(place_ref, q_ref, kv_ref, pos_ref, first_ref, low_ref, full_ref, sum_ref, acc_ref, tot_ref):
        j = pl.program_id(0)

        @pl.when(j == 0)
        def _():
            acc_ref[...] = jnp.zeros_like(acc_ref)
            tot_ref[...] = jnp.zeros_like(tot_ref)

        @pl.when(j <= place_ref[0])
        def _():
            key_pos = key_position(j, p, place_ref[1], (1, p), 1)
            for r in range(0, m, step):
                rows = pl.ds(r, step)
                raw = mm(q_ref[rows, :], kv_ref[:p, :], NT)
                soft = SOFT_CAP * jnp.tanh(raw * (scale / SOFT_CAP))
                seen = (key_pos >= first_ref[rows, :]) & (key_pos <= pos_ref[rows, :])
                terms = jnp.where(seen, jnp.exp(soft), 0.0)
                tot_ref[rows, :] += jnp.sum(terms, axis=1, keepdims=True)
                acc_ref[rows, :] += mm(terms.astype(BF16), kv_ref[p:, :], NN)

        @pl.when(j == n - 1)
        def _():
            total = tot_ref[...]
            mixed = acc_ref[...] / total
            full_ref[...] = mixed
            low_ref[...] = mixed.astype(BF16)
            sum_ref[...] = total

    whole = lambda shape: pl.BlockSpec(shape, lambda j, s: (0, 0))
    return pl.pallas_call(
        body,
        grid_spec=pltpu.PrefetchScalarGridSpec(
            num_scalar_prefetch=1,
            grid=(n,),
            in_specs=[
                whole((m, e)),
                pl.BlockSpec((None, 2 * p, e), lambda j, s: (jnp.minimum(j, s[0]), 0, 0)),
                whole((m, 1)),
                whole((m, 1)),
            ],
            out_specs=[whole((m, e)), whole((m, e)), whole((m, 1))],
            scratch_shapes=[pltpu.VMEM((m, e), F32), pltpu.VMEM((m, 1), F32)],
        ),
        out_shape=[
            jax.ShapeDtypeStruct((m, e), BF16),
            jax.ShapeDtypeStruct((m, e), F32),
            jax.ShapeDtypeStruct((m, 1), F32),
        ],
        compiler_params=params(),
        cost_estimate=pl.CostEstimate(
            flops=4 * m * n * p * e, bytes_accessed=4 * n * p * e, transcendentals=2 * m * n * p
        ),
    )(place, queries, keys_values, query_pos, first_pos)


def attend_back(place, queries, grads, keys_values, inverse, delta, query_pos, first_pos, scale, p):
    m, e = queries.shape
    n = keys_values.shape[0]
    step = 256

    def body(
        place_ref, q_ref, g_ref, kv_ref, inv_ref, delta_ref, pos_ref, first_ref, dq_ref, dkv_ref, acc_ref, dk_ref, dv_ref
    ):
        j = pl.program_id(0)

        @pl.when(j == 0)
        def _():
            acc_ref[...] = jnp.zeros_like(acc_ref)

        @pl.when(j <= place_ref[0])
        def _():
            key_pos = key_position(j, p, place_ref[1], (p, 1), 0)
            for r in range(0, m, step):
                rows = pl.ds(r, step)
                raw = mm(kv_ref[:p, :], q_ref[rows, :], NT)
                capped = jnp.tanh(raw * (scale / SOFT_CAP))
                seen = (key_pos >= first_ref[:, rows]) & (key_pos <= pos_ref[:, rows])
                probs = jnp.where(seen, jnp.exp(SOFT_CAP * capped), 0.0) * inv_ref[:, rows]
                grad_probs = mm(kv_ref[p:, :], g_ref[rows, :], NT)
                grad_raw = probs * (grad_probs - delta_ref[:, rows]) * (1.0 - capped * capped)
                grad_low = grad_raw.astype(BF16)
                value_part = mm(probs.astype(BF16), g_ref[rows, :], NN)
                key_part = mm(grad_low, q_ref[rows, :], NN)
                if r == 0:
                    dv_ref[...] = value_part
                    dk_ref[...] = key_part
                else:
                    dv_ref[...] += value_part
                    dk_ref[...] += key_part
                acc_ref[rows, :] += mm(grad_low, kv_ref[:p, :], TN)
            dkv_ref[0] = dk_ref[...].astype(BF16)
            dkv_ref[1] = dv_ref[...].astype(BF16)

        @pl.when(j > place_ref[0])
        def _():
            dkv_ref[...] = jnp.zeros_like(dkv_ref)

        @pl.when(j == n - 1)
        def _():
            dq_ref[...] = (acc_ref[...] * scale).astype(BF16)

    whole = lambda shape: pl.BlockSpec(shape, lambda j, s: (0, 0))
    return pl.pallas_call(
        body,
        grid_spec=pltpu.PrefetchScalarGridSpec(
            num_scalar_prefetch=1,
            grid=(n,),
            in_specs=[
                whole((m, e)),
                whole((m, e)),
                pl.BlockSpec((None, 2 * p, e), lambda j, s: (jnp.minimum(j, s[0]), 0, 0)),
                whole((1, m)),
                whole((1, m)),
                whole((1, m)),
                whole((1, m)),
            ],
            out_specs=[whole((m, e)), pl.BlockSpec((None, 2, p, e), lambda j, s: (j, 0, 0, 0))],
            scratch_shapes=[pltpu.VMEM((m, e), F32), pltpu.VMEM((p, e), F32), pltpu.VMEM((p, e), F32)],
        ),
        out_shape=[jax.ShapeDtypeStruct((m, e), BF16), jax.ShapeDtypeStruct((n, 2, p, e), BF16)],
        compiler_params=params(),
        cost_estimate=pl.CostEstimate(
            flops=10 * m * n * p * e, bytes_accessed=8 * n * p * e, transcendentals=2 * m * n * p
        ),
    )(place, queries, grads, keys_values, inverse, delta, query_pos, first_pos)


def gelu_pair(gate):
    outer = math.sqrt(2.0 / math.pi)
    square = gate * gate
    bent = jnp.tanh(outer * gate * (1.0 + 0.044715 * square))
    half = 0.5 * (1.0 + bent)
    slope = half + 0.5 * gate * (1.0 - bent * bent) * outer * (1.0 + 3.0 * 0.044715 * square)
    return gate * half, slope


def feed_forward(rows, cots, blocks, split):
    t, d = rows.shape
    count, _, c = blocks.shape
    extra = 1 if split else 0
    full = (count - 2 * extra) // 3
    half = c // 2
    step = min(512, t)
    wide = d // 3

    def body(x_ref, y_ref, g_ref, u_ref, w_ref, out_ref, dx_ref, dg_ref, du_ref, dw_ref, xt, yt, acc, dacc, hid, gg, gu, sems):
        f = pl.program_id(0)

        @pl.when(f == 0)
        def _():
            acc[...] = jnp.zeros_like(acc)
            dacc[...] = jnp.zeros_like(dacc)

            @pl.loop(0, d // c)
            def _(k):
                cols = pl.ds(pl.multiple_of(k * c, c), c)
                xt[cols, :] = x_ref[:, cols].T
                yt[cols, :] = y_ref[:, cols].T

        @pl.when(f < full)
        def _():
            @pl.loop(0, t // step)
            def _(i):
                part = pl.ds(pl.multiple_of(i * step, step), step)
                gate = mm(x_ref[part, :], g_ref[...], NN)
                up = mm(x_ref[part, :], u_ref[...], NN)
                grad = mm(y_ref[part, :], w_ref[...], NN)
                active, slope = gelu_pair(gate)
                hid[part, :] = (active * up).astype(BF16)
                gg[part, :] = (grad * up * slope).astype(BF16)
                gu[part, :] = (grad * active).astype(BF16)

                @pl.loop(0, d // wide)
                def _(k):
                    cols = pl.ds(pl.multiple_of(k * wide, wide), wide)
                    acc[part, cols] += mm(hid[part, :], w_ref[cols, :], NT)
                    dacc[part, cols] += mm(gg[part, :], g_ref[cols, :], NT) + mm(gu[part, :], u_ref[cols, :], NT)

            @pl.loop(0, d // wide)
            def _(k):
                cols = pl.ds(pl.multiple_of(k * wide, wide), wide)
                dg_ref[cols, :] = mm(xt[cols, :], gg[...], NN).astype(BF16)
                du_ref[cols, :] = mm(xt[cols, :], gu[...], NN).astype(BF16)
                dw_ref[cols, :] = mm(yt[cols, :], hid[...], NN).astype(BF16)

        if split:

            @pl.when(f == full)
            def _():
                @pl.loop(0, t // step)
                def _(i):
                    part = pl.ds(pl.multiple_of(i * step, step), step)
                    both = mm(x_ref[part, :], g_ref[...], NN)
                    gate, up = both[:, :half], both[:, half:]
                    grad = mm(y_ref[part, :], w_ref[:, :half], NN)
                    active, slope = gelu_pair(gate)
                    hid[part, :half] = (active * up).astype(BF16)
                    gg[part, :half] = (grad * up * slope).astype(BF16)
                    gg[part, half:] = (grad * active).astype(BF16)

                    @pl.loop(0, d // wide)
                    def _(k):
                        cols = pl.ds(pl.multiple_of(k * wide, wide), wide)
                        acc[part, cols] += mm(hid[part, :half], w_ref[cols, :half], NT)
                        dacc[part, cols] += mm(gg[part, :], g_ref[cols, :], NT)

                @pl.loop(0, d // wide)
                def _(k):
                    cols = pl.ds(pl.multiple_of(k * wide, wide), wide)
                    dg_ref[cols, :] = mm(xt[cols, :], gg[...], NN).astype(BF16)
                    dw_ref[cols, :half] = mm(yt[cols, :], hid[:, :half], NN).astype(BF16)
                    dw_ref[cols, half:] = jnp.zeros((wide, half), BF16)

        @pl.when(f == full + extra - 1)
        def _():
            spare = (hid, gg, gu)
            copies = []
            for k in range(2 * (d // c)):
                total, target = ((acc, out_ref), (dacc, dx_ref))[k % 2]
                cols = pl.ds((k // 2) * c, c)
                if k >= 3:
                    copies[k - 3].wait()
                spare[k % 3][...] = total[:, cols].astype(BF16)
                copies.append(pltpu.make_async_copy(spare[k % 3], target.at[:, cols], sems.at[k % 3]))
                copies[k].start()
            for copy in copies[-3:]:
                copy.wait()

    once = pl.Buffered(1)
    gate_at = lambda f: (jnp.where(f < full, f, 3 * full), 0, 0)
    up_at = lambda f: (jnp.where(f < full, full + f, 2 * full - 1), 0, 0)
    down_at = lambda f: (jnp.where(f < full, 2 * full + f, 3 * full + 1), 0, 0)
    block = (None, d, c)
    whole = pl.BlockSpec((t, d), lambda f: (0, 0), pipeline_mode=once)
    apart = pl.BlockSpec(memory_space=pl.ANY)
    gate_out = lambda f: (f, 0, 0)
    up_out = lambda f: (jnp.minimum(f, full - 1), 0, 0)
    return pl.pallas_call(
        body,
        grid=(full + extra,),
        in_specs=[
            whole,
            whole,
            pl.BlockSpec(block, gate_at),
            pl.BlockSpec(block, up_at),
            pl.BlockSpec(block, down_at),
        ],
        out_specs=[
            apart,
            apart,
            pl.BlockSpec(block, gate_out),
            pl.BlockSpec(block, up_out),
            pl.BlockSpec(block, gate_out),
        ],
        out_shape=[
            jax.ShapeDtypeStruct((t, d), BF16),
            jax.ShapeDtypeStruct((t, d), BF16),
            jax.ShapeDtypeStruct((full + extra, d, c), BF16),
            jax.ShapeDtypeStruct((full, d, c), BF16),
            jax.ShapeDtypeStruct((full + extra, d, c), BF16),
        ],
        scratch_shapes=[
            pltpu.VMEM((d, t), BF16),
            pltpu.VMEM((d, t), BF16),
            pltpu.VMEM((t, d), F32),
            pltpu.VMEM((t, d), F32),
            pltpu.VMEM((t, c), BF16),
            pltpu.VMEM((t, c), BF16),
            pltpu.VMEM((t, c), BF16),
            pltpu.SemaphoreType.DMA((3,)),
        ],
        compiler_params=params(),
        cost_estimate=pl.CostEstimate(
            flops=6 * count * t * d * c, bytes_accessed=4 * count * d * c + 8 * t * d, transcendentals=t * c * full
        ),
    )(rows, cots, blocks, blocks, blocks)


def top(spec, a, b):
    return jnp.einsum(spec, a, b, precision=TOP_PRECISION)


def newton_factor(grams, growth):
    size = grams.shape[-1]
    eye = jnp.eye(size, dtype=F32)
    norm = jnp.sqrt(jnp.sum(grams * eye, axis=(1, 2), keepdims=True))
    inverse = 1.0 / (norm + 1e-07)
    gram = grams * (inverse * inverse)
    factor = None
    for sweep in range(NEWTON_STEPS):
        square = top("bij,bjk->bik", gram, gram)
        poly = NEWTON_LINEAR * eye + NEWTON_SQUARE * gram + NEWTON_CUBIC * square
        factor = poly if sweep == 0 else top("bij,bjk->bik", factor, poly)
        if sweep < NEWTON_STEPS - 1:
            gram = top("bij,bjk->bik", top("bij,bjk->bik", gram, poly), poly)
    return factor * (growth * inverse)


def fold(squares):
    h = squares.shape[1] // 2
    return jnp.stack([squares[:, :h, :h], squares[:, :h, h:], squares[:, h:, h:]], axis=1)


def unfold(parts):
    first, off, last = parts[:, 0], parts[:, 1], parts[:, 2]
    upper = jnp.concatenate([first, off], axis=2)
    lower = jnp.concatenate([jnp.swapaxes(off, 1, 2), last], axis=2)
    return jnp.concatenate([upper, lower], axis=1)


def gram_sums(ring, momentum):
    count, _, c = momentum.shape
    size = ring.size
    cap = -(-count // size)
    grams = fold(top("bre,brf->bef", momentum, momentum))
    grams = jnp.pad(grams, ((0, cap * size - count), (0, 0), (0, 0), (0, 0))).reshape(size, 3 * cap, c // 2, c // 2)
    mine = yield from ring.scatter(lambda i: lax.dynamic_index_in_dim(grams, i, 0, keepdims=False), 3 * cap // 2)
    return unfold(mine.reshape(cap, 3, c // 2, c // 2))


def all_factors(ring, factors, count):
    cap, c, _ = factors.shape
    parts = fold(factors.astype(BF16)).reshape(3 * cap, c // 2, c // 2)
    parts = yield from ring.gather(parts, 3 * cap // 2)
    return unfold(parts.reshape(ring.size * cap, 3, c // 2, c // 2)[:count])


def on_device(block_in, cotangent, seq_ids, weights, momentum, gains, gain_first, gain_second):
    tok_rows, model_width = block_in.shape
    rows_dp, group_blocks, head_dim = weights.shape
    head_count = lax.axis_size("head")
    data_count = lax.axis_size("dp")
    group_rows = tok_rows * head_count
    key_heads = KV // head_count
    query_heads = H // head_count
    ffn_blocks = FF // (head_dim * head_count)
    out_mark = query_heads + 2 * key_heads
    gate_mark = out_mark + query_heads
    half_dim = head_dim // 2
    full = ffn_blocks // 2
    scale = head_dim ** (-0.5)
    growth = math.sqrt(max(1.0, model_width / head_dim))
    data_index = lax.axis_index("dp")
    head_index = lax.axis_index("head")
    parity = (data_index >> 1) & 1
    ring = Ring()

    weights = jnp.transpose(weights, (1, 0, 2))
    momentum = jnp.transpose(momentum, (1, 0, 2))
    attn_low = weights[:gate_mark].astype(BF16)
    inputs = block_in.astype(F32)
    normed_one, norm_one_back = jax.vjp(rms_scale, inputs, gains[0])
    ids_column = jnp.pad(seq_ids.astype(BF16)[:, None], ((0, 0), (0, 127)))

    early = full - 1
    kinds = [weights[gate_mark + k * ffn_blocks : gate_mark + (k + 1) * ffn_blocks] for k in range(3)]

    def pack_early(side):
        return jnp.concatenate([kind[side * full : side * full + early] for kind in kinds], axis=0)

    def pack_late(side):
        lanes = slice(side * half_dim, (side + 1) * half_dim)
        whole = [kind[side * full + early : (side + 1) * full] for kind in kinds]
        gate, up, down = (kind[2 * full : 2 * full + 1, :, lanes] for kind in kinds)
        mixed = jnp.concatenate([gate, up], axis=2)
        alone = jnp.concatenate([down, jnp.zeros_like(down)], axis=2)
        return jnp.concatenate(whole + [mixed, alone], axis=0)

    def own_and_other(pack):
        sides = (pack(0).astype(BF16), pack(1).astype(BF16))
        return jnp.where(parity == 1, sides[1], sides[0]), jnp.where(parity == 1, sides[0], sides[1])

    qkv_ring = Flow(ring.gather(attn_low[:out_mark], out_mark // 2))
    group_flow = Flow(head_gather(jnp.concatenate([normed_one.astype(BF16), ids_column], axis=1)))
    cot_flow = Flow(wide_gather(cotangent))
    stage([qkv_ring, group_flow], idle=[cot_flow])
    spread = [Flow(spread_blocks(*own_and_other(pack))) for pack in (pack_early, pack_late)]
    stage([qkv_ring, group_flow], idle=[cot_flow] + spread)
    stage([qkv_ring, cot_flow], idle=spread)
    stage([qkv_ring, cot_flow], idle=spread)
    finish(qkv_ring)
    group_in = group_flow.value
    qkv_blocks = jnp.transpose(qkv_ring.value, (1, 0, 2, 3)).reshape(out_mark, model_width, head_dim)
    (projected,) = stage([spread[0], cot_flow], [block_project(group_in, qkv_blocks)], idle=spread)
    group_cot = cot_flow.value
    queries = projected[:query_heads].reshape(query_heads * group_rows, head_dim)
    group_ids = group_in[:, model_width]
    kv_rows = 2 * key_heads * group_rows
    out_rows = query_heads * rows_dp
    id_rows = group_rows // head_dim
    packed = jnp.concatenate(
        [
            projected[query_heads:].reshape(kv_rows, head_dim),
            attn_low[out_mark:].reshape(out_rows, head_dim),
            jnp.pad(group_ids.reshape(id_rows, head_dim), ((0, 16 - id_rows), (0, 0))),
        ],
        axis=0,
    )
    key_ring = Flow(ring.gather(packed, packed.shape[0] // 32 * 16))
    while key_ring.sends is not None:
        stage([key_ring], idle=spread)
    keys_values = key_ring.value
    out_blocks = keys_values[:, kv_rows : kv_rows + out_rows].reshape(data_count, query_heads, rows_dp, head_dim)
    out_blocks = jnp.transpose(out_blocks, (1, 0, 2, 3)).reshape(query_heads, model_width, head_dim)
    all_ids = keys_values[:, kv_rows + out_rows : kv_rows + out_rows + id_rows].reshape(-1)

    local = jnp.arange(group_rows, dtype=jnp.int32) ^ (head_index * tok_rows)
    query_pos = data_index * group_rows + local
    first_pos = jnp.sum((all_ids[None, :] < group_ids[:, None]).astype(jnp.int32), axis=1)
    query_pos = jnp.tile(query_pos, query_heads)
    first_pos = jnp.tile(first_pos, query_heads)
    place = jnp.stack([data_index, head_index * tok_rows]).astype(jnp.int32)
    mixed_low, mixed_full, totals = attend(
        place, queries, keys_values, query_pos[:, None], first_pos[:, None], scale, group_rows
    )
    mixed_heads = mixed_low.reshape(query_heads, group_rows, head_dim)
    mixed_heads, mixed_full, totals, attn_part = stage(
        [spread[0]], [mixed_heads, mixed_full, totals, block_back(mixed_heads, out_blocks)], idle=spread
    )
    attn_flow = Flow(head_scatter(attn_part))
    stage([attn_flow], idle=spread)
    stage([attn_flow, spread[0]], idle=spread)
    finish(spread[0])
    residual = inputs + attn_flow.value
    normed_two, norm_two_back = jax.vjp(rms_scale, residual, gains[1])
    wide_flow = Flow(wide_gather(normed_two.astype(BF16)))
    stage([wide_flow, spread[1]])
    stage([wide_flow, spread[1]])
    finish(wide_flow)
    wide_ffn = wide_flow.value

    outs = stage([spread[1]], feed_forward(wide_ffn, group_cot, spread[0].value, False))
    finish(spread[1])
    down_early, dx_early, *grads_early = outs

    def taker(grads):
        cuts = [grad.reshape(grad.shape[0], data_count, rows_dp, head_dim) for grad in grads]

        def take(index):
            return jnp.concatenate([lax.dynamic_index_in_dim(cut, index, 1, keepdims=False) for cut in cuts], axis=0)

        return take

    reduce = [Flow(reduce_blocks(taker(grads_early)))]
    outs = stage([reduce[0]], feed_forward(wide_ffn, group_cot, spread[1].value, True))
    down_late, dx_late, grad_gate, grad_up, grad_down = outs
    reduce.append(Flow(reduce_blocks(taker([grad_gate[:1], grad_up, grad_down[:1], grad_gate[1:], grad_down[1:]]))))
    dx_flow = Flow(wide_scatter(dx_early.astype(F32) + dx_late.astype(F32)))
    out_flow = Flow(wide_scatter(down_early.astype(F32) + down_late.astype(F32)))
    stage([dx_flow], idle=reduce + [out_flow])
    stage([dx_flow, reduce[0]], idle=reduce + [out_flow])
    stage([dx_flow], idle=reduce + [out_flow])
    grad_residual_norm, grad_gain_two = norm_two_back(dx_flow.value)
    grad_residual = cotangent.astype(F32) + grad_residual_norm
    grad_flow = Flow(head_gather(grad_residual.astype(BF16)))
    stage([grad_flow] + reduce, idle=[out_flow])
    stage([grad_flow, out_flow], idle=reduce)
    finish(reduce[0])
    group_grad = grad_flow.value

    grad_heads = block_project(group_grad, out_blocks)
    grad_mixed = grad_heads.reshape(query_heads * group_rows, head_dim)
    delta = jnp.sum(grad_mixed.astype(F32) * mixed_full, axis=1)
    grad_queries, grad_keys_values = attend_back(
        place,
        queries,
        grad_mixed,
        keys_values,
        1.0 / totals.reshape(1, -1),
        delta[None, :],
        query_pos[None, :],
        first_pos[None, :],
        scale,
        group_rows,
    )
    grad_queries, grad_keys_values = stage([reduce[1], out_flow], [grad_queries, grad_keys_values])
    key_flow = Flow(
        ring.scatter(lambda i: lax.dynamic_index_in_dim(grad_keys_values, i, 0, keepdims=False), key_heads)
    )
    stage([key_flow, out_flow], idle=reduce)
    finish(out_flow)
    block_out = (residual + out_flow.value).astype(BF16)
    while key_flow.sends is not None:
        stage([key_flow], idle=reduce)
    key_value_sums = key_flow.value
    grad_projected = jnp.concatenate(
        [
            grad_queries.reshape(query_heads, group_rows, head_dim),
            (key_value_sums[:key_heads] * scale).astype(BF16),
            key_value_sums[key_heads:].astype(BF16),
        ],
        axis=0,
    )
    qkv_part, out_part, attn_dx = stage(
        [reduce[1]],
        [
            block_outer(group_in, grad_projected, model_width),
            block_outer(group_grad, mixed_heads, model_width),
            block_back(grad_projected, qkv_blocks),
        ],
    )
    finish(reduce[1])

    own_early, other_early = reduce[0].value
    own_late, other_late = reduce[1].value
    pick = lambda own, other: (jnp.where(parity == 1, other, own), jnp.where(parity == 1, own, other))
    sides_early, sides_late = pick(own_early, other_early), pick(own_late, other_late)

    def unpack(kind):
        if kind < 2:
            rest = [side[3, :, kind * half_dim : (kind + 1) * half_dim] for side in sides_late]
        else:
            rest = [side[4, :, :half_dim] for side in sides_late]
        parts = []
        for first, second in zip(sides_early, sides_late):
            parts += [first[kind * early : (kind + 1) * early], second[kind : kind + 1]]
        return jnp.concatenate(parts + [jnp.concatenate(rest, axis=1)[None]], axis=0)

    ffn_grads = jnp.concatenate([unpack(0), unpack(1), unpack(2)], axis=0)
    late = 2
    ffn_momentum = MUON_BETA * momentum[gate_mark:] + ffn_grads
    gram_flow = Flow(gram_sums(ring, ffn_momentum[:-late]))

    attn_part = jnp.concatenate([qkv_part, out_part], axis=0).reshape(gate_mark, data_count, rows_dp, head_dim)
    weight_flow = Flow(
        ring.scatter(lambda i: lax.dynamic_index_in_dim(attn_part, i, 1, keepdims=False), gate_mark // 2)
    )
    last_flow = Flow(head_scatter(attn_dx))
    while weight_flow.sends is not None:
        stage([weight_flow, gram_flow, last_flow])
    finish(last_flow, gram_flow)
    grad_input_norm, grad_gain_one = norm_one_back(last_flow.value)
    grad_input = grad_residual + grad_input_norm
    gain_flow = Flow(total_sum(jnp.stack([grad_gain_one, grad_gain_two])))
    attn_grads = weight_flow.value
    attn_momentum = MUON_BETA * momentum[:gate_mark] + attn_grads
    late_momentum = jnp.concatenate([attn_momentum, ffn_momentum[-late:]], axis=0)
    late_gram_flow = Flow(gram_sums(ring, late_momentum))
    factor_flow = Flow(all_factors(ring, newton_factor(gram_flow.value, growth), ffn_momentum.shape[0] - late))
    while late_gram_flow.sends is not None:
        stage([late_gram_flow, factor_flow, gain_flow])
    finish(factor_flow)
    late_factor_flow = Flow(
        all_factors(ring, newton_factor(late_gram_flow.value, growth), late_momentum.shape[0])
    )
    finish(late_factor_flow, gain_flow)
    gain_grads = gain_flow.value
    ffn_factors, late_factors = factor_flow.value, late_factor_flow.value

    weight_grads = jnp.concatenate([attn_grads, ffn_grads], axis=0)
    new_momentum = jnp.concatenate([attn_momentum, ffn_momentum], axis=0)
    factors = jnp.concatenate([late_factors[:gate_mark], ffn_factors, late_factors[gate_mark:]], axis=0)
    update = jnp.einsum("bre,bef->brf", new_momentum.astype(BF16), factors, preferred_element_type=F32)
    new_weights = weights * (1.0 - MUON_RATE * MUON_DECAY) - MUON_RATE * update

    new_gain_first = BETA_ONE * gain_first + (1.0 - BETA_ONE) * gain_grads
    new_gain_second = BETA_TWO * gain_second + (1.0 - BETA_TWO) * gain_grads * gain_grads
    first_hat = new_gain_first / (1.0 - BETA_ONE**UPDATE_STEP)
    second_hat = new_gain_second / (1.0 - BETA_TWO**UPDATE_STEP)
    new_gains = gains - ADAM_RATE * first_hat / (jnp.sqrt(second_hat) + ADAM_EPS)
    back = lambda array: jnp.transpose(array, (1, 0, 2))
    return (
        block_out,
        grad_input,
        back(weight_grads),
        back(new_momentum),
        back(new_weights),
        gain_grads,
        new_gain_first,
        new_gain_second,
        new_gains,
    )


def solution(mesh):
    return jax.shard_map(
        on_device,
        mesh=mesh,
        in_specs=(
            P(("dp", "head"), None),
            P(("dp", "head"), None),
            P(("dp", "head")),
            P("dp", "head", None),
            P("dp", "head", None),
            P(),
            P(),
            P(),
        ),
        out_specs=(
            P(("dp", "head"), None),
            P(("dp", "head"), None),
            P("dp", "head", None),
            P("dp", "head", None),
            P("dp", "head", None),
            P(),
            P(),
            P(),
            P(),
        ),
        check_vma=False,
    )
```

```python
import functools
import math

import jax
import jax.numpy as jnp
from jax import lax
from jax.experimental import pallas as pl
from jax.experimental.pallas import tpu as pltpu
from jax.sharding import PartitionSpec as P

H = 8
KV = 4
FF = 9216
NEWTON_STEPS = 5
UPDATE_STEP = 10

NORM_EPS = 1e-06
SOFT_CAP = 50.0
MUON_RATE = 0.2
MUON_DECAY = 0.01
MUON_BETA = 0.95
ADAM_RATE = 0.3
BETA_ONE = 0.9
BETA_TWO = 0.95
ADAM_EPS = 1e-08
NEWTON_LINEAR = 3.4445
NEWTON_SQUARE = -4.775
NEWTON_CUBIC = 2.0315
TOP_PRECISION = lax.Precision.HIGHEST

BF16 = jnp.bfloat16
F32 = jnp.float32
VMEM_LIMIT = 62 * 1024 * 1024
NN = (((1,), (0,)), ((), ()))
NT = (((1,), (1,)), ((), ()))
TN = (((0,), (0,)), ((), ()))


def mm(a, b, dims):
    return lax.dot_general(a, b, dims, preferred_element_type=F32)


def rms_scale(rows, gain):
    inverse = lax.rsqrt(jnp.mean(rows * rows, axis=-1, keepdims=True) + NORM_EPS)
    return rows * inverse * gain


class Flow:
    def __init__(self, steps):
        self.steps = steps
        self.value = None
        self.sends = None
        self.advance(None)

    def advance(self, arrived):
        try:
            self.sends = self.steps.send(arrived)
        except StopIteration as stop:
            self.sends = None
            self.value = stop.value


def stage(flows, extra=(), idle=()):
    flows = [flow for flow in flows if flow.sends is not None]
    idle = [flow for flow in idle if flow.sends is not None and flow not in flows]
    arrived = [[lax.ppermute(*send) for send in flow.sends] for flow in flows]
    held = [[send[0] for send in flow.sends] for flow in idle]
    arrived, held, extra = lax.optimization_barrier((arrived, held, list(extra)))
    for flow, got in zip(flows, arrived):
        flow.advance(got)
    for flow, kept in zip(idle, held):
        flow.sends = [(value,) + send[1:] for value, send in zip(kept, flow.sends)]
    return extra


def run(steps):
    flow = Flow(steps)
    while flow.sends is not None:
        flow.advance([lax.ppermute(*send) for send in flow.sends])
    return flow.value


def finish(*flows):
    while any(flow.sends is not None for flow in flows):
        stage(flows)


def swap(value, axis, mask):
    size = lax.axis_size(axis)
    return (value, axis, [(i, i ^ mask) for i in range(size)])


def head_gather(rows):
    (other,) = yield [swap(rows, "head", 2)]
    pair = jnp.stack([rows, other], axis=0)
    (other,) = yield [swap(pair, "head", 1)]
    quad = jnp.stack([pair, other], axis=1)
    return quad.reshape((4 * rows.shape[0],) + rows.shape[1:])


def wide_gather(rows):
    (other,) = yield [swap(rows, "dp", 2)]
    both = jnp.stack([rows, other], axis=0)
    (other,) = yield [swap(both, "head", 2)]
    pair = jnp.stack([both, other], axis=1)
    (other,) = yield [swap(pair, "head", 1)]
    quad = jnp.stack([pair, other], axis=2)
    return quad.reshape((8 * rows.shape[0],) + rows.shape[1:])


def add_low(kept, other):
    return (kept.astype(F32) + other.astype(F32)).astype(BF16)


def head_scatter(part):
    rows = part.shape[0] // 4
    quad = part.reshape(2, 2, rows, -1)
    (other,) = yield [swap(quad[:, 1].astype(BF16), "head", 1)]
    pair = add_low(quad[:, 0], other)
    (other,) = yield [swap(pair[1], "head", 2)]
    return pair[0].astype(F32) + other.astype(F32)


def wide_scatter(part):
    rows = part.shape[0] // 8
    octet = part.reshape(2, 2, 2, rows, -1)
    (other,) = yield [swap(octet[:, :, 1].astype(BF16), "head", 1)]
    quad = add_low(octet[:, :, 0], other)
    (other,) = yield [swap(quad[:, 1], "head", 2)]
    pair = add_low(quad[:, 0], other)
    (other,) = yield [swap(pair[1], "dp", 2)]
    return pair[0].astype(F32) + other.astype(F32)


def total_sum(value):
    for axis in ("head", "dp"):
        mask = 1
        while mask < lax.axis_size(axis):
            (other,) = yield [swap(value, axis, mask)]
            value = value + other
            mask *= 2
    return value


class Ring:
    def __init__(self):
        size = lax.axis_size("dp")
        order = list(range(0, size, 2)) + list(range(size - 1, 0, -2))
        around = [[order[(order.index(i) + offset) % size] for offset in range(size)] for i in range(size)]
        self.size = size
        self.around = jnp.array(around, jnp.int32)[lax.axis_index("dp")]
        self.up = [(order[k], order[(k + 1) % size]) for k in range(size)]
        self.down = [(order[(k + 1) % size], order[k]) for k in range(size)]

    def index(self, offset):
        return self.around[offset % self.size]

    def gather(self, value, mid):
        half = self.size // 2
        zeros = (0,) * (value.ndim - 1)
        out = jnp.zeros((self.size,) + value.shape, value.dtype)
        out = lax.dynamic_update_index_in_dim(out, value, self.index(0), 0)
        ahead, back = value, value
        for step in range(1, half):
            ahead, back = yield [(ahead, "dp", self.up), (back, "dp", self.down)]
            out = lax.dynamic_update_index_in_dim(out, ahead, self.index(-step), 0)
            out = lax.dynamic_update_index_in_dim(out, back, self.index(step), 0)
        first, second = yield [(ahead[:mid], "dp", self.up), (back[mid:], "dp", self.down)]
        far = self.index(half)
        out = lax.dynamic_update_slice(out, first[None], (far, 0) + zeros)
        return lax.dynamic_update_slice(out, second[None], (far, mid) + zeros)

    def scatter(self, take, mid):
        half = self.size // 2
        far = take(self.index(half))
        kind = far.dtype
        up, down = yield [(far[:mid], "dp", self.up), (far[mid:], "dp", self.down)]
        for step in range(half - 1, 0, -1):
            part = take(self.index(step)).astype(F32)
            ahead = jnp.concatenate([part[:mid] + up, part[mid:]]) if step == half - 1 else part + up
            part = take(self.index(-step)).astype(F32)
            back = jnp.concatenate([part[:mid], part[mid:] + down]) if step == half - 1 else part + down
            up, down = yield [(ahead.astype(kind), "dp", self.up), (back.astype(kind), "dp", self.down)]
        return take(self.index(0)).astype(F32) + up.astype(F32) + down.astype(F32)


def plane_groups():
    planes = lax.axis_size("dp") // 2
    offsets = list(range(planes - 1, 0, -2)) + list(range(planes - 2, -1, -2))
    return [offsets[k : k + 2] for k in range(0, planes, 2)]


def spread_blocks(mine, other):
    ready = [(0, mine)]
    pieces = {}
    for group in plane_groups() + [[]]:
        offsets = [offset for offset in group if offset]
        sends = [swap(other if offset & 1 else mine, "dp", offset << 1) for offset in offsets]
        arrived = yield sends + [swap(piece, "dp", 1) for _, piece in ready]
        for (offset, piece), far in zip(ready, arrived[len(sends) :]):
            pieces[offset << 1] = piece
            pieces[offset << 1 | 1] = far
        ready = list(zip(offsets, arrived))
    return [pieces[k] for k in range(len(pieces))]


def reduce_blocks(take):
    me = lax.axis_index("dp")
    sums = [None, None]
    ready = []
    for group in plane_groups() + [[]]:
        sends = [swap(take(me ^ (offset << 1) ^ 1), "dp", 1) for offset in group]
        moves = [(offset, total) for offset, total in ready if offset]
        arrived = yield sends + [swap(total.astype(BF16), "dp", offset << 1) for offset, total in moves]
        for offset, total in [(0, total) for offset, total in ready if not offset] + [
            (offset, got) for (offset, _), got in zip(moves, arrived[len(sends) :])
        ]:
            side = offset & 1
            total = total.astype(F32)
            sums[side] = total if sums[side] is None else sums[side] + total
        ready = [
            (offset, take(me ^ (offset << 1)).astype(F32) + got.astype(F32)) for offset, got in zip(group, arrived)
        ]
    return sums


def params(**more):
    return pltpu.CompilerParams(vmem_limit_bytes=VMEM_LIMIT, **more)


def block_project(rows, blocks):
    t = rows.shape[0]
    count, d, c = blocks.shape

    def body(x_ref, w_ref, o_ref):
        o_ref[...] = mm(x_ref[...], w_ref[...], NN).astype(BF16)

    return pl.pallas_call(
        body,
        grid=(count,),
        in_specs=[
            pl.BlockSpec((t, d), lambda b: (0, 0)),
            pl.BlockSpec((None, d, c), lambda b: (b, 0, 0)),
        ],
        out_specs=pl.BlockSpec((None, t, c), lambda b: (b, 0, 0)),
        out_shape=jax.ShapeDtypeStruct((count, t, c), BF16),
        compiler_params=params(),
        cost_estimate=pl.CostEstimate(
            flops=2 * count * t * d * c, bytes_accessed=2 * (t * d + count * (d * c + t * c)), transcendentals=0
        ),
    )(rows, blocks)


def block_back(cols, blocks):
    count, t, c = cols.shape
    d = blocks.shape[1]

    def body(x_ref, w_ref, o_ref, acc_ref):
        b = pl.program_id(0)

        @pl.when(b == 0)
        def _():
            acc_ref[...] = jnp.zeros_like(acc_ref)

        acc_ref[...] += mm(x_ref[...], w_ref[...], NT)

        @pl.when(b == count - 1)
        def _():
            o_ref[...] = acc_ref[...].astype(BF16)

    return pl.pallas_call(
        body,
        grid=(count,),
        in_specs=[
            pl.BlockSpec((None, t, c), lambda b: (b, 0, 0)),
            pl.BlockSpec((None, d, c), lambda b: (b, 0, 0)),
        ],
        out_specs=pl.BlockSpec((t, d), lambda b: (0, 0)),
        out_shape=jax.ShapeDtypeStruct((t, d), BF16),
        scratch_shapes=[pltpu.VMEM((t, d), F32)],
        compiler_params=params(),
        cost_estimate=pl.CostEstimate(
            flops=2 * count * t * d * c, bytes_accessed=2 * (t * d + count * (d * c + t * c)), transcendentals=0
        ),
    )(cols, blocks)


def block_outer(rows, cols, d):
    t = rows.shape[0]
    count, _, c = cols.shape

    def body(x_ref, y_ref, o_ref, xt_ref):
        @pl.when(pl.program_id(0) == 0)
        def _():
            xt_ref[...] = x_ref[...].T

        o_ref[...] = mm(xt_ref[...], y_ref[...], NN).astype(BF16)

    return pl.pallas_call(
        body,
        grid=(count,),
        in_specs=[
            pl.BlockSpec((t, d), lambda b: (0, 0)),
            pl.BlockSpec((None, t, c), lambda b: (b, 0, 0)),
        ],
        out_specs=pl.BlockSpec((None, d, c), lambda b: (b, 0, 0)),
        out_shape=jax.ShapeDtypeStruct((count, d, c), BF16),
        scratch_shapes=[pltpu.VMEM((d, t), BF16)],
        compiler_params=params(),
        cost_estimate=pl.CostEstimate(
            flops=2 * count * t * d * c, bytes_accessed=2 * (t * d + count * (d * c + t * c)), transcendentals=0
        ),
    )(rows, cols)


def key_position(block, width, head_shift, shape, axis):
    local = lax.broadcasted_iota(jnp.int32, shape, axis)
    return block * width + jnp.bitwise_xor(local, head_shift)


def attend(place, queries, keys_values, query_pos, first_pos, scale, p):
    m, e = queries.shape
    n = keys_values.shape[0]
    step = 256

    def body(place_ref, q_ref, kv_ref, pos_ref, first_ref, low_ref, full_ref, sum_ref, acc_ref, tot_ref):
        j = pl.program_id(0)

        @pl.when(j == 0)
        def _():
            acc_ref[...] = jnp.zeros_like(acc_ref)
            tot_ref[...] = jnp.zeros_like(tot_ref)

        @pl.when(j <= place_ref[0])
        def _():
            key_pos = key_position(j, p, place_ref[1], (1, p), 1)
            for r in range(0, m, step):
                rows = pl.ds(r, step)
                raw = mm(q_ref[rows, :], kv_ref[:p, :], NT)
                soft = SOFT_CAP * jnp.tanh(raw * (scale / SOFT_CAP))
                seen = (key_pos >= first_ref[rows, :]) & (key_pos <= pos_ref[rows, :])
                terms = jnp.where(seen, jnp.exp(soft), 0.0)
                tot_ref[rows, :] += jnp.sum(terms, axis=1, keepdims=True)
                acc_ref[rows, :] += mm(terms.astype(BF16), kv_ref[p:, :], NN)

        @pl.when(j == n - 1)
        def _():
            total = tot_ref[...]
            mixed = acc_ref[...] / total
            full_ref[...] = mixed
            low_ref[...] = mixed.astype(BF16)
            sum_ref[...] = total

    whole = lambda shape: pl.BlockSpec(shape, lambda j, s: (0, 0))
    return pl.pallas_call(
        body,
        grid_spec=pltpu.PrefetchScalarGridSpec(
            num_scalar_prefetch=1,
            grid=(n,),
            in_specs=[
                whole((m, e)),
                pl.BlockSpec((None, 2 * p, e), lambda j, s: (jnp.minimum(j, s[0]), 0, 0)),
                whole((m, 1)),
                whole((m, 1)),
            ],
            out_specs=[whole((m, e)), whole((m, e)), whole((m, 1))],
            scratch_shapes=[pltpu.VMEM((m, e), F32), pltpu.VMEM((m, 1), F32)],
        ),
        out_shape=[
            jax.ShapeDtypeStruct((m, e), BF16),
            jax.ShapeDtypeStruct((m, e), F32),
            jax.ShapeDtypeStruct((m, 1), F32),
        ],
        compiler_params=params(),
        cost_estimate=pl.CostEstimate(
            flops=4 * m * n * p * e, bytes_accessed=4 * n * p * e, transcendentals=2 * m * n * p
        ),
    )(place, queries, keys_values, query_pos, first_pos)


def attend_back(place, queries, grads, keys_values, inverse, delta, query_pos, first_pos, scale, p):
    m, e = queries.shape
    n = keys_values.shape[0]
    step = 256

    def body(
        place_ref, q_ref, g_ref, kv_ref, inv_ref, delta_ref, pos_ref, first_ref, dq_ref, dkv_ref, acc_ref, dk_ref, dv_ref
    ):
        j = pl.program_id(0)

        @pl.when(j == 0)
        def _():
            acc_ref[...] = jnp.zeros_like(acc_ref)

        @pl.when(j <= place_ref[0])
        def _():
            key_pos = key_position(j, p, place_ref[1], (p, 1), 0)
            for r in range(0, m, step):
                rows = pl.ds(r, step)
                raw = mm(kv_ref[:p, :], q_ref[rows, :], NT)
                capped = jnp.tanh(raw * (scale / SOFT_CAP))
                seen = (key_pos >= first_ref[:, rows]) & (key_pos <= pos_ref[:, rows])
                probs = jnp.where(seen, jnp.exp(SOFT_CAP * capped), 0.0) * inv_ref[:, rows]
                grad_probs = mm(kv_ref[p:, :], g_ref[rows, :], NT)
                grad_raw = probs * (grad_probs - delta_ref[:, rows]) * (1.0 - capped * capped)
                grad_low = grad_raw.astype(BF16)
                value_part = mm(probs.astype(BF16), g_ref[rows, :], NN)
                key_part = mm(grad_low, q_ref[rows, :], NN)
                if r == 0:
                    dv_ref[...] = value_part
                    dk_ref[...] = key_part
                else:
                    dv_ref[...] += value_part
                    dk_ref[...] += key_part
                acc_ref[rows, :] += mm(grad_low, kv_ref[:p, :], TN)
            dkv_ref[0] = dk_ref[...].astype(BF16)
            dkv_ref[1] = dv_ref[...].astype(BF16)

        @pl.when(j > place_ref[0])
        def _():
            dkv_ref[...] = jnp.zeros_like(dkv_ref)

        @pl.when(j == n - 1)
        def _():
            dq_ref[...] = (acc_ref[...] * scale).astype(BF16)

    whole = lambda shape: pl.BlockSpec(shape, lambda j, s: (0, 0))
    return pl.pallas_call(
        body,
        grid_spec=pltpu.PrefetchScalarGridSpec(
            num_scalar_prefetch=1,
            grid=(n,),
            in_specs=[
                whole((m, e)),
                whole((m, e)),
                pl.BlockSpec((None, 2 * p, e), lambda j, s: (jnp.minimum(j, s[0]), 0, 0)),
                whole((1, m)),
                whole((1, m)),
                whole((1, m)),
                whole((1, m)),
            ],
            out_specs=[whole((m, e)), pl.BlockSpec((None, 2, p, e), lambda j, s: (j, 0, 0, 0))],
            scratch_shapes=[pltpu.VMEM((m, e), F32), pltpu.VMEM((p, e), F32), pltpu.VMEM((p, e), F32)],
        ),
        out_shape=[jax.ShapeDtypeStruct((m, e), BF16), jax.ShapeDtypeStruct((n, 2, p, e), BF16)],
        compiler_params=params(),
        cost_estimate=pl.CostEstimate(
            flops=10 * m * n * p * e, bytes_accessed=8 * n * p * e, transcendentals=2 * m * n * p
        ),
    )(place, queries, grads, keys_values, inverse, delta, query_pos, first_pos)


def gelu_pair(gate):
    outer = math.sqrt(2.0 / math.pi)
    square = gate * gate
    bent = jnp.tanh(outer * gate * (1.0 + 0.044715 * square))
    half = 0.5 * (1.0 + bent)
    slope = half + 0.5 * gate * (1.0 - bent * bent) * outer * (1.0 + 3.0 * 0.044715 * square)
    return gate * half, slope


def feed_forward(place, rows, cots, pieces, before):
    t, d = rows.shape
    count = len(pieces)
    _, r, u = pieces[0].shape
    tall = min(512, t)
    wide = d // 3
    cuts = [(k, min(256, u - k)) for k in range(0, u, 256)]

    def body(place_ref, x_ref, y_ref, *refs):
        piece_refs, refs = refs[:count], refs[count:]
        before_refs, refs = refs[: len(before)], refs[len(before) :]
        out_ref, dx_ref, dw_ref, w, xt, yt, hid, gg, gu, sems, out_sems = refs
        copies = []
        for k in range(count):
            spot = pl.multiple_of(jnp.bitwise_xor(place_ref[0], k) * r, 16) if count > 1 else 0
            copies.append(pltpu.make_async_copy(piece_refs[k], w.at[:, pl.ds(spot, r), :], sems.at[k]))
            copies[k].start()

        @pl.loop(0, d // 256)
        def _(k):
            cols = pl.ds(pl.multiple_of(k * 256, 256), 256)
            xt[cols, :] = x_ref[:, cols].T
            yt[cols, :] = y_ref[:, cols].T

        for copy in copies:
            copy.wait()

        @pl.loop(0, t // tall)
        def _(i):
            part = pl.ds(pl.multiple_of(i * tall, tall), tall)
            for start, size in cuts:
                units = pl.ds(start, size)
                gate = mm(x_ref[part, :], w[0, :, units], NN)
                up = mm(x_ref[part, :], w[1, :, units], NN)
                grad = mm(y_ref[part, :], w[2, :, units], NN)
                active, slope = gelu_pair(gate)
                hid[part, units] = (active * up).astype(BF16)
                gg[part, units] = (grad * up * slope).astype(BF16)
                gu[part, units] = (grad * active).astype(BF16)

        @pl.loop(0, t // tall)
        def _(i):
            part = pl.ds(pl.multiple_of(i * tall, tall), tall)

            @pl.loop(0, d // wide)
            def _(k):
                cols = pl.ds(pl.multiple_of(k * wide, wide), wide)
                out = mm(hid[part, :], w[2, cols, :], NT)
                dx = mm(gg[part, :], w[0, cols, :], NT) + mm(gu[part, :], w[1, cols, :], NT)
                if before:
                    out = out + before_refs[0][part, cols].astype(F32)
                    dx = dx + before_refs[1][part, cols].astype(F32)
                out_ref[part, cols] = out.astype(BF16)
                dx_ref[part, cols] = dx.astype(BF16)

        copies = []
        for kind, (left, right) in enumerate(((xt, gg), (xt, gu), (yt, hid))):

            @pl.loop(0, d // wide)
            def _(k):
                cols = pl.ds(pl.multiple_of(k * wide, wide), wide)
                w[kind, cols, :] = mm(left[cols, :], right[...], NN).astype(BF16)

            copies.append(pltpu.make_async_copy(w.at[kind], dw_ref.at[kind], out_sems.at[kind]))
            copies[kind].start()
        for copy in copies:
            copy.wait()

    once = pl.Buffered(1)
    whole = pl.BlockSpec((t, d), lambda f, s: (0, 0), pipeline_mode=once)
    apart = pl.BlockSpec(memory_space=pl.ANY)
    return pl.pallas_call(
        body,
        grid_spec=pltpu.PrefetchScalarGridSpec(
            num_scalar_prefetch=1,
            grid=(1,),
            in_specs=[whole, whole] + [apart] * count + [whole] * len(before),
            out_specs=[whole, whole, apart],
            scratch_shapes=[
                pltpu.VMEM((3, d, u), BF16),
                pltpu.VMEM((d, t), BF16),
                pltpu.VMEM((d, t), BF16),
                pltpu.VMEM((t, u), BF16),
                pltpu.VMEM((t, u), BF16),
                pltpu.VMEM((t, u), BF16),
                pltpu.SemaphoreType.DMA((count,)),
                pltpu.SemaphoreType.DMA((3,)),
            ],
        ),
        out_shape=[
            jax.ShapeDtypeStruct((t, d), BF16),
            jax.ShapeDtypeStruct((t, d), BF16),
            jax.ShapeDtypeStruct((3, d, u), BF16),
        ],
        compiler_params=params(),
        cost_estimate=pl.CostEstimate(
            flops=18 * t * d * u, bytes_accessed=12 * d * u + 8 * t * d, transcendentals=t * u
        ),
    )(place, rows, cots, *pieces, *before)


def gram_parts(m):
    h = m.shape[1] // 2
    gram = lax.dot_general(m, m, TN, precision=TOP_PRECISION, preferred_element_type=F32)
    return gram[:h, :h], gram[:h, h:], gram[h:, h:]


def ffn_moment(low_early, low_late, high_early, high_late, momentum, first, blocks, slots, last_slots):
    total, r, c = momentum.shape
    early = low_early.shape[2] // c
    h = c // 2
    full = early + 1
    main = 3 * blocks - last_slots
    steps = slots + last_slots

    def body(le_ref, ll_ref, he_ref, hl_ref, m_ref, wg_ref, nm_ref, gram_ref):
        j = pl.program_id(0)
        f = lax.rem(j, blocks)

        @pl.when(j >= 3 * blocks)
        def _():
            gram_ref[...] = jnp.zeros_like(gram_ref)

        @pl.when(j < 3 * blocks)
        def _():
            for side, (early_ref, late_ref) in enumerate(((le_ref, ll_ref), (he_ref, hl_ref))):

                @pl.when((f >= side * full) & (f < side * full + early))
                def _():
                    lanes = pl.ds(pl.multiple_of((f - side * full) * c, c), c)
                    wg_ref[...] = early_ref[:, lanes]

                @pl.when(f == side * full + early)
                def _():
                    wg_ref[...] = late_ref[:, :c]

            @pl.when(f == 2 * full)
            def _():
                wg_ref[:, :h] = ll_ref[:, c:]
                wg_ref[:, h:] = hl_ref[:, c:]

            new = MUON_BETA * m_ref[...] + wg_ref[...]
            nm_ref[...] = new
            gram_ref[0], gram_ref[1], gram_ref[2] = gram_parts(new)

    kind = lambda j: (jnp.minimum(j // blocks, 2), 0, 0)
    block = lambda j: (first + jnp.minimum(j, 3 * blocks - 1), 0, 0)

    def slot(j):
        late = slots + j - main
        spare = main + j - 3 * blocks
        return (jnp.where(j < main, j, jnp.where(j < 3 * blocks, late, spare)), 0, 0, 0)

    u, v = low_early.shape[2], low_late.shape[2]
    return pl.pallas_call(
        body,
        grid=(steps,),
        in_specs=[
            pl.BlockSpec((None, r, u), kind),
            pl.BlockSpec((None, r, v), kind),
            pl.BlockSpec((None, r, u), kind),
            pl.BlockSpec((None, r, v), kind),
            pl.BlockSpec((None, r, c), block),
        ],
        out_specs=[
            pl.BlockSpec((None, r, c), block),
            pl.BlockSpec((None, r, c), block),
            pl.BlockSpec((None, 3, h, h), slot),
        ],
        out_shape=[
            jax.ShapeDtypeStruct((total, r, c), F32),
            jax.ShapeDtypeStruct((total, r, c), F32),
            jax.ShapeDtypeStruct((steps, 3, h, h), F32),
        ],
        compiler_params=params(),
        cost_estimate=pl.CostEstimate(
            flops=12 * 3 * blocks * r * c * c, bytes_accessed=16 * 3 * blocks * r * c, transcendentals=0
        ),
    )(low_early, low_late, high_early, high_late, momentum)


def attn_moment(grads, momentum, weight_grads, new_momentum):
    count, r, c = grads.shape
    h = c // 2

    def body(g_ref, m_ref, wg_in, nm_in, wg_ref, nm_ref, gram_ref):
        new = MUON_BETA * m_ref[...] + g_ref[...]
        wg_ref[...] = g_ref[...]
        nm_ref[...] = new
        gram_ref[0], gram_ref[1], gram_ref[2] = gram_parts(new)

    block = pl.BlockSpec((None, r, c), lambda j: (j, 0, 0))
    apart = pl.BlockSpec(memory_space=pl.ANY)
    return pl.pallas_call(
        body,
        grid=(count,),
        in_specs=[block, block, apart, apart],
        out_specs=[block, block, pl.BlockSpec((None, 3, h, h), lambda j: (j, 0, 0, 0))],
        out_shape=[
            jax.ShapeDtypeStruct(momentum.shape, F32),
            jax.ShapeDtypeStruct(momentum.shape, F32),
            jax.ShapeDtypeStruct((count, 3, h, h), F32),
        ],
        input_output_aliases={2: 0, 3: 1},
        compiler_params=params(),
        cost_estimate=pl.CostEstimate(
            flops=12 * count * r * c * c, bytes_accessed=16 * count * r * c, transcendentals=0
        ),
    )(grads, momentum, weight_grads, new_momentum)


def top(spec, a, b):
    return jnp.einsum(spec, a, b, precision=TOP_PRECISION)


def newton_factor(grams, growth):
    size = grams.shape[-1]
    eye = jnp.eye(size, dtype=F32)
    norm = jnp.sqrt(jnp.sum(grams * eye, axis=(1, 2), keepdims=True))
    inverse = 1.0 / (norm + 1e-07)
    gram = grams * (inverse * inverse)
    factor = None
    for sweep in range(NEWTON_STEPS):
        square = top("bij,bjk->bik", gram, gram)
        poly = NEWTON_LINEAR * eye + NEWTON_SQUARE * gram + NEWTON_CUBIC * square
        factor = poly if sweep == 0 else top("bij,bjk->bik", factor, poly)
        if sweep < NEWTON_STEPS - 1:
            gram = top("bij,bjk->bik", top("bij,bjk->bik", gram, poly), poly)
    return factor * (growth * inverse)


def fold(squares):
    h = squares.shape[1] // 2
    return jnp.stack([squares[:, :h, :h], squares[:, :h, h:], squares[:, h:, h:]], axis=1)


def unfold(parts):
    first, off, last = parts[:, 0], parts[:, 1], parts[:, 2]
    upper = jnp.concatenate([first, off], axis=2)
    lower = jnp.concatenate([jnp.swapaxes(off, 1, 2), last], axis=2)
    return jnp.concatenate([upper, lower], axis=1)


def gram_sums(ring, parts):
    _, _, h, _ = parts.shape
    rows = parts.shape[0] // ring.size * 3
    parts = parts.reshape(ring.size, rows, h, h)
    mine = yield from ring.scatter(lambda i: lax.dynamic_index_in_dim(parts, i, 0, keepdims=False), rows // 2)
    return unfold(mine.reshape(rows // 3, 3, h, h))


def all_factors(ring, factors, count):
    cap, c, _ = factors.shape
    parts = fold(factors.astype(BF16)).reshape(3 * cap, c // 2, c // 2)
    parts = yield from ring.gather(parts, 3 * cap // 2)
    return unfold(parts.reshape(ring.size * cap, 3, c // 2, c // 2)[:count])


def on_device(block_in, cotangent, seq_ids, weights, momentum, gains, gain_first, gain_second):
    tok_rows, model_width = block_in.shape
    rows_dp, group_blocks, head_dim = weights.shape
    head_count = lax.axis_size("head")
    data_count = lax.axis_size("dp")
    group_rows = tok_rows * head_count
    key_heads = KV // head_count
    query_heads = H // head_count
    ffn_blocks = FF // (head_dim * head_count)
    out_mark = query_heads + 2 * key_heads
    gate_mark = out_mark + query_heads
    half_dim = head_dim // 2
    full = ffn_blocks // 2
    scale = head_dim ** (-0.5)
    growth = math.sqrt(max(1.0, model_width / head_dim))
    data_index = lax.axis_index("dp")
    head_index = lax.axis_index("head")
    parity = (data_index >> 1) & 1
    ring = Ring()

    weights = jnp.transpose(weights, (1, 0, 2))
    momentum = jnp.transpose(momentum, (1, 0, 2))
    attn_low = weights[:gate_mark].astype(BF16)
    inputs = block_in.astype(F32)
    normed_one, norm_one_back = jax.vjp(rms_scale, inputs, gains[0])
    ids_column = jnp.pad(seq_ids.astype(BF16)[:, None], ((0, 0), (0, 127)))

    early = full - 1
    kinds = [weights[gate_mark + k * ffn_blocks : gate_mark + (k + 1) * ffn_blocks] for k in range(3)]

    def pack(side, late):
        tiles = range(side * full + early, (side + 1) * full) if late else range(side * full, side * full + early)
        lanes = slice(side * half_dim, (side + 1) * half_dim)
        rest = [2 * full] if late else []
        rows = [
            jnp.concatenate([kind[f] for f in tiles] + [kind[f, :, lanes] for f in rest], axis=1) for kind in kinds
        ]
        return jnp.stack(rows).astype(BF16)

    def own_and_other(late):
        sides = (pack(0, late), pack(1, late))
        return jnp.where(parity == 1, sides[1], sides[0]), jnp.where(parity == 1, sides[0], sides[1])

    group_in = run(head_gather(jnp.concatenate([normed_one.astype(BF16), ids_column], axis=1)))
    qkv_parts = run(ring.gather(attn_low[:out_mark], out_mark // 2))
    qkv_blocks = jnp.transpose(qkv_parts, (1, 0, 2, 3)).reshape(out_mark, model_width, head_dim)
    sides = [own_and_other(False), own_and_other(True)]
    attn_low, inputs, group_in, qkv_blocks, sides = lax.optimization_barrier(
        (attn_low, inputs, group_in, qkv_blocks, sides)
    )
    spread = [Flow(spread_blocks(*side)) for side in sides]

    projected = block_project(group_in, qkv_blocks)
    queries = projected[:query_heads].reshape(query_heads * group_rows, head_dim)
    group_ids = group_in[:, model_width]
    kv_rows = 2 * key_heads * group_rows
    out_rows = query_heads * rows_dp
    id_rows = group_rows // head_dim
    packed = jnp.concatenate(
        [
            projected[query_heads:].reshape(kv_rows, head_dim),
            attn_low[out_mark:].reshape(out_rows, head_dim),
            jnp.pad(group_ids.reshape(id_rows, head_dim), ((0, 16 - id_rows), (0, 0))),
        ],
        axis=0,
    )
    keys_values = run(ring.gather(packed, packed.shape[0] // 32 * 16))
    queries, keys_values = stage([spread[0]], [queries, keys_values], idle=spread)
    out_blocks = keys_values[:, kv_rows : kv_rows + out_rows].reshape(data_count, query_heads, rows_dp, head_dim)
    out_blocks = jnp.transpose(out_blocks, (1, 0, 2, 3)).reshape(query_heads, model_width, head_dim)
    all_ids = keys_values[:, kv_rows + out_rows : kv_rows + out_rows + id_rows].reshape(-1)

    local = jnp.arange(group_rows, dtype=jnp.int32) ^ (head_index * tok_rows)
    query_pos = data_index * group_rows + local
    first_pos = jnp.sum((all_ids[None, :] < group_ids[:, None]).astype(jnp.int32), axis=1)
    query_pos = jnp.tile(query_pos, query_heads)
    first_pos = jnp.tile(first_pos, query_heads)
    place = jnp.stack([data_index, head_index * tok_rows]).astype(jnp.int32)
    mixed_low, mixed_full, totals = attend(
        place, queries, keys_values, query_pos[:, None], first_pos[:, None], scale, group_rows
    )
    mixed_heads = mixed_low.reshape(query_heads, group_rows, head_dim)
    attn_add = run(head_scatter(block_back(mixed_heads, out_blocks)))
    residual = inputs + attn_add
    cot_flow = Flow(wide_gather(cotangent))
    residual, mixed_heads, mixed_full, totals, out_blocks = stage(
        [spread[0], cot_flow], [residual, mixed_heads, mixed_full, totals, out_blocks], idle=spread
    )
    normed_two, norm_two_back = jax.vjp(rms_scale, residual, gains[1])
    wide_ffn = run(wide_gather(normed_two.astype(BF16)))
    (wide_ffn,) = stage([spread[0], spread[1], cot_flow], [wide_ffn])
    finish(spread[0])
    stage([spread[1], cot_flow])
    finish(cot_flow)
    group_cot = cot_flow.value

    def whole_rows(pieces):
        if rows_dp % 16 == 0:
            return pieces
        out = jnp.zeros((3, data_count) + pieces[0].shape[1:], BF16)
        for k, piece in enumerate(pieces):
            out = lax.dynamic_update_index_in_dim(out, piece, data_index ^ k, 1)
        return [out.reshape(3, model_width, -1)]

    outs = stage([spread[1]], feed_forward(place, wide_ffn, group_cot, whole_rows(spread[0].value), ()))
    finish(spread[1])
    down_early, dx_early, grads_early = outs

    def taker(grads):
        cut = grads.reshape(3, data_count, rows_dp, grads.shape[2])
        return lambda index: lax.dynamic_index_in_dim(cut, index, 1, keepdims=False)

    reduce = [Flow(reduce_blocks(taker(grads_early)))]
    down_part, dx_part, grads_late = stage(
        [reduce[0]],
        feed_forward(place, wide_ffn, group_cot, whole_rows(spread[1].value), (down_early, dx_early)),
    )
    reduce.append(Flow(reduce_blocks(taker(grads_late))))
    out_flow = Flow(wide_scatter(down_part))
    grad_normed_two = run(wide_scatter(dx_part))
    grad_residual_norm, grad_gain_two = norm_two_back(grad_normed_two)
    grad_residual = cotangent.astype(F32) + grad_residual_norm
    group_grad = run(head_gather(grad_residual.astype(BF16)))
    grad_residual, grad_gain_two, group_grad = stage(
        reduce + [out_flow], [grad_residual, grad_gain_two, group_grad]
    )

    grad_heads = block_project(group_grad, out_blocks)
    grad_mixed = grad_heads.reshape(query_heads * group_rows, head_dim)
    delta = jnp.sum(grad_mixed.astype(F32) * mixed_full, axis=1)
    grad_queries, grad_keys_values = attend_back(
        place,
        queries,
        grad_mixed,
        keys_values,
        1.0 / totals.reshape(1, -1),
        delta[None, :],
        query_pos[None, :],
        first_pos[None, :],
        scale,
        group_rows,
    )
    grad_queries, grad_keys_values = stage(reduce + [out_flow], [grad_queries, grad_keys_values])
    finish(reduce[0])
    key_value_sums = run(
        ring.scatter(lambda i: lax.dynamic_index_in_dim(grad_keys_values, i, 0, keepdims=False), key_heads)
    )
    (key_value_sums,) = stage([reduce[1], out_flow], [key_value_sums])
    finish(reduce[1], out_flow)
    block_out = (residual + out_flow.value).astype(BF16)
    grad_projected = jnp.concatenate(
        [
            grad_queries.reshape(query_heads, group_rows, head_dim),
            (key_value_sums[:key_heads] * scale).astype(BF16),
            key_value_sums[key_heads:].astype(BF16),
        ],
        axis=0,
    )
    qkv_part = block_outer(group_in, grad_projected, model_width)
    out_part = block_outer(group_grad, mixed_heads, model_width)
    attn_dx = block_back(grad_projected, qkv_blocks)
    attn_part = jnp.concatenate([qkv_part, out_part], axis=0).reshape(gate_mark, data_count, rows_dp, head_dim)
    weight_flow = Flow(
        ring.scatter(lambda i: lax.dynamic_index_in_dim(attn_part, i, 1, keepdims=False), gate_mark // 2)
    )
    last_flow = Flow(head_scatter(attn_dx))

    late = 2
    slots = -(-(3 * ffn_blocks - late) // data_count) * data_count
    own_early, other_early = reduce[0].value
    own_late, other_late = reduce[1].value
    pick = lambda own, other: (jnp.where(parity == 1, other, own), jnp.where(parity == 1, own, other))
    (low_early, high_early), (low_late, high_late) = pick(own_early, other_early), pick(own_late, other_late)
    weight_grads, new_momentum, grams = stage(
        [weight_flow, last_flow],
        ffn_moment(low_early, low_late, high_early, high_late, momentum, gate_mark, ffn_blocks, slots, late),
    )
    gram_flow = Flow(gram_sums(ring, grams[:slots]))
    while weight_flow.sends is not None:
        stage([weight_flow, gram_flow, last_flow])
    finish(last_flow)
    grad_input_norm, grad_gain_one = norm_one_back(last_flow.value)
    grad_input = grad_residual + grad_input_norm
    gain_flow = Flow(total_sum(jnp.stack([grad_gain_one, grad_gain_two])))
    weight_grads, new_momentum, attn_grams = stage(
        [gram_flow, gain_flow], attn_moment(weight_flow.value, momentum, weight_grads, new_momentum)
    )
    late_count = gate_mark + late
    late_slots = -(-late_count // data_count) * data_count
    late_grams = jnp.concatenate([attn_grams, grams[slots:]], axis=0)
    late_grams = jnp.pad(late_grams, ((0, late_slots - late_count), (0, 0), (0, 0), (0, 0)))
    late_gram_flow = Flow(gram_sums(ring, late_grams))
    finish(gram_flow)
    (factors,) = stage([late_gram_flow, gain_flow], [newton_factor(gram_flow.value, growth)])
    factor_flow = Flow(all_factors(ring, factors, 3 * ffn_blocks - late))
    while late_gram_flow.sends is not None:
        stage([late_gram_flow, factor_flow, gain_flow])
    (late_factors,) = stage([factor_flow, gain_flow], [newton_factor(late_gram_flow.value, growth)])
    late_factor_flow = Flow(all_factors(ring, late_factors, late_count))
    finish(late_factor_flow, factor_flow, gain_flow)
    gain_grads = gain_flow.value
    ffn_factors, late_factors = factor_flow.value, late_factor_flow.value

    factors = jnp.concatenate([late_factors[:gate_mark], ffn_factors, late_factors[gate_mark:]], axis=0)
    update = jnp.einsum("bre,bef->brf", new_momentum.astype(BF16), factors, preferred_element_type=F32)
    new_weights = weights * (1.0 - MUON_RATE * MUON_DECAY) - MUON_RATE * update

    new_gain_first = BETA_ONE * gain_first + (1.0 - BETA_ONE) * gain_grads
    new_gain_second = BETA_TWO * gain_second + (1.0 - BETA_TWO) * gain_grads * gain_grads
    first_hat = new_gain_first / (1.0 - BETA_ONE**UPDATE_STEP)
    second_hat = new_gain_second / (1.0 - BETA_TWO**UPDATE_STEP)
    new_gains = gains - ADAM_RATE * first_hat / (jnp.sqrt(second_hat) + ADAM_EPS)
    back = lambda array: jnp.transpose(array, (1, 0, 2))
    return (
        block_out,
        grad_input,
        back(weight_grads),
        back(new_momentum),
        back(new_weights),
        gain_grads,
        new_gain_first,
        new_gain_second,
        new_gains,
    )


def solution(mesh):
    return jax.shard_map(
        on_device,
        mesh=mesh,
        in_specs=(
            P(("dp", "head"), None),
            P(("dp", "head"), None),
            P(("dp", "head")),
            P("dp", "head", None),
            P("dp", "head", None),
            P(),
            P(),
            P(),
        ),
        out_specs=(
            P(("dp", "head"), None),
            P(("dp", "head"), None),
            P("dp", "head", None),
            P("dp", "head", None),
            P("dp", "head", None),
            P(),
            P(),
            P(),
            P(),
        ),
        check_vma=False,
    )
```

```python
import functools
import math

import jax
import jax.numpy as jnp
from jax import lax
from jax.experimental import pallas as pl
from jax.experimental.pallas import tpu as pltpu
from jax.sharding import PartitionSpec as P

H = 8
KV = 4
FF = 9216
NEWTON_STEPS = 5
UPDATE_STEP = 10

NORM_EPS = 1e-06
SOFT_CAP = 50.0
MUON_RATE = 0.2
MUON_DECAY = 0.01
MUON_BETA = 0.95
ADAM_RATE = 0.3
BETA_ONE = 0.9
BETA_TWO = 0.95
ADAM_EPS = 1e-08
NEWTON_LINEAR = 3.4445
NEWTON_SQUARE = -4.775
NEWTON_CUBIC = 2.0315
TOP_PRECISION = lax.Precision.HIGHEST

BF16 = jnp.bfloat16
F32 = jnp.float32
VMEM_LIMIT = 62 * 1024 * 1024
NN = (((1,), (0,)), ((), ()))
NT = (((1,), (1,)), ((), ()))
TN = (((0,), (0,)), ((), ()))


def mm(a, b, dims):
    return lax.dot_general(a, b, dims, preferred_element_type=F32)


def rms_scale(rows, gain):
    inverse = lax.rsqrt(jnp.mean(rows * rows, axis=-1, keepdims=True) + NORM_EPS)
    return rows * inverse * gain


class Flow:
    def __init__(self, steps):
        self.steps = steps
        self.value = None
        self.sends = None
        self.advance(None)

    def advance(self, arrived):
        try:
            self.sends = self.steps.send(arrived)
        except StopIteration as stop:
            self.sends = None
            self.value = stop.value


def stage(flows, extra=(), idle=()):
    flows = [flow for flow in flows if flow.sends is not None]
    idle = [flow for flow in idle if flow.sends is not None and flow not in flows]
    arrived = [[lax.ppermute(*send) for send in flow.sends] for flow in flows]
    held = [[send[0] for send in flow.sends] for flow in idle]
    arrived, held, extra = lax.optimization_barrier((arrived, held, list(extra)))
    for flow, got in zip(flows, arrived):
        flow.advance(got)
    for flow, kept in zip(idle, held):
        flow.sends = [(value,) + send[1:] for value, send in zip(kept, flow.sends)]
    return extra


def run(steps):
    flow = Flow(steps)
    while flow.sends is not None:
        flow.advance([lax.ppermute(*send) for send in flow.sends])
    return flow.value


def finish(*flows):
    while any(flow.sends is not None for flow in flows):
        stage(flows)


def swap(value, axis, mask):
    size = lax.axis_size(axis)
    return (value, axis, [(i, i ^ mask) for i in range(size)])


def head_gather(rows):
    (other,) = yield [swap(rows, "head", 2)]
    pair = jnp.concatenate([rows, other], axis=0)
    (other,) = yield [swap(pair, "head", 1)]
    return jnp.concatenate([pair, other], axis=0)


def wide_gather(rows):
    (other,) = yield [swap(rows, "dp", 2)]
    both = jnp.concatenate([rows, other], axis=0)
    (other,) = yield [swap(both, "head", 2)]
    pair = jnp.concatenate([both, other], axis=0)
    (other,) = yield [swap(pair, "head", 1)]
    return [pair, other]


def add_low(kept, other):
    return (kept.astype(F32) + other.astype(F32)).astype(BF16)


def scatter_rows(part, moves):
    for axis, mask in moves:
        half = part.shape[0] // 2
        (other,) = yield [swap(part[half:].astype(BF16), axis, mask)]
        part = part[:half].astype(F32) + other.astype(F32)
    return part


HEAD_MOVES = (("head", 1), ("head", 2))
WIDE_MOVES = (("head", 1), ("head", 2), ("dp", 2))


def total_sum(value):
    for axis in ("head", "dp"):
        mask = 1
        while mask < lax.axis_size(axis):
            (other,) = yield [swap(value, axis, mask)]
            value = value + other
            mask *= 2
    return value


class Ring:
    def __init__(self):
        size = lax.axis_size("dp")
        order = list(range(0, size, 2)) + list(range(size - 1, 0, -2))
        around = [[order[(order.index(i) + offset) % size] for offset in range(size)] for i in range(size)]
        self.size = size
        self.around = jnp.array(around, jnp.int32)[lax.axis_index("dp")]
        self.up = [(order[k], order[(k + 1) % size]) for k in range(size)]
        self.down = [(order[(k + 1) % size], order[k]) for k in range(size)]

    def index(self, offset):
        return self.around[offset % self.size]

    def gather(self, value, mid):
        half = self.size // 2
        zeros = (0,) * (value.ndim - 1)
        out = jnp.zeros((self.size,) + value.shape, value.dtype)
        out = lax.dynamic_update_index_in_dim(out, value, self.index(0), 0)
        ahead, back = value, value
        for step in range(1, half):
            ahead, back = yield [(ahead, "dp", self.up), (back, "dp", self.down)]
            out = lax.dynamic_update_index_in_dim(out, ahead, self.index(-step), 0)
            out = lax.dynamic_update_index_in_dim(out, back, self.index(step), 0)
        first, second = yield [(ahead[:mid], "dp", self.up), (back[mid:], "dp", self.down)]
        far = self.index(half)
        out = lax.dynamic_update_slice(out, first[None], (far, 0) + zeros)
        return lax.dynamic_update_slice(out, second[None], (far, mid) + zeros)

    def scatter(self, take, mid):
        half = self.size // 2
        far = take(self.index(half))
        kind = far.dtype
        up, down = yield [(far[:mid], "dp", self.up), (far[mid:], "dp", self.down)]
        for step in range(half - 1, 0, -1):
            part = take(self.index(step)).astype(F32)
            ahead = jnp.concatenate([part[:mid] + up, part[mid:]]) if step == half - 1 else part + up
            part = take(self.index(-step)).astype(F32)
            back = jnp.concatenate([part[:mid], part[mid:] + down]) if step == half - 1 else part + down
            up, down = yield [(ahead.astype(kind), "dp", self.up), (back.astype(kind), "dp", self.down)]
        return take(self.index(0)).astype(F32) + up.astype(F32) + down.astype(F32)


def once(sends, take):
    def steps():
        take((yield sends))

    return Flow(steps())


def plane_group(key):
    planes = lax.axis_size("dp") // 2
    return [key] if key < 2 else list(range(key, planes, 2))


class Spread:
    def __init__(self, mine, other):
        self.mine, self.other = mine, other
        self.pieces = {0: mine}

    def z(self, key):
        group = plane_group(key)

        def take(arrived):
            for offset, piece in zip(group, arrived):
                self.pieces[offset << 1] = piece

        return once([swap(self.other if key & 1 else self.mine, "dp", offset << 1) for offset in group], take)

    def y(self, key):
        group = plane_group(key)

        def take(arrived):
            for offset, piece in zip(group, arrived):
                self.pieces[offset << 1 | 1] = piece

        return once([swap(self.pieces[offset << 1], "dp", 1) for offset in group], take)

    def value(self):
        return [self.pieces[k] for k in range(lax.axis_size("dp"))]


class Reduce:
    def __init__(self, rows):
        self.rows = rows
        self.totals = {}
        self.sums = [None, None]

    def y(self, key):
        me = lax.axis_index("dp")
        group = plane_group(key)

        def take(arrived):
            for offset, got in zip(group, arrived):
                self.totals[offset] = self.rows(me ^ (offset << 1)).astype(F32) + got.astype(F32)
                if offset:
                    self.totals[offset] = self.totals[offset].astype(BF16)
                else:
                    self.add(0, self.totals[0])

        return once([swap(self.rows(me ^ (offset << 1) ^ 1), "dp", 1) for offset in group], take)

    def z(self, key):
        group = plane_group(key)

        def take(arrived):
            for offset, got in zip(group, arrived):
                self.add(offset & 1, got.astype(F32))

        return once([swap(self.totals[offset], "dp", offset << 1) for offset in group], take)

    def add(self, side, value):
        self.sums[side] = value if self.sums[side] is None else self.sums[side] + value


def params(**more):
    return pltpu.CompilerParams(vmem_limit_bytes=VMEM_LIMIT, **more)


def block_project(rows, blocks):
    t = rows.shape[0]
    count, d, c = blocks.shape

    def body(x_ref, w_ref, o_ref):
        o_ref[...] = mm(x_ref[...], w_ref[...], NN).astype(BF16)

    return pl.pallas_call(
        body,
        grid=(count,),
        in_specs=[
            pl.BlockSpec((t, d), lambda b: (0, 0)),
            pl.BlockSpec((None, d, c), lambda b: (b, 0, 0)),
        ],
        out_specs=pl.BlockSpec((None, t, c), lambda b: (b, 0, 0)),
        out_shape=jax.ShapeDtypeStruct((count, t, c), BF16),
        compiler_params=params(),
        cost_estimate=pl.CostEstimate(
            flops=2 * count * t * d * c, bytes_accessed=2 * (t * d + count * (d * c + t * c)), transcendentals=0
        ),
    )(rows, blocks)


def block_back(cols, blocks):
    count, t, c = cols.shape
    d = blocks.shape[1]

    def body(x_ref, w_ref, o_ref, acc_ref):
        b = pl.program_id(0)

        @pl.when(b == 0)
        def _():
            acc_ref[...] = jnp.zeros_like(acc_ref)

        acc_ref[...] += mm(x_ref[...], w_ref[...], NT)

        @pl.when(b == count - 1)
        def _():
            o_ref[...] = acc_ref[...].astype(BF16)

    return pl.pallas_call(
        body,
        grid=(count,),
        in_specs=[
            pl.BlockSpec((None, t, c), lambda b: (b, 0, 0)),
            pl.BlockSpec((None, d, c), lambda b: (b, 0, 0)),
        ],
        out_specs=pl.BlockSpec((t, d), lambda b: (0, 0)),
        out_shape=jax.ShapeDtypeStruct((t, d), BF16),
        scratch_shapes=[pltpu.VMEM((t, d), F32)],
        compiler_params=params(),
        cost_estimate=pl.CostEstimate(
            flops=2 * count * t * d * c, bytes_accessed=2 * (t * d + count * (d * c + t * c)), transcendentals=0
        ),
    )(cols, blocks)


def block_outer(first, second, first_cols, second_cols, d):
    t = first.shape[0]
    count, _, c = first_cols.shape
    more = second_cols.shape[0]

    def body(x_ref, y_ref, p_ref, q_ref, o_ref, t_ref):
        b = pl.program_id(0)

        @pl.when(b == 0)
        def _():
            t_ref[...] = x_ref[...].T

        @pl.when(b == count)
        def _():
            t_ref[...] = y_ref[...].T

        @pl.when(b < count)
        def _():
            o_ref[...] = mm(t_ref[...], p_ref[...], NN).astype(BF16)

        @pl.when(b >= count)
        def _():
            o_ref[...] = mm(t_ref[...], q_ref[...], NN).astype(BF16)

    return pl.pallas_call(
        body,
        grid=(count + more,),
        in_specs=[
            pl.BlockSpec((t, d), lambda b: (0, 0)),
            pl.BlockSpec((t, d), lambda b: (0, 0)),
            pl.BlockSpec((None, t, c), lambda b: (jnp.minimum(b, count - 1), 0, 0)),
            pl.BlockSpec((None, t, c), lambda b: (jnp.maximum(b - count, 0), 0, 0)),
        ],
        out_specs=pl.BlockSpec((None, d, c), lambda b: (b, 0, 0)),
        out_shape=jax.ShapeDtypeStruct((count + more, d, c), BF16),
        scratch_shapes=[pltpu.VMEM((d, t), BF16)],
        compiler_params=params(),
        cost_estimate=pl.CostEstimate(
            flops=2 * (count + more) * t * d * c,
            bytes_accessed=2 * (2 * t * d + (count + more) * (d * c + t * c)),
            transcendentals=0,
        ),
    )(first, second, first_cols, second_cols)


def in_group(local, width, head_shift):
    quarter = width // 4
    low = jnp.bitwise_and(local, quarter - 1)
    one = jnp.where(jnp.bitwise_and(local, quarter) != 0, 2 * quarter, 0)
    two = jnp.where(jnp.bitwise_and(local, 2 * quarter) != 0, quarter, 0)
    return jnp.bitwise_xor(low + one + two, head_shift)


def key_position(block, width, head_shift, shape, axis):
    local = lax.broadcasted_iota(jnp.int32, shape, axis)
    return block * width + in_group(local, width, head_shift)


def attend(place, queries, keys_values, query_pos, first_pos, scale, p):
    m, e = queries.shape
    n = keys_values.shape[0]
    step = 256

    def body(place_ref, q_ref, kv_ref, pos_ref, first_ref, low_ref, full_ref, sum_ref, acc_ref, tot_ref):
        j = pl.program_id(0)

        @pl.when(j == 0)
        def _():
            acc_ref[...] = jnp.zeros_like(acc_ref)
            tot_ref[...] = jnp.zeros_like(tot_ref)

        @pl.when(j <= place_ref[0])
        def _():
            key_pos = key_position(j, p, place_ref[1], (1, p), 1)
            for r in range(0, m, step):
                rows = pl.ds(r, step)
                raw = mm(q_ref[rows, :], kv_ref[:p, :], NT)
                soft = SOFT_CAP * jnp.tanh(raw * (scale / SOFT_CAP))
                seen = (key_pos >= first_ref[rows, :]) & (key_pos <= pos_ref[rows, :])
                terms = jnp.where(seen, jnp.exp(soft), 0.0)
                tot_ref[rows, :] += jnp.sum(terms, axis=1, keepdims=True)
                acc_ref[rows, :] += mm(terms.astype(BF16), kv_ref[p:, :], NN)

        @pl.when(j == n - 1)
        def _():
            total = tot_ref[...]
            mixed = acc_ref[...] / total
            full_ref[...] = mixed
            low_ref[...] = mixed.astype(BF16)
            sum_ref[...] = total

    whole = lambda shape: pl.BlockSpec(shape, lambda j, s: (0, 0))
    return pl.pallas_call(
        body,
        grid_spec=pltpu.PrefetchScalarGridSpec(
            num_scalar_prefetch=1,
            grid=(n,),
            in_specs=[
                whole((m, e)),
                pl.BlockSpec((None, 2 * p, e), lambda j, s: (jnp.minimum(j, s[0]), 0, 0)),
                whole((m, 1)),
                whole((m, 1)),
            ],
            out_specs=[whole((m, e)), whole((m, e)), whole((m, 1))],
            scratch_shapes=[pltpu.VMEM((m, e), F32), pltpu.VMEM((m, 1), F32)],
        ),
        out_shape=[
            jax.ShapeDtypeStruct((m, e), BF16),
            jax.ShapeDtypeStruct((m, e), F32),
            jax.ShapeDtypeStruct((m, 1), F32),
        ],
        compiler_params=params(),
        cost_estimate=pl.CostEstimate(
            flops=4 * m * n * p * e, bytes_accessed=4 * n * p * e, transcendentals=2 * m * n * p
        ),
    )(place, queries, keys_values, query_pos, first_pos)


def attend_back(place, queries, grads, keys_values, inverse, delta, query_pos, first_pos, scale, p):
    m, e = queries.shape
    n = keys_values.shape[0]
    step = 256

    def body(
        place_ref, q_ref, g_ref, kv_ref, inv_ref, delta_ref, pos_ref, first_ref, dq_ref, dkv_ref, acc_ref, dk_ref, dv_ref
    ):
        j = pl.program_id(0)

        @pl.when(j == 0)
        def _():
            acc_ref[...] = jnp.zeros_like(acc_ref)

        @pl.when(j <= place_ref[0])
        def _():
            key_pos = key_position(j, p, place_ref[1], (p, 1), 0)
            for r in range(0, m, step):
                rows = pl.ds(r, step)
                raw = mm(kv_ref[:p, :], q_ref[rows, :], NT)
                capped = jnp.tanh(raw * (scale / SOFT_CAP))
                seen = (key_pos >= first_ref[:, rows]) & (key_pos <= pos_ref[:, rows])
                probs = jnp.where(seen, jnp.exp(SOFT_CAP * capped), 0.0) * inv_ref[:, rows]
                grad_probs = mm(kv_ref[p:, :], g_ref[rows, :], NT)
                grad_raw = probs * (grad_probs - delta_ref[:, rows]) * (1.0 - capped * capped)
                grad_low = grad_raw.astype(BF16)
                value_part = mm(probs.astype(BF16), g_ref[rows, :], NN)
                key_part = mm(grad_low, q_ref[rows, :], NN)
                if r == 0:
                    dv_ref[...] = value_part
                    dk_ref[...] = key_part
                else:
                    dv_ref[...] += value_part
                    dk_ref[...] += key_part
                acc_ref[rows, :] += mm(grad_low, kv_ref[:p, :], TN)
            dkv_ref[0] = dk_ref[...].astype(BF16)
            dkv_ref[1] = dv_ref[...].astype(BF16)

        @pl.when(j > place_ref[0])
        def _():
            dkv_ref[...] = jnp.zeros_like(dkv_ref)

        @pl.when(j == n - 1)
        def _():
            dq_ref[...] = (acc_ref[...] * scale).astype(BF16)

    whole = lambda shape: pl.BlockSpec(shape, lambda j, s: (0, 0))
    return pl.pallas_call(
        body,
        grid_spec=pltpu.PrefetchScalarGridSpec(
            num_scalar_prefetch=1,
            grid=(n,),
            in_specs=[
                whole((m, e)),
                whole((m, e)),
                pl.BlockSpec((None, 2 * p, e), lambda j, s: (jnp.minimum(j, s[0]), 0, 0)),
                whole((1, m)),
                whole((1, m)),
                whole((1, m)),
                whole((1, m)),
            ],
            out_specs=[whole((m, e)), pl.BlockSpec((None, 2, p, e), lambda j, s: (j, 0, 0, 0))],
            scratch_shapes=[pltpu.VMEM((m, e), F32), pltpu.VMEM((p, e), F32), pltpu.VMEM((p, e), F32)],
        ),
        out_shape=[jax.ShapeDtypeStruct((m, e), BF16), jax.ShapeDtypeStruct((n, 2, p, e), BF16)],
        compiler_params=params(),
        cost_estimate=pl.CostEstimate(
            flops=10 * m * n * p * e, bytes_accessed=8 * n * p * e, transcendentals=2 * m * n * p
        ),
    )(place, queries, grads, keys_values, inverse, delta, query_pos, first_pos)


def gelu_pair(gate):
    outer = math.sqrt(2.0 / math.pi)
    square = gate * gate
    bent = jnp.tanh(outer * gate * (1.0 + 0.044715 * square))
    half = 0.5 * (1.0 + bent)
    slope = half + 0.5 * gate * (1.0 - bent * bent) * outer * (1.0 + 3.0 * 0.044715 * square)
    return gate * half, slope


def ffn_front(place, rows, cots, early, late):
    part_rows, d = rows[0].shape
    t = 2 * part_rows
    count = len(early)
    r = early[0].shape[1]
    u, v = early[0].shape[2], late[0].shape[2]
    tall = min(512, t)
    wide = d // 3
    cuts = [(k, min(256, u + v - k)) for k in range(0, u + v, 256)]

    def body(place_ref, x0, x1, y0, y1, *refs):
        early_refs, late_refs = refs[:count], refs[count : 2 * count]
        hs_ref, w_out, dwe_ref, dwl_ref, x, y, w, xt, yt, hs, row_sems, sems, out_sems = refs[2 * count :]
        row_copies = []
        for k, (source, target) in enumerate(((x0, x), (x1, x), (y0, y), (y1, y))):
            target = target.at[pl.ds((k % 2) * part_rows, part_rows), :]
            row_copies.append(pltpu.make_async_copy(source, target, row_sems.at[k]))
            row_copies[k].start()
        copies = []
        for k in range(count):
            spot = pl.multiple_of(jnp.bitwise_xor(place_ref[0], k) * r, 16) if count > 1 else 0
            for source, lanes, way in ((early_refs[k], pl.ds(0, u), 0), (late_refs[k], pl.ds(u, v), 1)):
                copy = pltpu.make_async_copy(source, w.at[:, pl.ds(spot, r), lanes], sems.at[way, k])
                copy.start()
                copies.append(copy)
        for copy in row_copies:
            copy.wait()

        @pl.loop(0, d // 256)
        def _(k):
            cols = pl.ds(pl.multiple_of(k * 256, 256), 256)
            xt[cols, :] = x[:, cols].T
            yt[cols, :] = y[:, cols].T

        for copy in copies:
            copy.wait()
        kept = pltpu.make_async_copy(w, w_out, out_sems.at[0])
        kept.start()

        @pl.loop(0, t // tall)
        def _(i):
            part = pl.ds(pl.multiple_of(i * tall, tall), tall)
            for start, size in cuts:
                units = pl.ds(start, size)
                gate = mm(x[part, :], w[0, :, units], NN)
                up = mm(x[part, :], w[1, :, units], NN)
                grad = mm(y[part, :], w[2, :, units], NN)
                active, slope = gelu_pair(gate)
                hs[0, part, units] = (active * up).astype(BF16)
                hs[1, part, units] = (grad * up * slope).astype(BF16)
                hs[2, part, units] = (grad * active).astype(BF16)

        sides = pltpu.make_async_copy(hs, hs_ref, out_sems.at[1])
        sides.start()
        kept.wait()
        copies = []
        for kind, (left, right) in enumerate(((xt, 1), (xt, 2), (yt, 0))):

            @pl.loop(0, d // wide)
            def _(k):
                cols = pl.ds(pl.multiple_of(k * wide, wide), wide)
                w[kind, cols, :] = mm(left[cols, :], hs[right], NN).astype(BF16)

            for way, (lanes, target) in enumerate(((pl.ds(0, u), dwe_ref), (pl.ds(u, v), dwl_ref))):
                copy = pltpu.make_async_copy(w.at[kind, :, lanes], target.at[kind], out_sems.at[2 + 2 * kind + way])
                copy.start()
                copies.append(copy)
        sides.wait()
        for copy in copies:
            copy.wait()

    apart = pl.BlockSpec(memory_space=pl.ANY)
    return pl.pallas_call(
        body,
        grid_spec=pltpu.PrefetchScalarGridSpec(
            num_scalar_prefetch=1,
            grid=(1,),
            in_specs=[apart] * (4 + 2 * count),
            out_specs=[apart] * 4,
            scratch_shapes=[
                pltpu.VMEM((t, d), BF16),
                pltpu.VMEM((t, d), BF16),
                pltpu.VMEM((3, d, u + v), BF16),
                pltpu.VMEM((d, t), BF16),
                pltpu.VMEM((d, t), BF16),
                pltpu.VMEM((3, t, u + v), BF16),
                pltpu.SemaphoreType.DMA((4,)),
                pltpu.SemaphoreType.DMA((2, count)),
                pltpu.SemaphoreType.DMA((8,)),
            ],
        ),
        out_shape=[
            jax.ShapeDtypeStruct((3, t, u + v), BF16),
            jax.ShapeDtypeStruct((3, d, u + v), BF16),
            jax.ShapeDtypeStruct((3, d, u), BF16),
            jax.ShapeDtypeStruct((3, d, v), BF16),
        ],
        compiler_params=params(),
        cost_estimate=pl.CostEstimate(
            flops=12 * t * d * (u + v), bytes_accessed=12 * d * (u + v) + 4 * t * d, transcendentals=t * (u + v)
        ),
    )(place, *rows, *cots, *early, *late)


def ffn_back(sides, blocks):
    _, t, u = sides.shape
    d = blocks.shape[1]
    wide = 256

    def body(s_ref, w_ref, out_ref, dx_ref):
        out_ref[...] = mm(s_ref[0], w_ref[2], NT).astype(BF16)
        dx_ref[...] = (mm(s_ref[1], w_ref[0], NT) + mm(s_ref[2], w_ref[1], NT)).astype(BF16)

    return pl.pallas_call(
        body,
        grid=(d // wide,),
        in_specs=[
            pl.BlockSpec((3, t, u), lambda k: (0, 0, 0), pipeline_mode=pl.Buffered(1)),
            pl.BlockSpec((3, wide, u), lambda k: (0, k, 0)),
        ],
        out_specs=[pl.BlockSpec((t, wide), lambda k: (0, k)), pl.BlockSpec((t, wide), lambda k: (0, k))],
        out_shape=[jax.ShapeDtypeStruct((t, d), BF16), jax.ShapeDtypeStruct((t, d), BF16)],
        compiler_params=params(),
        cost_estimate=pl.CostEstimate(
            flops=6 * t * d * u, bytes_accessed=6 * d * u + 6 * t * u + 4 * t * d, transcendentals=0
        ),
    )(sides, blocks)


def gram_parts(m):
    h = m.shape[1] // 2
    high = m.astype(BF16)
    low = (m - high.astype(F32)).astype(BF16)
    mixed = mm(high, low, TN)
    gram = mm(high, high, TN) + mm(low, low, TN) + mixed + mixed.T
    return gram[:h, :h], gram[:h, h:], gram[h:, h:]


TRIO = 3


def ffn_moment(low_early, low_late, high_early, high_late, momentum, first, blocks, places):
    total, r, c = momentum.shape
    early = low_early.shape[2] // c
    h = c // 2
    full = early + 1
    each = blocks // TRIO

    def body(le_ref, ll_ref, he_ref, hl_ref, m_ref, wg_ref, nm_ref, gram_ref):
        j = pl.program_id(0)

        @pl.when(j >= TRIO * each)
        def _():
            gram_ref[...] = jnp.zeros_like(gram_ref)

        for turn in range(each):

            @pl.when((j < TRIO * each) & (lax.rem(j, each) == turn))
            def _():
                for i in range(TRIO):
                    side, f = divmod(turn * TRIO + i, full)
                    if side == 2:
                        wg_ref[i, :, :h] = ll_ref[:, c:]
                        wg_ref[i, :, h:] = hl_ref[:, c:]
                    elif f < early:
                        wg_ref[i] = (le_ref, he_ref)[side][:, f * c : (f + 1) * c]
                    else:
                        wg_ref[i] = (ll_ref, hl_ref)[side][:, :c]

        @pl.when(j < TRIO * each)
        def _():
            for i in range(TRIO):
                new = MUON_BETA * m_ref[i] + wg_ref[i]
                nm_ref[i] = new
                gram_ref[i, 0], gram_ref[i, 1], gram_ref[i, 2] = gram_parts(new)

    kind = lambda j: (jnp.minimum(j // each, 2), 0, 0)
    block = lambda j: (first // TRIO + jnp.minimum(j, TRIO * each - 1), 0, 0)
    u, v = low_early.shape[2], low_late.shape[2]
    return pl.pallas_call(
        body,
        grid=(places // TRIO,),
        in_specs=[
            pl.BlockSpec((None, r, u), kind),
            pl.BlockSpec((None, r, v), kind),
            pl.BlockSpec((None, r, u), kind),
            pl.BlockSpec((None, r, v), kind),
            pl.BlockSpec((TRIO, r, c), block),
        ],
        out_specs=[
            pl.BlockSpec((TRIO, r, c), block),
            pl.BlockSpec((TRIO, r, c), block),
            pl.BlockSpec((TRIO, 3, h, h), lambda j: (j, 0, 0, 0)),
        ],
        out_shape=[
            jax.ShapeDtypeStruct((total, r, c), F32),
            jax.ShapeDtypeStruct((total, r, c), F32),
            jax.ShapeDtypeStruct((places, 3, h, h), F32),
        ],
        compiler_params=params(),
        cost_estimate=pl.CostEstimate(
            flops=6 * 3 * blocks * r * c * c, bytes_accessed=16 * 3 * blocks * r * c, transcendentals=0
        ),
    )(low_early, low_late, high_early, high_late, momentum)


def attn_moment(grads, momentum, weight_grads, new_momentum):
    count, r, c = grads.shape
    h = c // 2

    def body(g_ref, m_ref, wg_in, nm_in, wg_ref, nm_ref, gram_ref):
        for i in range(TRIO):
            new = MUON_BETA * m_ref[i] + g_ref[i]
            wg_ref[i] = g_ref[i]
            nm_ref[i] = new
            gram_ref[i, 0], gram_ref[i, 1], gram_ref[i, 2] = gram_parts(new)

    block = pl.BlockSpec((TRIO, r, c), lambda j: (j, 0, 0))
    apart = pl.BlockSpec(memory_space=pl.ANY)
    return pl.pallas_call(
        body,
        grid=(count // TRIO,),
        in_specs=[block, block, apart, apart],
        out_specs=[block, block, pl.BlockSpec((TRIO, 3, h, h), lambda j: (j, 0, 0, 0))],
        out_shape=[
            jax.ShapeDtypeStruct(momentum.shape, F32),
            jax.ShapeDtypeStruct(momentum.shape, F32),
            jax.ShapeDtypeStruct((count, 3, h, h), F32),
        ],
        input_output_aliases={2: 0, 3: 1},
        compiler_params=params(),
        cost_estimate=pl.CostEstimate(
            flops=6 * count * r * c * c, bytes_accessed=16 * count * r * c, transcendentals=0
        ),
    )(grads, momentum, weight_grads, new_momentum)


def renew(weights, momentum, factors, spots, updated):
    _, r, c = weights.shape
    h = c // 2
    steps = len(spots)
    table = jnp.array([spot for spot, _ in spots] + [f for _, places in spots for f in places], jnp.int32)

    def body(s_ref, w_ref, m_ref, *refs):
        factor_refs, o_ref = refs[:TRIO], refs[-1]
        for i in range(TRIO):
            left = m_ref[i, :, :h].astype(BF16)
            right = m_ref[i, :, h:].astype(BF16)
            first, off, last = factor_refs[i][0], factor_refs[i][1], factor_refs[i][2]
            start = mm(left, first, NN) + mm(right, off, NT)
            rest = mm(left, off, NN) + mm(right, last, NN)
            keep = 1.0 - MUON_RATE * MUON_DECAY
            o_ref[i, :, :h] = w_ref[i, :, :h] * keep - MUON_RATE * start
            o_ref[i, :, h:] = w_ref[i, :, h:] * keep - MUON_RATE * rest

    block = pl.BlockSpec((TRIO, r, c), lambda j, s: (s[j], 0, 0))

    def factor_at(i):
        return pl.BlockSpec((None, 3, h, h), lambda j, s: (s[steps + TRIO * j + i], 0, 0, 0))

    apart = [pl.BlockSpec(memory_space=pl.ANY)] * len(updated)
    return pl.pallas_call(
        body,
        grid_spec=pltpu.PrefetchScalarGridSpec(
            num_scalar_prefetch=1,
            grid=(steps,),
            in_specs=[block, block] + [factor_at(i) for i in range(TRIO)] + apart,
            out_specs=block,
        ),
        out_shape=jax.ShapeDtypeStruct(weights.shape, F32),
        input_output_aliases={3 + TRIO: 0} if updated else {},
        compiler_params=params(),
        cost_estimate=pl.CostEstimate(
            flops=2 * TRIO * steps * r * c * c, bytes_accessed=12 * TRIO * steps * r * c, transcendentals=0
        ),
    )(table, weights, momentum, *([factors] * TRIO), *updated)


def top(spec, a, b):
    return jnp.einsum(spec, a, b, precision=TOP_PRECISION)


def newton_factor(grams, growth):
    size = grams.shape[-1]
    eye = jnp.eye(size, dtype=F32)
    norm = jnp.sqrt(jnp.sum(grams * eye, axis=(1, 2), keepdims=True))
    inverse = 1.0 / (norm + 1e-07)
    gram = grams * (inverse * inverse)
    factor = None
    for sweep in range(NEWTON_STEPS):
        square = top("bij,bjk->bik", gram, gram)
        poly = NEWTON_LINEAR * eye + NEWTON_SQUARE * gram + NEWTON_CUBIC * square
        factor = poly if sweep == 0 else top("bij,bjk->bik", factor, poly)
        if sweep < NEWTON_STEPS - 1:
            gram = top("bij,bjk->bik", top("bij,bjk->bik", gram, poly), poly)
    return factor * (growth * inverse)


def fold(squares):
    h = squares.shape[1] // 2
    return jnp.stack([squares[:, :h, :h], squares[:, :h, h:], squares[:, h:, h:]], axis=1)


def unfold(parts):
    first, off, last = parts[:, 0], parts[:, 1], parts[:, 2]
    upper = jnp.concatenate([first, off], axis=2)
    lower = jnp.concatenate([jnp.swapaxes(off, 1, 2), last], axis=2)
    return jnp.concatenate([upper, lower], axis=1)


def gram_sums(ring, parts, cap):
    h = parts.shape[2]
    parts = parts.reshape(-1, h, h)
    rows = 3 * cap
    mine = yield from ring.scatter(lambda i: lax.dynamic_slice_in_dim(parts, i * rows, rows, 0), rows // 2)
    return unfold(mine.reshape(cap, 3, h, h))


def all_factors(ring, factors):
    cap, c, _ = factors.shape
    parts = fold(factors.astype(BF16)).reshape(3 * cap, c // 2, c // 2)
    parts = yield from ring.gather(parts, 3 * cap // 2)
    return parts.reshape(ring.size * cap, 3, c // 2, c // 2)


def on_device(block_in, cotangent, seq_ids, weights, momentum, gains, gain_first, gain_second):
    tok_rows, model_width = block_in.shape
    rows_dp, group_blocks, head_dim = weights.shape
    head_count = lax.axis_size("head")
    data_count = lax.axis_size("dp")
    group_rows = tok_rows * head_count
    key_heads = KV // head_count
    query_heads = H // head_count
    ffn_blocks = FF // (head_dim * head_count)
    out_mark = query_heads + 2 * key_heads
    gate_mark = out_mark + query_heads
    half_dim = head_dim // 2
    full = ffn_blocks // 2
    scale = head_dim ** (-0.5)
    growth = math.sqrt(max(1.0, model_width / head_dim))
    data_index = lax.axis_index("dp")
    head_index = lax.axis_index("head")
    parity = (data_index >> 1) & 1
    ring = Ring()

    weights = jnp.transpose(weights, (1, 0, 2))
    momentum = jnp.transpose(momentum, (1, 0, 2))
    attn_low = weights[:gate_mark].astype(BF16)
    inputs = block_in.astype(F32)
    normed_one, norm_one_back = jax.vjp(rms_scale, inputs, gains[0])
    ids_column = jnp.pad(seq_ids.astype(BF16)[:, None], ((0, 0), (0, 127)))

    early = full - 1

    def pack(side, late):
        tiles = range(side * full + early, (side + 1) * full) if late else range(side * full, side * full + early)
        lanes = slice(side * half_dim, (side + 1) * half_dim)
        rest = [2 * full] if late else []
        rows = [
            jnp.concatenate([kind[f] for f in tiles] + [kind[f, :, lanes] for f in rest], axis=1) for kind in kinds
        ]
        return jnp.stack(rows).astype(BF16)

    def own_and_other(late):
        sides = (pack(0, late), pack(1, late))
        return jnp.where(parity == 1, sides[1], sides[0]), jnp.where(parity == 1, sides[0], sides[1])

    qkv_flow = Flow(ring.gather(attn_low[:out_mark], out_mark // 2))
    group_flow = Flow(head_gather(jnp.concatenate([normed_one.astype(BF16), ids_column], axis=1)))
    cot_flow = Flow(wide_gather(cotangent))
    stage([qkv_flow, group_flow])
    weights, attn_low = stage([qkv_flow, group_flow], [weights, attn_low])
    kinds = [weights[gate_mark + k * ffn_blocks : gate_mark + (k + 1) * ffn_blocks] for k in range(3)]
    sides = own_and_other(False) + own_and_other(True)
    sides = stage([qkv_flow], sides)
    finish(qkv_flow)
    spread = [Spread(*sides[:2]), Spread(*sides[2:])]
    group_in = group_flow.value
    qkv_blocks = jnp.transpose(qkv_flow.value, (1, 0, 2, 3)).reshape(out_mark, model_width, head_dim)

    projected = block_project(group_in, qkv_blocks)
    queries = projected[:query_heads].reshape(query_heads * group_rows, head_dim)
    group_ids = group_in[:, model_width]
    kv_rows = 2 * key_heads * group_rows
    out_rows = query_heads * rows_dp
    id_rows = group_rows // head_dim
    packed = jnp.concatenate(
        [
            projected[query_heads:].reshape(kv_rows, head_dim),
            attn_low[out_mark:].reshape(out_rows, head_dim),
            jnp.pad(group_ids.reshape(id_rows, head_dim), ((0, 16 - id_rows), (0, 0))),
        ],
        axis=0,
    )
    keys_values = run(ring.gather(packed, packed.shape[0] // 32 * 16))
    out_blocks = keys_values[:, kv_rows : kv_rows + out_rows].reshape(data_count, query_heads, rows_dp, head_dim)
    out_blocks = jnp.transpose(out_blocks, (1, 0, 2, 3)).reshape(query_heads, model_width, head_dim)
    queries, keys_values, out_blocks = stage(
        [spread[0].z(3), spread[0].z(1), spread[0].y(0)], [queries, keys_values, out_blocks]
    )
    all_ids = keys_values[:, kv_rows + out_rows : kv_rows + out_rows + id_rows].reshape(-1)

    local = in_group(jnp.arange(group_rows, dtype=jnp.int32), group_rows, head_index * tok_rows)
    query_pos = data_index * group_rows + local
    first_pos = jnp.sum((all_ids[None, :] < group_ids[:, None]).astype(jnp.int32), axis=1)
    query_pos = jnp.tile(query_pos, query_heads)
    first_pos = jnp.tile(first_pos, query_heads)
    place = jnp.stack([data_index, head_index * tok_rows]).astype(jnp.int32)
    mixed_low, mixed_full, totals = attend(
        place, queries, keys_values, query_pos[:, None], first_pos[:, None], scale, group_rows
    )
    mixed_heads = mixed_low.reshape(query_heads, group_rows, head_dim)
    mixed_heads, mixed_full, totals, attn_part = stage(
        [spread[0].z(2), spread[0].y(3), spread[0].y(1)],
        [mixed_heads, mixed_full, totals, block_back(mixed_heads, out_blocks)],
    )
    attn_flow = Flow(scatter_rows(attn_part, HEAD_MOVES))
    stage([attn_flow, spread[0].y(2), cot_flow])
    stage([attn_flow, spread[1].z(3), spread[1].z(1), spread[1].y(0)])
    residual = inputs + attn_flow.value
    normed_two, norm_two_back = jax.vjp(rms_scale, residual, gains[1])
    wide_flow = Flow(wide_gather(normed_two.astype(BF16)))
    stage([wide_flow, cot_flow, spread[1].y(1)])
    stage([wide_flow, spread[1].z(2), spread[1].y(3)])
    stage([wide_flow, cot_flow, spread[1].y(2)])
    finish(wide_flow, cot_flow)

    def whole_rows(pieces):
        if rows_dp % 16 == 0:
            return pieces
        out = jnp.zeros((3, data_count) + pieces[0].shape[1:], BF16)
        for k, piece in enumerate(pieces):
            out = lax.dynamic_update_index_in_dim(out, piece, data_index ^ k, 1)
        return [out.reshape(3, model_width, -1)]

    ffn_sides, ffn_full, grads_early, grads_late = ffn_front(
        place, wide_flow.value, cot_flow.value, whole_rows(spread[0].value()), whole_rows(spread[1].value())
    )

    def taker(grads):
        cut = grads.reshape(3, data_count, rows_dp, grads.shape[2])
        return lambda index: lax.dynamic_index_in_dim(cut, index, 1, keepdims=False)

    reduce = [Reduce(taker(grads_early)), Reduce(taker(grads_late))]
    down_part, dx_part = stage([reduce[0].y(3)], ffn_back(ffn_sides, ffn_full))
    dx_flow = Flow(scatter_rows(dx_part, WIDE_MOVES))
    out_flow = Flow(scatter_rows(down_part, WIDE_MOVES))
    stage([dx_flow, reduce[1].y(3)])
    stage([dx_flow, reduce[0].z(3), reduce[0].y(2), reduce[1].y(2)])
    stage([dx_flow, reduce[1].z(3), reduce[1].y(1), out_flow])
    grad_residual_norm, grad_gain_two = norm_two_back(dx_flow.value)
    grad_residual = cotangent.astype(F32) + grad_residual_norm
    grad_flow = Flow(head_gather(grad_residual.astype(BF16)))
    stage([grad_flow, reduce[1].z(2), reduce[0].y(1)])
    stage([grad_flow, reduce[1].z(1)])
    group_grad = grad_flow.value

    grad_heads = block_project(group_grad, out_blocks)
    grad_mixed = grad_heads.reshape(query_heads * group_rows, head_dim)
    delta = jnp.sum(grad_mixed.astype(F32) * mixed_full, axis=1)
    grad_queries, grad_keys_values = attend_back(
        place,
        queries,
        grad_mixed,
        keys_values,
        1.0 / totals.reshape(1, -1),
        delta[None, :],
        query_pos[None, :],
        first_pos[None, :],
        scale,
        group_rows,
    )
    grad_queries, grad_keys_values = stage(
        [reduce[0].z(2), reduce[0].y(0), reduce[1].y(0), out_flow], [grad_queries, grad_keys_values]
    )
    key_flow = Flow(
        ring.scatter(lambda i: lax.dynamic_index_in_dim(grad_keys_values, i, 0, keepdims=False), key_heads)
    )
    stage([key_flow, reduce[0].z(1)])
    stage([key_flow, out_flow])
    finish(key_flow, out_flow)
    key_value_sums = key_flow.value
    block_out = (residual + out_flow.value).astype(BF16)

    late = 2
    main = 3 * ffn_blocks - late
    cap = -(-main // data_count)
    places = -(-max(cap * data_count, 3 * ffn_blocks) // TRIO) * TRIO
    own_early, other_early = reduce[0].sums
    own_late, other_late = reduce[1].sums
    pick = lambda own, other: (jnp.where(parity == 1, other, own), jnp.where(parity == 1, own, other))
    (low_early, high_early), (low_late, high_late) = pick(own_early, other_early), pick(own_late, other_late)
    grad_projected = jnp.concatenate(
        [
            grad_queries.reshape(query_heads, group_rows, head_dim),
            (key_value_sums[:key_heads] * scale).astype(BF16),
            key_value_sums[key_heads:].astype(BF16),
        ],
        axis=0,
    )
    attn_outer = block_outer(group_in, group_grad, grad_projected, mixed_heads, model_width)
    attn_outer = attn_outer.reshape(gate_mark, data_count, rows_dp, head_dim)
    weight_flow = Flow(
        ring.scatter(lambda i: lax.dynamic_index_in_dim(attn_outer, i, 1, keepdims=False), gate_mark // 2)
    )
    weight_grads, new_momentum, grams, attn_dx = stage(
        [weight_flow],
        [
            *ffn_moment(low_early, low_late, high_early, high_late, momentum, gate_mark, ffn_blocks, places),
            block_back(grad_projected, qkv_blocks),
        ],
    )
    last_flow = Flow(scatter_rows(attn_dx, HEAD_MOVES))
    gram_flow = Flow(gram_sums(ring, grams, cap))
    while weight_flow.sends is not None:
        stage([weight_flow, gram_flow, last_flow])
    finish(last_flow)
    grad_input_norm, grad_gain_one = norm_one_back(last_flow.value)
    grad_input = grad_residual + grad_input_norm
    gain_flow = Flow(total_sum(jnp.stack([grad_gain_one, grad_gain_two])))
    weight_grads, new_momentum, attn_grams = stage(
        [gram_flow, gain_flow], attn_moment(weight_flow.value, momentum, weight_grads, new_momentum)
    )
    late_count = gate_mark + late
    late_cap = -(-late_count // data_count)
    late_grams = jnp.concatenate([attn_grams, grams[main : main + late]], axis=0)
    late_grams = jnp.pad(late_grams, ((0, late_cap * data_count - late_count), (0, 0), (0, 0), (0, 0)))
    late_gram_flow = Flow(gram_sums(ring, late_grams, late_cap))
    finish(gram_flow)
    (factors,) = stage([late_gram_flow, gain_flow], [newton_factor(gram_flow.value, growth)])
    factor_flow = Flow(all_factors(ring, factors))
    while late_gram_flow.sends is not None:
        stage([late_gram_flow, factor_flow, gain_flow])
    (late_factors,) = stage([factor_flow, gain_flow], [newton_factor(late_gram_flow.value, growth)])
    finish(factor_flow)
    late_factor_flow = Flow(all_factors(ring, late_factors))

    threes = main // TRIO
    early_spots = [(gate_mark // TRIO + k, [TRIO * k + i for i in range(TRIO)]) for k in range(threes)]
    (new_weights,) = stage(
        [late_factor_flow, gain_flow], [renew(weights, new_momentum, factor_flow.value, early_spots, [])]
    )
    finish(late_factor_flow, gain_flow)
    gain_grads = gain_flow.value
    rest = jnp.concatenate([late_factor_flow.value[:late_count], factor_flow.value[TRIO * threes : main]], axis=0)
    blocks_of = list(range(gate_mark)) + [None] * late + [gate_mark + k for k in range(TRIO * threes, main)]
    for k in range(late):
        blocks_of[gate_mark + k] = gate_mark + main + k
    late_spots = [
        (spot, [blocks_of.index(TRIO * spot + i) for i in range(TRIO)])
        for spot in sorted({block // TRIO for block in blocks_of})
    ]
    new_weights = renew(weights, new_momentum, rest, late_spots, [new_weights])

    new_gain_first = BETA_ONE * gain_first + (1.0 - BETA_ONE) * gain_grads
    new_gain_second = BETA_TWO * gain_second + (1.0 - BETA_TWO) * gain_grads * gain_grads
    first_hat = new_gain_first / (1.0 - BETA_ONE**UPDATE_STEP)
    second_hat = new_gain_second / (1.0 - BETA_TWO**UPDATE_STEP)
    new_gains = gains - ADAM_RATE * first_hat / (jnp.sqrt(second_hat) + ADAM_EPS)
    back = lambda array: jnp.transpose(array, (1, 0, 2))
    return (
        block_out,
        grad_input,
        back(weight_grads),
        back(new_momentum),
        back(new_weights),
        gain_grads,
        new_gain_first,
        new_gain_second,
        new_gains,
    )


def solution(mesh):
    return jax.shard_map(
        on_device,
        mesh=mesh,
        in_specs=(
            P(("dp", "head"), None),
            P(("dp", "head"), None),
            P(("dp", "head")),
            P("dp", "head", None),
            P("dp", "head", None),
            P(),
            P(),
            P(),
        ),
        out_specs=(
            P(("dp", "head"), None),
            P(("dp", "head"), None),
            P("dp", "head", None),
            P("dp", "head", None),
            P("dp", "head", None),
            P(),
            P(),
            P(),
            P(),
        ),
        check_vma=False,
    )
```

```python
import functools
import math

import jax
import jax.numpy as jnp
from jax import lax
from jax.experimental import pallas as pl
from jax.experimental.pallas import tpu as pltpu
from jax.sharding import PartitionSpec as P

H = 8
KV = 4
FF = 9216
NEWTON_STEPS = 5
UPDATE_STEP = 10

NORM_EPS = 1e-06
SOFT_CAP = 50.0
MUON_RATE = 0.2
MUON_DECAY = 0.01
MUON_BETA = 0.95
ADAM_RATE = 0.3
BETA_ONE = 0.9
BETA_TWO = 0.95
ADAM_EPS = 1e-08
NEWTON_LINEAR = 3.4445
NEWTON_SQUARE = -4.775
NEWTON_CUBIC = 2.0315
TOP_PRECISION = lax.Precision.HIGHEST

BF16 = jnp.bfloat16
F32 = jnp.float32
VMEM_LIMIT = 62 * 1024 * 1024
NN = (((1,), (0,)), ((), ()))
NT = (((1,), (1,)), ((), ()))
TN = (((0,), (0,)), ((), ()))


def mm(a, b, dims):
    return lax.dot_general(a, b, dims, preferred_element_type=F32)


def rms_scale(rows, gain):
    inverse = lax.rsqrt(jnp.mean(rows * rows, axis=-1, keepdims=True) + NORM_EPS)
    return rows * inverse * gain


class Flow:
    def __init__(self, steps):
        self.steps = steps
        self.value = None
        self.sends = None
        self.advance(None)

    def advance(self, arrived):
        try:
            self.sends = self.steps.send(arrived)
        except StopIteration as stop:
            self.sends = None
            self.value = stop.value


def stage(flows, extra=(), idle=()):
    flows = [flow for flow in flows if flow.sends is not None]
    idle = [flow for flow in idle if flow.sends is not None and flow not in flows]
    arrived = [[lax.ppermute(*send) for send in flow.sends] for flow in flows]
    held = [[send[0] for send in flow.sends] for flow in idle]
    arrived, held, extra = lax.optimization_barrier((arrived, held, list(extra)))
    for flow, got in zip(flows, arrived):
        flow.advance(got)
    for flow, kept in zip(idle, held):
        flow.sends = [(value,) + send[1:] for value, send in zip(kept, flow.sends)]
    return extra


def run(steps):
    flow = Flow(steps)
    while flow.sends is not None:
        flow.advance([lax.ppermute(*send) for send in flow.sends])
    return flow.value


def finish(*flows):
    while any(flow.sends is not None for flow in flows):
        stage(flows)


def swap(value, axis, mask):
    size = lax.axis_size(axis)
    return (value, axis, [(i, i ^ mask) for i in range(size)])


def head_gather(rows):
    (other,) = yield [swap(rows, "head", 2)]
    pair = jnp.concatenate([rows, other], axis=0)
    (other,) = yield [swap(pair, "head", 1)]
    return jnp.concatenate([pair, other], axis=0)


def wide_gather(rows):
    (other,) = yield [swap(rows, "dp", 2)]
    both = jnp.concatenate([rows, other], axis=0)
    (other,) = yield [swap(both, "head", 2)]
    pair = jnp.concatenate([both, other], axis=0)
    (other,) = yield [swap(pair, "head", 1)]
    return [pair, other]


def add_low(kept, other):
    return (kept.astype(F32) + other.astype(F32)).astype(BF16)


def scatter_rows(kept, sent, moves):
    for k, (axis, mask) in enumerate(moves):
        (other,) = yield [swap(sent, axis, mask)]
        part = kept.astype(F32) + other.astype(F32)
        if k < len(moves) - 1:
            half = part.shape[0] // 2
            kept, sent = part[:half], part[half:].astype(BF16)
    return part


HEAD_MOVES = (("head", 1), ("head", 2))
WIDE_MOVES = (("head", 1), ("head", 2), ("dp", 2))


def total_sum(value):
    for axis in ("head", "dp"):
        mask = 1
        while mask < lax.axis_size(axis):
            (other,) = yield [swap(value, axis, mask)]
            value = value + other
            mask *= 2
    return value


class Ring:
    def __init__(self):
        size = lax.axis_size("dp")
        order = list(range(0, size, 2)) + list(range(size - 1, 0, -2))
        around = [[order[(order.index(i) + offset) % size] for offset in range(size)] for i in range(size)]
        self.size = size
        self.around = jnp.array(around, jnp.int32)[lax.axis_index("dp")]
        self.up = [(order[k], order[(k + 1) % size]) for k in range(size)]
        self.down = [(order[(k + 1) % size], order[k]) for k in range(size)]

    def index(self, offset):
        return self.around[offset % self.size]

    def gather(self, value, mid):
        half = self.size // 2
        zeros = (0,) * (value.ndim - 1)
        out = jnp.zeros((self.size,) + value.shape, value.dtype)
        out = lax.dynamic_update_index_in_dim(out, value, self.index(0), 0)
        ahead, back = value, value
        for step in range(1, half):
            ahead, back = yield [(ahead, "dp", self.up), (back, "dp", self.down)]
            out = lax.dynamic_update_index_in_dim(out, ahead, self.index(-step), 0)
            out = lax.dynamic_update_index_in_dim(out, back, self.index(step), 0)
        first, second = yield [(ahead[:mid], "dp", self.up), (back[mid:], "dp", self.down)]
        far = self.index(half)
        out = lax.dynamic_update_slice(out, first[None], (far, 0) + zeros)
        return lax.dynamic_update_slice(out, second[None], (far, mid) + zeros)

    def scatter(self, take, mid):
        half = self.size // 2
        far = take(self.index(half))
        kind = far.dtype
        up, down = yield [(far[:mid], "dp", self.up), (far[mid:], "dp", self.down)]
        for step in range(half - 1, 0, -1):
            part = take(self.index(step)).astype(F32)
            ahead = jnp.concatenate([part[:mid] + up, part[mid:]]) if step == half - 1 else part + up
            part = take(self.index(-step)).astype(F32)
            back = jnp.concatenate([part[:mid], part[mid:] + down]) if step == half - 1 else part + down
            up, down = yield [(ahead.astype(kind), "dp", self.up), (back.astype(kind), "dp", self.down)]
        return take(self.index(0)).astype(F32) + up.astype(F32) + down.astype(F32)


def once(sends, take):
    def steps():
        take((yield sends))

    return Flow(steps())


def plane_group(key):
    planes = lax.axis_size("dp") // 2
    return [key] if key < 2 else list(range(key, planes, 2))


class Spread:
    def __init__(self, mine, other):
        self.mine, self.other = mine, other
        self.pieces = {0: mine}

    def z(self, key):
        group = plane_group(key)

        def take(arrived):
            for offset, piece in zip(group, arrived):
                self.pieces[offset << 1] = piece

        return once([swap(self.other if key & 1 else self.mine, "dp", offset << 1) for offset in group], take)

    def y(self, key):
        group = plane_group(key)

        def take(arrived):
            for offset, piece in zip(group, arrived):
                self.pieces[offset << 1 | 1] = piece

        return once([swap(self.pieces[offset << 1], "dp", 1) for offset in group], take)

    def value(self):
        return [self.pieces[k] for k in range(lax.axis_size("dp"))]


class Reduce:
    def __init__(self, rows):
        self.rows = rows
        self.totals = {}
        self.sums = [None, None]

    def y(self, key):
        me = lax.axis_index("dp")
        group = plane_group(key)

        def take(arrived):
            for offset, got in zip(group, arrived):
                self.totals[offset] = self.rows(me ^ (offset << 1)).astype(F32) + got.astype(F32)
                if offset:
                    self.totals[offset] = self.totals[offset].astype(BF16)
                else:
                    self.add(0, self.totals[0])

        return once([swap(self.rows(me ^ (offset << 1) ^ 1), "dp", 1) for offset in group], take)

    def z(self, key):
        group = plane_group(key)

        def take(arrived):
            for offset, got in zip(group, arrived):
                self.add(offset & 1, got.astype(F32))

        return once([swap(self.totals[offset], "dp", offset << 1) for offset in group], take)

    def add(self, side, value):
        self.sums[side] = value if self.sums[side] is None else self.sums[side] + value


def params(**more):
    return pltpu.CompilerParams(vmem_limit_bytes=VMEM_LIMIT, **more)


def block_project(rows, blocks):
    t = rows.shape[0]
    count, d, c = blocks.shape

    def body(x_ref, w_ref, o_ref):
        o_ref[...] = mm(x_ref[...], w_ref[...], NN).astype(BF16)

    return pl.pallas_call(
        body,
        grid=(count,),
        in_specs=[
            pl.BlockSpec((t, d), lambda b: (0, 0)),
            pl.BlockSpec((None, d, c), lambda b: (b, 0, 0)),
        ],
        out_specs=pl.BlockSpec((None, t, c), lambda b: (b, 0, 0)),
        out_shape=jax.ShapeDtypeStruct((count, t, c), BF16),
        compiler_params=params(),
        cost_estimate=pl.CostEstimate(
            flops=2 * count * t * d * c, bytes_accessed=2 * (t * d + count * (d * c + t * c)), transcendentals=0
        ),
    )(rows, blocks)


def block_back(cols, blocks):
    count, t, c = cols.shape
    d = blocks.shape[1]
    half = t // 2

    def body(x_ref, w_ref, o_ref, p_ref, acc_ref):
        b = pl.program_id(0)

        @pl.when(b == 0)
        def _():
            acc_ref[...] = jnp.zeros_like(acc_ref)

        acc_ref[...] += mm(x_ref[...], w_ref[...], NT)

        @pl.when(b == count - 1)
        def _():
            o_ref[...] = acc_ref[:half, :].astype(BF16)
            p_ref[...] = acc_ref[half:, :].astype(BF16)

    result = pl.BlockSpec((half, d), lambda b: (0, 0))
    return pl.pallas_call(
        body,
        grid=(count,),
        in_specs=[
            pl.BlockSpec((None, t, c), lambda b: (b, 0, 0)),
            pl.BlockSpec((None, d, c), lambda b: (b, 0, 0)),
        ],
        out_specs=[result, result],
        out_shape=[jax.ShapeDtypeStruct((half, d), BF16)] * 2,
        scratch_shapes=[pltpu.VMEM((t, d), F32)],
        compiler_params=params(),
        cost_estimate=pl.CostEstimate(
            flops=2 * count * t * d * c, bytes_accessed=2 * (t * d + count * (d * c + t * c)), transcendentals=0
        ),
    )(cols, blocks)


def block_outer(rows, cols, d):
    t = rows[0].shape[0]
    c = cols[0].shape[2]
    starts = [0]
    for col in cols:
        starts.append(starts[-1] + col.shape[0])
    count = len(rows)
    total = starts[-1]

    def body(*refs):
        o_ref, t_ref = refs[2 * count :]
        b = pl.program_id(0)
        for k in range(count):

            @pl.when(b == starts[k])
            def _():
                t_ref[...] = refs[k][...].T

            @pl.when((b >= starts[k]) & (b < starts[k + 1]))
            def _():
                o_ref[...] = mm(t_ref[...], refs[count + k][...], NN).astype(BF16)

    def col_at(k):
        return pl.BlockSpec((None, t, c), lambda b: (jnp.clip(b - starts[k], 0, starts[k + 1] - starts[k] - 1), 0, 0))

    return pl.pallas_call(
        body,
        grid=(total,),
        in_specs=[pl.BlockSpec((t, d), lambda b: (0, 0))] * count + [col_at(k) for k in range(count)],
        out_specs=pl.BlockSpec((None, d, c), lambda b: (b, 0, 0)),
        out_shape=jax.ShapeDtypeStruct((total, d, c), BF16),
        scratch_shapes=[pltpu.VMEM((d, t), BF16)],
        compiler_params=params(),
        cost_estimate=pl.CostEstimate(
            flops=2 * total * t * d * c,
            bytes_accessed=2 * (count * t * d + total * (d * c + t * c)),
            transcendentals=0,
        ),
    )(*rows, *cols)


def in_group(local, width, head_shift):
    quarter = width // 4
    low = jnp.bitwise_and(local, quarter - 1)
    one = jnp.where(jnp.bitwise_and(local, quarter) != 0, 2 * quarter, 0)
    two = jnp.where(jnp.bitwise_and(local, 2 * quarter) != 0, quarter, 0)
    return jnp.bitwise_xor(low + one + two, head_shift)


def key_position(block, width, head_shift, shape, axis):
    local = lax.broadcasted_iota(jnp.int32, shape, axis)
    return block * width + in_group(local, width, head_shift)


def attend(place, queries, keys_values, query_pos, first_pos, scale, p):
    m, e = queries.shape
    n = keys_values.shape[0]
    step = 256

    def body(place_ref, q_ref, kv_ref, pos_ref, first_ref, low_ref, full_ref, sum_ref, acc_ref, tot_ref):
        j = pl.program_id(0)

        @pl.when(j == 0)
        def _():
            acc_ref[...] = jnp.zeros_like(acc_ref)
            tot_ref[...] = jnp.zeros_like(tot_ref)

        @pl.when(j <= place_ref[0])
        def _():
            key_pos = key_position(j, p, place_ref[1], (1, p), 1)
            for r in range(0, m, step):
                rows = pl.ds(r, step)
                raw = mm(q_ref[rows, :], kv_ref[:p, :], NT)
                soft = SOFT_CAP * jnp.tanh(raw * (scale / SOFT_CAP))
                seen = (key_pos >= first_ref[rows, :]) & (key_pos <= pos_ref[rows, :])
                terms = jnp.where(seen, jnp.exp(soft), 0.0)
                tot_ref[rows, :] += jnp.sum(terms, axis=1, keepdims=True)
                acc_ref[rows, :] += mm(terms.astype(BF16), kv_ref[p:, :], NN)

        @pl.when(j == n - 1)
        def _():
            total = tot_ref[...]
            mixed = acc_ref[...] / total
            full_ref[...] = mixed
            low_ref[...] = mixed.astype(BF16)
            sum_ref[...] = total

    whole = lambda shape: pl.BlockSpec(shape, lambda j, s: (0, 0))
    return pl.pallas_call(
        body,
        grid_spec=pltpu.PrefetchScalarGridSpec(
            num_scalar_prefetch=1,
            grid=(n,),
            in_specs=[
                whole((m, e)),
                pl.BlockSpec((None, 2 * p, e), lambda j, s: (jnp.minimum(j, s[0]), 0, 0)),
                whole((m, 1)),
                whole((m, 1)),
            ],
            out_specs=[whole((m, e)), whole((m, e)), whole((m, 1))],
            scratch_shapes=[pltpu.VMEM((m, e), F32), pltpu.VMEM((m, 1), F32)],
        ),
        out_shape=[
            jax.ShapeDtypeStruct((m, e), BF16),
            jax.ShapeDtypeStruct((m, e), F32),
            jax.ShapeDtypeStruct((m, 1), F32),
        ],
        compiler_params=params(),
        cost_estimate=pl.CostEstimate(
            flops=4 * m * n * p * e, bytes_accessed=4 * n * p * e, transcendentals=2 * m * n * p
        ),
    )(place, queries, keys_values, query_pos, first_pos)


def attend_back(place, queries, grads, keys_values, inverse, delta, query_pos, first_pos, scale, p):
    m, e = queries.shape
    n = keys_values.shape[0]
    step = 256

    def body(
        place_ref, q_ref, g_ref, kv_ref, inv_ref, delta_ref, pos_ref, first_ref, dq_ref, dkv_ref, acc_ref, dk_ref, dv_ref
    ):
        j = pl.program_id(0)

        @pl.when(j == 0)
        def _():
            acc_ref[...] = jnp.zeros_like(acc_ref)

        @pl.when(j <= place_ref[0])
        def _():
            key_pos = key_position(j, p, place_ref[1], (p, 1), 0)
            for r in range(0, m, step):
                rows = pl.ds(r, step)
                raw = mm(kv_ref[:p, :], q_ref[rows, :], NT)
                capped = jnp.tanh(raw * (scale / SOFT_CAP))
                seen = (key_pos >= first_ref[:, rows]) & (key_pos <= pos_ref[:, rows])
                probs = jnp.where(seen, jnp.exp(SOFT_CAP * capped), 0.0) * inv_ref[:, rows]
                grad_probs = mm(kv_ref[p:, :], g_ref[rows, :], NT)
                grad_raw = probs * (grad_probs - delta_ref[:, rows]) * (1.0 - capped * capped)
                grad_low = grad_raw.astype(BF16)
                value_part = mm(probs.astype(BF16), g_ref[rows, :], NN)
                key_part = mm(grad_low, q_ref[rows, :], NN)
                if r == 0:
                    dv_ref[...] = value_part
                    dk_ref[...] = key_part
                else:
                    dv_ref[...] += value_part
                    dk_ref[...] += key_part
                acc_ref[rows, :] += mm(grad_low, kv_ref[:p, :], TN)
            dkv_ref[0] = dk_ref[...].astype(BF16)
            dkv_ref[1] = dv_ref[...].astype(BF16)

        @pl.when(j > place_ref[0])
        def _():
            dkv_ref[...] = jnp.zeros_like(dkv_ref)

        @pl.when(j == n - 1)
        def _():
            dq_ref[...] = (acc_ref[...] * scale).astype(BF16)

    whole = lambda shape: pl.BlockSpec(shape, lambda j, s: (0, 0))
    return pl.pallas_call(
        body,
        grid_spec=pltpu.PrefetchScalarGridSpec(
            num_scalar_prefetch=1,
            grid=(n,),
            in_specs=[
                whole((m, e)),
                whole((m, e)),
                pl.BlockSpec((None, 2 * p, e), lambda j, s: (jnp.minimum(j, s[0]), 0, 0)),
                whole((1, m)),
                whole((1, m)),
                whole((1, m)),
                whole((1, m)),
            ],
            out_specs=[whole((m, e)), pl.BlockSpec((None, 2, p, e), lambda j, s: (j, 0, 0, 0))],
            scratch_shapes=[pltpu.VMEM((m, e), F32), pltpu.VMEM((p, e), F32), pltpu.VMEM((p, e), F32)],
        ),
        out_shape=[jax.ShapeDtypeStruct((m, e), BF16), jax.ShapeDtypeStruct((n, 2, p, e), BF16)],
        compiler_params=params(),
        cost_estimate=pl.CostEstimate(
            flops=10 * m * n * p * e, bytes_accessed=8 * n * p * e, transcendentals=2 * m * n * p
        ),
    )(place, queries, grads, keys_values, inverse, delta, query_pos, first_pos)


def gelu_pair(gate):
    outer = math.sqrt(2.0 / math.pi)
    square = gate * gate
    bent = jnp.tanh(outer * gate * (1.0 + 0.044715 * square))
    half = 0.5 * (1.0 + bent)
    slope = half + 0.5 * gate * (1.0 - bent * bent) * outer * (1.0 + 3.0 * 0.044715 * square)
    return gate * half, slope


def ffn_front(place, rows, cots, early, late):
    part_rows, d = rows[0].shape
    t = 2 * part_rows
    count = len(early)
    r = early[0].shape[1]
    u, v = early[0].shape[2], late[0].shape[2]
    tall = min(512, t)
    wide = d // 3
    cuts = [(k, min(256, u + v - k)) for k in range(0, u + v, 256)]

    def body(place_ref, x0, x1, y0, y1, *refs):
        early_refs, late_refs = refs[:count], refs[count : 2 * count]
        hs_ref, w_out, dwe_ref, dwl_ref, x, y, w, xt, yt, hs, row_sems, sems, out_sems = refs[2 * count :]
        row_copies = []
        for k, (source, target) in enumerate(((x0, x), (x1, x), (y0, y), (y1, y))):
            target = target.at[pl.ds((k % 2) * part_rows, part_rows), :]
            row_copies.append(pltpu.make_async_copy(source, target, row_sems.at[k]))
            row_copies[k].start()
        copies = []
        for k in range(count):
            spot = pl.multiple_of(jnp.bitwise_xor(place_ref[0], k) * r, 16) if count > 1 else 0
            for source, lanes, way in ((early_refs[k], pl.ds(0, u), 0), (late_refs[k], pl.ds(u, v), 1)):
                copy = pltpu.make_async_copy(source, w.at[:, pl.ds(spot, r), lanes], sems.at[way, k])
                copy.start()
                copies.append(copy)
        for copy in row_copies:
            copy.wait()

        @pl.loop(0, d // 256)
        def _(k):
            cols = pl.ds(pl.multiple_of(k * 256, 256), 256)
            xt[cols, :] = x[:, cols].T
            yt[cols, :] = y[:, cols].T

        for copy in copies:
            copy.wait()
        kept = pltpu.make_async_copy(w, w_out, out_sems.at[0])
        kept.start()

        @pl.loop(0, t // tall)
        def _(i):
            part = pl.ds(pl.multiple_of(i * tall, tall), tall)
            for start, size in cuts:
                units = pl.ds(start, size)
                gate = mm(x[part, :], w[0, :, units], NN)
                up = mm(x[part, :], w[1, :, units], NN)
                grad = mm(y[part, :], w[2, :, units], NN)
                active, slope = gelu_pair(gate)
                hs[0, part, units] = (active * up).astype(BF16)
                hs[1, part, units] = (grad * up * slope).astype(BF16)
                hs[2, part, units] = (grad * active).astype(BF16)

        sides = pltpu.make_async_copy(hs, hs_ref, out_sems.at[1])
        sides.start()
        kept.wait()
        copies = []
        for kind, (left, right) in enumerate(((xt, 1), (xt, 2), (yt, 0))):

            @pl.loop(0, d // wide)
            def _(k):
                cols = pl.ds(pl.multiple_of(k * wide, wide), wide)
                w[kind, cols, :] = mm(left[cols, :], hs[right], NN).astype(BF16)

            for way, (lanes, target) in enumerate(((pl.ds(0, u), dwe_ref), (pl.ds(u, v), dwl_ref))):
                copy = pltpu.make_async_copy(w.at[kind, :, lanes], target.at[kind], out_sems.at[2 + 2 * kind + way])
                copy.start()
                copies.append(copy)
        sides.wait()
        for copy in copies:
            copy.wait()

    apart = pl.BlockSpec(memory_space=pl.ANY)
    return pl.pallas_call(
        body,
        grid_spec=pltpu.PrefetchScalarGridSpec(
            num_scalar_prefetch=1,
            grid=(1,),
            in_specs=[apart] * (4 + 2 * count),
            out_specs=[apart] * 4,
            scratch_shapes=[
                pltpu.VMEM((t, d), BF16),
                pltpu.VMEM((t, d), BF16),
                pltpu.VMEM((3, d, u + v), BF16),
                pltpu.VMEM((d, t), BF16),
                pltpu.VMEM((d, t), BF16),
                pltpu.VMEM((3, t, u + v), BF16),
                pltpu.SemaphoreType.DMA((4,)),
                pltpu.SemaphoreType.DMA((2, count)),
                pltpu.SemaphoreType.DMA((8,)),
            ],
        ),
        out_shape=[
            jax.ShapeDtypeStruct((3, t, u + v), BF16),
            jax.ShapeDtypeStruct((3, d, u + v), BF16),
            jax.ShapeDtypeStruct((3, d, u), BF16),
            jax.ShapeDtypeStruct((3, d, v), BF16),
        ],
        compiler_params=params(),
        cost_estimate=pl.CostEstimate(
            flops=12 * t * d * (u + v), bytes_accessed=12 * d * (u + v) + 4 * t * d, transcendentals=t * (u + v)
        ),
    )(place, *rows, *cots, *early, *late)


def ffn_back(sides, blocks):
    _, t, u = sides.shape
    d = blocks.shape[1]
    wide = 256
    half = t // 2

    def body(s_ref, w_ref, *refs):
        for k in range(2):
            part = pl.ds(k * half, half)
            refs[k][...] = mm(s_ref[0, part, :], w_ref[2], NT).astype(BF16)
            refs[2 + k][...] = (mm(s_ref[1, part, :], w_ref[0], NT) + mm(s_ref[2, part, :], w_ref[1], NT)).astype(BF16)

    return pl.pallas_call(
        body,
        grid=(d // wide,),
        in_specs=[
            pl.BlockSpec((3, t, u), lambda k: (0, 0, 0), pipeline_mode=pl.Buffered(1)),
            pl.BlockSpec((3, wide, u), lambda k: (0, k, 0)),
        ],
        out_specs=[pl.BlockSpec((half, wide), lambda k: (0, k))] * 4,
        out_shape=[jax.ShapeDtypeStruct((half, d), BF16)] * 4,
        compiler_params=params(),
        cost_estimate=pl.CostEstimate(
            flops=6 * t * d * u, bytes_accessed=6 * d * u + 6 * t * u + 4 * t * d, transcendentals=0
        ),
    )(sides, blocks)


def gram_parts(m):
    h = m.shape[1] // 2
    high = m.astype(BF16)
    low = (m - high.astype(F32)).astype(BF16)
    mixed = mm(high, low, TN)
    gram = mm(high, high, TN) + mm(low, low, TN) + mixed + mixed.T
    return gram[:h, :h], gram[:h, h:], gram[h:, h:]


TRIO = 3


def ffn_moment(low_early, low_late, high_early, high_late, momentum, first, blocks, places):
    total, r, c = momentum.shape
    early = low_early.shape[2] // c
    h = c // 2
    full = early + 1
    each = blocks // TRIO

    def body(le_ref, ll_ref, he_ref, hl_ref, m_ref, wg_ref, nm_ref, gram_ref):
        j = pl.program_id(0)

        @pl.when(j >= TRIO * each)
        def _():
            gram_ref[...] = jnp.zeros_like(gram_ref)

        for turn in range(each):

            @pl.when((j < TRIO * each) & (lax.rem(j, each) == turn))
            def _():
                for i in range(TRIO):
                    side, f = divmod(turn * TRIO + i, full)
                    if side == 2:
                        wg_ref[i, :, :h] = ll_ref[:, c:]
                        wg_ref[i, :, h:] = hl_ref[:, c:]
                    elif f < early:
                        wg_ref[i] = (le_ref, he_ref)[side][:, f * c : (f + 1) * c]
                    else:
                        wg_ref[i] = (ll_ref, hl_ref)[side][:, :c]

        @pl.when(j < TRIO * each)
        def _():
            for i in range(TRIO):
                new = MUON_BETA * m_ref[i] + wg_ref[i]
                nm_ref[i] = new
                gram_ref[i, 0], gram_ref[i, 1], gram_ref[i, 2] = gram_parts(new)

    kind = lambda j: (jnp.minimum(j // each, 2), 0, 0)
    block = lambda j: (first // TRIO + jnp.minimum(j, TRIO * each - 1), 0, 0)
    u, v = low_early.shape[2], low_late.shape[2]
    return pl.pallas_call(
        body,
        grid=(places // TRIO,),
        in_specs=[
            pl.BlockSpec((None, r, u), kind),
            pl.BlockSpec((None, r, v), kind),
            pl.BlockSpec((None, r, u), kind),
            pl.BlockSpec((None, r, v), kind),
            pl.BlockSpec((TRIO, r, c), block),
        ],
        out_specs=[
            pl.BlockSpec((TRIO, r, c), block),
            pl.BlockSpec((TRIO, r, c), block),
            pl.BlockSpec((TRIO, 3, h, h), lambda j: (j, 0, 0, 0)),
        ],
        out_shape=[
            jax.ShapeDtypeStruct((total, r, c), F32),
            jax.ShapeDtypeStruct((total, r, c), F32),
            jax.ShapeDtypeStruct((places, 3, h, h), F32),
        ],
        compiler_params=params(),
        cost_estimate=pl.CostEstimate(
            flops=6 * 3 * blocks * r * c * c, bytes_accessed=16 * 3 * blocks * r * c, transcendentals=0
        ),
    )(low_early, low_late, high_early, high_late, momentum)


def attn_moment(grads, pairs, momentum, weight_grads, new_momentum):
    count, r, c = grads.shape
    h = c // 2

    def body(s_ref, g_ref, m_ref, wg_in, nm_in, wg_ref, nm_ref, gram_ref):
        for i in range(2):
            new = MUON_BETA * m_ref[i] + g_ref[i]
            wg_ref[i] = g_ref[i]
            nm_ref[i] = new
            gram_ref[i, 0], gram_ref[i, 1], gram_ref[i, 2] = gram_parts(new)

    block = pl.BlockSpec((2, r, c), lambda j, s: (s[j], 0, 0))
    apart = pl.BlockSpec(memory_space=pl.ANY)
    return pl.pallas_call(
        body,
        grid_spec=pltpu.PrefetchScalarGridSpec(
            num_scalar_prefetch=1,
            grid=(count // 2,),
            in_specs=[pl.BlockSpec((2, r, c), lambda j, s: (j, 0, 0)), block, apart, apart],
            out_specs=[block, block, pl.BlockSpec((2, 3, h, h), lambda j, s: (j, 0, 0, 0))],
        ),
        out_shape=[
            jax.ShapeDtypeStruct(momentum.shape, F32),
            jax.ShapeDtypeStruct(momentum.shape, F32),
            jax.ShapeDtypeStruct((count, 3, h, h), F32),
        ],
        input_output_aliases={3: 0, 4: 1},
        compiler_params=params(),
        cost_estimate=pl.CostEstimate(
            flops=6 * count * r * c * c, bytes_accessed=16 * count * r * c, transcendentals=0
        ),
    )(jnp.array(pairs, jnp.int32), grads, momentum, weight_grads, new_momentum)


def renew(weights, momentum, factors, spots, updated):
    _, r, c = weights.shape
    h = c // 2
    steps = len(spots)
    table = jnp.array([spot for spot, _ in spots] + [f for _, places in spots for f in places], jnp.int32)

    def body(s_ref, w_ref, m_ref, *refs):
        factor_refs, o_ref = refs[:TRIO], refs[-1]
        for i in range(TRIO):
            left = m_ref[i, :, :h].astype(BF16)
            right = m_ref[i, :, h:].astype(BF16)
            first, off, last = factor_refs[i][0], factor_refs[i][1], factor_refs[i][2]
            start = mm(left, first, NN) + mm(right, off, NT)
            rest = mm(left, off, NN) + mm(right, last, NN)
            keep = 1.0 - MUON_RATE * MUON_DECAY
            o_ref[i, :, :h] = w_ref[i, :, :h] * keep - MUON_RATE * start
            o_ref[i, :, h:] = w_ref[i, :, h:] * keep - MUON_RATE * rest

    block = pl.BlockSpec((TRIO, r, c), lambda j, s: (s[j], 0, 0))

    def factor_at(i):
        return pl.BlockSpec((None, 3, h, h), lambda j, s: (s[steps + TRIO * j + i], 0, 0, 0))

    apart = [pl.BlockSpec(memory_space=pl.ANY)] * len(updated)
    return pl.pallas_call(
        body,
        grid_spec=pltpu.PrefetchScalarGridSpec(
            num_scalar_prefetch=1,
            grid=(steps,),
            in_specs=[block, block] + [factor_at(i) for i in range(TRIO)] + apart,
            out_specs=block,
        ),
        out_shape=jax.ShapeDtypeStruct(weights.shape, F32),
        input_output_aliases={3 + TRIO: 0} if updated else {},
        compiler_params=params(),
        cost_estimate=pl.CostEstimate(
            flops=2 * TRIO * steps * r * c * c, bytes_accessed=12 * TRIO * steps * r * c, transcendentals=0
        ),
    )(table, weights, momentum, *([factors] * TRIO), *updated)


def top(spec, a, b):
    return jnp.einsum(spec, a, b, precision=TOP_PRECISION)


def newton_factor(grams, growth):
    size = grams.shape[-1]
    eye = jnp.eye(size, dtype=F32)
    norm = jnp.sqrt(jnp.sum(grams * eye, axis=(1, 2), keepdims=True))
    inverse = 1.0 / (norm + 1e-07)
    gram = grams * (inverse * inverse)
    factor = None
    for sweep in range(NEWTON_STEPS):
        square = top("bij,bjk->bik", gram, gram)
        poly = NEWTON_LINEAR * eye + NEWTON_SQUARE * gram + NEWTON_CUBIC * square
        factor = poly if sweep == 0 else top("bij,bjk->bik", factor, poly)
        if sweep < NEWTON_STEPS - 1:
            gram = top("bij,bjk->bik", top("bij,bjk->bik", gram, poly), poly)
    return factor * (growth * inverse)


def fold(squares):
    h = squares.shape[1] // 2
    return jnp.stack([squares[:, :h, :h], squares[:, :h, h:], squares[:, h:, h:]], axis=1)


def unfold(parts):
    first, off, last = parts[:, 0], parts[:, 1], parts[:, 2]
    upper = jnp.concatenate([first, off], axis=2)
    lower = jnp.concatenate([jnp.swapaxes(off, 1, 2), last], axis=2)
    return jnp.concatenate([upper, lower], axis=1)


def gram_sums(ring, parts, cap):
    h = parts.shape[2]
    parts = parts.reshape(-1, h, h)
    rows = 3 * cap
    mine = yield from ring.scatter(lambda i: lax.dynamic_slice_in_dim(parts, i * rows, rows, 0), rows // 2)
    return unfold(mine.reshape(cap, 3, h, h))


def all_factors(ring, factors):
    cap, c, _ = factors.shape
    parts = fold(factors.astype(BF16)).reshape(3 * cap, c // 2, c // 2)
    parts = yield from ring.gather(parts, 3 * cap // 2)
    return parts.reshape(ring.size * cap, 3, c // 2, c // 2)


def on_device(block_in, cotangent, seq_ids, weights, momentum, gains, gain_first, gain_second):
    tok_rows, model_width = block_in.shape
    rows_dp, group_blocks, head_dim = weights.shape
    head_count = lax.axis_size("head")
    data_count = lax.axis_size("dp")
    group_rows = tok_rows * head_count
    key_heads = KV // head_count
    query_heads = H // head_count
    ffn_blocks = FF // (head_dim * head_count)
    out_mark = query_heads + 2 * key_heads
    gate_mark = out_mark + query_heads
    half_dim = head_dim // 2
    full = ffn_blocks // 2
    scale = head_dim ** (-0.5)
    growth = math.sqrt(max(1.0, model_width / head_dim))
    data_index = lax.axis_index("dp")
    head_index = lax.axis_index("head")
    parity = (data_index >> 1) & 1
    ring = Ring()

    weights = jnp.transpose(weights, (1, 0, 2))
    momentum = jnp.transpose(momentum, (1, 0, 2))
    attn_low = weights[:gate_mark].astype(BF16)
    inputs = block_in.astype(F32)
    normed_one, norm_one_back = jax.vjp(rms_scale, inputs, gains[0])
    ids_column = jnp.pad(seq_ids.astype(BF16)[:, None], ((0, 0), (0, 127)))

    early = full - 1

    def pack(side, late):
        tiles = range(side * full + early, (side + 1) * full) if late else range(side * full, side * full + early)
        lanes = slice(side * half_dim, (side + 1) * half_dim)
        rest = [2 * full] if late else []
        rows = [
            jnp.concatenate([kind[f] for f in tiles] + [kind[f, :, lanes] for f in rest], axis=1) for kind in kinds
        ]
        return jnp.stack(rows).astype(BF16)

    def own_and_other(late):
        sides = (pack(0, late), pack(1, late))
        return jnp.where(parity == 1, sides[1], sides[0]), jnp.where(parity == 1, sides[0], sides[1])

    group_in = run(head_gather(jnp.concatenate([normed_one.astype(BF16), ids_column], axis=1)))
    qkv_parts = run(ring.gather(attn_low[:out_mark], out_mark // 2))
    qkv_blocks = jnp.transpose(qkv_parts, (1, 0, 2, 3)).reshape(out_mark, model_width, head_dim)
    group_in, qkv_blocks, weights, attn_low, cotangent = lax.optimization_barrier(
        (group_in, qkv_blocks, weights, attn_low, cotangent)
    )
    kinds = [weights[gate_mark + k * ffn_blocks : gate_mark + (k + 1) * ffn_blocks] for k in range(3)]
    spread = [Spread(*own_and_other(False)), Spread(*own_and_other(True))]
    projected = block_project(group_in, qkv_blocks)
    queries = projected[:query_heads].reshape(query_heads * group_rows, head_dim)
    group_ids = group_in[:, model_width]
    kv_rows = 2 * key_heads * group_rows
    out_rows = query_heads * rows_dp
    id_rows = group_rows // head_dim
    packed = jnp.concatenate(
        [
            projected[query_heads:].reshape(kv_rows, head_dim),
            attn_low[out_mark:].reshape(out_rows, head_dim),
            jnp.pad(group_ids.reshape(id_rows, head_dim), ((0, 16 - id_rows), (0, 0))),
        ],
        axis=0,
    )
    keys_values = run(ring.gather(packed, packed.shape[0] // 32 * 16))
    out_blocks = keys_values[:, kv_rows : kv_rows + out_rows].reshape(data_count, query_heads, rows_dp, head_dim)
    out_blocks = jnp.transpose(out_blocks, (1, 0, 2, 3)).reshape(query_heads, model_width, head_dim)
    group_cot = run(wide_gather(cotangent))
    queries, keys_values, out_blocks, group_cot = stage(
        [spread[0].z(3), spread[0].z(1), spread[0].y(0), spread[1].y(0)],
        [queries, keys_values, out_blocks, group_cot],
    )
    all_ids = keys_values[:, kv_rows + out_rows : kv_rows + out_rows + id_rows].reshape(-1)

    local = in_group(jnp.arange(group_rows, dtype=jnp.int32), group_rows, head_index * tok_rows)
    query_pos = data_index * group_rows + local
    first_pos = jnp.sum((all_ids[None, :] < group_ids[:, None]).astype(jnp.int32), axis=1)
    query_pos = jnp.tile(query_pos, query_heads)
    first_pos = jnp.tile(first_pos, query_heads)
    place = jnp.stack([data_index, head_index * tok_rows]).astype(jnp.int32)
    mixed_low, mixed_full, totals = attend(
        place, queries, keys_values, query_pos[:, None], first_pos[:, None], scale, group_rows
    )
    mixed_heads = mixed_low.reshape(query_heads, group_rows, head_dim)
    mixed_heads, mixed_full, totals, attn_part = stage(
        [spread[0].z(2), spread[0].y(3), spread[0].y(1)],
        [mixed_heads, mixed_full, totals, block_back(mixed_heads, out_blocks)],
    )
    attn_flow = Flow(scatter_rows(*attn_part, HEAD_MOVES))
    stage([attn_flow])
    stage([attn_flow, spread[0].y(2), spread[1].z(3), spread[1].z(1)])
    residual = inputs + attn_flow.value
    normed_two, norm_two_back = jax.vjp(rms_scale, residual, gains[1])
    wide_flow = Flow(wide_gather(normed_two.astype(BF16)))
    stage([wide_flow, spread[1].y(1)])
    stage([wide_flow, spread[1].z(2), spread[1].y(3)])
    stage([wide_flow, spread[1].y(2)])
    finish(wide_flow)

    def whole_rows(pieces):
        if rows_dp % 16 == 0:
            return pieces
        out = jnp.zeros((3, data_count) + pieces[0].shape[1:], BF16)
        for k, piece in enumerate(pieces):
            out = lax.dynamic_update_index_in_dim(out, piece, data_index ^ k, 1)
        return [out.reshape(3, model_width, -1)]

    ffn_sides, ffn_full, grads_early, grads_late = ffn_front(
        place, wide_flow.value, group_cot, whole_rows(spread[0].value()), whole_rows(spread[1].value())
    )

    def taker(grads):
        cut = grads.reshape(3, data_count, rows_dp, grads.shape[2])
        return lambda index: lax.dynamic_index_in_dim(cut, index, 1, keepdims=False)

    reduce = [Reduce(taker(grads_early)), Reduce(taker(grads_late))]
    *down_part, dx_kept, dx_sent = stage([reduce[0].y(3)], ffn_back(ffn_sides, ffn_full))
    dx_steps = scatter_rows(dx_kept, dx_sent, WIDE_MOVES)
    out_flow = Flow(scatter_rows(*down_part, WIDE_MOVES))
    dx_flow = Flow(dx_steps)
    dx_flow.advance([lax.ppermute(*send) for send in dx_flow.sends])
    stage([dx_flow, reduce[0].z(3), reduce[0].y(1), reduce[1].y(3)])
    stage([dx_flow, reduce[1].z(3), reduce[1].y(2), reduce[1].y(1), out_flow])
    grad_residual_norm, grad_gain_two = norm_two_back(dx_flow.value)
    grad_residual = cotangent.astype(F32) + grad_residual_norm
    grad_flow = Flow(head_gather(grad_residual.astype(BF16)))
    stage([grad_flow, reduce[1].z(2), reduce[0].z(1), reduce[0].y(2)])
    grad_flow.advance([lax.ppermute(*send) for send in grad_flow.sends])
    group_grad = grad_flow.value

    grad_heads = block_project(group_grad, out_blocks)
    grad_mixed = grad_heads.reshape(query_heads * group_rows, head_dim)
    delta = jnp.sum(grad_mixed.astype(F32) * mixed_full, axis=1)
    grad_queries, grad_keys_values = attend_back(
        place,
        queries,
        grad_mixed,
        keys_values,
        1.0 / totals.reshape(1, -1),
        delta[None, :],
        query_pos[None, :],
        first_pos[None, :],
        scale,
        group_rows,
    )
    group_grad, grad_queries, grad_keys_values = stage(
        [reduce[0].z(2), reduce[1].z(1), reduce[0].y(0), reduce[1].y(0), out_flow],
        [group_grad, grad_queries, grad_keys_values],
    )
    grad_queries = grad_queries.reshape(query_heads, group_rows, head_dim)

    late = 2
    main = 3 * ffn_blocks - late
    cap = -(-main // data_count)
    places = -(-max(cap * data_count, 3 * ffn_blocks) // TRIO) * TRIO
    own_early, other_early = reduce[0].sums
    own_late, other_late = reduce[1].sums
    pick = lambda own, other: (jnp.where(parity == 1, other, own), jnp.where(parity == 1, own, other))
    (low_early, high_early), (low_late, high_late) = pick(own_early, other_early), pick(own_late, other_late)

    def weight_sums(outer):
        cut = outer.reshape(outer.shape[0], data_count, rows_dp, head_dim)
        return Flow(ring.scatter(lambda i: lax.dynamic_index_in_dim(cut, i, 1, keepdims=False), outer.shape[0] // 2))

    key_flow = Flow(
        ring.scatter(lambda i: lax.dynamic_index_in_dim(grad_keys_values, i, 0, keepdims=False), key_heads)
    )
    (outer,) = stage(
        [key_flow, out_flow], [block_outer([group_in, group_grad], [grad_queries, mixed_heads], model_width)]
    )
    block_out = (residual + out_flow.value).astype(BF16)
    first_flow = weight_sums(outer)
    weight_grads, new_momentum, grams = stage(
        [key_flow, first_flow],
        ffn_moment(low_early, low_late, high_early, high_late, momentum, gate_mark, ffn_blocks, places),
    )
    gram_flow = Flow(gram_sums(ring, grams, cap))
    stage([key_flow, first_flow, gram_flow])
    while key_flow.sends is not None:
        stage([key_flow, first_flow, gram_flow])
    key_value_sums = key_flow.value
    grad_keys = (key_value_sums[:key_heads] * scale).astype(BF16)
    grad_values = key_value_sums[key_heads:].astype(BF16)
    grad_keys_values = jnp.concatenate([grad_keys, grad_values], axis=0)
    (outer,) = stage([first_flow, gram_flow], [block_outer([group_in], [grad_keys_values], model_width)])
    finish(first_flow)
    second_flow = weight_sums(outer)
    pairs = [k for k in range(gate_mark // 2) if not query_heads <= 2 * k < out_mark]
    grad_projected = jnp.concatenate([grad_queries, grad_keys_values], axis=0)
    *attn_dx, weight_grads, new_momentum, first_grams = stage(
        [second_flow, gram_flow],
        [
            *block_back(grad_projected, qkv_blocks),
            *attn_moment(first_flow.value, pairs, momentum, weight_grads, new_momentum),
        ],
    )
    last_flow = Flow(scatter_rows(*attn_dx, HEAD_MOVES))
    while second_flow.sends is not None:
        stage([second_flow, gram_flow, last_flow])
    finish(last_flow, gram_flow)
    grad_input_norm, grad_gain_one = norm_one_back(last_flow.value)
    grad_input = grad_residual + grad_input_norm
    gain_flow = Flow(total_sum(jnp.stack([grad_gain_one, grad_gain_two])))
    weight_grads, new_momentum, second_grams = attn_moment(
        second_flow.value, list(range(query_heads // 2, out_mark // 2)), momentum, weight_grads, new_momentum
    )
    late_count = gate_mark + late
    late_cap = -(-late_count // data_count)
    late_grams = jnp.concatenate([first_grams, second_grams, grams[main : main + late]], axis=0)
    late_grams = jnp.pad(late_grams, ((0, late_cap * data_count - late_count), (0, 0), (0, 0), (0, 0)))
    late_sums, factors = stage(
        [gain_flow], [run(gram_sums(ring, late_grams, late_cap)), newton_factor(gram_flow.value, growth)]
    )
    factors, late_factors = stage(
        [gain_flow], [run(all_factors(ring, factors)), newton_factor(late_sums, growth)]
    )
    late_factor_flow = Flow(all_factors(ring, late_factors))

    threes = main // TRIO
    early_spots = [(gate_mark // TRIO + k, [TRIO * k + i for i in range(TRIO)]) for k in range(threes)]
    (new_weights,) = stage(
        [late_factor_flow, gain_flow], [renew(weights, new_momentum, factors, early_spots, [])]
    )
    finish(late_factor_flow, gain_flow)
    gain_grads = gain_flow.value
    rest = jnp.concatenate([late_factor_flow.value[:late_count], factors[TRIO * threes : main]], axis=0)
    blocks_of = [2 * pair + i for pair in pairs for i in range(2)] + list(range(query_heads, out_mark))
    blocks_of += [gate_mark + main + k for k in range(late)] + [gate_mark + k for k in range(TRIO * threes, main)]
    late_spots = [
        (spot, [blocks_of.index(TRIO * spot + i) for i in range(TRIO)])
        for spot in sorted({block // TRIO for block in blocks_of})
    ]
    new_weights = renew(weights, new_momentum, rest, late_spots, [new_weights])

    new_gain_first = BETA_ONE * gain_first + (1.0 - BETA_ONE) * gain_grads
    new_gain_second = BETA_TWO * gain_second + (1.0 - BETA_TWO) * gain_grads * gain_grads
    first_hat = new_gain_first / (1.0 - BETA_ONE**UPDATE_STEP)
    second_hat = new_gain_second / (1.0 - BETA_TWO**UPDATE_STEP)
    new_gains = gains - ADAM_RATE * first_hat / (jnp.sqrt(second_hat) + ADAM_EPS)
    back = lambda array: jnp.transpose(array, (1, 0, 2))
    return (
        block_out,
        grad_input,
        back(weight_grads),
        back(new_momentum),
        back(new_weights),
        gain_grads,
        new_gain_first,
        new_gain_second,
        new_gains,
    )


def solution(mesh):
    return jax.shard_map(
        on_device,
        mesh=mesh,
        in_specs=(
            P(("dp", "head"), None),
            P(("dp", "head"), None),
            P(("dp", "head")),
            P("dp", "head", None),
            P("dp", "head", None),
            P(),
            P(),
            P(),
        ),
        out_specs=(
            P(("dp", "head"), None),
            P(("dp", "head"), None),
            P("dp", "head", None),
            P("dp", "head", None),
            P("dp", "head", None),
            P(),
            P(),
            P(),
            P(),
        ),
        check_vma=False,
    )
```

```python
import functools
import math

import jax
import jax.numpy as jnp
from jax import lax
from jax.experimental import pallas as pl
from jax.experimental.pallas import tpu as pltpu
from jax.sharding import PartitionSpec as P

H = 8
KV = 4
FF = 9216
NEWTON_STEPS = 5
UPDATE_STEP = 10

NORM_EPS = 1e-06
SOFT_CAP = 50.0
MUON_RATE = 0.2
MUON_DECAY = 0.01
MUON_BETA = 0.95
ADAM_RATE = 0.3
BETA_ONE = 0.9
BETA_TWO = 0.95
ADAM_EPS = 1e-08
NEWTON_LINEAR = 3.4445
NEWTON_SQUARE = -4.775
NEWTON_CUBIC = 2.0315
TOP_PRECISION = lax.Precision.HIGHEST

BF16 = jnp.bfloat16
F32 = jnp.float32
VMEM_LIMIT = 62 * 1024 * 1024
NN = (((1,), (0,)), ((), ()))
NT = (((1,), (1,)), ((), ()))
TN = (((0,), (0,)), ((), ()))


def mm(a, b, dims):
    return lax.dot_general(a, b, dims, preferred_element_type=F32)


def rms_scale(rows, gain):
    inverse = lax.rsqrt(jnp.mean(rows * rows, axis=-1, keepdims=True) + NORM_EPS)
    return rows * inverse * gain


class Flow:
    def __init__(self, steps):
        self.steps = steps
        self.value = None
        self.sends = None
        self.advance(None)

    def advance(self, arrived):
        try:
            self.sends = self.steps.send(arrived)
        except StopIteration as stop:
            self.sends = None
            self.value = stop.value


def stage(flows, extra=(), idle=()):
    flows = [flow for flow in flows if flow.sends is not None]
    idle = [flow for flow in idle if flow.sends is not None and flow not in flows]
    arrived = [[lax.ppermute(*send) for send in flow.sends] for flow in flows]
    held = [[send[0] for send in flow.sends] for flow in idle]
    arrived, held, extra = lax.optimization_barrier((arrived, held, list(extra)))
    for flow, got in zip(flows, arrived):
        flow.advance(got)
    for flow, kept in zip(idle, held):
        flow.sends = [(value,) + send[1:] for value, send in zip(kept, flow.sends)]
    return extra


def run(steps):
    flow = Flow(steps)
    while flow.sends is not None:
        flow.advance([lax.ppermute(*send) for send in flow.sends])
    return flow.value


def finish(*flows):
    while any(flow.sends is not None for flow in flows):
        stage(flows)


def swap(value, axis, mask):
    size = lax.axis_size(axis)
    return (value, axis, [(i, i ^ mask) for i in range(size)])


def head_gather(rows):
    (other,) = yield [swap(rows, "head", 2)]
    pair = jnp.concatenate([rows, other], axis=0)
    (other,) = yield [swap(pair, "head", 1)]
    return jnp.concatenate([pair, other], axis=0)


def wide_gather(rows):
    (other,) = yield [swap(rows, "dp", 4)]
    both = jnp.concatenate([rows, other], axis=0)
    (other,) = yield [swap(both, "head", 2)]
    pair = jnp.concatenate([both, other], axis=0)
    (other,) = yield [swap(pair, "head", 1)]
    return [pair, other]


def add_low(kept, other):
    return (kept.astype(F32) + other.astype(F32)).astype(BF16)


def scatter_rows(kept, sent, moves):
    for k, (axis, mask) in enumerate(moves):
        (other,) = yield [swap(sent, axis, mask)]
        part = kept.astype(F32) + other.astype(F32)
        if k < len(moves) - 1:
            half = part.shape[0] // 2
            kept, sent = part[:half], part[half:].astype(BF16)
    return part


HEAD_MOVES = (("head", 1), ("head", 2))
WIDE_MOVES = (("head", 1), ("head", 2), ("dp", 4))


def total_sum(value):
    for axis in ("head", "dp"):
        mask = 1
        while mask < lax.axis_size(axis):
            (other,) = yield [swap(value, axis, mask)]
            value = value + other
            mask *= 2
    return value


class Ring:
    def __init__(self):
        size = lax.axis_size("dp")
        order = list(range(0, size, 2)) + list(range(size - 1, 0, -2))
        around = [[order[(order.index(i) + offset) % size] for offset in range(size)] for i in range(size)]
        self.size = size
        self.around = jnp.array(around, jnp.int32)[lax.axis_index("dp")]
        self.up = [(order[k], order[(k + 1) % size]) for k in range(size)]
        self.down = [(order[(k + 1) % size], order[k]) for k in range(size)]

    def index(self, offset):
        return self.around[offset % self.size]

    def gather(self, value, mid):
        half = self.size // 2
        zeros = (0,) * (value.ndim - 1)
        out = jnp.zeros((self.size,) + value.shape, value.dtype)
        out = lax.dynamic_update_index_in_dim(out, value, self.index(0), 0)
        ahead, back = value, value
        for step in range(1, half):
            ahead, back = yield [(ahead, "dp", self.up), (back, "dp", self.down)]
            out = lax.dynamic_update_index_in_dim(out, ahead, self.index(-step), 0)
            out = lax.dynamic_update_index_in_dim(out, back, self.index(step), 0)
        first, second = yield [(ahead[:mid], "dp", self.up), (back[mid:], "dp", self.down)]
        far = self.index(half)
        out = lax.dynamic_update_slice(out, first[None], (far, 0) + zeros)
        return lax.dynamic_update_slice(out, second[None], (far, mid) + zeros)

    def scatter(self, take, mid):
        half = self.size // 2
        far = take(self.index(half))
        kind = far.dtype
        up, down = yield [(far[:mid], "dp", self.up), (far[mid:], "dp", self.down)]
        for step in range(half - 1, 0, -1):
            part = take(self.index(step)).astype(F32)
            ahead = jnp.concatenate([part[:mid] + up, part[mid:]]) if step == half - 1 else part + up
            part = take(self.index(-step)).astype(F32)
            back = jnp.concatenate([part[:mid], part[mid:] + down]) if step == half - 1 else part + down
            up, down = yield [(ahead.astype(kind), "dp", self.up), (back.astype(kind), "dp", self.down)]
        return take(self.index(0)).astype(F32) + up.astype(F32) + down.astype(F32)


def once(sends, take):
    def steps():
        take((yield sends))

    return Flow(steps())


SIDE_BIT = 2


def plane_classes():
    planes = range(lax.axis_size("dp") // 2)
    kept = [m for m in planes if m & 3 in (0, 3)]
    passed = [m for m in planes if m & 3 in (1, 2)]
    return {0: [0], 1: [1], 2: [m for m in passed if m != 1], 3: [m for m in kept if m]}


class Spread:
    def __init__(self, mine, other):
        self.mine, self.other = mine, other
        self.pieces = {0: mine}

    def move(self, moves):
        def take(arrived):
            for (_, _, _, number), piece in zip(moves, arrived):
                self.pieces[number] = piece

        return once([swap(value, "dp", offset << 1 | bit) for value, offset, bit, _ in moves], take)

    def cross(self):
        group = plane_classes()[3]
        return self.move([(self.other if m & SIDE_BIT else self.mine, m, 0, m << 1) for m in group])

    def near(self, key):
        group = plane_classes()[key]
        return self.move([(self.pieces[m << 1], 1, 0, (m ^ 1) << 1) for m in group])

    def y(self, key):
        group = plane_classes()[key]
        return self.move([(self.pieces[m << 1], 0, 1, m << 1 | 1) for m in group])

    def value(self):
        return [self.pieces[k] for k in range(lax.axis_size("dp"))]


class Reduce:
    def __init__(self, rows):
        self.rows = rows
        self.parts = {}
        self.sums = [None, None]

    def part(self, offset):
        terms = [term.astype(F32) for term in self.parts[offset]]
        return functools.reduce(jnp.add, terms)

    def hold(self, offset, *terms):
        self.parts.setdefault(offset, []).extend(terms)

    def y(self, key):
        me = lax.axis_index("dp")
        group = plane_classes()[key]

        def take(arrived):
            for offset, got in zip(group, arrived):
                self.hold(offset, self.rows(me ^ (offset << 1)), got)

        return once([swap(self.rows(me ^ (offset << 1) ^ 1), "dp", 1) for offset in group], take)

    def near(self, key):
        group = plane_classes()[key]

        def take(arrived):
            for offset, got in zip(group, arrived):
                self.hold(offset ^ 1, got)

        return once([swap(self.part(offset).astype(BF16), "dp", 2) for offset in group], take)

    def cross(self):
        group = plane_classes()[3]

        def take(arrived):
            for offset, got in zip(group, arrived):
                self.add(1 if offset & SIDE_BIT else 0, got.astype(F32))

        return once([swap(self.part(offset).astype(BF16), "dp", offset << 1) for offset in group], take)

    def add(self, side, value):
        self.sums[side] = value if self.sums[side] is None else self.sums[side] + value

    def value(self):
        self.add(0, self.part(0))
        return self.sums


def params(**more):
    return pltpu.CompilerParams(vmem_limit_bytes=VMEM_LIMIT, **more)


def block_project(rows, blocks):
    t = rows.shape[0]
    count, d, c = blocks.shape

    def body(x_ref, w_ref, o_ref):
        o_ref[...] = mm(x_ref[...], w_ref[...], NN).astype(BF16)

    return pl.pallas_call(
        body,
        grid=(count,),
        in_specs=[
            pl.BlockSpec((t, d), lambda b: (0, 0)),
            pl.BlockSpec((None, d, c), lambda b: (b, 0, 0)),
        ],
        out_specs=pl.BlockSpec((None, t, c), lambda b: (b, 0, 0)),
        out_shape=jax.ShapeDtypeStruct((count, t, c), BF16),
        compiler_params=params(),
        cost_estimate=pl.CostEstimate(
            flops=2 * count * t * d * c, bytes_accessed=2 * (t * d + count * (d * c + t * c)), transcendentals=0
        ),
    )(rows, blocks)


def block_back(cols, blocks):
    count, t, c = cols.shape
    d = blocks.shape[1]
    half = t // 2

    def body(x_ref, w_ref, o_ref, p_ref, acc_ref):
        b = pl.program_id(0)

        @pl.when(b == 0)
        def _():
            acc_ref[...] = jnp.zeros_like(acc_ref)

        acc_ref[...] += mm(x_ref[...], w_ref[...], NT)

        @pl.when(b == count - 1)
        def _():
            o_ref[...] = acc_ref[:half, :].astype(BF16)
            p_ref[...] = acc_ref[half:, :].astype(BF16)

    result = pl.BlockSpec((half, d), lambda b: (0, 0))
    return pl.pallas_call(
        body,
        grid=(count,),
        in_specs=[
            pl.BlockSpec((None, t, c), lambda b: (b, 0, 0)),
            pl.BlockSpec((None, d, c), lambda b: (b, 0, 0)),
        ],
        out_specs=[result, result],
        out_shape=[jax.ShapeDtypeStruct((half, d), BF16)] * 2,
        scratch_shapes=[pltpu.VMEM((t, d), F32)],
        compiler_params=params(),
        cost_estimate=pl.CostEstimate(
            flops=2 * count * t * d * c, bytes_accessed=2 * (t * d + count * (d * c + t * c)), transcendentals=0
        ),
    )(cols, blocks)


def block_outer(rows, cols, d):
    t = rows[0].shape[0]
    c = cols[0].shape[2]
    starts = [0]
    for col in cols:
        starts.append(starts[-1] + col.shape[0])
    count = len(rows)
    total = starts[-1]

    def body(*refs):
        o_ref, t_ref = refs[2 * count :]
        b = pl.program_id(0)
        for k in range(count):

            @pl.when(b == starts[k])
            def _():
                t_ref[...] = refs[k][...].T

            @pl.when((b >= starts[k]) & (b < starts[k + 1]))
            def _():
                o_ref[...] = mm(t_ref[...], refs[count + k][...], NN).astype(BF16)

    def col_at(k):
        return pl.BlockSpec((None, t, c), lambda b: (jnp.clip(b - starts[k], 0, starts[k + 1] - starts[k] - 1), 0, 0))

    return pl.pallas_call(
        body,
        grid=(total,),
        in_specs=[pl.BlockSpec((t, d), lambda b: (0, 0))] * count + [col_at(k) for k in range(count)],
        out_specs=pl.BlockSpec((None, d, c), lambda b: (b, 0, 0)),
        out_shape=jax.ShapeDtypeStruct((total, d, c), BF16),
        scratch_shapes=[pltpu.VMEM((d, t), BF16)],
        compiler_params=params(),
        cost_estimate=pl.CostEstimate(
            flops=2 * total * t * d * c,
            bytes_accessed=2 * (count * t * d + total * (d * c + t * c)),
            transcendentals=0,
        ),
    )(*rows, *cols)


def in_group(local, width, head_shift):
    quarter = width // 4
    low = jnp.bitwise_and(local, quarter - 1)
    one = jnp.where(jnp.bitwise_and(local, quarter) != 0, 2 * quarter, 0)
    two = jnp.where(jnp.bitwise_and(local, 2 * quarter) != 0, quarter, 0)
    return jnp.bitwise_xor(low + one + two, head_shift)


def key_position(block, width, head_shift, shape, axis):
    local = lax.broadcasted_iota(jnp.int32, shape, axis)
    return block * width + in_group(local, width, head_shift)


def attend(place, queries, keys_values, query_pos, first_pos, scale, p):
    m, e = queries.shape
    n = keys_values.shape[0]
    step = 256

    def body(place_ref, q_ref, kv_ref, pos_ref, first_ref, low_ref, full_ref, sum_ref, acc_ref, tot_ref):
        j = pl.program_id(0)

        @pl.when(j == 0)
        def _():
            acc_ref[...] = jnp.zeros_like(acc_ref)
            tot_ref[...] = jnp.zeros_like(tot_ref)

        @pl.when(j <= place_ref[0])
        def _():
            key_pos = key_position(j, p, place_ref[1], (1, p), 1)
            for r in range(0, m, step):
                rows = pl.ds(r, step)
                raw = mm(q_ref[rows, :], kv_ref[:p, :], NT)
                soft = SOFT_CAP * jnp.tanh(raw * (scale / SOFT_CAP))
                seen = (key_pos >= first_ref[rows, :]) & (key_pos <= pos_ref[rows, :])
                terms = jnp.where(seen, jnp.exp(soft), 0.0)
                tot_ref[rows, :] += jnp.sum(terms, axis=1, keepdims=True)
                acc_ref[rows, :] += mm(terms.astype(BF16), kv_ref[p:, :], NN)

        @pl.when(j == n - 1)
        def _():
            total = tot_ref[...]
            mixed = acc_ref[...] / total
            full_ref[...] = mixed
            low_ref[...] = mixed.astype(BF16)
            sum_ref[...] = total

    whole = lambda shape: pl.BlockSpec(shape, lambda j, s: (0, 0))
    return pl.pallas_call(
        body,
        grid_spec=pltpu.PrefetchScalarGridSpec(
            num_scalar_prefetch=1,
            grid=(n,),
            in_specs=[
                whole((m, e)),
                pl.BlockSpec((None, 2 * p, e), lambda j, s: (jnp.minimum(j, s[0]), 0, 0)),
                whole((m, 1)),
                whole((m, 1)),
            ],
            out_specs=[whole((m, e)), whole((m, e)), whole((m, 1))],
            scratch_shapes=[pltpu.VMEM((m, e), F32), pltpu.VMEM((m, 1), F32)],
        ),
        out_shape=[
            jax.ShapeDtypeStruct((m, e), BF16),
            jax.ShapeDtypeStruct((m, e), F32),
            jax.ShapeDtypeStruct((m, 1), F32),
        ],
        compiler_params=params(),
        cost_estimate=pl.CostEstimate(
            flops=4 * m * n * p * e, bytes_accessed=4 * n * p * e, transcendentals=2 * m * n * p
        ),
    )(place, queries, keys_values, query_pos, first_pos)


def attend_back(place, queries, grads, keys_values, inverse, delta, query_pos, first_pos, scale, p):
    m, e = queries.shape
    n = keys_values.shape[0]
    step = 256

    def body(
        place_ref, q_ref, g_ref, kv_ref, inv_ref, delta_ref, pos_ref, first_ref, dq_ref, dkv_ref, acc_ref, dk_ref, dv_ref
    ):
        j = pl.program_id(0)

        @pl.when(j == 0)
        def _():
            acc_ref[...] = jnp.zeros_like(acc_ref)

        @pl.when(j <= place_ref[0])
        def _():
            key_pos = key_position(j, p, place_ref[1], (p, 1), 0)
            for r in range(0, m, step):
                rows = pl.ds(r, step)
                raw = mm(kv_ref[:p, :], q_ref[rows, :], NT)
                capped = jnp.tanh(raw * (scale / SOFT_CAP))
                seen = (key_pos >= first_ref[:, rows]) & (key_pos <= pos_ref[:, rows])
                probs = jnp.where(seen, jnp.exp(SOFT_CAP * capped), 0.0) * inv_ref[:, rows]
                grad_probs = mm(kv_ref[p:, :], g_ref[rows, :], NT)
                grad_raw = probs * (grad_probs - delta_ref[:, rows]) * (1.0 - capped * capped)
                grad_low = grad_raw.astype(BF16)
                value_part = mm(probs.astype(BF16), g_ref[rows, :], NN)
                key_part = mm(grad_low, q_ref[rows, :], NN)
                if r == 0:
                    dv_ref[...] = value_part
                    dk_ref[...] = key_part
                else:
                    dv_ref[...] += value_part
                    dk_ref[...] += key_part
                acc_ref[rows, :] += mm(grad_low, kv_ref[:p, :], TN)
            dkv_ref[0] = dk_ref[...].astype(BF16)
            dkv_ref[1] = dv_ref[...].astype(BF16)

        @pl.when(j > place_ref[0])
        def _():
            dkv_ref[...] = jnp.zeros_like(dkv_ref)

        @pl.when(j == n - 1)
        def _():
            dq_ref[...] = (acc_ref[...] * scale).astype(BF16)

    whole = lambda shape: pl.BlockSpec(shape, lambda j, s: (0, 0))
    return pl.pallas_call(
        body,
        grid_spec=pltpu.PrefetchScalarGridSpec(
            num_scalar_prefetch=1,
            grid=(n,),
            in_specs=[
                whole((m, e)),
                whole((m, e)),
                pl.BlockSpec((None, 2 * p, e), lambda j, s: (jnp.minimum(j, s[0]), 0, 0)),
                whole((1, m)),
                whole((1, m)),
                whole((1, m)),
                whole((1, m)),
            ],
            out_specs=[whole((m, e)), pl.BlockSpec((None, 2, p, e), lambda j, s: (j, 0, 0, 0))],
            scratch_shapes=[pltpu.VMEM((m, e), F32), pltpu.VMEM((p, e), F32), pltpu.VMEM((p, e), F32)],
        ),
        out_shape=[jax.ShapeDtypeStruct((m, e), BF16), jax.ShapeDtypeStruct((n, 2, p, e), BF16)],
        compiler_params=params(),
        cost_estimate=pl.CostEstimate(
            flops=10 * m * n * p * e, bytes_accessed=8 * n * p * e, transcendentals=2 * m * n * p
        ),
    )(place, queries, grads, keys_values, inverse, delta, query_pos, first_pos)


def gelu_pair(gate):
    outer = math.sqrt(2.0 / math.pi)
    square = gate * gate
    bent = jnp.tanh(outer * gate * (1.0 + 0.044715 * square))
    half = 0.5 * (1.0 + bent)
    slope = half + 0.5 * gate * (1.0 - bent * bent) * outer * (1.0 + 3.0 * 0.044715 * square)
    return gate * half, slope


def ffn_front(place, rows, cots, early, late):
    part_rows, d = rows[0].shape
    t = 2 * part_rows
    count = len(early)
    r = early[0].shape[1]
    u, v = early[0].shape[2], late[0].shape[2]
    tall = min(512, t)
    wide = d // 3
    cuts = [(k, min(256, u + v - k)) for k in range(0, u + v, 256)]

    def body(place_ref, x0, x1, y0, y1, *refs):
        early_refs, late_refs = refs[:count], refs[count : 2 * count]
        hs_ref, w_out, dwe_ref, dwl_ref, x, y, w, xt, yt, hs, row_sems, sems, out_sems = refs[2 * count :]
        row_copies = []
        for k, (source, target) in enumerate(((x0, x), (x1, x), (y0, y), (y1, y))):
            target = target.at[pl.ds((k % 2) * part_rows, part_rows), :]
            row_copies.append(pltpu.make_async_copy(source, target, row_sems.at[k]))
            row_copies[k].start()
        copies = []
        for k in range(count):
            spot = pl.multiple_of(jnp.bitwise_xor(place_ref[0], k) * r, 16) if count > 1 else 0
            for source, lanes, way in ((early_refs[k], pl.ds(0, u), 0), (late_refs[k], pl.ds(u, v), 1)):
                copy = pltpu.make_async_copy(source, w.at[:, pl.ds(spot, r), lanes], sems.at[way, k])
                copy.start()
                copies.append(copy)
        for copy in row_copies:
            copy.wait()

        @pl.loop(0, d // 256)
        def _(k):
            cols = pl.ds(pl.multiple_of(k * 256, 256), 256)
            xt[cols, :] = x[:, cols].T
            yt[cols, :] = y[:, cols].T

        for copy in copies:
            copy.wait()
        kept = pltpu.make_async_copy(w, w_out, out_sems.at[0])
        kept.start()

        @pl.loop(0, t // tall)
        def _(i):
            part = pl.ds(pl.multiple_of(i * tall, tall), tall)
            for start, size in cuts:
                units = pl.ds(start, size)
                gate = mm(x[part, :], w[0, :, units], NN)
                up = mm(x[part, :], w[1, :, units], NN)
                grad = mm(y[part, :], w[2, :, units], NN)
                active, slope = gelu_pair(gate)
                hs[0, part, units] = (active * up).astype(BF16)
                hs[1, part, units] = (grad * up * slope).astype(BF16)
                hs[2, part, units] = (grad * active).astype(BF16)

        sides = pltpu.make_async_copy(hs, hs_ref, out_sems.at[1])
        sides.start()
        kept.wait()
        copies = []
        for kind, (left, right) in enumerate(((xt, 1), (xt, 2), (yt, 0))):

            @pl.loop(0, d // wide)
            def _(k):
                cols = pl.ds(pl.multiple_of(k * wide, wide), wide)
                w[kind, cols, :] = mm(left[cols, :], hs[right], NN).astype(BF16)

            for way, (lanes, target) in enumerate(((pl.ds(0, u), dwe_ref), (pl.ds(u, v), dwl_ref))):
                copy = pltpu.make_async_copy(w.at[kind, :, lanes], target.at[kind], out_sems.at[2 + 2 * kind + way])
                copy.start()
                copies.append(copy)
        sides.wait()
        for copy in copies:
            copy.wait()

    apart = pl.BlockSpec(memory_space=pl.ANY)
    return pl.pallas_call(
        body,
        grid_spec=pltpu.PrefetchScalarGridSpec(
            num_scalar_prefetch=1,
            grid=(1,),
            in_specs=[apart] * (4 + 2 * count),
            out_specs=[apart] * 4,
            scratch_shapes=[
                pltpu.VMEM((t, d), BF16),
                pltpu.VMEM((t, d), BF16),
                pltpu.VMEM((3, d, u + v), BF16),
                pltpu.VMEM((d, t), BF16),
                pltpu.VMEM((d, t), BF16),
                pltpu.VMEM((3, t, u + v), BF16),
                pltpu.SemaphoreType.DMA((4,)),
                pltpu.SemaphoreType.DMA((2, count)),
                pltpu.SemaphoreType.DMA((8,)),
            ],
        ),
        out_shape=[
            jax.ShapeDtypeStruct((3, t, u + v), BF16),
            jax.ShapeDtypeStruct((3, d, u + v), BF16),
            jax.ShapeDtypeStruct((3, d, u), BF16),
            jax.ShapeDtypeStruct((3, d, v), BF16),
        ],
        compiler_params=params(),
        cost_estimate=pl.CostEstimate(
            flops=12 * t * d * (u + v), bytes_accessed=12 * d * (u + v) + 4 * t * d, transcendentals=t * (u + v)
        ),
    )(place, *rows, *cots, *early, *late)


def ffn_back(sides, blocks):
    _, t, u = sides.shape
    d = blocks.shape[1]
    wide = 256
    half = t // 2

    def body(s_ref, w_ref, *refs):
        for k in range(2):
            part = pl.ds(k * half, half)
            refs[k][...] = mm(s_ref[0, part, :], w_ref[2], NT).astype(BF16)
            refs[2 + k][...] = (mm(s_ref[1, part, :], w_ref[0], NT) + mm(s_ref[2, part, :], w_ref[1], NT)).astype(BF16)

    return pl.pallas_call(
        body,
        grid=(d // wide,),
        in_specs=[
            pl.BlockSpec((3, t, u), lambda k: (0, 0, 0), pipeline_mode=pl.Buffered(1)),
            pl.BlockSpec((3, wide, u), lambda k: (0, k, 0)),
        ],
        out_specs=[pl.BlockSpec((half, wide), lambda k: (0, k))] * 4,
        out_shape=[jax.ShapeDtypeStruct((half, d), BF16)] * 4,
        compiler_params=params(),
        cost_estimate=pl.CostEstimate(
            flops=6 * t * d * u, bytes_accessed=6 * d * u + 6 * t * u + 4 * t * d, transcendentals=0
        ),
    )(sides, blocks)


def gram_parts(m):
    h = m.shape[1] // 2
    high = m.astype(BF16)
    low = (m - high.astype(F32)).astype(BF16)
    mixed = mm(high, low, TN)
    gram = mm(high, high, TN) + mm(low, low, TN) + mixed + mixed.T
    return gram[:h, :h], gram[:h, h:], gram[h:, h:]


TRIO = 3


def ffn_moment(low_early, low_late, high_early, high_late, momentum, first, blocks, places):
    total, r, c = momentum.shape
    early = low_early.shape[2] // c
    h = c // 2
    full = early + 1
    each = blocks // TRIO

    def body(le_ref, ll_ref, he_ref, hl_ref, m_ref, wg_ref, nm_ref, gram_ref):
        j = pl.program_id(0)

        @pl.when(j >= TRIO * each)
        def _():
            gram_ref[...] = jnp.zeros_like(gram_ref)

        for turn in range(each):

            @pl.when((j < TRIO * each) & (lax.rem(j, each) == turn))
            def _():
                for i in range(TRIO):
                    side, f = divmod(turn * TRIO + i, full)
                    if side == 2:
                        wg_ref[i, :, :h] = ll_ref[:, c:]
                        wg_ref[i, :, h:] = hl_ref[:, c:]
                    elif f < early:
                        wg_ref[i] = (le_ref, he_ref)[side][:, f * c : (f + 1) * c]
                    else:
                        wg_ref[i] = (ll_ref, hl_ref)[side][:, :c]

        @pl.when(j < TRIO * each)
        def _():
            for i in range(TRIO):
                new = MUON_BETA * m_ref[i] + wg_ref[i]
                nm_ref[i] = new
                gram_ref[i, 0], gram_ref[i, 1], gram_ref[i, 2] = gram_parts(new)

    kind = lambda j: (jnp.minimum(j // each, 2), 0, 0)
    block = lambda j: (first // TRIO + jnp.minimum(j, TRIO * each - 1), 0, 0)
    u, v = low_early.shape[2], low_late.shape[2]
    return pl.pallas_call(
        body,
        grid=(places // TRIO,),
        in_specs=[
            pl.BlockSpec((None, r, u), kind),
            pl.BlockSpec((None, r, v), kind),
            pl.BlockSpec((None, r, u), kind),
            pl.BlockSpec((None, r, v), kind),
            pl.BlockSpec((TRIO, r, c), block),
        ],
        out_specs=[
            pl.BlockSpec((TRIO, r, c), block),
            pl.BlockSpec((TRIO, r, c), block),
            pl.BlockSpec((TRIO, 3, h, h), lambda j: (j, 0, 0, 0)),
        ],
        out_shape=[
            jax.ShapeDtypeStruct((total, r, c), F32),
            jax.ShapeDtypeStruct((total, r, c), F32),
            jax.ShapeDtypeStruct((places, 3, h, h), F32),
        ],
        compiler_params=params(),
        cost_estimate=pl.CostEstimate(
            flops=6 * 3 * blocks * r * c * c, bytes_accessed=16 * 3 * blocks * r * c, transcendentals=0
        ),
    )(low_early, low_late, high_early, high_late, momentum)


def attn_moment(grads, pairs, momentum, weight_grads, new_momentum):
    count, r, c = grads.shape
    h = c // 2

    def body(s_ref, g_ref, m_ref, wg_in, nm_in, wg_ref, nm_ref, gram_ref):
        for i in range(2):
            new = MUON_BETA * m_ref[i] + g_ref[i]
            wg_ref[i] = g_ref[i]
            nm_ref[i] = new
            gram_ref[i, 0], gram_ref[i, 1], gram_ref[i, 2] = gram_parts(new)

    block = pl.BlockSpec((2, r, c), lambda j, s: (s[j], 0, 0))
    apart = pl.BlockSpec(memory_space=pl.ANY)
    return pl.pallas_call(
        body,
        grid_spec=pltpu.PrefetchScalarGridSpec(
            num_scalar_prefetch=1,
            grid=(count // 2,),
            in_specs=[pl.BlockSpec((2, r, c), lambda j, s: (j, 0, 0)), block, apart, apart],
            out_specs=[block, block, pl.BlockSpec((2, 3, h, h), lambda j, s: (j, 0, 0, 0))],
        ),
        out_shape=[
            jax.ShapeDtypeStruct(momentum.shape, F32),
            jax.ShapeDtypeStruct(momentum.shape, F32),
            jax.ShapeDtypeStruct((count, 3, h, h), F32),
        ],
        input_output_aliases={3: 0, 4: 1},
        compiler_params=params(),
        cost_estimate=pl.CostEstimate(
            flops=6 * count * r * c * c, bytes_accessed=16 * count * r * c, transcendentals=0
        ),
    )(jnp.array(pairs, jnp.int32), grads, momentum, weight_grads, new_momentum)


def renew(weights, momentum, factors, spots, updated):
    _, r, c = weights.shape
    h = c // 2
    steps = len(spots)
    table = jnp.array([spot for spot, _ in spots] + [f for _, places in spots for f in places], jnp.int32)

    def body(s_ref, w_ref, m_ref, *refs):
        factor_refs, o_ref = refs[:TRIO], refs[-1]
        for i in range(TRIO):
            left = m_ref[i, :, :h].astype(BF16)
            right = m_ref[i, :, h:].astype(BF16)
            first, off, last = factor_refs[i][0], factor_refs[i][1], factor_refs[i][2]
            start = mm(left, first, NN) + mm(right, off, NT)
            rest = mm(left, off, NN) + mm(right, last, NN)
            keep = 1.0 - MUON_RATE * MUON_DECAY
            o_ref[i, :, :h] = w_ref[i, :, :h] * keep - MUON_RATE * start
            o_ref[i, :, h:] = w_ref[i, :, h:] * keep - MUON_RATE * rest

    block = pl.BlockSpec((TRIO, r, c), lambda j, s: (s[j], 0, 0))

    def factor_at(i):
        return pl.BlockSpec((None, 3, h, h), lambda j, s: (s[steps + TRIO * j + i], 0, 0, 0))

    apart = [pl.BlockSpec(memory_space=pl.ANY)] * len(updated)
    return pl.pallas_call(
        body,
        grid_spec=pltpu.PrefetchScalarGridSpec(
            num_scalar_prefetch=1,
            grid=(steps,),
            in_specs=[block, block] + [factor_at(i) for i in range(TRIO)] + apart,
            out_specs=block,
        ),
        out_shape=jax.ShapeDtypeStruct(weights.shape, F32),
        input_output_aliases={3 + TRIO: 0} if updated else {},
        compiler_params=params(),
        cost_estimate=pl.CostEstimate(
            flops=2 * TRIO * steps * r * c * c, bytes_accessed=12 * TRIO * steps * r * c, transcendentals=0
        ),
    )(table, weights, momentum, *([factors] * TRIO), *updated)


def top(spec, a, b):
    return jnp.einsum(spec, a, b, precision=TOP_PRECISION)


def newton_factor(grams, growth):
    size = grams.shape[-1]
    eye = jnp.eye(size, dtype=F32)
    norm = jnp.sqrt(jnp.sum(grams * eye, axis=(1, 2), keepdims=True))
    inverse = 1.0 / (norm + 1e-07)
    gram = grams * (inverse * inverse)
    factor = None
    for sweep in range(NEWTON_STEPS):
        square = top("bij,bjk->bik", gram, gram)
        poly = NEWTON_LINEAR * eye + NEWTON_SQUARE * gram + NEWTON_CUBIC * square
        factor = poly if sweep == 0 else top("bij,bjk->bik", factor, poly)
        if sweep < NEWTON_STEPS - 1:
            gram = top("bij,bjk->bik", top("bij,bjk->bik", gram, poly), poly)
    return factor * (growth * inverse)


def fold(squares):
    h = squares.shape[1] // 2
    return jnp.stack([squares[:, :h, :h], squares[:, :h, h:], squares[:, h:, h:]], axis=1)


def unfold(parts):
    first, off, last = parts[:, 0], parts[:, 1], parts[:, 2]
    upper = jnp.concatenate([first, off], axis=2)
    lower = jnp.concatenate([jnp.swapaxes(off, 1, 2), last], axis=2)
    return jnp.concatenate([upper, lower], axis=1)


def gram_sums(ring, parts, cap):
    h = parts.shape[2]
    parts = parts.reshape(-1, h, h)
    rows = 3 * cap
    mine = yield from ring.scatter(lambda i: lax.dynamic_slice_in_dim(parts, i * rows, rows, 0), rows // 2)
    return unfold(mine.reshape(cap, 3, h, h))


def all_factors(ring, factors):
    cap, c, _ = factors.shape
    parts = fold(factors.astype(BF16)).reshape(3 * cap, c // 2, c // 2)
    parts = yield from ring.gather(parts, 3 * cap // 2)
    return parts.reshape(ring.size * cap, 3, c // 2, c // 2)


def on_device(block_in, cotangent, seq_ids, weights, momentum, gains, gain_first, gain_second):
    tok_rows, model_width = block_in.shape
    rows_dp, group_blocks, head_dim = weights.shape
    head_count = lax.axis_size("head")
    data_count = lax.axis_size("dp")
    group_rows = tok_rows * head_count
    key_heads = KV // head_count
    query_heads = H // head_count
    ffn_blocks = FF // (head_dim * head_count)
    out_mark = query_heads + 2 * key_heads
    gate_mark = out_mark + query_heads
    half_dim = head_dim // 2
    full = ffn_blocks // 2
    scale = head_dim ** (-0.5)
    growth = math.sqrt(max(1.0, model_width / head_dim))
    data_index = lax.axis_index("dp")
    head_index = lax.axis_index("head")
    parity = (data_index >> 2) & 1
    ring = Ring()

    weights = jnp.transpose(weights, (1, 0, 2))
    momentum = jnp.transpose(momentum, (1, 0, 2))
    attn_low = weights[:gate_mark].astype(BF16)
    inputs = block_in.astype(F32)
    normed_one, norm_one_back = jax.vjp(rms_scale, inputs, gains[0])
    ids_column = jnp.pad(seq_ids.astype(BF16)[:, None], ((0, 0), (0, 127)))

    early = full - 1

    def pack(side, late):
        tiles = range(side * full + early, (side + 1) * full) if late else range(side * full, side * full + early)
        lanes = slice(side * half_dim, (side + 1) * half_dim)
        rest = [2 * full] if late else []
        rows = [
            jnp.concatenate([kind[f] for f in tiles] + [kind[f, :, lanes] for f in rest], axis=1) for kind in kinds
        ]
        return jnp.stack(rows).astype(BF16)

    def own_and_other(late):
        sides = (pack(0, late), pack(1, late))
        return jnp.where(parity == 1, sides[1], sides[0]), jnp.where(parity == 1, sides[0], sides[1])

    group_in = run(head_gather(jnp.concatenate([normed_one.astype(BF16), ids_column], axis=1)))
    qkv_parts = run(ring.gather(attn_low[:out_mark], out_mark // 2))
    qkv_blocks = jnp.transpose(qkv_parts, (1, 0, 2, 3)).reshape(out_mark, model_width, head_dim)
    cot_flow = Flow(wide_gather(cotangent))
    cot_flow.advance([lax.ppermute(*send) for send in cot_flow.sends])
    group_in, qkv_blocks, weights, attn_low = stage(
        [], [group_in, qkv_blocks, weights, attn_low], idle=[cot_flow]
    )
    kinds = [weights[gate_mark + k * ffn_blocks : gate_mark + (k + 1) * ffn_blocks] for k in range(3)]
    spread = [Spread(*own_and_other(False)), Spread(*own_and_other(True))]
    projected = block_project(group_in, qkv_blocks)
    queries = projected[:query_heads].reshape(query_heads * group_rows, head_dim)
    group_ids = group_in[:, model_width]
    kv_rows = 2 * key_heads * group_rows
    out_rows = query_heads * rows_dp
    id_rows = group_rows // head_dim
    packed = jnp.concatenate(
        [
            projected[query_heads:].reshape(kv_rows, head_dim),
            attn_low[out_mark:].reshape(out_rows, head_dim),
            jnp.pad(group_ids.reshape(id_rows, head_dim), ((0, 16 - id_rows), (0, 0))),
        ],
        axis=0,
    )
    keys_values = run(ring.gather(packed, packed.shape[0] // 32 * 16))
    out_blocks = keys_values[:, kv_rows : kv_rows + out_rows].reshape(data_count, query_heads, rows_dp, head_dim)
    out_blocks = jnp.transpose(out_blocks, (1, 0, 2, 3)).reshape(query_heads, model_width, head_dim)
    queries, keys_values, out_blocks = stage(
        [spread[0].cross(), spread[0].near(0), spread[0].y(0)], [queries, keys_values, out_blocks], idle=[cot_flow]
    )
    all_ids = keys_values[:, kv_rows + out_rows : kv_rows + out_rows + id_rows].reshape(-1)

    local = in_group(jnp.arange(group_rows, dtype=jnp.int32), group_rows, head_index * tok_rows)
    query_pos = data_index * group_rows + local
    first_pos = jnp.sum((all_ids[None, :] < group_ids[:, None]).astype(jnp.int32), axis=1)
    query_pos = jnp.tile(query_pos, query_heads)
    first_pos = jnp.tile(first_pos, query_heads)
    place = jnp.stack([data_index, head_index * tok_rows]).astype(jnp.int32)
    mixed_low, mixed_full, totals = attend(
        place, queries, keys_values, query_pos[:, None], first_pos[:, None], scale, group_rows
    )
    mixed_heads = mixed_low.reshape(query_heads, group_rows, head_dim)
    mixed_heads, mixed_full, totals, attn_part = stage(
        [spread[0].near(3), spread[0].y(1), spread[0].y(3), spread[1].cross(), cot_flow],
        [mixed_heads, mixed_full, totals, block_back(mixed_heads, out_blocks)],
    )
    attn_flow = Flow(scatter_rows(*attn_part, HEAD_MOVES))
    stage([attn_flow, spread[1].near(0), spread[1].y(0)], idle=[cot_flow])
    stage([attn_flow, spread[0].y(2), spread[1].near(3)], idle=[cot_flow])
    residual = inputs + attn_flow.value
    normed_two, norm_two_back = jax.vjp(rms_scale, residual, gains[1])
    wide_flow = Flow(wide_gather(normed_two.astype(BF16)))
    stage([wide_flow, spread[1].y(1), spread[1].y(3), cot_flow])
    stage([wide_flow, spread[1].y(2)])
    stage([wide_flow])
    finish(wide_flow, cot_flow)

    def whole_rows(pieces):
        if rows_dp % 16 == 0:
            return pieces
        out = jnp.zeros((3, data_count) + pieces[0].shape[1:], BF16)
        for k, piece in enumerate(pieces):
            out = lax.dynamic_update_index_in_dim(out, piece, data_index ^ k, 1)
        return [out.reshape(3, model_width, -1)]

    ffn_sides, ffn_full, grads_early, grads_late = ffn_front(
        place, wide_flow.value, cot_flow.value, whole_rows(spread[0].value()), whole_rows(spread[1].value())
    )

    def taker(grads):
        cut = grads.reshape(3, data_count, rows_dp, grads.shape[2])
        return lambda index: lax.dynamic_index_in_dim(cut, index, 1, keepdims=False)

    reduce = [Reduce(taker(grads_early)), Reduce(taker(grads_late))]
    *down_part, dx_kept, dx_sent = stage([reduce[0].y(2)], ffn_back(ffn_sides, ffn_full))
    out_flow = Flow(scatter_rows(*down_part, WIDE_MOVES))
    dx_flow = Flow(scatter_rows(dx_kept, dx_sent, WIDE_MOVES))
    dx_flow.advance([lax.ppermute(*send) for send in dx_flow.sends])
    stage([dx_flow, reduce[0].near(2), reduce[0].y(1), reduce[1].y(2)])
    stage([dx_flow, reduce[0].near(1), reduce[0].y(3), out_flow])
    grad_residual_norm, grad_gain_two = norm_two_back(dx_flow.value)
    grad_residual = cotangent.astype(F32) + grad_residual_norm
    grad_flow = Flow(head_gather(grad_residual.astype(BF16)))
    stage([grad_flow, reduce[1].near(2), reduce[1].y(1), reduce[1].y(3)])
    grad_flow.advance([lax.ppermute(*send) for send in grad_flow.sends])
    group_grad = grad_flow.value

    grad_heads = block_project(group_grad, out_blocks)
    grad_mixed = grad_heads.reshape(query_heads * group_rows, head_dim)
    delta = jnp.sum(grad_mixed.astype(F32) * mixed_full, axis=1)
    grad_queries, grad_keys_values = attend_back(
        place,
        queries,
        grad_mixed,
        keys_values,
        1.0 / totals.reshape(1, -1),
        delta[None, :],
        query_pos[None, :],
        first_pos[None, :],
        scale,
        group_rows,
    )
    group_grad, grad_queries, grad_keys_values = stage(
        [reduce[0].cross(), reduce[1].near(1), reduce[0].y(0), reduce[1].y(0), out_flow],
        [group_grad, grad_queries, grad_keys_values],
    )
    grad_queries = grad_queries.reshape(query_heads, group_rows, head_dim)

    late = 2
    main = 3 * ffn_blocks - late
    cap = -(-main // data_count)
    places = -(-max(cap * data_count, 3 * ffn_blocks) // TRIO) * TRIO
    def weight_sums(outer):
        cut = outer.reshape(outer.shape[0], data_count, rows_dp, head_dim)
        return Flow(ring.scatter(lambda i: lax.dynamic_index_in_dim(cut, i, 1, keepdims=False), outer.shape[0] // 2))

    key_flow = Flow(
        ring.scatter(lambda i: lax.dynamic_index_in_dim(grad_keys_values, i, 0, keepdims=False), key_heads)
    )
    pick = lambda own, other: (jnp.where(parity == 1, other, own), jnp.where(parity == 1, own, other))
    low_early, high_early = pick(*reduce[0].value())
    outer, low_early, high_early = stage(
        [key_flow, reduce[1].cross(), out_flow],
        [block_outer([group_in, group_grad], [grad_queries, mixed_heads], model_width), low_early, high_early],
    )
    low_late, high_late = pick(*reduce[1].value())
    block_out = (residual + out_flow.value).astype(BF16)
    first_flow = weight_sums(outer)
    weight_grads, new_momentum, grams = stage(
        [key_flow, first_flow],
        ffn_moment(low_early, low_late, high_early, high_late, momentum, gate_mark, ffn_blocks, places),
    )
    gram_flow = Flow(gram_sums(ring, grams, cap))
    stage([key_flow, first_flow, gram_flow])
    while key_flow.sends is not None:
        stage([key_flow, first_flow, gram_flow])
    key_value_sums = key_flow.value
    grad_keys = (key_value_sums[:key_heads] * scale).astype(BF16)
    grad_values = key_value_sums[key_heads:].astype(BF16)
    grad_keys_values = jnp.concatenate([grad_keys, grad_values], axis=0)
    (outer,) = stage([first_flow, gram_flow], [block_outer([group_in], [grad_keys_values], model_width)])
    finish(first_flow)
    second_flow = weight_sums(outer)
    pairs = [k for k in range(gate_mark // 2) if not query_heads <= 2 * k < out_mark]
    grad_projected = jnp.concatenate([grad_queries, grad_keys_values], axis=0)
    *attn_dx, weight_grads, new_momentum, first_grams = stage(
        [second_flow, gram_flow],
        [
            *block_back(grad_projected, qkv_blocks),
            *attn_moment(first_flow.value, pairs, momentum, weight_grads, new_momentum),
        ],
    )
    last_flow = Flow(scatter_rows(*attn_dx, HEAD_MOVES))
    while second_flow.sends is not None:
        stage([second_flow, gram_flow, last_flow])
    finish(last_flow, gram_flow)
    grad_input_norm, grad_gain_one = norm_one_back(last_flow.value)
    grad_input = grad_residual + grad_input_norm
    gain_flow = Flow(total_sum(jnp.stack([grad_gain_one, grad_gain_two])))
    weight_grads, new_momentum, second_grams = attn_moment(
        second_flow.value, list(range(query_heads // 2, out_mark // 2)), momentum, weight_grads, new_momentum
    )
    late_count = gate_mark + late
    late_cap = -(-late_count // data_count)
    late_grams = jnp.concatenate([first_grams, second_grams, grams[main : main + late]], axis=0)
    late_grams = jnp.pad(late_grams, ((0, late_cap * data_count - late_count), (0, 0), (0, 0), (0, 0)))
    factors = newton_factor(gram_flow.value, growth)
    late_sums, factors = stage(
        [gain_flow], [run(gram_sums(ring, late_grams, late_cap)), run(all_factors(ring, factors))]
    )
    (late_factors,) = stage([gain_flow], [newton_factor(late_sums, growth)])
    late_factor_flow = Flow(all_factors(ring, late_factors))

    threes = main // TRIO
    early_spots = [(gate_mark // TRIO + k, [TRIO * k + i for i in range(TRIO)]) for k in range(threes)]
    (new_weights,) = stage(
        [late_factor_flow, gain_flow], [renew(weights, new_momentum, factors, early_spots, [])]
    )
    finish(late_factor_flow, gain_flow)
    gain_grads = gain_flow.value
    rest = jnp.concatenate([late_factor_flow.value[:late_count], factors[TRIO * threes : main]], axis=0)
    blocks_of = [2 * pair + i for pair in pairs for i in range(2)] + list(range(query_heads, out_mark))
    blocks_of += [gate_mark + main + k for k in range(late)] + [gate_mark + k for k in range(TRIO * threes, main)]
    late_spots = [
        (spot, [blocks_of.index(TRIO * spot + i) for i in range(TRIO)])
        for spot in sorted({block // TRIO for block in blocks_of})
    ]
    new_weights = renew(weights, new_momentum, rest, late_spots, [new_weights])

    new_gain_first = BETA_ONE * gain_first + (1.0 - BETA_ONE) * gain_grads
    new_gain_second = BETA_TWO * gain_second + (1.0 - BETA_TWO) * gain_grads * gain_grads
    first_hat = new_gain_first / (1.0 - BETA_ONE**UPDATE_STEP)
    second_hat = new_gain_second / (1.0 - BETA_TWO**UPDATE_STEP)
    new_gains = gains - ADAM_RATE * first_hat / (jnp.sqrt(second_hat) + ADAM_EPS)
    back = lambda array: jnp.transpose(array, (1, 0, 2))
    return (
        block_out,
        grad_input,
        back(weight_grads),
        back(new_momentum),
        back(new_weights),
        gain_grads,
        new_gain_first,
        new_gain_second,
        new_gains,
    )


def solution(mesh):
    return jax.shard_map(
        on_device,
        mesh=mesh,
        in_specs=(
            P(("dp", "head"), None),
            P(("dp", "head"), None),
            P(("dp", "head")),
            P("dp", "head", None),
            P("dp", "head", None),
            P(),
            P(),
            P(),
        ),
        out_specs=(
            P(("dp", "head"), None),
            P(("dp", "head"), None),
            P("dp", "head", None),
            P("dp", "head", None),
            P("dp", "head", None),
            P(),
            P(),
            P(),
            P(),
        ),
        check_vma=False,
    )
```

```python
import functools
import math

import jax
import jax.numpy as jnp
from jax import lax
from jax.experimental import pallas as pl
from jax.experimental.pallas import tpu as pltpu
from jax.sharding import PartitionSpec as P

H = 8
KV = 4
FF = 9216
NEWTON_STEPS = 5
UPDATE_STEP = 10

NORM_EPS = 1e-06
SOFT_CAP = 50.0
MUON_RATE = 0.2
MUON_DECAY = 0.01
MUON_BETA = 0.95
ADAM_RATE = 0.3
BETA_ONE = 0.9
BETA_TWO = 0.95
ADAM_EPS = 1e-08
NEWTON_LINEAR = 3.4445
NEWTON_SQUARE = -4.775
NEWTON_CUBIC = 2.0315
TOP_PRECISION = lax.Precision.HIGHEST

BF16 = jnp.bfloat16
F32 = jnp.float32
VMEM_LIMIT = 62 * 1024 * 1024
NN = (((1,), (0,)), ((), ()))
NT = (((1,), (1,)), ((), ()))
TN = (((0,), (0,)), ((), ()))


def mm(a, b, dims):
    return lax.dot_general(a, b, dims, preferred_element_type=F32)


def rms_scale(rows, gain):
    inverse = lax.rsqrt(jnp.mean(rows * rows, axis=-1, keepdims=True) + NORM_EPS)
    return rows * inverse * gain


class Flow:
    def __init__(self, steps):
        self.steps = steps
        self.value = None
        self.sends = None
        self.advance(None)

    def advance(self, arrived):
        try:
            self.sends = self.steps.send(arrived)
        except StopIteration as stop:
            self.sends = None
            self.value = stop.value


def stage(flows, extra=(), idle=()):
    flows = [flow for flow in flows if flow.sends is not None]
    idle = [flow for flow in idle if flow.sends is not None and flow not in flows]
    arrived = [[lax.ppermute(*send) for send in flow.sends] for flow in flows]
    held = [[send[0] for send in flow.sends] for flow in idle]
    arrived, held, extra = lax.optimization_barrier((arrived, held, list(extra)))
    for flow, got in zip(flows, arrived):
        flow.advance(got)
    for flow, kept in zip(idle, held):
        flow.sends = [(value,) + send[1:] for value, send in zip(kept, flow.sends)]
    return extra


def run(steps):
    flow = Flow(steps)
    while flow.sends is not None:
        flow.advance([lax.ppermute(*send) for send in flow.sends])
    return flow.value


def finish(*flows):
    while any(flow.sends is not None for flow in flows):
        stage(flows)


def swap(value, axis, mask):
    size = lax.axis_size(axis)
    return (value, axis, [(i, i ^ mask) for i in range(size)])


def head_gather(rows):
    (other,) = yield [swap(rows, "head", 2)]
    pair = jnp.concatenate([rows, other], axis=0)
    (other,) = yield [swap(pair, "head", 1)]
    return jnp.concatenate([pair, other], axis=0)


def wide_gather(rows):
    (other,) = yield [swap(rows, "dp", 4)]
    both = jnp.concatenate([rows, other], axis=0)
    (other,) = yield [swap(both, "head", 2)]
    pair = jnp.concatenate([both, other], axis=0)
    (other,) = yield [swap(pair, "head", 1)]
    return [pair, other]


def add_low(kept, other):
    return (kept.astype(F32) + other.astype(F32)).astype(BF16)


def scatter_rows(kept, sent, moves):
    for k, (axis, mask) in enumerate(moves):
        (other,) = yield [swap(sent, axis, mask)]
        part = kept.astype(F32) + other.astype(F32)
        if k < len(moves) - 1:
            half = part.shape[0] // 2
            kept, sent = part[:half], part[half:].astype(BF16)
    return part


HEAD_MOVES = (("head", 1), ("head", 2))
WIDE_MOVES = (("head", 1), ("head", 2), ("dp", 4))


def total_sum(value):
    for axis in ("head", "dp"):
        mask = 1
        while mask < lax.axis_size(axis):
            (other,) = yield [swap(value, axis, mask)]
            value = value + other
            mask *= 2
    return value


class Ring:
    def __init__(self):
        size = lax.axis_size("dp")
        order = list(range(0, size, 2)) + list(range(size - 1, 0, -2))
        around = [[order[(order.index(i) + offset) % size] for offset in range(size)] for i in range(size)]
        self.size = size
        self.around = jnp.array(around, jnp.int32)[lax.axis_index("dp")]
        self.up = [(order[k], order[(k + 1) % size]) for k in range(size)]
        self.down = [(order[(k + 1) % size], order[k]) for k in range(size)]

    def index(self, offset):
        return self.around[offset % self.size]

    def gather(self, value, mid):
        half = self.size // 2
        zeros = (0,) * (value.ndim - 1)
        out = jnp.zeros((self.size,) + value.shape, value.dtype)
        out = lax.dynamic_update_index_in_dim(out, value, self.index(0), 0)
        ahead, back = value, value
        for step in range(1, half):
            ahead, back = yield [(ahead, "dp", self.up), (back, "dp", self.down)]
            out = lax.dynamic_update_index_in_dim(out, ahead, self.index(-step), 0)
            out = lax.dynamic_update_index_in_dim(out, back, self.index(step), 0)
        first, second = yield [(ahead[:mid], "dp", self.up), (back[mid:], "dp", self.down)]
        far = self.index(half)
        out = lax.dynamic_update_slice(out, first[None], (far, 0) + zeros)
        return lax.dynamic_update_slice(out, second[None], (far, mid) + zeros)

    def scatter(self, take, mid):
        half = self.size // 2
        far = take(self.index(half))
        kind = far.dtype
        up, down = yield [(far[:mid], "dp", self.up), (far[mid:], "dp", self.down)]
        for step in range(half - 1, 0, -1):
            part = take(self.index(step)).astype(F32)
            ahead = jnp.concatenate([part[:mid] + up, part[mid:]]) if step == half - 1 else part + up
            part = take(self.index(-step)).astype(F32)
            back = jnp.concatenate([part[:mid], part[mid:] + down]) if step == half - 1 else part + down
            up, down = yield [(ahead.astype(kind), "dp", self.up), (back.astype(kind), "dp", self.down)]
        return take(self.index(0)).astype(F32) + up.astype(F32) + down.astype(F32)


def once(sends, take):
    def steps():
        take((yield sends))

    return Flow(steps())


SIDE_BIT = 2


def plane_classes():
    planes = range(lax.axis_size("dp") // 2)
    kept = [m for m in planes if m & 3 in (0, 3)]
    passed = [m for m in planes if m & 3 in (1, 2)]
    return {0: [0], 1: [1], 2: [m for m in passed if m != 1], 3: [m for m in kept if m]}


class Spread:
    def __init__(self, mine, other):
        self.mine, self.other = mine, other
        self.pieces = {0: mine}

    def move(self, moves):
        def take(arrived):
            for (_, _, _, number), piece in zip(moves, arrived):
                self.pieces[number] = piece

        return once([swap(value, "dp", offset << 1 | bit) for value, offset, bit, _ in moves], take)

    def cross(self):
        group = plane_classes()[3]
        return self.move([(self.other if m & SIDE_BIT else self.mine, m, 0, m << 1) for m in group])

    def near(self, key):
        group = plane_classes()[key]
        return self.move([(self.pieces[m << 1], 1, 0, (m ^ 1) << 1) for m in group])

    def y(self, key):
        group = plane_classes()[key]
        return self.move([(self.pieces[m << 1], 0, 1, m << 1 | 1) for m in group])

    def value(self):
        return [self.pieces[k] for k in range(lax.axis_size("dp"))]


class Reduce:
    def __init__(self, rows):
        self.rows = rows
        self.parts = {}
        self.sums = [None, None]

    def part(self, offset):
        terms = [term.astype(F32) for term in self.parts[offset]]
        return functools.reduce(jnp.add, terms)

    def hold(self, offset, *terms):
        self.parts.setdefault(offset, []).extend(terms)

    def y(self, key):
        group = plane_classes()[key]

        def take(arrived):
            for offset, got in zip(group, arrived):
                self.hold(offset, self.rows(offset << 1), got)

        return once([swap(self.rows(offset << 1 | 1), "dp", 1) for offset in group], take)

    def near(self, key):
        group = plane_classes()[key]

        def take(arrived):
            for offset, got in zip(group, arrived):
                self.hold(offset ^ 1, got)

        return once([swap(self.part(offset).astype(BF16), "dp", 2) for offset in group], take)

    def cross(self):
        group = plane_classes()[3]

        def take(arrived):
            for offset, got in zip(group, arrived):
                self.add(1 if offset & SIDE_BIT else 0, got.astype(F32))

        return once([swap(self.part(offset).astype(BF16), "dp", offset << 1) for offset in group], take)

    def add(self, side, value):
        self.sums[side] = value if self.sums[side] is None else self.sums[side] + value

    def value(self):
        self.add(0, self.part(0))
        return self.sums


def params(**more):
    return pltpu.CompilerParams(vmem_limit_bytes=VMEM_LIMIT, **more)


TRIO = 3


def cast_blocks(blocks, count):
    _, r, c = blocks.shape

    def body(x_ref, o_ref):
        o_ref[...] = x_ref[...].astype(BF16)

    spec = pl.BlockSpec((TRIO, r, c), lambda k: (k, 0, 0))
    return pl.pallas_call(
        body,
        grid=(count // TRIO,),
        in_specs=[spec],
        out_specs=spec,
        out_shape=jax.ShapeDtypeStruct((count, r, c), BF16),
        compiler_params=params(),
        cost_estimate=pl.CostEstimate(flops=0, bytes_accessed=6 * count * r * c, transcendentals=0),
    )(blocks)


def pack_units(parity, blocks, first, kind_blocks, early):
    _, r, c = blocks.shape
    h = c // 2
    full = kind_blocks // 2
    each = kind_blocks // TRIO
    u, v = early * c, (full - early) * c + h

    def body(s_ref, *refs):
        parts, outs = refs[:each], refs[each:]

        def tile(f):
            return parts[f // TRIO].at[f % TRIO]

        for turn in range(2):

            @pl.when(s_ref[0] == turn)
            def _():
                for k in range(2):
                    side = turn ^ k
                    for i in range(full):
                        value = tile(side * full + i)[...].astype(BF16)
                        if i < early:
                            outs[2 * k][:, i * c : (i + 1) * c] = value
                        else:
                            outs[2 * k + 1][:, (i - early) * c : (i - early + 1) * c] = value
                    rest = tile(2 * full)[:, side * h : (side + 1) * h]
                    outs[2 * k + 1][:, v - h :] = rest.astype(BF16)

    def part(i):
        return pl.BlockSpec((TRIO, r, c), lambda k, s: (first // TRIO + each * k + i, 0, 0))

    wide = pl.BlockSpec((None, r, u), lambda k, s: (k, 0, 0))
    slim = pl.BlockSpec((None, r, v), lambda k, s: (k, 0, 0))
    shapes = [jax.ShapeDtypeStruct((3, r, u), BF16), jax.ShapeDtypeStruct((3, r, v), BF16)]
    return pl.pallas_call(
        body,
        grid_spec=pltpu.PrefetchScalarGridSpec(
            num_scalar_prefetch=1,
            grid=(3,),
            in_specs=[part(i) for i in range(each)],
            out_specs=[wide, slim, wide, slim],
        ),
        out_shape=shapes + shapes,
        compiler_params=params(),
        cost_estimate=pl.CostEstimate(flops=0, bytes_accessed=18 * kind_blocks * r * c, transcendentals=0),
    )(parity, *([blocks] * each))


def block_project(rows, blocks):
    t = rows.shape[0]
    count, d, c = blocks.shape

    def body(x_ref, w_ref, o_ref):
        o_ref[...] = mm(x_ref[...], w_ref[...], NN).astype(BF16)

    return pl.pallas_call(
        body,
        grid=(count,),
        in_specs=[
            pl.BlockSpec((t, d), lambda b: (0, 0)),
            pl.BlockSpec((None, d, c), lambda b: (b, 0, 0)),
        ],
        out_specs=pl.BlockSpec((None, t, c), lambda b: (b, 0, 0)),
        out_shape=jax.ShapeDtypeStruct((count, t, c), BF16),
        compiler_params=params(),
        cost_estimate=pl.CostEstimate(
            flops=2 * count * t * d * c, bytes_accessed=2 * (t * d + count * (d * c + t * c)), transcendentals=0
        ),
    )(rows, blocks)


def block_back(cols, blocks):
    count, t, c = cols.shape
    d = blocks.shape[1]
    half = t // 2

    def body(x_ref, w_ref, o_ref, p_ref, acc_ref):
        b = pl.program_id(0)

        @pl.when(b == 0)
        def _():
            acc_ref[...] = jnp.zeros_like(acc_ref)

        acc_ref[...] += mm(x_ref[...], w_ref[...], NT)

        @pl.when(b == count - 1)
        def _():
            o_ref[...] = acc_ref[:half, :].astype(BF16)
            p_ref[...] = acc_ref[half:, :].astype(BF16)

    result = pl.BlockSpec((half, d), lambda b: (0, 0))
    return pl.pallas_call(
        body,
        grid=(count,),
        in_specs=[
            pl.BlockSpec((None, t, c), lambda b: (b, 0, 0)),
            pl.BlockSpec((None, d, c), lambda b: (b, 0, 0)),
        ],
        out_specs=[result, result],
        out_shape=[jax.ShapeDtypeStruct((half, d), BF16)] * 2,
        scratch_shapes=[pltpu.VMEM((t, d), F32)],
        compiler_params=params(),
        cost_estimate=pl.CostEstimate(
            flops=2 * count * t * d * c, bytes_accessed=2 * (t * d + count * (d * c + t * c)), transcendentals=0
        ),
    )(cols, blocks)


def block_outer(rows, cols, d):
    t = rows[0].shape[0]
    c = cols[0].shape[2]
    starts = [0]
    for col in cols:
        starts.append(starts[-1] + col.shape[0])
    count = len(rows)
    total = starts[-1]

    def body(*refs):
        o_ref, t_ref = refs[2 * count :]
        b = pl.program_id(0)
        for k in range(count):

            @pl.when(b == starts[k])
            def _():
                t_ref[...] = refs[k][...].T

            @pl.when((b >= starts[k]) & (b < starts[k + 1]))
            def _():
                o_ref[...] = mm(t_ref[...], refs[count + k][...], NN).astype(BF16)

    def col_at(k):
        return pl.BlockSpec((None, t, c), lambda b: (jnp.clip(b - starts[k], 0, starts[k + 1] - starts[k] - 1), 0, 0))

    return pl.pallas_call(
        body,
        grid=(total,),
        in_specs=[pl.BlockSpec((t, d), lambda b: (0, 0))] * count + [col_at(k) for k in range(count)],
        out_specs=pl.BlockSpec((None, d, c), lambda b: (b, 0, 0)),
        out_shape=jax.ShapeDtypeStruct((total, d, c), BF16),
        scratch_shapes=[pltpu.VMEM((d, t), BF16)],
        compiler_params=params(),
        cost_estimate=pl.CostEstimate(
            flops=2 * total * t * d * c,
            bytes_accessed=2 * (count * t * d + total * (d * c + t * c)),
            transcendentals=0,
        ),
    )(*rows, *cols)


def in_group(local, width, head_shift):
    quarter = width // 4
    low = jnp.bitwise_and(local, quarter - 1)
    one = jnp.where(jnp.bitwise_and(local, quarter) != 0, 2 * quarter, 0)
    two = jnp.where(jnp.bitwise_and(local, 2 * quarter) != 0, quarter, 0)
    return jnp.bitwise_xor(low + one + two, head_shift)


def key_position(block, width, head_shift, shape, axis):
    local = lax.broadcasted_iota(jnp.int32, shape, axis)
    return block * width + in_group(local, width, head_shift)


def attend(place, queries, keys_values, query_pos, first_pos, scale, p):
    m, e = queries.shape
    n = keys_values.shape[0]
    step = 256

    def body(place_ref, q_ref, kv_ref, pos_ref, first_ref, low_ref, full_ref, sum_ref, acc_ref, tot_ref):
        j = pl.program_id(0)

        @pl.when(j == 0)
        def _():
            acc_ref[...] = jnp.zeros_like(acc_ref)
            tot_ref[...] = jnp.zeros_like(tot_ref)

        @pl.when(j <= place_ref[0])
        def _():
            key_pos = key_position(j, p, place_ref[1], (1, p), 1)
            for r in range(0, m, step):
                rows = pl.ds(r, step)
                raw = mm(q_ref[rows, :], kv_ref[:p, :], NT)
                soft = SOFT_CAP * jnp.tanh(raw * (scale / SOFT_CAP))
                seen = (key_pos >= first_ref[rows, :]) & (key_pos <= pos_ref[rows, :])
                terms = jnp.where(seen, jnp.exp(soft), 0.0)
                tot_ref[rows, :] += jnp.sum(terms, axis=1, keepdims=True)
                acc_ref[rows, :] += mm(terms.astype(BF16), kv_ref[p:, :], NN)

        @pl.when(j == n - 1)
        def _():
            total = tot_ref[...]
            mixed = acc_ref[...] / total
            full_ref[...] = mixed
            low_ref[...] = mixed.astype(BF16)
            sum_ref[...] = total

    whole = lambda shape: pl.BlockSpec(shape, lambda j, s: (0, 0))
    return pl.pallas_call(
        body,
        grid_spec=pltpu.PrefetchScalarGridSpec(
            num_scalar_prefetch=1,
            grid=(n,),
            in_specs=[
                whole((m, e)),
                pl.BlockSpec((None, 2 * p, e), lambda j, s: (jnp.minimum(j, s[0]), 0, 0)),
                whole((m, 1)),
                whole((m, 1)),
            ],
            out_specs=[whole((m, e)), whole((m, e)), whole((m, 1))],
            scratch_shapes=[pltpu.VMEM((m, e), F32), pltpu.VMEM((m, 1), F32)],
        ),
        out_shape=[
            jax.ShapeDtypeStruct((m, e), BF16),
            jax.ShapeDtypeStruct((m, e), F32),
            jax.ShapeDtypeStruct((m, 1), F32),
        ],
        compiler_params=params(),
        cost_estimate=pl.CostEstimate(
            flops=4 * m * n * p * e, bytes_accessed=4 * n * p * e, transcendentals=2 * m * n * p
        ),
    )(place, queries, keys_values, query_pos, first_pos)


def attend_back(place, queries, grads, keys_values, inverse, delta, query_pos, first_pos, scale, p):
    m, e = queries.shape
    n = keys_values.shape[0]
    step = 256

    def body(
        place_ref, q_ref, g_ref, kv_ref, inv_ref, delta_ref, pos_ref, first_ref, dq_ref, dkv_ref, acc_ref, dk_ref, dv_ref
    ):
        j = pl.program_id(0)

        @pl.when(j == 0)
        def _():
            acc_ref[...] = jnp.zeros_like(acc_ref)

        @pl.when(j <= place_ref[0])
        def _():
            key_pos = key_position(j, p, place_ref[1], (p, 1), 0)
            for r in range(0, m, step):
                rows = pl.ds(r, step)
                raw = mm(kv_ref[:p, :], q_ref[rows, :], NT)
                capped = jnp.tanh(raw * (scale / SOFT_CAP))
                seen = (key_pos >= first_ref[:, rows]) & (key_pos <= pos_ref[:, rows])
                probs = jnp.where(seen, jnp.exp(SOFT_CAP * capped), 0.0) * inv_ref[:, rows]
                grad_probs = mm(kv_ref[p:, :], g_ref[rows, :], NT)
                grad_raw = probs * (grad_probs - delta_ref[:, rows]) * (1.0 - capped * capped)
                grad_low = grad_raw.astype(BF16)
                value_part = mm(probs.astype(BF16), g_ref[rows, :], NN)
                key_part = mm(grad_low, q_ref[rows, :], NN)
                if r == 0:
                    dv_ref[...] = value_part
                    dk_ref[...] = key_part
                else:
                    dv_ref[...] += value_part
                    dk_ref[...] += key_part
                acc_ref[rows, :] += mm(grad_low, kv_ref[:p, :], TN)
            dkv_ref[0] = dk_ref[...].astype(BF16)
            dkv_ref[1] = dv_ref[...].astype(BF16)

        @pl.when(j > place_ref[0])
        def _():
            dkv_ref[...] = jnp.zeros_like(dkv_ref)

        @pl.when(j == n - 1)
        def _():
            dq_ref[...] = (acc_ref[...] * scale).astype(BF16)

    whole = lambda shape: pl.BlockSpec(shape, lambda j, s: (0, 0))
    return pl.pallas_call(
        body,
        grid_spec=pltpu.PrefetchScalarGridSpec(
            num_scalar_prefetch=1,
            grid=(n,),
            in_specs=[
                whole((m, e)),
                whole((m, e)),
                pl.BlockSpec((None, 2 * p, e), lambda j, s: (jnp.minimum(j, s[0]), 0, 0)),
                whole((1, m)),
                whole((1, m)),
                whole((1, m)),
                whole((1, m)),
            ],
            out_specs=[whole((m, e)), pl.BlockSpec((None, 2, p, e), lambda j, s: (j, 0, 0, 0))],
            scratch_shapes=[pltpu.VMEM((m, e), F32), pltpu.VMEM((p, e), F32), pltpu.VMEM((p, e), F32)],
        ),
        out_shape=[jax.ShapeDtypeStruct((m, e), BF16), jax.ShapeDtypeStruct((n, 2, p, e), BF16)],
        compiler_params=params(),
        cost_estimate=pl.CostEstimate(
            flops=10 * m * n * p * e, bytes_accessed=8 * n * p * e, transcendentals=2 * m * n * p
        ),
    )(place, queries, grads, keys_values, inverse, delta, query_pos, first_pos)


def gelu_pair(gate):
    outer = math.sqrt(2.0 / math.pi)
    square = gate * gate
    bent = jnp.tanh(outer * gate * (1.0 + 0.044715 * square))
    half = 0.5 * (1.0 + bent)
    slope = half + 0.5 * gate * (1.0 - bent * bent) * outer * (1.0 + 3.0 * 0.044715 * square)
    return gate * half, slope


def ffn_front(place, rows, cots, early, late):
    part_rows, d = rows[0].shape
    t = 2 * part_rows
    count = len(early)
    r = early[0].shape[1]
    u, v = early[0].shape[2], late[0].shape[2]
    tall = min(512, t)
    wide = d // 3
    cuts = [(k, min(256, u + v - k)) for k in range(0, u + v, 256)]

    def body(place_ref, x0, x1, y0, y1, *refs):
        early_refs, late_refs = refs[:count], refs[count : 2 * count]
        refs = refs[2 * count :]
        hs_ref, w_out = refs[:2]
        grad_refs = refs[2 : 2 + count], refs[2 + count : 2 + 2 * count]
        x, y, w, xt, yt, hs, row_sems, sems, out_sems, grad_sems = refs[2 + 2 * count :]
        row_copies = []
        for k, (source, target) in enumerate(((x0, x), (x1, x), (y0, y), (y1, y))):
            target = target.at[pl.ds((k % 2) * part_rows, part_rows), :]
            row_copies.append(pltpu.make_async_copy(source, target, row_sems.at[k]))
            row_copies[k].start()
        copies = []
        chunks = ((early_refs, pl.ds(0, u)), (late_refs, pl.ds(u, v)))

        def spot(k):
            return pl.ds(pl.multiple_of(jnp.bitwise_xor(place_ref[0], k) * r, 16) if count > 1 else 0, r)

        for k in range(count):
            for way, (sources, lanes) in enumerate(chunks):
                copy = pltpu.make_async_copy(sources[k], w.at[:, spot(k), lanes], sems.at[way, k])
                copy.start()
                copies.append(copy)
        for copy in row_copies:
            copy.wait()

        @pl.loop(0, d // 256)
        def _(k):
            cols = pl.ds(pl.multiple_of(k * 256, 256), 256)
            xt[cols, :] = x[:, cols].T
            yt[cols, :] = y[:, cols].T

        for copy in copies:
            copy.wait()
        kept = pltpu.make_async_copy(w, w_out, out_sems.at[0])
        kept.start()

        @pl.loop(0, t // tall)
        def _(i):
            part = pl.ds(pl.multiple_of(i * tall, tall), tall)
            for start, size in cuts:
                units = pl.ds(start, size)
                gate = mm(x[part, :], w[0, :, units], NN)
                up = mm(x[part, :], w[1, :, units], NN)
                grad = mm(y[part, :], w[2, :, units], NN)
                active, slope = gelu_pair(gate)
                hs[0, part, units] = (active * up).astype(BF16)
                hs[1, part, units] = (grad * up * slope).astype(BF16)
                hs[2, part, units] = (grad * active).astype(BF16)

        sides = pltpu.make_async_copy(hs, hs_ref, out_sems.at[1])
        sides.start()
        kept.wait()
        copies = []
        for kind, (left, right) in enumerate(((xt, 1), (xt, 2), (yt, 0))):

            @pl.loop(0, d // wide)
            def _(k):
                cols = pl.ds(pl.multiple_of(k * wide, wide), wide)
                w[kind, cols, :] = mm(left[cols, :], hs[right], NN).astype(BF16)

            for k in range(count):
                for way, (_, lanes) in enumerate(chunks):
                    target = grad_refs[way][k].at[kind]
                    copy = pltpu.make_async_copy(w.at[kind, spot(k), lanes], target, grad_sems.at[kind, way, k])
                    copy.start()
                    copies.append(copy)
        sides.wait()
        for copy in copies:
            copy.wait()

    apart = pl.BlockSpec(memory_space=pl.ANY)
    return pl.pallas_call(
        body,
        grid_spec=pltpu.PrefetchScalarGridSpec(
            num_scalar_prefetch=1,
            grid=(1,),
            in_specs=[apart] * (4 + 2 * count),
            out_specs=[apart] * (2 + 2 * count),
            scratch_shapes=[
                pltpu.VMEM((t, d), BF16),
                pltpu.VMEM((t, d), BF16),
                pltpu.VMEM((3, d, u + v), BF16),
                pltpu.VMEM((d, t), BF16),
                pltpu.VMEM((d, t), BF16),
                pltpu.VMEM((3, t, u + v), BF16),
                pltpu.SemaphoreType.DMA((4,)),
                pltpu.SemaphoreType.DMA((2, count)),
                pltpu.SemaphoreType.DMA((2,)),
                pltpu.SemaphoreType.DMA((3, 2, count)),
            ],
        ),
        out_shape=[
            jax.ShapeDtypeStruct((3, t, u + v), BF16),
            jax.ShapeDtypeStruct((3, d, u + v), BF16),
            *[jax.ShapeDtypeStruct((3, r, u), BF16)] * count,
            *[jax.ShapeDtypeStruct((3, r, v), BF16)] * count,
        ],
        compiler_params=params(),
        cost_estimate=pl.CostEstimate(
            flops=12 * t * d * (u + v), bytes_accessed=12 * d * (u + v) + 4 * t * d, transcendentals=t * (u + v)
        ),
    )(place, *rows, *cots, *early, *late)


def ffn_back(sides, blocks):
    _, t, u = sides.shape
    d = blocks.shape[1]
    wide = 256
    half = t // 2

    def body(s_ref, w_ref, *refs):
        for k in range(2):
            part = pl.ds(k * half, half)
            refs[k][...] = mm(s_ref[0, part, :], w_ref[2], NT).astype(BF16)
            refs[2 + k][...] = (mm(s_ref[1, part, :], w_ref[0], NT) + mm(s_ref[2, part, :], w_ref[1], NT)).astype(BF16)

    return pl.pallas_call(
        body,
        grid=(d // wide,),
        in_specs=[
            pl.BlockSpec((3, t, u), lambda k: (0, 0, 0), pipeline_mode=pl.Buffered(1)),
            pl.BlockSpec((3, wide, u), lambda k: (0, k, 0)),
        ],
        out_specs=[pl.BlockSpec((half, wide), lambda k: (0, k))] * 4,
        out_shape=[jax.ShapeDtypeStruct((half, d), BF16)] * 4,
        compiler_params=params(),
        cost_estimate=pl.CostEstimate(
            flops=6 * t * d * u, bytes_accessed=6 * d * u + 6 * t * u + 4 * t * d, transcendentals=0
        ),
    )(sides, blocks)


def gram_parts(m):
    h = m.shape[1] // 2
    high = m.astype(BF16)
    low = (m - high.astype(F32)).astype(BF16)
    mixed = mm(high, low, TN)
    gram = mm(high, high, TN) + mm(low, low, TN) + mixed + mixed.T
    return gram[:h, :h], gram[:h, h:], gram[h:, h:]


def ffn_moment(low_early, low_late, high_early, high_late, momentum, first, blocks, places):
    total, r, c = momentum.shape
    early = low_early.shape[2] // c
    h = c // 2
    full = early + 1
    each = blocks // TRIO

    def body(le_ref, ll_ref, he_ref, hl_ref, m_ref, wg_ref, nm_ref, gram_ref):
        j = pl.program_id(0)

        @pl.when(j >= TRIO * each)
        def _():
            gram_ref[...] = jnp.zeros_like(gram_ref)

        for turn in range(each):

            @pl.when((j < TRIO * each) & (lax.rem(j, each) == turn))
            def _():
                for i in range(TRIO):
                    side, f = divmod(turn * TRIO + i, full)
                    if side == 2:
                        wg_ref[i, :, :h] = ll_ref[:, c:]
                        wg_ref[i, :, h:] = hl_ref[:, c:]
                    elif f < early:
                        wg_ref[i] = (le_ref, he_ref)[side][:, f * c : (f + 1) * c]
                    else:
                        wg_ref[i] = (ll_ref, hl_ref)[side][:, :c]

        @pl.when(j < TRIO * each)
        def _():
            for i in range(TRIO):
                new = MUON_BETA * m_ref[i] + wg_ref[i]
                nm_ref[i] = new
                gram_ref[i, 0], gram_ref[i, 1], gram_ref[i, 2] = gram_parts(new)

    kind = lambda j: (jnp.minimum(j // each, 2), 0, 0)
    block = lambda j: (first // TRIO + jnp.minimum(j, TRIO * each - 1), 0, 0)
    u, v = low_early.shape[2], low_late.shape[2]
    return pl.pallas_call(
        body,
        grid=(places // TRIO,),
        in_specs=[
            pl.BlockSpec((None, r, u), kind),
            pl.BlockSpec((None, r, v), kind),
            pl.BlockSpec((None, r, u), kind),
            pl.BlockSpec((None, r, v), kind),
            pl.BlockSpec((TRIO, r, c), block),
        ],
        out_specs=[
            pl.BlockSpec((TRIO, r, c), block),
            pl.BlockSpec((TRIO, r, c), block),
            pl.BlockSpec((TRIO, 3, h, h), lambda j: (j, 0, 0, 0)),
        ],
        out_shape=[
            jax.ShapeDtypeStruct((total, r, c), F32),
            jax.ShapeDtypeStruct((total, r, c), F32),
            jax.ShapeDtypeStruct((places, 3, h, h), F32),
        ],
        compiler_params=params(),
        cost_estimate=pl.CostEstimate(
            flops=6 * 3 * blocks * r * c * c, bytes_accessed=16 * 3 * blocks * r * c, transcendentals=0
        ),
    )(low_early, low_late, high_early, high_late, momentum)


def attn_moment(grads, pairs, momentum, weight_grads, new_momentum):
    count, r, c = grads.shape
    h = c // 2

    def body(s_ref, g_ref, m_ref, wg_in, nm_in, wg_ref, nm_ref, gram_ref):
        for i in range(2):
            new = MUON_BETA * m_ref[i] + g_ref[i]
            wg_ref[i] = g_ref[i]
            nm_ref[i] = new
            gram_ref[i, 0], gram_ref[i, 1], gram_ref[i, 2] = gram_parts(new)

    block = pl.BlockSpec((2, r, c), lambda j, s: (s[j], 0, 0))
    apart = pl.BlockSpec(memory_space=pl.ANY)
    return pl.pallas_call(
        body,
        grid_spec=pltpu.PrefetchScalarGridSpec(
            num_scalar_prefetch=1,
            grid=(count // 2,),
            in_specs=[pl.BlockSpec((2, r, c), lambda j, s: (j, 0, 0)), block, apart, apart],
            out_specs=[block, block, pl.BlockSpec((2, 3, h, h), lambda j, s: (j, 0, 0, 0))],
        ),
        out_shape=[
            jax.ShapeDtypeStruct(momentum.shape, F32),
            jax.ShapeDtypeStruct(momentum.shape, F32),
            jax.ShapeDtypeStruct((count, 3, h, h), F32),
        ],
        input_output_aliases={3: 0, 4: 1},
        compiler_params=params(),
        cost_estimate=pl.CostEstimate(
            flops=6 * count * r * c * c, bytes_accessed=16 * count * r * c, transcendentals=0
        ),
    )(jnp.array(pairs, jnp.int32), grads, momentum, weight_grads, new_momentum)


def renew(weights, momentum, factors, spots, updated):
    _, r, c = weights.shape
    h = c // 2
    steps = len(spots)
    table = jnp.array([spot for spot, _ in spots] + [f for _, places in spots for f in places], jnp.int32)

    def body(s_ref, w_ref, m_ref, *refs):
        factor_refs, o_ref = refs[:TRIO], refs[-1]
        for i in range(TRIO):
            left = m_ref[i, :, :h].astype(BF16)
            right = m_ref[i, :, h:].astype(BF16)
            first, off, last = factor_refs[i][0], factor_refs[i][1], factor_refs[i][2]
            start = mm(left, first, NN) + mm(right, off, NT)
            rest = mm(left, off, NN) + mm(right, last, NN)
            keep = 1.0 - MUON_RATE * MUON_DECAY
            o_ref[i, :, :h] = w_ref[i, :, :h] * keep - MUON_RATE * start
            o_ref[i, :, h:] = w_ref[i, :, h:] * keep - MUON_RATE * rest

    block = pl.BlockSpec((TRIO, r, c), lambda j, s: (s[j], 0, 0))

    def factor_at(i):
        return pl.BlockSpec((None, 3, h, h), lambda j, s: (s[steps + TRIO * j + i], 0, 0, 0))

    apart = [pl.BlockSpec(memory_space=pl.ANY)] * len(updated)
    return pl.pallas_call(
        body,
        grid_spec=pltpu.PrefetchScalarGridSpec(
            num_scalar_prefetch=1,
            grid=(steps,),
            in_specs=[block, block] + [factor_at(i) for i in range(TRIO)] + apart,
            out_specs=block,
        ),
        out_shape=jax.ShapeDtypeStruct(weights.shape, F32),
        input_output_aliases={3 + TRIO: 0} if updated else {},
        compiler_params=params(),
        cost_estimate=pl.CostEstimate(
            flops=2 * TRIO * steps * r * c * c, bytes_accessed=12 * TRIO * steps * r * c, transcendentals=0
        ),
    )(table, weights, momentum, *([factors] * TRIO), *updated)


def top(spec, a, b):
    return jnp.einsum(spec, a, b, precision=TOP_PRECISION)


def newton_factor(grams, growth):
    size = grams.shape[-1]
    eye = jnp.eye(size, dtype=F32)
    norm = jnp.sqrt(jnp.sum(grams * eye, axis=(1, 2), keepdims=True))
    inverse = 1.0 / (norm + 1e-07)
    gram = grams * (inverse * inverse)
    factor = None
    for sweep in range(NEWTON_STEPS):
        square = top("bij,bjk->bik", gram, gram)
        poly = NEWTON_LINEAR * eye + NEWTON_SQUARE * gram + NEWTON_CUBIC * square
        factor = poly if sweep == 0 else top("bij,bjk->bik", factor, poly)
        if sweep < NEWTON_STEPS - 1:
            gram = top("bij,bjk->bik", top("bij,bjk->bik", gram, poly), poly)
    return factor * (growth * inverse)


def fold(squares):
    h = squares.shape[1] // 2
    return jnp.stack([squares[:, :h, :h], squares[:, :h, h:], squares[:, h:, h:]], axis=1)


def unfold(parts):
    first, off, last = parts[:, 0], parts[:, 1], parts[:, 2]
    upper = jnp.concatenate([first, off], axis=2)
    lower = jnp.concatenate([jnp.swapaxes(off, 1, 2), last], axis=2)
    return jnp.concatenate([upper, lower], axis=1)


def gram_sums(ring, parts, cap):
    h = parts.shape[2]
    parts = parts.reshape(-1, h, h)
    rows = 3 * cap
    mine = yield from ring.scatter(lambda i: lax.dynamic_slice_in_dim(parts, i * rows, rows, 0), rows // 2)
    return unfold(mine.reshape(cap, 3, h, h))


def all_factors(ring, factors):
    cap, c, _ = factors.shape
    parts = fold(factors.astype(BF16)).reshape(3 * cap, c // 2, c // 2)
    parts = yield from ring.gather(parts, 3 * cap // 2)
    return parts.reshape(ring.size * cap, 3, c // 2, c // 2)


def on_device(block_in, cotangent, seq_ids, weights, momentum, gains, gain_first, gain_second):
    tok_rows, model_width = block_in.shape
    rows_dp, group_blocks, head_dim = weights.shape
    head_count = lax.axis_size("head")
    data_count = lax.axis_size("dp")
    group_rows = tok_rows * head_count
    key_heads = KV // head_count
    query_heads = H // head_count
    ffn_blocks = FF // (head_dim * head_count)
    out_mark = query_heads + 2 * key_heads
    gate_mark = out_mark + query_heads
    half_dim = head_dim // 2
    full = ffn_blocks // 2
    scale = head_dim ** (-0.5)
    growth = math.sqrt(max(1.0, model_width / head_dim))
    data_index = lax.axis_index("dp")
    head_index = lax.axis_index("head")
    parity = (data_index >> 2) & 1
    ring = Ring()

    weights = jnp.transpose(weights, (1, 0, 2))
    momentum = jnp.transpose(momentum, (1, 0, 2))
    attn_low = cast_blocks(weights, gate_mark)
    inputs = block_in.astype(F32)
    normed_one, norm_one_back = jax.vjp(rms_scale, inputs, gains[0])
    ids_column = jnp.pad(seq_ids.astype(BF16)[:, None], ((0, 0), (0, 127)))

    early = full - 1
    mine_early, mine_late, other_early, other_late = pack_units(
        jnp.reshape(parity, (1,)), weights, gate_mark, ffn_blocks, early
    )
    spread = [Spread(mine_early, other_early), Spread(mine_late, other_late)]

    group_in = run(head_gather(jnp.concatenate([normed_one.astype(BF16), ids_column], axis=1)))
    qkv_parts = run(ring.gather(attn_low[:out_mark], out_mark // 2))
    qkv_blocks = jnp.transpose(qkv_parts, (1, 0, 2, 3)).reshape(out_mark, model_width, head_dim)
    cot_flow = Flow(wide_gather(cotangent))
    group_in, qkv_blocks, attn_low = stage(
        [spread[0].near(0), spread[0].y(0)], [group_in, qkv_blocks, attn_low], idle=[cot_flow]
    )
    projected = block_project(group_in, qkv_blocks)
    queries = projected[:query_heads].reshape(query_heads * group_rows, head_dim)
    group_ids = group_in[:, model_width]
    kv_rows = 2 * key_heads * group_rows
    out_rows = query_heads * rows_dp
    id_rows = group_rows // head_dim
    packed = jnp.concatenate(
        [
            projected[query_heads:].reshape(kv_rows, head_dim),
            attn_low[out_mark:].reshape(out_rows, head_dim),
            jnp.pad(group_ids.reshape(id_rows, head_dim), ((0, 16 - id_rows), (0, 0))),
        ],
        axis=0,
    )
    keys_values = run(ring.gather(packed, packed.shape[0] // 32 * 16))
    out_blocks = keys_values[:, kv_rows : kv_rows + out_rows].reshape(data_count, query_heads, rows_dp, head_dim)
    out_blocks = jnp.transpose(out_blocks, (1, 0, 2, 3)).reshape(query_heads, model_width, head_dim)
    queries, keys_values, out_blocks = stage(
        [cot_flow, spread[1].near(0)], [queries, keys_values, out_blocks]
    )
    all_ids = keys_values[:, kv_rows + out_rows : kv_rows + out_rows + id_rows].reshape(-1)

    local = in_group(jnp.arange(group_rows, dtype=jnp.int32), group_rows, head_index * tok_rows)
    query_pos = data_index * group_rows + local
    first_pos = jnp.sum((all_ids[None, :] < group_ids[:, None]).astype(jnp.int32), axis=1)
    query_pos = jnp.tile(query_pos, query_heads)
    first_pos = jnp.tile(first_pos, query_heads)
    place = jnp.stack([data_index, head_index * tok_rows]).astype(jnp.int32)
    mixed_low, mixed_full, totals = attend(
        place, queries, keys_values, query_pos[:, None], first_pos[:, None], scale, group_rows
    )
    mixed_heads = mixed_low.reshape(query_heads, group_rows, head_dim)
    mixed_heads, mixed_full, totals, attn_part = stage(
        [spread[0].cross(), spread[0].y(1), spread[1].y(0), cot_flow],
        [mixed_heads, mixed_full, totals, block_back(mixed_heads, out_blocks)],
    )
    attn_flow = Flow(scatter_rows(*attn_part, HEAD_MOVES))
    stage([attn_flow], idle=[cot_flow])
    stage([attn_flow, spread[0].near(3), spread[0].y(3), spread[1].cross(), spread[1].y(1)], idle=[cot_flow])
    residual = inputs + attn_flow.value
    normed_two, norm_two_back = jax.vjp(rms_scale, residual, gains[1])
    wide_flow = Flow(wide_gather(normed_two.astype(BF16)))
    stage([wide_flow, spread[0].y(2), spread[1].near(3), spread[1].y(3)], idle=[cot_flow])
    stage([wide_flow, spread[1].y(2), cot_flow])
    stage([wide_flow])
    finish(wide_flow, cot_flow)

    def whole_rows(pieces):
        if rows_dp % 16 == 0:
            return pieces
        out = jnp.zeros((3, data_count) + pieces[0].shape[1:], BF16)
        for k, piece in enumerate(pieces):
            out = lax.dynamic_update_index_in_dim(out, piece, data_index ^ k, 1)
        return [out.reshape(3, model_width, -1)]

    ffn_sides, ffn_full, *ffn_grads = ffn_front(
        place, wide_flow.value, cot_flow.value, whole_rows(spread[0].value()), whole_rows(spread[1].value())
    )

    def taker(pieces):
        if len(pieces) > 1:
            return lambda k: pieces[k]
        cut = pieces[0].reshape(3, data_count, rows_dp, pieces[0].shape[2])
        return lambda k: lax.dynamic_index_in_dim(cut, data_index ^ k, 1, keepdims=False)

    pieces = len(ffn_grads) // 2
    reduce = [Reduce(taker(ffn_grads[:pieces])), Reduce(taker(ffn_grads[pieces:]))]
    *down_part, dx_kept, dx_sent = stage([reduce[0].y(2)], ffn_back(ffn_sides, ffn_full))
    out_flow = Flow(scatter_rows(*down_part, WIDE_MOVES))
    dx_flow = Flow(scatter_rows(dx_kept, dx_sent, WIDE_MOVES))
    dx_flow.advance([lax.ppermute(*send) for send in dx_flow.sends])
    stage([dx_flow, reduce[0].near(2), reduce[0].y(1), reduce[1].y(2)])
    stage([dx_flow, reduce[0].near(1), reduce[0].y(3), out_flow])
    grad_residual_norm, grad_gain_two = norm_two_back(dx_flow.value)
    grad_residual = cotangent.astype(F32) + grad_residual_norm
    grad_flow = Flow(head_gather(grad_residual.astype(BF16)))
    stage([grad_flow, reduce[1].near(2), reduce[1].y(1), reduce[1].y(3)])
    grad_flow.advance([lax.ppermute(*send) for send in grad_flow.sends])
    group_grad = grad_flow.value

    grad_heads = block_project(group_grad, out_blocks)
    grad_mixed = grad_heads.reshape(query_heads * group_rows, head_dim)
    delta = jnp.sum(grad_mixed.astype(F32) * mixed_full, axis=1)
    grad_queries, grad_keys_values = attend_back(
        place,
        queries,
        grad_mixed,
        keys_values,
        1.0 / totals.reshape(1, -1),
        delta[None, :],
        query_pos[None, :],
        first_pos[None, :],
        scale,
        group_rows,
    )
    group_grad, grad_queries, grad_keys_values = stage(
        [reduce[0].cross(), reduce[1].near(1), reduce[0].y(0), reduce[1].y(0), out_flow],
        [group_grad, grad_queries, grad_keys_values],
    )
    grad_queries = grad_queries.reshape(query_heads, group_rows, head_dim)

    late = 2
    main = 3 * ffn_blocks - late
    cap = -(-main // data_count)
    places = -(-max(cap * data_count, 3 * ffn_blocks) // TRIO) * TRIO
    def weight_sums(outer):
        cut = outer.reshape(outer.shape[0], data_count, rows_dp, head_dim)
        return Flow(ring.scatter(lambda i: lax.dynamic_index_in_dim(cut, i, 1, keepdims=False), outer.shape[0] // 2))

    key_flow = Flow(
        ring.scatter(lambda i: lax.dynamic_index_in_dim(grad_keys_values, i, 0, keepdims=False), key_heads)
    )
    pick = lambda own, other: (jnp.where(parity == 1, other, own), jnp.where(parity == 1, own, other))
    low_early, high_early = pick(*reduce[0].value())
    outer, low_early, high_early = stage(
        [key_flow, reduce[1].cross(), out_flow],
        [block_outer([group_in, group_grad], [grad_queries, mixed_heads], model_width), low_early, high_early],
    )
    low_late, high_late = pick(*reduce[1].value())
    block_out = (residual + out_flow.value).astype(BF16)
    first_flow = weight_sums(outer)
    weight_grads, new_momentum, grams = stage(
        [key_flow, first_flow],
        ffn_moment(low_early, low_late, high_early, high_late, momentum, gate_mark, ffn_blocks, places),
    )
    gram_flow = Flow(gram_sums(ring, grams, cap))
    stage([key_flow, first_flow, gram_flow])
    while key_flow.sends is not None:
        stage([key_flow, first_flow, gram_flow])
    key_value_sums = key_flow.value
    grad_keys = (key_value_sums[:key_heads] * scale).astype(BF16)
    grad_values = key_value_sums[key_heads:].astype(BF16)
    grad_keys_values = jnp.concatenate([grad_keys, grad_values], axis=0)
    (outer,) = stage([first_flow, gram_flow], [block_outer([group_in], [grad_keys_values], model_width)])
    finish(first_flow)
    second_flow = weight_sums(outer)
    pairs = [k for k in range(gate_mark // 2) if not query_heads <= 2 * k < out_mark]
    grad_projected = jnp.concatenate([grad_queries, grad_keys_values], axis=0)
    *attn_dx, weight_grads, new_momentum, first_grams = stage(
        [second_flow, gram_flow],
        [
            *block_back(grad_projected, qkv_blocks),
            *attn_moment(first_flow.value, pairs, momentum, weight_grads, new_momentum),
        ],
    )
    last_flow = Flow(scatter_rows(*attn_dx, HEAD_MOVES))
    while second_flow.sends is not None:
        stage([second_flow, gram_flow, last_flow])
    finish(last_flow, gram_flow)
    grad_input_norm, grad_gain_one = norm_one_back(last_flow.value)
    grad_input = grad_residual + grad_input_norm
    gain_flow = Flow(total_sum(jnp.stack([grad_gain_one, grad_gain_two])))
    weight_grads, new_momentum, second_grams = attn_moment(
        second_flow.value, list(range(query_heads // 2, out_mark // 2)), momentum, weight_grads, new_momentum
    )
    late_count = gate_mark + late
    late_cap = -(-late_count // data_count)
    late_grams = jnp.concatenate([first_grams, second_grams, grams[main : main + late]], axis=0)
    late_grams = jnp.pad(late_grams, ((0, late_cap * data_count - late_count), (0, 0), (0, 0), (0, 0)))
    factors = newton_factor(gram_flow.value, growth)
    factors = run(all_factors(ring, factors))

    threes = main // TRIO
    early_spots = [(gate_mark // TRIO + k, [TRIO * k + i for i in range(TRIO)]) for k in range(threes)]
    new_weights = []
    for k in range(0, threes, 2):
        new_weights = [renew(weights, new_momentum, factors, early_spots[k : k + 2], new_weights)]
    late_sums, factors, *new_weights = stage(
        [gain_flow], [run(gram_sums(ring, late_grams, late_cap)), factors, *new_weights]
    )
    (late_factors,) = stage([gain_flow], [newton_factor(late_sums, growth)])
    late_factor_flow = Flow(all_factors(ring, late_factors))

    finish(late_factor_flow, gain_flow)
    gain_grads = gain_flow.value
    rest = jnp.concatenate([late_factor_flow.value[:late_count], factors[TRIO * threes : main]], axis=0)
    blocks_of = [2 * pair + i for pair in pairs for i in range(2)] + list(range(query_heads, out_mark))
    blocks_of += [gate_mark + main + k for k in range(late)] + [gate_mark + k for k in range(TRIO * threes, main)]
    late_spots = [
        (spot, [blocks_of.index(TRIO * spot + i) for i in range(TRIO)])
        for spot in sorted({block // TRIO for block in blocks_of})
    ]
    new_weights = renew(weights, new_momentum, rest, late_spots, new_weights)

    new_gain_first = BETA_ONE * gain_first + (1.0 - BETA_ONE) * gain_grads
    new_gain_second = BETA_TWO * gain_second + (1.0 - BETA_TWO) * gain_grads * gain_grads
    first_hat = new_gain_first / (1.0 - BETA_ONE**UPDATE_STEP)
    second_hat = new_gain_second / (1.0 - BETA_TWO**UPDATE_STEP)
    new_gains = gains - ADAM_RATE * first_hat / (jnp.sqrt(second_hat) + ADAM_EPS)
    back = lambda array: jnp.transpose(array, (1, 0, 2))
    return (
        block_out,
        grad_input,
        back(weight_grads),
        back(new_momentum),
        back(new_weights),
        gain_grads,
        new_gain_first,
        new_gain_second,
        new_gains,
    )


def solution(mesh):
    return jax.shard_map(
        on_device,
        mesh=mesh,
        in_specs=(
            P(("dp", "head"), None),
            P(("dp", "head"), None),
            P(("dp", "head")),
            P("dp", "head", None),
            P("dp", "head", None),
            P(),
            P(),
            P(),
        ),
        out_specs=(
            P(("dp", "head"), None),
            P(("dp", "head"), None),
            P("dp", "head", None),
            P("dp", "head", None),
            P("dp", "head", None),
            P(),
            P(),
            P(),
            P(),
        ),
        check_vma=False,
    )
```

```python
import functools
import math

import jax
import jax.numpy as jnp
from jax import lax
from jax.experimental import pallas as pl
from jax.experimental.pallas import tpu as pltpu
from jax.sharding import PartitionSpec as P

H = 8
KV = 4
FF = 9216
NEWTON_STEPS = 5
UPDATE_STEP = 10

NORM_EPS = 1e-06
SOFT_CAP = 50.0
MUON_RATE = 0.2
MUON_DECAY = 0.01
MUON_BETA = 0.95
ADAM_RATE = 0.3
BETA_ONE = 0.9
BETA_TWO = 0.95
ADAM_EPS = 1e-08
NEWTON_LINEAR = 3.4445
NEWTON_SQUARE = -4.775
NEWTON_CUBIC = 2.0315
TOP_PRECISION = lax.Precision.HIGHEST

BF16 = jnp.bfloat16
F32 = jnp.float32
VMEM_LIMIT = 62 * 1024 * 1024
NN = (((1,), (0,)), ((), ()))
NT = (((1,), (1,)), ((), ()))
TN = (((0,), (0,)), ((), ()))


def mm(a, b, dims):
    return lax.dot_general(a, b, dims, preferred_element_type=F32)


def rms_scale(rows, gain):
    inverse = lax.rsqrt(jnp.mean(rows * rows, axis=-1, keepdims=True) + NORM_EPS)
    return rows * inverse * gain


class Flow:
    def __init__(self, steps):
        self.steps = steps
        self.value = None
        self.sends = None
        self.advance(None)

    def advance(self, arrived):
        try:
            self.sends = self.steps.send(arrived)
        except StopIteration as stop:
            self.sends = None
            self.value = stop.value


def stage(flows, extra=(), idle=()):
    flows = [flow for flow in flows if flow.sends is not None]
    idle = [flow for flow in idle if flow.sends is not None and flow not in flows]
    arrived = [[lax.ppermute(*send) for send in flow.sends] for flow in flows]
    held = [[send[0] for send in flow.sends] for flow in idle]
    arrived, held, extra = lax.optimization_barrier((arrived, held, list(extra)))
    for flow, got in zip(flows, arrived):
        flow.advance(got)
    for flow, kept in zip(idle, held):
        flow.sends = [(value,) + send[1:] for value, send in zip(kept, flow.sends)]
    return extra


def run(steps):
    flow = Flow(steps)
    while flow.sends is not None:
        flow.advance([lax.ppermute(*send) for send in flow.sends])
    return flow.value


def finish(*flows):
    while any(flow.sends is not None for flow in flows):
        stage(flows)


def swap(value, axis, mask):
    size = lax.axis_size(axis)
    return (value, axis, [(i, i ^ mask) for i in range(size)])


def head_gather(rows):
    (other,) = yield [swap(rows, "head", 2)]
    pair = jnp.concatenate([rows, other], axis=0)
    (other,) = yield [swap(pair, "head", 1)]
    return jnp.concatenate([pair, other], axis=0)


def wide_gather(rows):
    (other,) = yield [swap(rows, "dp", 4)]
    both = jnp.concatenate([rows, other], axis=0)
    (other,) = yield [swap(both, "head", 2)]
    pair = jnp.concatenate([both, other], axis=0)
    (other,) = yield [swap(pair, "head", 1)]
    return [pair, other]


def add_low(kept, other):
    return (kept.astype(F32) + other.astype(F32)).astype(BF16)


def scatter_rows(kept, sent, moves):
    for k, (axis, mask) in enumerate(moves):
        (other,) = yield [swap(sent, axis, mask)]
        part = kept.astype(F32) + other.astype(F32)
        if k < len(moves) - 1:
            half = part.shape[0] // 2
            kept, sent = part[:half], part[half:].astype(BF16)
    return part


HEAD_MOVES = (("head", 1), ("head", 2))
WIDE_MOVES = (("head", 1), ("head", 2), ("dp", 4))


def total_sum(value):
    for axis in ("head", "dp"):
        mask = 1
        while mask < lax.axis_size(axis):
            (other,) = yield [swap(value, axis, mask)]
            value = value + other
            mask *= 2
    return value


class Ring:
    def __init__(self):
        size = lax.axis_size("dp")
        order = list(range(0, size, 2)) + list(range(size - 1, 0, -2))
        around = [[order[(order.index(i) + offset) % size] for offset in range(size)] for i in range(size)]
        self.size = size
        self.around = jnp.array(around, jnp.int32)[lax.axis_index("dp")]
        self.up = [(order[k], order[(k + 1) % size]) for k in range(size)]
        self.down = [(order[(k + 1) % size], order[k]) for k in range(size)]

    def index(self, offset):
        return self.around[offset % self.size]

    def gather(self, value, mid):
        half = self.size // 2
        zeros = (0,) * (value.ndim - 1)
        out = jnp.zeros((self.size,) + value.shape, value.dtype)
        out = lax.dynamic_update_index_in_dim(out, value, self.index(0), 0)
        ahead, back = value, value
        for step in range(1, half):
            ahead, back = yield [(ahead, "dp", self.up), (back, "dp", self.down)]
            out = lax.dynamic_update_index_in_dim(out, ahead, self.index(-step), 0)
            out = lax.dynamic_update_index_in_dim(out, back, self.index(step), 0)
        first, second = yield [(ahead[:mid], "dp", self.up), (back[mid:], "dp", self.down)]
        far = self.index(half)
        out = lax.dynamic_update_slice(out, first[None], (far, 0) + zeros)
        return lax.dynamic_update_slice(out, second[None], (far, mid) + zeros)

    def scatter(self, take, mid):
        half = self.size // 2
        far = take(self.index(half))
        kind = far.dtype
        up, down = yield [(far[:mid], "dp", self.up), (far[mid:], "dp", self.down)]
        for step in range(half - 1, 0, -1):
            part = take(self.index(step)).astype(F32)
            ahead = jnp.concatenate([part[:mid] + up, part[mid:]]) if step == half - 1 else part + up
            part = take(self.index(-step)).astype(F32)
            back = jnp.concatenate([part[:mid], part[mid:] + down]) if step == half - 1 else part + down
            up, down = yield [(ahead.astype(kind), "dp", self.up), (back.astype(kind), "dp", self.down)]
        return take(self.index(0)).astype(F32) + up.astype(F32) + down.astype(F32)


def once(sends, take):
    def steps():
        take((yield sends))

    return Flow(steps())


SIDE_BIT = 2


def plane_classes():
    planes = range(lax.axis_size("dp") // 2)
    kept = [m for m in planes if m & 3 in (0, 3)]
    passed = [m for m in planes if m & 3 in (1, 2)]
    return {0: [0], 1: [1], 2: [m for m in passed if m != 1], 3: [m for m in kept if m]}


class Spread:
    def __init__(self, mine, other):
        self.mine, self.other = mine, other
        self.pieces = {0: mine}

    def move(self, moves):
        def take(arrived):
            for (_, _, _, number), piece in zip(moves, arrived):
                self.pieces[number] = piece

        return once([swap(value, "dp", offset << 1 | bit) for value, offset, bit, _ in moves], take)

    def cross(self):
        group = plane_classes()[3]
        return self.move([(self.other if m & SIDE_BIT else self.mine, m, 0, m << 1) for m in group])

    def near(self, key):
        group = plane_classes()[key]
        return self.move([(self.pieces[m << 1], 1, 0, (m ^ 1) << 1) for m in group])

    def y(self, key):
        group = plane_classes()[key]
        return self.move([(self.pieces[m << 1], 0, 1, m << 1 | 1) for m in group])

    def value(self):
        return [self.pieces[k] for k in range(lax.axis_size("dp"))]


class Reduce:
    def __init__(self, rows):
        self.rows = rows
        self.parts = {}
        self.sums = [None, None]

    def part(self, offset):
        terms = [term.astype(F32) for term in self.parts[offset]]
        return functools.reduce(jnp.add, terms)

    def hold(self, offset, *terms):
        self.parts.setdefault(offset, []).extend(terms)

    def y(self, key):
        group = plane_classes()[key]

        def take(arrived):
            for offset, got in zip(group, arrived):
                self.hold(offset, self.rows(offset << 1), got)

        return once([swap(self.rows(offset << 1 | 1), "dp", 1) for offset in group], take)

    def near(self, key):
        group = plane_classes()[key]

        def take(arrived):
            for offset, got in zip(group, arrived):
                self.hold(offset ^ 1, got)

        return once([swap(self.part(offset).astype(BF16), "dp", 2) for offset in group], take)

    def cross(self):
        group = plane_classes()[3]

        def take(arrived):
            for offset, got in zip(group, arrived):
                self.add(1 if offset & SIDE_BIT else 0, got.astype(F32))

        return once([swap(self.part(offset).astype(BF16), "dp", offset << 1) for offset in group], take)

    def add(self, side, value):
        self.sums[side] = value if self.sums[side] is None else self.sums[side] + value

    def value(self):
        self.add(0, self.part(0))
        return self.sums


def params(**more):
    return pltpu.CompilerParams(vmem_limit_bytes=VMEM_LIMIT, **more)


TRIO = 3


def cast_blocks(blocks, count):
    _, r, c = blocks.shape

    def body(x_ref, o_ref):
        o_ref[...] = x_ref[...].astype(BF16)

    spec = pl.BlockSpec((TRIO, r, c), lambda k: (k, 0, 0))
    return pl.pallas_call(
        body,
        grid=(count // TRIO,),
        in_specs=[spec],
        out_specs=spec,
        out_shape=jax.ShapeDtypeStruct((count, r, c), BF16),
        compiler_params=params(),
        cost_estimate=pl.CostEstimate(flops=0, bytes_accessed=6 * count * r * c, transcendentals=0),
    )(blocks)


def pack_units(parity, blocks, first, kind_blocks, early):
    _, r, c = blocks.shape
    h = c // 2
    full = kind_blocks // 2
    each = kind_blocks // TRIO
    u, v = early * c, (full - early) * c + h

    def body(s_ref, *refs):
        parts, outs = refs[:each], refs[each:]

        def tile(f):
            return parts[f // TRIO].at[f % TRIO]

        for turn in range(2):

            @pl.when(s_ref[0] == turn)
            def _():
                for k in range(2):
                    side = turn ^ k
                    for i in range(full):
                        value = tile(side * full + i)[...].astype(BF16)
                        if i < early:
                            outs[2 * k][:, i * c : (i + 1) * c] = value
                        else:
                            outs[2 * k + 1][:, (i - early) * c : (i - early + 1) * c] = value
                    rest = tile(2 * full)[:, side * h : (side + 1) * h]
                    outs[2 * k + 1][:, v - h :] = rest.astype(BF16)

    def part(i):
        return pl.BlockSpec((TRIO, r, c), lambda k, s: (first // TRIO + each * k + i, 0, 0))

    wide = pl.BlockSpec((None, r, u), lambda k, s: (k, 0, 0))
    slim = pl.BlockSpec((None, r, v), lambda k, s: (k, 0, 0))
    shapes = [jax.ShapeDtypeStruct((3, r, u), BF16), jax.ShapeDtypeStruct((3, r, v), BF16)]
    return pl.pallas_call(
        body,
        grid_spec=pltpu.PrefetchScalarGridSpec(
            num_scalar_prefetch=1,
            grid=(3,),
            in_specs=[part(i) for i in range(each)],
            out_specs=[wide, slim, wide, slim],
        ),
        out_shape=shapes + shapes,
        compiler_params=params(),
        cost_estimate=pl.CostEstimate(flops=0, bytes_accessed=18 * kind_blocks * r * c, transcendentals=0),
    )(parity, *([blocks] * each))


def block_project(rows, blocks):
    t = rows.shape[0]
    count, d, c = blocks.shape

    def body(x_ref, w_ref, o_ref):
        o_ref[...] = mm(x_ref[...], w_ref[...], NN).astype(BF16)

    return pl.pallas_call(
        body,
        grid=(count,),
        in_specs=[
            pl.BlockSpec((t, d), lambda b: (0, 0)),
            pl.BlockSpec((None, d, c), lambda b: (b, 0, 0)),
        ],
        out_specs=pl.BlockSpec((None, t, c), lambda b: (b, 0, 0)),
        out_shape=jax.ShapeDtypeStruct((count, t, c), BF16),
        compiler_params=params(),
        cost_estimate=pl.CostEstimate(
            flops=2 * count * t * d * c, bytes_accessed=2 * (t * d + count * (d * c + t * c)), transcendentals=0
        ),
    )(rows, blocks)


def block_back(cols, blocks):
    count, t, c = cols.shape
    d = blocks.shape[1]
    half = t // 2

    def body(x_ref, w_ref, o_ref, p_ref, acc_ref):
        b = pl.program_id(0)

        @pl.when(b == 0)
        def _():
            acc_ref[...] = jnp.zeros_like(acc_ref)

        acc_ref[...] += mm(x_ref[...], w_ref[...], NT)

        @pl.when(b == count - 1)
        def _():
            o_ref[...] = acc_ref[:half, :].astype(BF16)
            p_ref[...] = acc_ref[half:, :].astype(BF16)

    result = pl.BlockSpec((half, d), lambda b: (0, 0))
    return pl.pallas_call(
        body,
        grid=(count,),
        in_specs=[
            pl.BlockSpec((None, t, c), lambda b: (b, 0, 0)),
            pl.BlockSpec((None, d, c), lambda b: (b, 0, 0)),
        ],
        out_specs=[result, result],
        out_shape=[jax.ShapeDtypeStruct((half, d), BF16)] * 2,
        scratch_shapes=[pltpu.VMEM((t, d), F32)],
        compiler_params=params(),
        cost_estimate=pl.CostEstimate(
            flops=2 * count * t * d * c, bytes_accessed=2 * (t * d + count * (d * c + t * c)), transcendentals=0
        ),
    )(cols, blocks)


def block_outer(rows, cols, d):
    t = rows[0].shape[0]
    c = cols[0].shape[2]
    starts = [0]
    for col in cols:
        starts.append(starts[-1] + col.shape[0])
    count = len(rows)
    total = starts[-1]

    def body(*refs):
        o_ref, t_ref = refs[2 * count :]
        b = pl.program_id(0)
        for k in range(count):

            @pl.when(b == starts[k])
            def _():
                t_ref[...] = refs[k][...].T

            @pl.when((b >= starts[k]) & (b < starts[k + 1]))
            def _():
                o_ref[...] = mm(t_ref[...], refs[count + k][...], NN).astype(BF16)

    def col_at(k):
        return pl.BlockSpec((None, t, c), lambda b: (jnp.clip(b - starts[k], 0, starts[k + 1] - starts[k] - 1), 0, 0))

    return pl.pallas_call(
        body,
        grid=(total,),
        in_specs=[pl.BlockSpec((t, d), lambda b: (0, 0))] * count + [col_at(k) for k in range(count)],
        out_specs=pl.BlockSpec((None, d, c), lambda b: (b, 0, 0)),
        out_shape=jax.ShapeDtypeStruct((total, d, c), BF16),
        scratch_shapes=[pltpu.VMEM((d, t), BF16)],
        compiler_params=params(),
        cost_estimate=pl.CostEstimate(
            flops=2 * total * t * d * c,
            bytes_accessed=2 * (count * t * d + total * (d * c + t * c)),
            transcendentals=0,
        ),
    )(*rows, *cols)


def in_group(local, width, head_shift):
    quarter = width // 4
    low = jnp.bitwise_and(local, quarter - 1)
    one = jnp.where(jnp.bitwise_and(local, quarter) != 0, 2 * quarter, 0)
    two = jnp.where(jnp.bitwise_and(local, 2 * quarter) != 0, quarter, 0)
    return jnp.bitwise_xor(low + one + two, head_shift)


def key_position(block, width, head_shift, shape, axis):
    local = lax.broadcasted_iota(jnp.int32, shape, axis)
    return block * width + in_group(local, width, head_shift)


def attend(place, queries, keys_values, query_pos, first_pos, scale, p):
    m, e = queries.shape
    n = keys_values.shape[0]
    step = 256

    def body(place_ref, q_ref, kv_ref, pos_ref, first_ref, low_ref, full_ref, sum_ref, acc_ref, tot_ref):
        j = pl.program_id(0)

        @pl.when(j == 0)
        def _():
            acc_ref[...] = jnp.zeros_like(acc_ref)
            tot_ref[...] = jnp.zeros_like(tot_ref)

        @pl.when(j <= place_ref[0])
        def _():
            key_pos = key_position(j, p, place_ref[1], (1, p), 1)
            for r in range(0, m, step):
                rows = pl.ds(r, step)
                raw = mm(q_ref[rows, :], kv_ref[:p, :], NT)
                soft = SOFT_CAP * jnp.tanh(raw * (scale / SOFT_CAP))
                seen = (key_pos >= first_ref[rows, :]) & (key_pos <= pos_ref[rows, :])
                terms = jnp.where(seen, jnp.exp(soft), 0.0)
                tot_ref[rows, :] += jnp.sum(terms, axis=1, keepdims=True)
                acc_ref[rows, :] += mm(terms.astype(BF16), kv_ref[p:, :], NN)

        @pl.when(j == n - 1)
        def _():
            total = tot_ref[...]
            mixed = acc_ref[...] / total
            full_ref[...] = mixed
            low_ref[...] = mixed.astype(BF16)
            sum_ref[...] = total

    whole = lambda shape: pl.BlockSpec(shape, lambda j, s: (0, 0))
    return pl.pallas_call(
        body,
        grid_spec=pltpu.PrefetchScalarGridSpec(
            num_scalar_prefetch=1,
            grid=(n,),
            in_specs=[
                whole((m, e)),
                pl.BlockSpec((None, 2 * p, e), lambda j, s: (jnp.minimum(j, s[0]), 0, 0)),
                whole((m, 1)),
                whole((m, 1)),
            ],
            out_specs=[whole((m, e)), whole((m, e)), whole((m, 1))],
            scratch_shapes=[pltpu.VMEM((m, e), F32), pltpu.VMEM((m, 1), F32)],
        ),
        out_shape=[
            jax.ShapeDtypeStruct((m, e), BF16),
            jax.ShapeDtypeStruct((m, e), F32),
            jax.ShapeDtypeStruct((m, 1), F32),
        ],
        compiler_params=params(),
        cost_estimate=pl.CostEstimate(
            flops=4 * m * n * p * e, bytes_accessed=4 * n * p * e, transcendentals=2 * m * n * p
        ),
    )(place, queries, keys_values, query_pos, first_pos)


def attend_back(place, queries, grads, keys_values, inverse, delta, query_pos, first_pos, scale, p):
    m, e = queries.shape
    n = keys_values.shape[0]
    step = 256

    def body(
        place_ref, q_ref, g_ref, kv_ref, inv_ref, delta_ref, pos_ref, first_ref, dq_ref, dkv_ref, acc_ref, dk_ref, dv_ref
    ):
        j = pl.program_id(0)

        @pl.when(j == 0)
        def _():
            acc_ref[...] = jnp.zeros_like(acc_ref)

        @pl.when(j <= place_ref[0])
        def _():
            key_pos = key_position(j, p, place_ref[1], (p, 1), 0)
            for r in range(0, m, step):
                rows = pl.ds(r, step)
                raw = mm(kv_ref[:p, :], q_ref[rows, :], NT)
                capped = jnp.tanh(raw * (scale / SOFT_CAP))
                seen = (key_pos >= first_ref[:, rows]) & (key_pos <= pos_ref[:, rows])
                probs = jnp.where(seen, jnp.exp(SOFT_CAP * capped), 0.0) * inv_ref[:, rows]
                grad_probs = mm(kv_ref[p:, :], g_ref[rows, :], NT)
                grad_raw = probs * (grad_probs - delta_ref[:, rows]) * (1.0 - capped * capped)
                grad_low = grad_raw.astype(BF16)
                value_part = mm(probs.astype(BF16), g_ref[rows, :], NN)
                key_part = mm(grad_low, q_ref[rows, :], NN)
                if r == 0:
                    dv_ref[...] = value_part
                    dk_ref[...] = key_part
                else:
                    dv_ref[...] += value_part
                    dk_ref[...] += key_part
                acc_ref[rows, :] += mm(grad_low, kv_ref[:p, :], TN)
            dkv_ref[0] = dk_ref[...].astype(BF16)
            dkv_ref[1] = dv_ref[...].astype(BF16)

        @pl.when(j > place_ref[0])
        def _():
            dkv_ref[...] = jnp.zeros_like(dkv_ref)

        @pl.when(j == n - 1)
        def _():
            dq_ref[...] = (acc_ref[...] * scale).astype(BF16)

    whole = lambda shape: pl.BlockSpec(shape, lambda j, s: (0, 0))
    return pl.pallas_call(
        body,
        grid_spec=pltpu.PrefetchScalarGridSpec(
            num_scalar_prefetch=1,
            grid=(n,),
            in_specs=[
                whole((m, e)),
                whole((m, e)),
                pl.BlockSpec((None, 2 * p, e), lambda j, s: (jnp.minimum(j, s[0]), 0, 0)),
                whole((1, m)),
                whole((1, m)),
                whole((1, m)),
                whole((1, m)),
            ],
            out_specs=[whole((m, e)), pl.BlockSpec((None, 2, p, e), lambda j, s: (j, 0, 0, 0))],
            scratch_shapes=[pltpu.VMEM((m, e), F32), pltpu.VMEM((p, e), F32), pltpu.VMEM((p, e), F32)],
        ),
        out_shape=[jax.ShapeDtypeStruct((m, e), BF16), jax.ShapeDtypeStruct((n, 2, p, e), BF16)],
        compiler_params=params(),
        cost_estimate=pl.CostEstimate(
            flops=10 * m * n * p * e, bytes_accessed=8 * n * p * e, transcendentals=2 * m * n * p
        ),
    )(place, queries, grads, keys_values, inverse, delta, query_pos, first_pos)


def gelu_pair(gate):
    outer = math.sqrt(2.0 / math.pi)
    square = gate * gate
    bent = jnp.tanh(outer * gate * (1.0 + 0.044715 * square))
    half = 0.5 * (1.0 + bent)
    slope = half + 0.5 * gate * (1.0 - bent * bent) * outer * (1.0 + 3.0 * 0.044715 * square)
    return gate * half, slope


def ffn_front(place, rows, cots, early, late):
    part_rows, d = rows[0].shape
    t = 2 * part_rows
    count = len(early)
    r = early[0].shape[1]
    u, v = early[0].shape[2], late[0].shape[2]
    tall = min(512, t)
    wide = d // 3
    cuts = [(k, min(256, u + v - k)) for k in range(0, u + v, 256)]

    def body(place_ref, x0, x1, y0, y1, *refs):
        early_refs, late_refs = refs[:count], refs[count : 2 * count]
        refs = refs[2 * count :]
        hs_ref, w_out = refs[:2]
        grad_refs = refs[2 : 2 + count], refs[2 + count : 2 + 2 * count]
        x, y, w, xt, yt, hs, row_sems, sems, out_sems, grad_sems = refs[2 + 2 * count :]
        row_copies = []
        for k, (source, target) in enumerate(((x0, x), (x1, x), (y0, y), (y1, y))):
            target = target.at[pl.ds((k % 2) * part_rows, part_rows), :]
            row_copies.append(pltpu.make_async_copy(source, target, row_sems.at[k]))
            row_copies[k].start()
        copies = []
        chunks = ((early_refs, pl.ds(0, u)), (late_refs, pl.ds(u, v)))

        def spot(k):
            return pl.ds(pl.multiple_of(jnp.bitwise_xor(place_ref[0], k) * r, 16) if count > 1 else 0, r)

        for k in range(count):
            for way, (sources, lanes) in enumerate(chunks):
                copy = pltpu.make_async_copy(sources[k], w.at[:, spot(k), lanes], sems.at[way, k])
                copy.start()
                copies.append(copy)
        for copy in row_copies:
            copy.wait()

        @pl.loop(0, d // 256)
        def _(k):
            cols = pl.ds(pl.multiple_of(k * 256, 256), 256)
            xt[cols, :] = x[:, cols].T
            yt[cols, :] = y[:, cols].T

        for copy in copies:
            copy.wait()
        kept = pltpu.make_async_copy(w, w_out, out_sems.at[0])
        kept.start()

        @pl.loop(0, t // tall)
        def _(i):
            part = pl.ds(pl.multiple_of(i * tall, tall), tall)
            for start, size in cuts:
                units = pl.ds(start, size)
                gate = mm(x[part, :], w[0, :, units], NN)
                up = mm(x[part, :], w[1, :, units], NN)
                grad = mm(y[part, :], w[2, :, units], NN)
                active, slope = gelu_pair(gate)
                hs[0, part, units] = (active * up).astype(BF16)
                hs[1, part, units] = (grad * up * slope).astype(BF16)
                hs[2, part, units] = (grad * active).astype(BF16)

        sides = pltpu.make_async_copy(hs, hs_ref, out_sems.at[1])
        sides.start()
        kept.wait()
        copies = []
        for kind, (left, right) in enumerate(((xt, 1), (xt, 2), (yt, 0))):

            @pl.loop(0, d // wide)
            def _(k):
                cols = pl.ds(pl.multiple_of(k * wide, wide), wide)
                w[kind, cols, :] = mm(left[cols, :], hs[right], NN).astype(BF16)

            for k in range(count):
                for way, (_, lanes) in enumerate(chunks):
                    target = grad_refs[way][k].at[kind]
                    copy = pltpu.make_async_copy(w.at[kind, spot(k), lanes], target, grad_sems.at[kind, way, k])
                    copy.start()
                    copies.append(copy)
        sides.wait()
        for copy in copies:
            copy.wait()

    apart = pl.BlockSpec(memory_space=pl.ANY)
    return pl.pallas_call(
        body,
        grid_spec=pltpu.PrefetchScalarGridSpec(
            num_scalar_prefetch=1,
            grid=(1,),
            in_specs=[apart] * (4 + 2 * count),
            out_specs=[apart] * (2 + 2 * count),
            scratch_shapes=[
                pltpu.VMEM((t, d), BF16),
                pltpu.VMEM((t, d), BF16),
                pltpu.VMEM((3, d, u + v), BF16),
                pltpu.VMEM((d, t), BF16),
                pltpu.VMEM((d, t), BF16),
                pltpu.VMEM((3, t, u + v), BF16),
                pltpu.SemaphoreType.DMA((4,)),
                pltpu.SemaphoreType.DMA((2, count)),
                pltpu.SemaphoreType.DMA((2,)),
                pltpu.SemaphoreType.DMA((3, 2, count)),
            ],
        ),
        out_shape=[
            jax.ShapeDtypeStruct((3, t, u + v), BF16),
            jax.ShapeDtypeStruct((3, d, u + v), BF16),
            *[jax.ShapeDtypeStruct((3, r, u), BF16)] * count,
            *[jax.ShapeDtypeStruct((3, r, v), BF16)] * count,
        ],
        compiler_params=params(),
        cost_estimate=pl.CostEstimate(
            flops=12 * t * d * (u + v), bytes_accessed=12 * d * (u + v) + 4 * t * d, transcendentals=t * (u + v)
        ),
    )(place, *rows, *cots, *early, *late)


def ffn_back(sides, blocks):
    _, t, u = sides.shape
    d = blocks.shape[1]
    wide = 256
    half = t // 2

    def body(s_ref, w_ref, *refs):
        for k in range(2):
            part = pl.ds(k * half, half)
            refs[k][...] = mm(s_ref[0, part, :], w_ref[2], NT).astype(BF16)
            refs[2 + k][...] = (mm(s_ref[1, part, :], w_ref[0], NT) + mm(s_ref[2, part, :], w_ref[1], NT)).astype(BF16)

    return pl.pallas_call(
        body,
        grid=(d // wide,),
        in_specs=[
            pl.BlockSpec((3, t, u), lambda k: (0, 0, 0), pipeline_mode=pl.Buffered(1)),
            pl.BlockSpec((3, wide, u), lambda k: (0, k, 0)),
        ],
        out_specs=[pl.BlockSpec((half, wide), lambda k: (0, k))] * 4,
        out_shape=[jax.ShapeDtypeStruct((half, d), BF16)] * 4,
        compiler_params=params(),
        cost_estimate=pl.CostEstimate(
            flops=6 * t * d * u, bytes_accessed=6 * d * u + 6 * t * u + 4 * t * d, transcendentals=0
        ),
    )(sides, blocks)


def gram_parts(m):
    h = m.shape[1] // 2
    high = m.astype(BF16)
    low = (m - high.astype(F32)).astype(BF16)
    mixed = mm(high, low, TN)
    gram = mm(high, high, TN) + mm(low, low, TN) + mixed + mixed.T
    return gram[:h, :h], gram[:h, h:], gram[h:, h:]


def ffn_moment(low_early, low_late, high_early, high_late, momentum, first, blocks, places):
    total, r, c = momentum.shape
    early = low_early.shape[2] // c
    h = c // 2
    full = early + 1
    each = blocks // TRIO

    def body(le_ref, ll_ref, he_ref, hl_ref, m_ref, wg_ref, nm_ref, gram_ref):
        j = pl.program_id(0)

        @pl.when(j >= TRIO * each)
        def _():
            gram_ref[...] = jnp.zeros_like(gram_ref)

        for turn in range(each):

            @pl.when((j < TRIO * each) & (lax.rem(j, each) == turn))
            def _():
                for i in range(TRIO):
                    side, f = divmod(turn * TRIO + i, full)
                    if side == 2:
                        wg_ref[i, :, :h] = ll_ref[:, c:]
                        wg_ref[i, :, h:] = hl_ref[:, c:]
                    elif f < early:
                        wg_ref[i] = (le_ref, he_ref)[side][:, f * c : (f + 1) * c]
                    else:
                        wg_ref[i] = (ll_ref, hl_ref)[side][:, :c]

        @pl.when(j < TRIO * each)
        def _():
            for i in range(TRIO):
                new = MUON_BETA * m_ref[i] + wg_ref[i]
                nm_ref[i] = new
                gram_ref[i, 0], gram_ref[i, 1], gram_ref[i, 2] = gram_parts(new)

    kind = lambda j: (jnp.minimum(j // each, 2), 0, 0)
    block = lambda j: (first // TRIO + jnp.minimum(j, TRIO * each - 1), 0, 0)
    u, v = low_early.shape[2], low_late.shape[2]
    return pl.pallas_call(
        body,
        grid=(places // TRIO,),
        in_specs=[
            pl.BlockSpec((None, r, u), kind),
            pl.BlockSpec((None, r, v), kind),
            pl.BlockSpec((None, r, u), kind),
            pl.BlockSpec((None, r, v), kind),
            pl.BlockSpec((TRIO, r, c), block),
        ],
        out_specs=[
            pl.BlockSpec((TRIO, r, c), block),
            pl.BlockSpec((TRIO, r, c), block),
            pl.BlockSpec((TRIO, 3, h, h), lambda j: (j, 0, 0, 0)),
        ],
        out_shape=[
            jax.ShapeDtypeStruct((total, r, c), F32),
            jax.ShapeDtypeStruct((total, r, c), F32),
            jax.ShapeDtypeStruct((places, 3, h, h), F32),
        ],
        compiler_params=params(),
        cost_estimate=pl.CostEstimate(
            flops=6 * 3 * blocks * r * c * c, bytes_accessed=16 * 3 * blocks * r * c, transcendentals=0
        ),
    )(low_early, low_late, high_early, high_late, momentum)


def attn_moment(grads, pairs, momentum, weight_grads, new_momentum):
    count, r, c = grads.shape
    h = c // 2

    def body(s_ref, g_ref, m_ref, wg_in, nm_in, wg_ref, nm_ref, gram_ref):
        for i in range(2):
            new = MUON_BETA * m_ref[i] + g_ref[i]
            wg_ref[i] = g_ref[i]
            nm_ref[i] = new
            gram_ref[i, 0], gram_ref[i, 1], gram_ref[i, 2] = gram_parts(new)

    block = pl.BlockSpec((2, r, c), lambda j, s: (s[j], 0, 0))
    apart = pl.BlockSpec(memory_space=pl.ANY)
    return pl.pallas_call(
        body,
        grid_spec=pltpu.PrefetchScalarGridSpec(
            num_scalar_prefetch=1,
            grid=(count // 2,),
            in_specs=[pl.BlockSpec((2, r, c), lambda j, s: (j, 0, 0)), block, apart, apart],
            out_specs=[block, block, pl.BlockSpec((2, 3, h, h), lambda j, s: (j, 0, 0, 0))],
        ),
        out_shape=[
            jax.ShapeDtypeStruct(momentum.shape, F32),
            jax.ShapeDtypeStruct(momentum.shape, F32),
            jax.ShapeDtypeStruct((count, 3, h, h), F32),
        ],
        input_output_aliases={3: 0, 4: 1},
        compiler_params=params(),
        cost_estimate=pl.CostEstimate(
            flops=6 * count * r * c * c, bytes_accessed=16 * count * r * c, transcendentals=0
        ),
    )(jnp.array(pairs, jnp.int32), grads, momentum, weight_grads, new_momentum)


def renew(weights, momentum, factors, spots, updated):
    _, r, c = weights.shape
    h = c // 2
    steps = len(spots)
    table = jnp.array([spot for spot, _ in spots] + [f for _, places in spots for f in places], jnp.int32)

    def body(s_ref, w_ref, m_ref, *refs):
        factor_refs, o_ref = refs[:TRIO], refs[-1]
        for i in range(TRIO):
            left = m_ref[i, :, :h].astype(BF16)
            right = m_ref[i, :, h:].astype(BF16)
            first, off, last = factor_refs[i][0], factor_refs[i][1], factor_refs[i][2]
            start = mm(left, first, NN) + mm(right, off, NT)
            rest = mm(left, off, NN) + mm(right, last, NN)
            keep = 1.0 - MUON_RATE * MUON_DECAY
            o_ref[i, :, :h] = w_ref[i, :, :h] * keep - MUON_RATE * start
            o_ref[i, :, h:] = w_ref[i, :, h:] * keep - MUON_RATE * rest

    block = pl.BlockSpec((TRIO, r, c), lambda j, s: (s[j], 0, 0))

    def factor_at(i):
        return pl.BlockSpec((None, 3, h, h), lambda j, s: (s[steps + TRIO * j + i], 0, 0, 0))

    apart = [pl.BlockSpec(memory_space=pl.ANY)] * len(updated)
    return pl.pallas_call(
        body,
        grid_spec=pltpu.PrefetchScalarGridSpec(
            num_scalar_prefetch=1,
            grid=(steps,),
            in_specs=[block, block] + [factor_at(i) for i in range(TRIO)] + apart,
            out_specs=block,
        ),
        out_shape=jax.ShapeDtypeStruct(weights.shape, F32),
        input_output_aliases={3 + TRIO: 0} if updated else {},
        compiler_params=params(),
        cost_estimate=pl.CostEstimate(
            flops=2 * TRIO * steps * r * c * c, bytes_accessed=12 * TRIO * steps * r * c, transcendentals=0
        ),
    )(table, weights, momentum, *([factors] * TRIO), *updated)


def top(spec, a, b):
    return jnp.einsum(spec, a, b, precision=TOP_PRECISION)


def newton_factor(grams, growth):
    size = grams.shape[-1]
    eye = jnp.eye(size, dtype=F32)
    norm = jnp.sqrt(jnp.sum(grams * eye, axis=(1, 2), keepdims=True))
    inverse = 1.0 / (norm + 1e-07)
    gram = grams * (inverse * inverse)
    factor = None
    for sweep in range(NEWTON_STEPS):
        square = top("bij,bjk->bik", gram, gram)
        poly = NEWTON_LINEAR * eye + NEWTON_SQUARE * gram + NEWTON_CUBIC * square
        factor = poly if sweep == 0 else top("bij,bjk->bik", factor, poly)
        if sweep < NEWTON_STEPS - 1:
            gram = top("bij,bjk->bik", top("bij,bjk->bik", gram, poly), poly)
    return factor * (growth * inverse)


def fold(squares):
    h = squares.shape[1] // 2
    return jnp.stack([squares[:, :h, :h], squares[:, :h, h:], squares[:, h:, h:]], axis=1)


def unfold(parts):
    first, off, last = parts[:, 0], parts[:, 1], parts[:, 2]
    upper = jnp.concatenate([first, off], axis=2)
    lower = jnp.concatenate([jnp.swapaxes(off, 1, 2), last], axis=2)
    return jnp.concatenate([upper, lower], axis=1)


def gram_sums(ring, parts, cap):
    h = parts.shape[2]
    parts = parts.reshape(-1, h, h)
    rows = 3 * cap
    mine = yield from ring.scatter(lambda i: lax.dynamic_slice_in_dim(parts, i * rows, rows, 0), rows // 2)
    return unfold(mine.reshape(cap, 3, h, h))


def all_factors(ring, factors):
    cap, c, _ = factors.shape
    parts = fold(factors.astype(BF16)).reshape(3 * cap, c // 2, c // 2)
    parts = yield from ring.gather(parts, 3 * cap // 2)
    return parts.reshape(ring.size * cap, 3, c // 2, c // 2)


def on_device(block_in, cotangent, seq_ids, weights, momentum, gains, gain_first, gain_second):
    tok_rows, model_width = block_in.shape
    rows_dp, group_blocks, head_dim = weights.shape
    head_count = lax.axis_size("head")
    data_count = lax.axis_size("dp")
    group_rows = tok_rows * head_count
    key_heads = KV // head_count
    query_heads = H // head_count
    ffn_blocks = FF // (head_dim * head_count)
    out_mark = query_heads + 2 * key_heads
    gate_mark = out_mark + query_heads
    half_dim = head_dim // 2
    full = ffn_blocks // 2
    scale = head_dim ** (-0.5)
    growth = math.sqrt(max(1.0, model_width / head_dim))
    data_index = lax.axis_index("dp")
    head_index = lax.axis_index("head")
    parity = (data_index >> 2) & 1
    ring = Ring()

    weights = jnp.transpose(weights, (1, 0, 2))
    momentum = jnp.transpose(momentum, (1, 0, 2))
    attn_low = cast_blocks(weights, gate_mark)
    inputs = block_in.astype(F32)
    normed_one, norm_one_back = jax.vjp(rms_scale, inputs, gains[0])
    ids_column = jnp.pad(seq_ids.astype(BF16)[:, None], ((0, 0), (0, 127)))

    early = full - 1
    mine_early, mine_late, other_early, other_late = pack_units(
        jnp.reshape(parity, (1,)), weights, gate_mark, ffn_blocks, early
    )
    spread = [Spread(mine_early, other_early), Spread(mine_late, other_late)]

    group_in = run(head_gather(jnp.concatenate([normed_one.astype(BF16), ids_column], axis=1)))
    qkv_parts = run(ring.gather(attn_low[:out_mark], out_mark // 2))
    qkv_blocks = jnp.transpose(qkv_parts, (1, 0, 2, 3)).reshape(out_mark, model_width, head_dim)
    cot_flow = Flow(wide_gather(cotangent))
    group_in, qkv_blocks, attn_low = stage(
        [spread[0].near(0), spread[0].y(0)], [group_in, qkv_blocks, attn_low], idle=[cot_flow]
    )
    projected = block_project(group_in, qkv_blocks)
    queries = projected[:query_heads].reshape(query_heads * group_rows, head_dim)
    group_ids = group_in[:, model_width]
    kv_rows = 2 * key_heads * group_rows
    out_rows = query_heads * rows_dp
    id_rows = group_rows // head_dim
    packed = jnp.concatenate(
        [
            projected[query_heads:].reshape(kv_rows, head_dim),
            attn_low[out_mark:].reshape(out_rows, head_dim),
            jnp.pad(group_ids.reshape(id_rows, head_dim), ((0, 16 - id_rows), (0, 0))),
        ],
        axis=0,
    )
    keys_values = run(ring.gather(packed, packed.shape[0] // 32 * 16))
    out_blocks = keys_values[:, kv_rows : kv_rows + out_rows].reshape(data_count, query_heads, rows_dp, head_dim)
    out_blocks = jnp.transpose(out_blocks, (1, 0, 2, 3)).reshape(query_heads, model_width, head_dim)
    queries, keys_values, out_blocks = stage(
        [cot_flow, spread[0].y(1), spread[1].near(0)], [queries, keys_values, out_blocks]
    )
    all_ids = keys_values[:, kv_rows + out_rows : kv_rows + out_rows + id_rows].reshape(-1)

    local = in_group(jnp.arange(group_rows, dtype=jnp.int32), group_rows, head_index * tok_rows)
    query_pos = data_index * group_rows + local
    first_pos = jnp.sum((all_ids[None, :] < group_ids[:, None]).astype(jnp.int32), axis=1)
    query_pos = jnp.tile(query_pos, query_heads)
    first_pos = jnp.tile(first_pos, query_heads)
    place = jnp.stack([data_index, head_index * tok_rows]).astype(jnp.int32)
    mixed_low, mixed_full, totals = attend(
        place, queries, keys_values, query_pos[:, None], first_pos[:, None], scale, group_rows
    )
    mixed_heads = mixed_low.reshape(query_heads, group_rows, head_dim)
    mixed_heads, mixed_full, totals, attn_part = stage(
        [spread[0].cross(), spread[1].y(0), spread[1].y(1), cot_flow],
        [mixed_heads, mixed_full, totals, block_back(mixed_heads, out_blocks)],
    )
    attn_flow = Flow(scatter_rows(*attn_part, HEAD_MOVES))
    attn_flow.advance([lax.ppermute(*send) for send in attn_flow.sends])
    stage([attn_flow, spread[0].near(3), spread[0].y(3), spread[1].cross()], idle=[cot_flow])
    residual = inputs + attn_flow.value
    normed_two, norm_two_back = jax.vjp(rms_scale, residual, gains[1])
    wide_flow = Flow(wide_gather(normed_two.astype(BF16)))
    stage([wide_flow, spread[0].y(2), spread[1].near(3), spread[1].y(3)], idle=[cot_flow])
    stage([wide_flow, spread[1].y(2), cot_flow])
    stage([wide_flow])
    finish(wide_flow, cot_flow)

    def whole_rows(pieces):
        if rows_dp % 16 == 0:
            return pieces
        out = jnp.zeros((3, data_count) + pieces[0].shape[1:], BF16)
        for k, piece in enumerate(pieces):
            out = lax.dynamic_update_index_in_dim(out, piece, data_index ^ k, 1)
        return [out.reshape(3, model_width, -1)]

    ffn_sides, ffn_full, *ffn_grads = ffn_front(
        place, wide_flow.value, cot_flow.value, whole_rows(spread[0].value()), whole_rows(spread[1].value())
    )

    def taker(pieces):
        if len(pieces) > 1:
            return lambda k: pieces[k]
        cut = pieces[0].reshape(3, data_count, rows_dp, pieces[0].shape[2])
        return lambda k: lax.dynamic_index_in_dim(cut, data_index ^ k, 1, keepdims=False)

    pieces = len(ffn_grads) // 2
    reduce = [Reduce(taker(ffn_grads[:pieces])), Reduce(taker(ffn_grads[pieces:]))]
    *down_part, dx_kept, dx_sent = stage([reduce[0].y(2)], ffn_back(ffn_sides, ffn_full))
    out_flow = Flow(scatter_rows(*down_part, WIDE_MOVES))
    dx_flow = Flow(scatter_rows(dx_kept, dx_sent, WIDE_MOVES))
    dx_flow.advance([lax.ppermute(*send) for send in dx_flow.sends])
    stage([dx_flow, reduce[0].near(2), reduce[0].y(3), reduce[1].y(2)])
    stage([dx_flow, reduce[0].y(1), reduce[1].near(2), out_flow])
    grad_residual_norm, grad_gain_two = norm_two_back(dx_flow.value)
    grad_residual = cotangent.astype(F32) + grad_residual_norm
    grad_flow = Flow(head_gather(grad_residual.astype(BF16)))
    stage([grad_flow, reduce[0].near(1), reduce[1].y(1), reduce[1].y(3)])
    grad_flow.advance([lax.ppermute(*send) for send in grad_flow.sends])
    group_grad = grad_flow.value

    grad_heads = block_project(group_grad, out_blocks)
    grad_mixed = grad_heads.reshape(query_heads * group_rows, head_dim)
    delta = jnp.sum(grad_mixed.astype(F32) * mixed_full, axis=1)
    grad_queries, grad_keys_values = attend_back(
        place,
        queries,
        grad_mixed,
        keys_values,
        1.0 / totals.reshape(1, -1),
        delta[None, :],
        query_pos[None, :],
        first_pos[None, :],
        scale,
        group_rows,
    )
    group_grad, grad_queries, grad_keys_values = stage(
        [reduce[0].cross(), reduce[1].near(1), reduce[0].y(0), reduce[1].y(0)],
        [group_grad, grad_queries, grad_keys_values],
    )
    grad_queries = grad_queries.reshape(query_heads, group_rows, head_dim)

    late = 2
    main = 3 * ffn_blocks - late
    cap = -(-main // data_count)
    places = -(-max(cap * data_count, 3 * ffn_blocks) // TRIO) * TRIO
    def weight_sums(outer):
        cut = outer.reshape(outer.shape[0], data_count, rows_dp, head_dim)
        return Flow(ring.scatter(lambda i: lax.dynamic_index_in_dim(cut, i, 1, keepdims=False), outer.shape[0] // 2))

    key_flow = Flow(
        ring.scatter(lambda i: lax.dynamic_index_in_dim(grad_keys_values, i, 0, keepdims=False), key_heads)
    )
    pick = lambda own, other: (jnp.where(parity == 1, other, own), jnp.where(parity == 1, own, other))
    low_early, high_early = pick(*reduce[0].value())
    outer, low_early, high_early = stage(
        [key_flow, reduce[1].cross(), out_flow],
        [block_outer([group_in, group_grad], [grad_queries, mixed_heads], model_width), low_early, high_early],
    )
    low_late, high_late = pick(*reduce[1].value())
    first_flow = weight_sums(outer)
    weight_grads, new_momentum, grams = stage(
        [key_flow, first_flow],
        ffn_moment(low_early, low_late, high_early, high_late, momentum, gate_mark, ffn_blocks, places),
    )
    gram_flow = Flow(gram_sums(ring, grams, cap))
    stage([key_flow, first_flow, gram_flow])
    while key_flow.sends is not None:
        stage([key_flow, first_flow, gram_flow])
    key_value_sums = key_flow.value
    grad_keys = (key_value_sums[:key_heads] * scale).astype(BF16)
    grad_values = key_value_sums[key_heads:].astype(BF16)
    grad_keys_values = jnp.concatenate([grad_keys, grad_values], axis=0)
    (outer,) = stage([first_flow, gram_flow], [block_outer([group_in], [grad_keys_values], model_width)])
    finish(first_flow)
    second_flow = weight_sums(outer)
    pairs = [k for k in range(gate_mark // 2) if not query_heads <= 2 * k < out_mark]
    grad_projected = jnp.concatenate([grad_queries, grad_keys_values], axis=0)
    *attn_dx, weight_grads, new_momentum, first_grams = stage(
        [second_flow, gram_flow],
        [
            *block_back(grad_projected, qkv_blocks),
            *attn_moment(first_flow.value, pairs, momentum, weight_grads, new_momentum),
        ],
    )
    last_flow = Flow(scatter_rows(*attn_dx, HEAD_MOVES))
    while second_flow.sends is not None:
        stage([second_flow, gram_flow, last_flow, out_flow])
    finish(last_flow, gram_flow, out_flow)
    block_out = (residual + out_flow.value).astype(BF16)
    grad_input_norm, grad_gain_one = norm_one_back(last_flow.value)
    grad_input = grad_residual + grad_input_norm
    gain_flow = Flow(total_sum(jnp.stack([grad_gain_one, grad_gain_two])))
    weight_grads, new_momentum, second_grams = attn_moment(
        second_flow.value, list(range(query_heads // 2, out_mark // 2)), momentum, weight_grads, new_momentum
    )
    late_count = gate_mark + late
    late_cap = -(-late_count // data_count)
    late_grams = jnp.concatenate([first_grams, second_grams, grams[main : main + late]], axis=0)
    late_grams = jnp.pad(late_grams, ((0, late_cap * data_count - late_count), (0, 0), (0, 0), (0, 0)))
    factors = newton_factor(gram_flow.value, growth)
    factors = run(all_factors(ring, factors))

    threes = main // TRIO
    early_spots = [(gate_mark // TRIO + k, [TRIO * k + i for i in range(TRIO)]) for k in range(threes)]
    late_sums, factors = stage([gain_flow], [run(gram_sums(ring, late_grams, late_cap)), factors])
    (late_factors,) = stage([gain_flow], [newton_factor(late_sums, growth)])
    late_factor_flow = Flow(all_factors(ring, late_factors))
    new_weights = []
    for k in range(0, threes, 2):
        new_weights = stage(
            [late_factor_flow, gain_flow],
            [renew(weights, new_momentum, factors, early_spots[k : k + 2], new_weights)],
        )

    finish(late_factor_flow, gain_flow)
    gain_grads = gain_flow.value
    rest = jnp.concatenate([late_factor_flow.value[:late_count], factors[TRIO * threes : main]], axis=0)
    blocks_of = [2 * pair + i for pair in pairs for i in range(2)] + list(range(query_heads, out_mark))
    blocks_of += [gate_mark + main + k for k in range(late)] + [gate_mark + k for k in range(TRIO * threes, main)]
    late_spots = [
        (spot, [blocks_of.index(TRIO * spot + i) for i in range(TRIO)])
        for spot in sorted({block // TRIO for block in blocks_of})
    ]
    new_weights = renew(weights, new_momentum, rest, late_spots, new_weights)

    new_gain_first = BETA_ONE * gain_first + (1.0 - BETA_ONE) * gain_grads
    new_gain_second = BETA_TWO * gain_second + (1.0 - BETA_TWO) * gain_grads * gain_grads
    first_hat = new_gain_first / (1.0 - BETA_ONE**UPDATE_STEP)
    second_hat = new_gain_second / (1.0 - BETA_TWO**UPDATE_STEP)
    new_gains = gains - ADAM_RATE * first_hat / (jnp.sqrt(second_hat) + ADAM_EPS)
    back = lambda array: jnp.transpose(array, (1, 0, 2))
    return (
        block_out,
        grad_input,
        back(weight_grads),
        back(new_momentum),
        back(new_weights),
        gain_grads,
        new_gain_first,
        new_gain_second,
        new_gains,
    )


def solution(mesh):
    return jax.shard_map(
        on_device,
        mesh=mesh,
        in_specs=(
            P(("dp", "head"), None),
            P(("dp", "head"), None),
            P(("dp", "head")),
            P("dp", "head", None),
            P("dp", "head", None),
            P(),
            P(),
            P(),
        ),
        out_specs=(
            P(("dp", "head"), None),
            P(("dp", "head"), None),
            P("dp", "head", None),
            P("dp", "head", None),
            P("dp", "head", None),
            P(),
            P(),
            P(),
            P(),
        ),
        check_vma=False,
    )
```

```python
import functools
import math

import jax
import jax.numpy as jnp
from jax import lax
from jax.experimental import pallas as pl
from jax.experimental.pallas import tpu as pltpu
from jax.sharding import PartitionSpec as P

H = 8
KV = 4
FF = 9216
NEWTON_STEPS = 5
UPDATE_STEP = 10

NORM_EPS = 1e-06
SOFT_CAP = 50.0
MUON_RATE = 0.2
MUON_DECAY = 0.01
MUON_BETA = 0.95
ADAM_RATE = 0.3
BETA_ONE = 0.9
BETA_TWO = 0.95
ADAM_EPS = 1e-08
NEWTON_LINEAR = 3.4445
NEWTON_SQUARE = -4.775
NEWTON_CUBIC = 2.0315
TOP_PRECISION = lax.Precision.HIGHEST

BF16 = jnp.bfloat16
F32 = jnp.float32
VMEM_LIMIT = 62 * 1024 * 1024
NN = (((1,), (0,)), ((), ()))
NT = (((1,), (1,)), ((), ()))
TN = (((0,), (0,)), ((), ()))


def mm(a, b, dims):
    return lax.dot_general(a, b, dims, preferred_element_type=F32)


def rms_scale(rows, gain):
    inverse = lax.rsqrt(jnp.mean(rows * rows, axis=-1, keepdims=True) + NORM_EPS)
    return rows * inverse * gain


class Flow:
    def __init__(self, steps):
        self.steps = steps
        self.value = None
        self.sends = None
        self.advance(None)

    def advance(self, arrived):
        try:
            self.sends = self.steps.send(arrived)
        except StopIteration as stop:
            self.sends = None
            self.value = stop.value


def stage(flows, extra=(), idle=()):
    flows = [flow for flow in flows if flow.sends is not None]
    idle = [flow for flow in idle if flow.sends is not None and flow not in flows]
    arrived = [[lax.ppermute(*send) for send in flow.sends] for flow in flows]
    held = [[send[0] for send in flow.sends] for flow in idle]
    arrived, held, extra = lax.optimization_barrier((arrived, held, list(extra)))
    for flow, got in zip(flows, arrived):
        flow.advance(got)
    for flow, kept in zip(idle, held):
        flow.sends = [(value,) + send[1:] for value, send in zip(kept, flow.sends)]
    return extra


def run(steps):
    flow = Flow(steps)
    while flow.sends is not None:
        flow.advance([lax.ppermute(*send) for send in flow.sends])
    return flow.value


def finish(*flows):
    while any(flow.sends is not None for flow in flows):
        stage(flows)


def swap(value, axis, mask):
    size = lax.axis_size(axis)
    return (value, axis, [(i, i ^ mask) for i in range(size)])


def head_gather(rows):
    (other,) = yield [swap(rows, "head", 2)]
    pair = jnp.concatenate([rows, other], axis=0)
    (other,) = yield [swap(pair, "head", 1)]
    return jnp.concatenate([pair, other], axis=0)


def wide_gather(rows):
    (other,) = yield [swap(rows, "dp", 4)]
    both = jnp.concatenate([rows, other], axis=0)
    (other,) = yield [swap(both, "head", 2)]
    pair = jnp.concatenate([both, other], axis=0)
    (other,) = yield [swap(pair, "head", 1)]
    return [pair, other]


def add_low(kept, other):
    return (kept.astype(F32) + other.astype(F32)).astype(BF16)


def scatter_rows(kept, sent, moves):
    for k, (axis, mask) in enumerate(moves):
        (other,) = yield [swap(sent, axis, mask)]
        part = kept.astype(F32) + other.astype(F32)
        if k < len(moves) - 1:
            half = part.shape[0] // 2
            kept, sent = part[:half], part[half:].astype(BF16)
    return part


HEAD_MOVES = (("head", 1), ("head", 2))
WIDE_MOVES = (("head", 1), ("head", 2), ("dp", 4))


def total_sum(value):
    for axis in ("head", "dp"):
        mask = 1
        while mask < lax.axis_size(axis):
            (other,) = yield [swap(value, axis, mask)]
            value = value + other
            mask *= 2
    return value


class Ring:
    def __init__(self):
        size = lax.axis_size("dp")
        order = list(range(0, size, 2)) + list(range(size - 1, 0, -2))
        around = [[order[(order.index(i) + offset) % size] for offset in range(size)] for i in range(size)]
        self.size = size
        self.around = jnp.array(around, jnp.int32)[lax.axis_index("dp")]
        self.up = [(order[k], order[(k + 1) % size]) for k in range(size)]
        self.down = [(order[(k + 1) % size], order[k]) for k in range(size)]

    def index(self, offset):
        return self.around[offset % self.size]

    def gather(self, value, mid):
        half = self.size // 2
        zeros = (0,) * (value.ndim - 1)
        out = jnp.zeros((self.size,) + value.shape, value.dtype)
        out = lax.dynamic_update_index_in_dim(out, value, self.index(0), 0)
        ahead, back = value, value
        for step in range(1, half):
            ahead, back = yield [(ahead, "dp", self.up), (back, "dp", self.down)]
            out = lax.dynamic_update_index_in_dim(out, ahead, self.index(-step), 0)
            out = lax.dynamic_update_index_in_dim(out, back, self.index(step), 0)
        first, second = yield [(ahead[:mid], "dp", self.up), (back[mid:], "dp", self.down)]
        far = self.index(half)
        out = lax.dynamic_update_slice(out, first[None], (far, 0) + zeros)
        return lax.dynamic_update_slice(out, second[None], (far, mid) + zeros)

    def scatter(self, take, mid):
        half = self.size // 2
        far = take(self.index(half))
        kind = far.dtype
        up, down = yield [(far[:mid], "dp", self.up), (far[mid:], "dp", self.down)]
        for step in range(half - 1, 0, -1):
            part = take(self.index(step)).astype(F32)
            ahead = jnp.concatenate([part[:mid] + up, part[mid:]]) if step == half - 1 else part + up
            part = take(self.index(-step)).astype(F32)
            back = jnp.concatenate([part[:mid], part[mid:] + down]) if step == half - 1 else part + down
            up, down = yield [(ahead.astype(kind), "dp", self.up), (back.astype(kind), "dp", self.down)]
        return take(self.index(0)).astype(F32) + up.astype(F32) + down.astype(F32)


def once(sends, take):
    def steps():
        take((yield sends))

    return Flow(steps())


SIDE_BIT = 2


def plane_classes():
    planes = range(lax.axis_size("dp") // 2)
    kept = [m for m in planes if m & 1 == 0]
    passed = [m for m in planes if m & 1 == 1]
    return {0: [0], 1: [1], 2: [m for m in passed if m != 1], 3: [m for m in kept if m]}


class Spread:
    def __init__(self, mine, other):
        self.mine, self.other = mine, other
        self.pieces = {0: mine}

    def move(self, moves):
        def take(arrived):
            for (_, _, _, number), piece in zip(moves, arrived):
                self.pieces[number] = piece

        return once([swap(value, "dp", offset << 1 | bit) for value, offset, bit, _ in moves], take)

    def cross(self):
        group = plane_classes()[3]
        return self.move([(self.other if m & SIDE_BIT else self.mine, m, 0, m << 1) for m in group])

    def near(self, key):
        group = plane_classes()[key]
        return self.move([(self.pieces[m << 1], 1, 0, (m ^ 1) << 1) for m in group])

    def y(self, key):
        group = plane_classes()[key]
        return self.move([(self.pieces[m << 1], 0, 1, m << 1 | 1) for m in group])

    def value(self):
        return [self.pieces[k] for k in range(lax.axis_size("dp"))]


class Reduce:
    def __init__(self, rows):
        self.rows = rows
        self.parts = {}
        self.sums = [None, None]

    def part(self, offset):
        terms = [term.astype(F32) for term in self.parts[offset]]
        return functools.reduce(jnp.add, terms)

    def hold(self, offset, *terms):
        self.parts.setdefault(offset, []).extend(terms)

    def y(self, key):
        group = plane_classes()[key]

        def take(arrived):
            for offset, got in zip(group, arrived):
                self.hold(offset, self.rows(offset << 1), got)

        return once([swap(self.rows(offset << 1 | 1), "dp", 1) for offset in group], take)

    def near(self, key):
        group = plane_classes()[key]

        def take(arrived):
            for offset, got in zip(group, arrived):
                self.hold(offset ^ 1, got)

        return once([swap(self.part(offset).astype(BF16), "dp", 2) for offset in group], take)

    def cross(self):
        group = plane_classes()[3]

        def take(arrived):
            for offset, got in zip(group, arrived):
                self.add(1 if offset & SIDE_BIT else 0, got.astype(F32))

        return once([swap(self.part(offset).astype(BF16), "dp", offset << 1) for offset in group], take)

    def add(self, side, value):
        self.sums[side] = value if self.sums[side] is None else self.sums[side] + value

    def value(self):
        self.add(0, self.part(0))
        return self.sums


def params(**more):
    return pltpu.CompilerParams(vmem_limit_bytes=VMEM_LIMIT, **more)


TRIO = 3


def cast_blocks(blocks, count):
    _, r, c = blocks.shape

    def body(x_ref, o_ref):
        o_ref[...] = x_ref[...].astype(BF16)

    spec = pl.BlockSpec((TRIO, r, c), lambda k: (k, 0, 0))
    return pl.pallas_call(
        body,
        grid=(count // TRIO,),
        in_specs=[spec],
        out_specs=spec,
        out_shape=jax.ShapeDtypeStruct((count, r, c), BF16),
        compiler_params=params(),
        cost_estimate=pl.CostEstimate(flops=0, bytes_accessed=6 * count * r * c, transcendentals=0),
    )(blocks)


def pack_units(parity, blocks, first, kind_blocks, early):
    _, r, c = blocks.shape
    h = c // 2
    full = kind_blocks // 2
    each = kind_blocks // TRIO
    u, v = early * c, (full - early) * c + h

    def body(s_ref, *refs):
        parts, outs = refs[:each], refs[each:]

        def tile(f):
            return parts[f // TRIO].at[f % TRIO]

        for turn in range(2):

            @pl.when(s_ref[0] == turn)
            def _():
                for k in range(2):
                    side = turn ^ k
                    for i in range(full):
                        value = tile(side * full + i)[...].astype(BF16)
                        if i < early:
                            outs[2 * k][:, i * c : (i + 1) * c] = value
                        else:
                            outs[2 * k + 1][:, (i - early) * c : (i - early + 1) * c] = value
                    rest = tile(2 * full)[:, side * h : (side + 1) * h]
                    outs[2 * k + 1][:, v - h :] = rest.astype(BF16)

    def part(i):
        return pl.BlockSpec((TRIO, r, c), lambda k, s: (first // TRIO + each * k + i, 0, 0))

    wide = pl.BlockSpec((None, r, u), lambda k, s: (k, 0, 0))
    slim = pl.BlockSpec((None, r, v), lambda k, s: (k, 0, 0))
    shapes = [jax.ShapeDtypeStruct((3, r, u), BF16), jax.ShapeDtypeStruct((3, r, v), BF16)]
    return pl.pallas_call(
        body,
        grid_spec=pltpu.PrefetchScalarGridSpec(
            num_scalar_prefetch=1,
            grid=(3,),
            in_specs=[part(i) for i in range(each)],
            out_specs=[wide, slim, wide, slim],
        ),
        out_shape=shapes + shapes,
        compiler_params=params(),
        cost_estimate=pl.CostEstimate(flops=0, bytes_accessed=18 * kind_blocks * r * c, transcendentals=0),
    )(parity, *([blocks] * each))


def block_project(rows, blocks):
    t = rows.shape[0]
    count, d, c = blocks.shape

    def body(x_ref, w_ref, o_ref):
        o_ref[...] = mm(x_ref[...], w_ref[...], NN).astype(BF16)

    return pl.pallas_call(
        body,
        grid=(count,),
        in_specs=[
            pl.BlockSpec((t, d), lambda b: (0, 0)),
            pl.BlockSpec((None, d, c), lambda b: (b, 0, 0)),
        ],
        out_specs=pl.BlockSpec((None, t, c), lambda b: (b, 0, 0)),
        out_shape=jax.ShapeDtypeStruct((count, t, c), BF16),
        compiler_params=params(),
        cost_estimate=pl.CostEstimate(
            flops=2 * count * t * d * c, bytes_accessed=2 * (t * d + count * (d * c + t * c)), transcendentals=0
        ),
    )(rows, blocks)


def block_back(cols, blocks):
    count, t, c = cols.shape
    d = blocks.shape[1]
    half = t // 2

    def body(x_ref, w_ref, o_ref, p_ref, acc_ref):
        b = pl.program_id(0)

        @pl.when(b == 0)
        def _():
            acc_ref[...] = jnp.zeros_like(acc_ref)

        acc_ref[...] += mm(x_ref[...], w_ref[...], NT)

        @pl.when(b == count - 1)
        def _():
            o_ref[...] = acc_ref[:half, :].astype(BF16)
            p_ref[...] = acc_ref[half:, :].astype(BF16)

    result = pl.BlockSpec((half, d), lambda b: (0, 0))
    return pl.pallas_call(
        body,
        grid=(count,),
        in_specs=[
            pl.BlockSpec((None, t, c), lambda b: (b, 0, 0)),
            pl.BlockSpec((None, d, c), lambda b: (b, 0, 0)),
        ],
        out_specs=[result, result],
        out_shape=[jax.ShapeDtypeStruct((half, d), BF16)] * 2,
        scratch_shapes=[pltpu.VMEM((t, d), F32)],
        compiler_params=params(),
        cost_estimate=pl.CostEstimate(
            flops=2 * count * t * d * c, bytes_accessed=2 * (t * d + count * (d * c + t * c)), transcendentals=0
        ),
    )(cols, blocks)


def block_outer(rows, cols, d):
    t = rows[0].shape[0]
    c = cols[0].shape[2]
    starts = [0]
    for col in cols:
        starts.append(starts[-1] + col.shape[0])
    count = len(rows)
    total = starts[-1]

    def body(*refs):
        o_ref, t_ref = refs[2 * count :]
        b = pl.program_id(0)
        for k in range(count):

            @pl.when(b == starts[k])
            def _():
                t_ref[...] = refs[k][...].T

            @pl.when((b >= starts[k]) & (b < starts[k + 1]))
            def _():
                o_ref[...] = mm(t_ref[...], refs[count + k][...], NN).astype(BF16)

    def col_at(k):
        return pl.BlockSpec((None, t, c), lambda b: (jnp.clip(b - starts[k], 0, starts[k + 1] - starts[k] - 1), 0, 0))

    return pl.pallas_call(
        body,
        grid=(total,),
        in_specs=[pl.BlockSpec((t, d), lambda b: (0, 0))] * count + [col_at(k) for k in range(count)],
        out_specs=pl.BlockSpec((None, d, c), lambda b: (b, 0, 0)),
        out_shape=jax.ShapeDtypeStruct((total, d, c), BF16),
        scratch_shapes=[pltpu.VMEM((d, t), BF16)],
        compiler_params=params(),
        cost_estimate=pl.CostEstimate(
            flops=2 * total * t * d * c,
            bytes_accessed=2 * (count * t * d + total * (d * c + t * c)),
            transcendentals=0,
        ),
    )(*rows, *cols)


def in_group(local, width, head_shift):
    quarter = width // 4
    low = jnp.bitwise_and(local, quarter - 1)
    one = jnp.where(jnp.bitwise_and(local, quarter) != 0, 2 * quarter, 0)
    two = jnp.where(jnp.bitwise_and(local, 2 * quarter) != 0, quarter, 0)
    return jnp.bitwise_xor(low + one + two, head_shift)


def key_position(block, width, head_shift, shape, axis):
    local = lax.broadcasted_iota(jnp.int32, shape, axis)
    return block * width + in_group(local, width, head_shift)


def attend(place, queries, keys_values, query_pos, first_pos, scale, p):
    m, e = queries.shape
    n = keys_values.shape[0]
    step = 256

    def body(place_ref, q_ref, kv_ref, pos_ref, first_ref, low_ref, full_ref, sum_ref, acc_ref, tot_ref):
        j = pl.program_id(0)

        @pl.when(j == 0)
        def _():
            acc_ref[...] = jnp.zeros_like(acc_ref)
            tot_ref[...] = jnp.zeros_like(tot_ref)

        @pl.when(j <= place_ref[0])
        def _():
            key_pos = key_position(j, p, place_ref[1], (1, p), 1)
            for r in range(0, m, step):
                rows = pl.ds(r, step)
                raw = mm(q_ref[rows, :], kv_ref[:p, :], NT)
                soft = SOFT_CAP * jnp.tanh(raw * (scale / SOFT_CAP))
                seen = (key_pos >= first_ref[rows, :]) & (key_pos <= pos_ref[rows, :])
                terms = jnp.where(seen, jnp.exp(soft), 0.0)
                tot_ref[rows, :] += jnp.sum(terms, axis=1, keepdims=True)
                acc_ref[rows, :] += mm(terms.astype(BF16), kv_ref[p:, :], NN)

        @pl.when(j == n - 1)
        def _():
            total = tot_ref[...]
            mixed = acc_ref[...] / total
            full_ref[...] = mixed
            low_ref[...] = mixed.astype(BF16)
            sum_ref[...] = total

    whole = lambda shape: pl.BlockSpec(shape, lambda j, s: (0, 0))
    return pl.pallas_call(
        body,
        grid_spec=pltpu.PrefetchScalarGridSpec(
            num_scalar_prefetch=1,
            grid=(n,),
            in_specs=[
                whole((m, e)),
                pl.BlockSpec((None, 2 * p, e), lambda j, s: (jnp.minimum(j, s[0]), 0, 0)),
                whole((m, 1)),
                whole((m, 1)),
            ],
            out_specs=[whole((m, e)), whole((m, e)), whole((m, 1))],
            scratch_shapes=[pltpu.VMEM((m, e), F32), pltpu.VMEM((m, 1), F32)],
        ),
        out_shape=[
            jax.ShapeDtypeStruct((m, e), BF16),
            jax.ShapeDtypeStruct((m, e), F32),
            jax.ShapeDtypeStruct((m, 1), F32),
        ],
        compiler_params=params(),
        cost_estimate=pl.CostEstimate(
            flops=4 * m * n * p * e, bytes_accessed=4 * n * p * e, transcendentals=2 * m * n * p
        ),
    )(place, queries, keys_values, query_pos, first_pos)


def attend_back(place, queries, grads, keys_values, inverse, delta, query_pos, first_pos, scale, p):
    m, e = queries.shape
    n = keys_values.shape[0]
    step = 256

    def body(
        place_ref, q_ref, g_ref, kv_ref, inv_ref, delta_ref, pos_ref, first_ref, dq_ref, dkv_ref, acc_ref, dk_ref, dv_ref
    ):
        j = pl.program_id(0)

        @pl.when(j == 0)
        def _():
            acc_ref[...] = jnp.zeros_like(acc_ref)

        @pl.when(j <= place_ref[0])
        def _():
            key_pos = key_position(j, p, place_ref[1], (p, 1), 0)
            for r in range(0, m, step):
                rows = pl.ds(r, step)
                raw = mm(kv_ref[:p, :], q_ref[rows, :], NT)
                capped = jnp.tanh(raw * (scale / SOFT_CAP))
                seen = (key_pos >= first_ref[:, rows]) & (key_pos <= pos_ref[:, rows])
                probs = jnp.where(seen, jnp.exp(SOFT_CAP * capped), 0.0) * inv_ref[:, rows]
                grad_probs = mm(kv_ref[p:, :], g_ref[rows, :], NT)
                grad_raw = probs * (grad_probs - delta_ref[:, rows]) * (1.0 - capped * capped)
                grad_low = grad_raw.astype(BF16)
                value_part = mm(probs.astype(BF16), g_ref[rows, :], NN)
                key_part = mm(grad_low, q_ref[rows, :], NN)
                if r == 0:
                    dv_ref[...] = value_part
                    dk_ref[...] = key_part
                else:
                    dv_ref[...] += value_part
                    dk_ref[...] += key_part
                acc_ref[rows, :] += mm(grad_low, kv_ref[:p, :], TN)
            dkv_ref[0] = dk_ref[...].astype(BF16)
            dkv_ref[1] = dv_ref[...].astype(BF16)

        @pl.when(j > place_ref[0])
        def _():
            dkv_ref[...] = jnp.zeros_like(dkv_ref)

        @pl.when(j == n - 1)
        def _():
            dq_ref[...] = (acc_ref[...] * scale).astype(BF16)

    whole = lambda shape: pl.BlockSpec(shape, lambda j, s: (0, 0))
    return pl.pallas_call(
        body,
        grid_spec=pltpu.PrefetchScalarGridSpec(
            num_scalar_prefetch=1,
            grid=(n,),
            in_specs=[
                whole((m, e)),
                whole((m, e)),
                pl.BlockSpec((None, 2 * p, e), lambda j, s: (jnp.minimum(j, s[0]), 0, 0)),
                whole((1, m)),
                whole((1, m)),
                whole((1, m)),
                whole((1, m)),
            ],
            out_specs=[whole((m, e)), pl.BlockSpec((None, 2, p, e), lambda j, s: (j, 0, 0, 0))],
            scratch_shapes=[pltpu.VMEM((m, e), F32), pltpu.VMEM((p, e), F32), pltpu.VMEM((p, e), F32)],
        ),
        out_shape=[jax.ShapeDtypeStruct((m, e), BF16), jax.ShapeDtypeStruct((n, 2, p, e), BF16)],
        compiler_params=params(),
        cost_estimate=pl.CostEstimate(
            flops=10 * m * n * p * e, bytes_accessed=8 * n * p * e, transcendentals=2 * m * n * p
        ),
    )(place, queries, grads, keys_values, inverse, delta, query_pos, first_pos)


def gelu_pair(gate):
    outer = math.sqrt(2.0 / math.pi)
    square = gate * gate
    bent = jnp.tanh(outer * gate * (1.0 + 0.044715 * square))
    half = 0.5 * (1.0 + bent)
    slope = half + 0.5 * gate * (1.0 - bent * bent) * outer * (1.0 + 3.0 * 0.044715 * square)
    return gate * half, slope


def ffn_front(place, rows, cots, early, late):
    part_rows, d = rows[0].shape
    t = 2 * part_rows
    count = len(early)
    r = early[0].shape[1]
    u, v = early[0].shape[2], late[0].shape[2]
    tall = min(512, t)
    wide = d // 3
    cuts = [(k, min(256, u + v - k)) for k in range(0, u + v, 256)]

    def body(place_ref, x0, x1, y0, y1, *refs):
        early_refs, late_refs = refs[:count], refs[count : 2 * count]
        refs = refs[2 * count :]
        hs_ref, w_out = refs[:2]
        grad_refs = refs[2 : 2 + count], refs[2 + count : 2 + 2 * count]
        x, y, w, xt, yt, hs, row_sems, sems, out_sems, grad_sems = refs[2 + 2 * count :]
        row_copies = []
        for k, (source, target) in enumerate(((x0, x), (x1, x), (y0, y), (y1, y))):
            target = target.at[pl.ds((k % 2) * part_rows, part_rows), :]
            row_copies.append(pltpu.make_async_copy(source, target, row_sems.at[k]))
            row_copies[k].start()
        copies = []
        chunks = ((early_refs, pl.ds(0, u)), (late_refs, pl.ds(u, v)))

        def spot(k):
            return pl.ds(pl.multiple_of(jnp.bitwise_xor(place_ref[0], k) * r, 16) if count > 1 else 0, r)

        for k in range(count):
            for way, (sources, lanes) in enumerate(chunks):
                copy = pltpu.make_async_copy(sources[k], w.at[:, spot(k), lanes], sems.at[way, k])
                copy.start()
                copies.append(copy)
        for copy in row_copies:
            copy.wait()

        @pl.loop(0, d // 256)
        def _(k):
            cols = pl.ds(pl.multiple_of(k * 256, 256), 256)
            xt[cols, :] = x[:, cols].T
            yt[cols, :] = y[:, cols].T

        for copy in copies:
            copy.wait()
        kept = pltpu.make_async_copy(w, w_out, out_sems.at[0])
        kept.start()

        @pl.loop(0, t // tall)
        def _(i):
            part = pl.ds(pl.multiple_of(i * tall, tall), tall)
            for start, size in cuts:
                units = pl.ds(start, size)
                gate = mm(x[part, :], w[0, :, units], NN)
                up = mm(x[part, :], w[1, :, units], NN)
                grad = mm(y[part, :], w[2, :, units], NN)
                active, slope = gelu_pair(gate)
                hs[0, part, units] = (active * up).astype(BF16)
                hs[1, part, units] = (grad * up * slope).astype(BF16)
                hs[2, part, units] = (grad * active).astype(BF16)

        sides = pltpu.make_async_copy(hs, hs_ref, out_sems.at[1])
        sides.start()
        kept.wait()
        copies = []
        for kind, (left, right) in enumerate(((xt, 1), (xt, 2), (yt, 0))):

            @pl.loop(0, d // wide)
            def _(k):
                cols = pl.ds(pl.multiple_of(k * wide, wide), wide)
                w[kind, cols, :] = mm(left[cols, :], hs[right], NN).astype(BF16)

            for k in range(count):
                for way, (_, lanes) in enumerate(chunks):
                    target = grad_refs[way][k].at[kind]
                    copy = pltpu.make_async_copy(w.at[kind, spot(k), lanes], target, grad_sems.at[kind, way, k])
                    copy.start()
                    copies.append(copy)
        sides.wait()
        for copy in copies:
            copy.wait()

    apart = pl.BlockSpec(memory_space=pl.ANY)
    return pl.pallas_call(
        body,
        grid_spec=pltpu.PrefetchScalarGridSpec(
            num_scalar_prefetch=1,
            grid=(1,),
            in_specs=[apart] * (4 + 2 * count),
            out_specs=[apart] * (2 + 2 * count),
            scratch_shapes=[
                pltpu.VMEM((t, d), BF16),
                pltpu.VMEM((t, d), BF16),
                pltpu.VMEM((3, d, u + v), BF16),
                pltpu.VMEM((d, t), BF16),
                pltpu.VMEM((d, t), BF16),
                pltpu.VMEM((3, t, u + v), BF16),
                pltpu.SemaphoreType.DMA((4,)),
                pltpu.SemaphoreType.DMA((2, count)),
                pltpu.SemaphoreType.DMA((2,)),
                pltpu.SemaphoreType.DMA((3, 2, count)),
            ],
        ),
        out_shape=[
            jax.ShapeDtypeStruct((3, t, u + v), BF16),
            jax.ShapeDtypeStruct((3, d, u + v), BF16),
            *[jax.ShapeDtypeStruct((3, r, u), BF16)] * count,
            *[jax.ShapeDtypeStruct((3, r, v), BF16)] * count,
        ],
        compiler_params=params(),
        cost_estimate=pl.CostEstimate(
            flops=12 * t * d * (u + v), bytes_accessed=12 * d * (u + v) + 4 * t * d, transcendentals=t * (u + v)
        ),
    )(place, *rows, *cots, *early, *late)


def ffn_back(sides, blocks):
    _, t, u = sides.shape
    d = blocks.shape[1]
    wide = 256
    half = t // 2

    def body(s_ref, w_ref, *refs):
        for k in range(2):
            part = pl.ds(k * half, half)
            refs[k][...] = mm(s_ref[0, part, :], w_ref[2], NT).astype(BF16)
            refs[2 + k][...] = (mm(s_ref[1, part, :], w_ref[0], NT) + mm(s_ref[2, part, :], w_ref[1], NT)).astype(BF16)

    return pl.pallas_call(
        body,
        grid=(d // wide,),
        in_specs=[
            pl.BlockSpec((3, t, u), lambda k: (0, 0, 0), pipeline_mode=pl.Buffered(1)),
            pl.BlockSpec((3, wide, u), lambda k: (0, k, 0)),
        ],
        out_specs=[pl.BlockSpec((half, wide), lambda k: (0, k))] * 4,
        out_shape=[jax.ShapeDtypeStruct((half, d), BF16)] * 4,
        compiler_params=params(),
        cost_estimate=pl.CostEstimate(
            flops=6 * t * d * u, bytes_accessed=6 * d * u + 6 * t * u + 4 * t * d, transcendentals=0
        ),
    )(sides, blocks)


def gram_parts(m):
    h = m.shape[1] // 2
    high = m.astype(BF16)
    low = (m - high.astype(F32)).astype(BF16)
    mixed = mm(high, low, TN)
    gram = mm(high, high, TN) + mm(low, low, TN) + mixed + mixed.T
    return gram[:h, :h], gram[:h, h:], gram[h:, h:]


def ffn_moment(low_early, low_late, high_early, high_late, momentum, first, blocks, places):
    total, r, c = momentum.shape
    early = low_early.shape[2] // c
    h = c // 2
    full = early + 1
    each = blocks // TRIO

    def body(le_ref, ll_ref, he_ref, hl_ref, m_ref, wg_ref, nm_ref, gram_ref):
        j = pl.program_id(0)

        @pl.when(j >= TRIO * each)
        def _():
            gram_ref[...] = jnp.zeros_like(gram_ref)

        for turn in range(each):

            @pl.when((j < TRIO * each) & (lax.rem(j, each) == turn))
            def _():
                for i in range(TRIO):
                    side, f = divmod(turn * TRIO + i, full)
                    if side == 2:
                        wg_ref[i, :, :h] = ll_ref[:, c:]
                        wg_ref[i, :, h:] = hl_ref[:, c:]
                    elif f < early:
                        wg_ref[i] = (le_ref, he_ref)[side][:, f * c : (f + 1) * c]
                    else:
                        wg_ref[i] = (ll_ref, hl_ref)[side][:, :c]

        @pl.when(j < TRIO * each)
        def _():
            for i in range(TRIO):
                new = MUON_BETA * m_ref[i] + wg_ref[i]
                nm_ref[i] = new
                gram_ref[i, 0], gram_ref[i, 1], gram_ref[i, 2] = gram_parts(new)

    kind = lambda j: (jnp.minimum(j // each, 2), 0, 0)
    block = lambda j: (first // TRIO + jnp.minimum(j, TRIO * each - 1), 0, 0)
    u, v = low_early.shape[2], low_late.shape[2]
    return pl.pallas_call(
        body,
        grid=(places // TRIO,),
        in_specs=[
            pl.BlockSpec((None, r, u), kind),
            pl.BlockSpec((None, r, v), kind),
            pl.BlockSpec((None, r, u), kind),
            pl.BlockSpec((None, r, v), kind),
            pl.BlockSpec((TRIO, r, c), block),
        ],
        out_specs=[
            pl.BlockSpec((TRIO, r, c), block),
            pl.BlockSpec((TRIO, r, c), block),
            pl.BlockSpec((TRIO, 3, h, h), lambda j: (j, 0, 0, 0)),
        ],
        out_shape=[
            jax.ShapeDtypeStruct((total, r, c), F32),
            jax.ShapeDtypeStruct((total, r, c), F32),
            jax.ShapeDtypeStruct((places, 3, h, h), F32),
        ],
        compiler_params=params(),
        cost_estimate=pl.CostEstimate(
            flops=6 * 3 * blocks * r * c * c, bytes_accessed=16 * 3 * blocks * r * c, transcendentals=0
        ),
    )(low_early, low_late, high_early, high_late, momentum)


def attn_moment(grads, pairs, momentum, weight_grads, new_momentum):
    count, r, c = grads.shape
    h = c // 2

    def body(s_ref, g_ref, m_ref, wg_in, nm_in, wg_ref, nm_ref, gram_ref):
        for i in range(2):
            new = MUON_BETA * m_ref[i] + g_ref[i]
            wg_ref[i] = g_ref[i]
            nm_ref[i] = new
            gram_ref[i, 0], gram_ref[i, 1], gram_ref[i, 2] = gram_parts(new)

    block = pl.BlockSpec((2, r, c), lambda j, s: (s[j], 0, 0))
    apart = pl.BlockSpec(memory_space=pl.ANY)
    return pl.pallas_call(
        body,
        grid_spec=pltpu.PrefetchScalarGridSpec(
            num_scalar_prefetch=1,
            grid=(count // 2,),
            in_specs=[pl.BlockSpec((2, r, c), lambda j, s: (j, 0, 0)), block, apart, apart],
            out_specs=[block, block, pl.BlockSpec((2, 3, h, h), lambda j, s: (j, 0, 0, 0))],
        ),
        out_shape=[
            jax.ShapeDtypeStruct(momentum.shape, F32),
            jax.ShapeDtypeStruct(momentum.shape, F32),
            jax.ShapeDtypeStruct((count, 3, h, h), F32),
        ],
        input_output_aliases={3: 0, 4: 1},
        compiler_params=params(),
        cost_estimate=pl.CostEstimate(
            flops=6 * count * r * c * c, bytes_accessed=16 * count * r * c, transcendentals=0
        ),
    )(jnp.array(pairs, jnp.int32), grads, momentum, weight_grads, new_momentum)


def renew(weights, momentum, factors, spots, updated):
    _, r, c = weights.shape
    h = c // 2
    steps = len(spots)
    table = jnp.array([spot for spot, _ in spots] + [f for _, places in spots for f in places], jnp.int32)

    def body(s_ref, w_ref, m_ref, *refs):
        factor_refs, o_ref = refs[:TRIO], refs[-1]
        for i in range(TRIO):
            left = m_ref[i, :, :h].astype(BF16)
            right = m_ref[i, :, h:].astype(BF16)
            first, off, last = factor_refs[i][0], factor_refs[i][1], factor_refs[i][2]
            start = mm(left, first, NN) + mm(right, off, NT)
            rest = mm(left, off, NN) + mm(right, last, NN)
            keep = 1.0 - MUON_RATE * MUON_DECAY
            o_ref[i, :, :h] = w_ref[i, :, :h] * keep - MUON_RATE * start
            o_ref[i, :, h:] = w_ref[i, :, h:] * keep - MUON_RATE * rest

    block = pl.BlockSpec((TRIO, r, c), lambda j, s: (s[j], 0, 0))

    def factor_at(i):
        return pl.BlockSpec((None, 3, h, h), lambda j, s: (s[steps + TRIO * j + i], 0, 0, 0))

    apart = [pl.BlockSpec(memory_space=pl.ANY)] * len(updated)
    return pl.pallas_call(
        body,
        grid_spec=pltpu.PrefetchScalarGridSpec(
            num_scalar_prefetch=1,
            grid=(steps,),
            in_specs=[block, block] + [factor_at(i) for i in range(TRIO)] + apart,
            out_specs=block,
        ),
        out_shape=jax.ShapeDtypeStruct(weights.shape, F32),
        input_output_aliases={3 + TRIO: 0} if updated else {},
        compiler_params=params(),
        cost_estimate=pl.CostEstimate(
            flops=2 * TRIO * steps * r * c * c, bytes_accessed=12 * TRIO * steps * r * c, transcendentals=0
        ),
    )(table, weights, momentum, *([factors] * TRIO), *updated)


def top(spec, a, b):
    return jnp.einsum(spec, a, b, precision=TOP_PRECISION)


def newton_start(grams, growth):
    eye = jnp.eye(grams.shape[-1], dtype=F32)
    norm = jnp.sqrt(jnp.sum(grams * eye, axis=(1, 2), keepdims=True))
    inverse = 1.0 / (norm + 1e-07)
    return [grams * (inverse * inverse), growth * inverse]


def newton_sweep(state, sweep):
    gram, factor = state
    eye = jnp.eye(gram.shape[-1], dtype=F32)
    square = top("bij,bjk->bik", gram, gram)
    poly = NEWTON_LINEAR * eye + NEWTON_SQUARE * gram + NEWTON_CUBIC * square
    factor = poly * factor if sweep == 0 else top("bij,bjk->bik", factor, poly)
    if sweep < NEWTON_STEPS - 1:
        gram = top("bij,bjk->bik", top("bij,bjk->bik", gram, poly), poly)
    return [gram, factor]


def newton_factor(grams, growth):
    state = newton_start(grams, growth)
    for sweep in range(NEWTON_STEPS):
        state = newton_sweep(state, sweep)
    return state[1]


def fold(squares):
    h = squares.shape[1] // 2
    return jnp.stack([squares[:, :h, :h], squares[:, :h, h:], squares[:, h:, h:]], axis=1)


def unfold(parts):
    first, off, last = parts[:, 0], parts[:, 1], parts[:, 2]
    upper = jnp.concatenate([first, off], axis=2)
    lower = jnp.concatenate([jnp.swapaxes(off, 1, 2), last], axis=2)
    return jnp.concatenate([upper, lower], axis=1)


def gram_sums(ring, parts, cap):
    h = parts.shape[2]
    parts = parts.reshape(-1, h, h)
    rows = 3 * cap
    mine = yield from ring.scatter(lambda i: lax.dynamic_slice_in_dim(parts, i * rows, rows, 0), rows // 2)
    return unfold(mine.reshape(cap, 3, h, h))


def all_factors(ring, factors):
    cap, c, _ = factors.shape
    parts = fold(factors.astype(BF16)).reshape(3 * cap, c // 2, c // 2)
    parts = yield from ring.gather(parts, 3 * cap // 2)
    return parts.reshape(ring.size * cap, 3, c // 2, c // 2)


def on_device(block_in, cotangent, seq_ids, weights, momentum, gains, gain_first, gain_second):
    tok_rows, model_width = block_in.shape
    rows_dp, group_blocks, head_dim = weights.shape
    head_count = lax.axis_size("head")
    data_count = lax.axis_size("dp")
    group_rows = tok_rows * head_count
    key_heads = KV // head_count
    query_heads = H // head_count
    ffn_blocks = FF // (head_dim * head_count)
    out_mark = query_heads + 2 * key_heads
    gate_mark = out_mark + query_heads
    half_dim = head_dim // 2
    full = ffn_blocks // 2
    scale = head_dim ** (-0.5)
    growth = math.sqrt(max(1.0, model_width / head_dim))
    data_index = lax.axis_index("dp")
    head_index = lax.axis_index("head")
    parity = (data_index >> 2) & 1
    ring = Ring()

    weights = jnp.transpose(weights, (1, 0, 2))
    momentum = jnp.transpose(momentum, (1, 0, 2))
    attn_low = cast_blocks(weights, gate_mark)
    inputs = block_in.astype(F32)
    normed_one, norm_one_back = jax.vjp(rms_scale, inputs, gains[0])
    ids_column = jnp.pad(seq_ids.astype(BF16)[:, None], ((0, 0), (0, 127)))

    early = full - 1
    mine_early, mine_late, other_early, other_late = pack_units(
        jnp.reshape(parity, (1,)), weights, gate_mark, ffn_blocks, early
    )
    spread = [Spread(mine_early, other_early), Spread(mine_late, other_late)]

    group_in = run(head_gather(jnp.concatenate([normed_one.astype(BF16), ids_column], axis=1)))
    qkv_parts = run(ring.gather(attn_low[:out_mark], out_mark // 2))
    qkv_blocks = jnp.transpose(qkv_parts, (1, 0, 2, 3)).reshape(out_mark, model_width, head_dim)
    cot_flow = Flow(wide_gather(cotangent))
    group_in, qkv_blocks, attn_low = stage(
        [spread[0].near(0), spread[0].y(0)], [group_in, qkv_blocks, attn_low], idle=[cot_flow]
    )
    cross_flow = spread[0].cross()
    projected = block_project(group_in, qkv_blocks)
    queries = projected[:query_heads].reshape(query_heads * group_rows, head_dim)
    group_ids = group_in[:, model_width]
    kv_rows = 2 * key_heads * group_rows
    out_rows = query_heads * rows_dp
    id_rows = group_rows // head_dim
    packed = jnp.concatenate(
        [
            projected[query_heads:].reshape(kv_rows, head_dim),
            attn_low[out_mark:].reshape(out_rows, head_dim),
            jnp.pad(group_ids.reshape(id_rows, head_dim), ((0, 16 - id_rows), (0, 0))),
        ],
        axis=0,
    )
    keys_values = run(ring.gather(packed, packed.shape[0] // 32 * 16))
    out_blocks = keys_values[:, kv_rows : kv_rows + out_rows].reshape(data_count, query_heads, rows_dp, head_dim)
    out_blocks = jnp.transpose(out_blocks, (1, 0, 2, 3)).reshape(query_heads, model_width, head_dim)
    queries, keys_values, out_blocks = stage(
        [cot_flow, spread[0].y(1), spread[1].near(0)], [queries, keys_values, out_blocks], idle=[cross_flow]
    )
    all_ids = keys_values[:, kv_rows + out_rows : kv_rows + out_rows + id_rows].reshape(-1)

    local = in_group(jnp.arange(group_rows, dtype=jnp.int32), group_rows, head_index * tok_rows)
    query_pos = data_index * group_rows + local
    first_pos = jnp.sum((all_ids[None, :] < group_ids[:, None]).astype(jnp.int32), axis=1)
    query_pos = jnp.tile(query_pos, query_heads)
    first_pos = jnp.tile(first_pos, query_heads)
    place = jnp.stack([data_index, head_index * tok_rows]).astype(jnp.int32)
    mixed_low, mixed_full, totals = attend(
        place, queries, keys_values, query_pos[:, None], first_pos[:, None], scale, group_rows
    )
    mixed_heads = mixed_low.reshape(query_heads, group_rows, head_dim)
    attn_add = run(scatter_rows(*block_back(mixed_heads, out_blocks), HEAD_MOVES))
    mixed_heads, mixed_full, totals, attn_add = stage(
        [cross_flow, spread[1].y(0), spread[1].y(1), cot_flow],
        [mixed_heads, mixed_full, totals, attn_add],
    )
    residual = inputs + attn_add
    normed_two, norm_two_back = jax.vjp(rms_scale, residual, gains[1])
    wide_flow = Flow(wide_gather(normed_two.astype(BF16)))
    stage([wide_flow, spread[0].near(3), spread[0].y(3), spread[1].cross()], idle=[cot_flow])
    stage([wide_flow, spread[0].y(2), spread[1].near(3), spread[1].y(3)], idle=[cot_flow])
    stage([wide_flow, spread[1].y(2), cot_flow])
    finish(wide_flow, cot_flow)

    def whole_rows(pieces):
        if rows_dp % 16 == 0:
            return pieces
        out = jnp.zeros((3, data_count) + pieces[0].shape[1:], BF16)
        for k, piece in enumerate(pieces):
            out = lax.dynamic_update_index_in_dim(out, piece, data_index ^ k, 1)
        return [out.reshape(3, model_width, -1)]

    ffn_sides, ffn_full, *ffn_grads = ffn_front(
        place, wide_flow.value, cot_flow.value, whole_rows(spread[0].value()), whole_rows(spread[1].value())
    )

    def taker(pieces):
        if len(pieces) > 1:
            return lambda k: pieces[k]
        cut = pieces[0].reshape(3, data_count, rows_dp, pieces[0].shape[2])
        return lambda k: lax.dynamic_index_in_dim(cut, data_index ^ k, 1, keepdims=False)

    pieces = len(ffn_grads) // 2
    reduce = [Reduce(taker(ffn_grads[:pieces])), Reduce(taker(ffn_grads[pieces:]))]
    *down_part, dx_kept, dx_sent = stage([reduce[0].y(2)], ffn_back(ffn_sides, ffn_full))
    out_flow = Flow(scatter_rows(*down_part, WIDE_MOVES))
    dx_flow = Flow(scatter_rows(dx_kept, dx_sent, WIDE_MOVES))
    dx_flow.advance([lax.ppermute(*send) for send in dx_flow.sends])
    stage([dx_flow, reduce[0].near(2), reduce[0].y(3), reduce[1].y(2)])
    stage([dx_flow, reduce[0].y(1), reduce[1].near(2), out_flow])
    grad_residual_norm, grad_gain_two = norm_two_back(dx_flow.value)
    grad_residual = cotangent.astype(F32) + grad_residual_norm
    grad_flow = Flow(head_gather(grad_residual.astype(BF16)))
    stage([grad_flow, reduce[0].near(1), reduce[1].y(1), reduce[1].y(3)])
    grad_flow.advance([lax.ppermute(*send) for send in grad_flow.sends])
    group_grad = grad_flow.value

    grad_heads = block_project(group_grad, out_blocks)
    grad_mixed = grad_heads.reshape(query_heads * group_rows, head_dim)
    delta = jnp.sum(grad_mixed.astype(F32) * mixed_full, axis=1)
    grad_queries, grad_keys_values = attend_back(
        place,
        queries,
        grad_mixed,
        keys_values,
        1.0 / totals.reshape(1, -1),
        delta[None, :],
        query_pos[None, :],
        first_pos[None, :],
        scale,
        group_rows,
    )
    group_grad, grad_queries, grad_keys_values = stage(
        [reduce[0].cross(), reduce[1].near(1), reduce[0].y(0), reduce[1].y(0)],
        [group_grad, grad_queries, grad_keys_values],
    )
    grad_queries = grad_queries.reshape(query_heads, group_rows, head_dim)

    late = 2
    main = 3 * ffn_blocks - late
    cap = -(-main // data_count)
    places = -(-max(cap * data_count, 3 * ffn_blocks) // TRIO) * TRIO
    def weight_sums(outer):
        cut = outer.reshape(outer.shape[0], data_count, rows_dp, head_dim)
        return Flow(ring.scatter(lambda i: lax.dynamic_index_in_dim(cut, i, 1, keepdims=False), outer.shape[0] // 2))

    key_flow = Flow(
        ring.scatter(lambda i: lax.dynamic_index_in_dim(grad_keys_values, i, 0, keepdims=False), key_heads)
    )
    pick = lambda own, other: (jnp.where(parity == 1, other, own), jnp.where(parity == 1, own, other))
    low_early, high_early = pick(*reduce[0].value())
    outer, low_early, high_early = stage(
        [key_flow, reduce[1].cross(), out_flow],
        [block_outer([group_in, group_grad], [grad_queries, mixed_heads], model_width), low_early, high_early],
    )
    low_late, high_late = pick(*reduce[1].value())
    first_flow = weight_sums(outer)
    weight_grads, new_momentum, grams = stage(
        [key_flow, first_flow],
        ffn_moment(low_early, low_late, high_early, high_late, momentum, gate_mark, ffn_blocks, places),
    )
    gram_flow = Flow(gram_sums(ring, grams, cap))
    stage([key_flow, first_flow, gram_flow])
    while key_flow.sends is not None:
        stage([key_flow, first_flow, gram_flow])
    key_value_sums = key_flow.value
    grad_keys = (key_value_sums[:key_heads] * scale).astype(BF16)
    grad_values = key_value_sums[key_heads:].astype(BF16)
    grad_keys_values = jnp.concatenate([grad_keys, grad_values], axis=0)
    (outer,) = stage([first_flow, gram_flow], [block_outer([group_in], [grad_keys_values], model_width)])
    finish(first_flow)
    second_flow = weight_sums(outer)
    pairs = [k for k in range(gate_mark // 2) if not query_heads <= 2 * k < out_mark]
    grad_projected = jnp.concatenate([grad_queries, grad_keys_values], axis=0)
    *attn_dx, weight_grads, new_momentum, first_grams = stage(
        [second_flow, gram_flow],
        [
            *block_back(grad_projected, qkv_blocks),
            *attn_moment(first_flow.value, pairs, momentum, weight_grads, new_momentum),
        ],
    )
    last_flow = Flow(scatter_rows(*attn_dx, HEAD_MOVES))
    finish(gram_flow)
    state, sweep = newton_start(gram_flow.value, growth), 0
    while second_flow.sends is not None:
        if sweep < 3:
            state = newton_sweep(state, sweep)
            sweep += 1
        state = stage([second_flow, last_flow, out_flow], state)
    finish(last_flow, out_flow)
    block_out = (residual + out_flow.value).astype(BF16)
    grad_input_norm, grad_gain_one = norm_one_back(last_flow.value)
    grad_input = grad_residual + grad_input_norm
    gain_flow = Flow(total_sum(jnp.stack([grad_gain_one, grad_gain_two])))
    weight_grads, new_momentum, second_grams = attn_moment(
        second_flow.value, list(range(query_heads // 2, out_mark // 2)), momentum, weight_grads, new_momentum
    )
    late_count = gate_mark + late
    late_cap = -(-late_count // data_count)
    late_grams = jnp.concatenate([first_grams, second_grams, grams[main : main + late]], axis=0)
    late_grams = jnp.pad(late_grams, ((0, late_cap * data_count - late_count), (0, 0), (0, 0), (0, 0)))
    late_gram_flow = Flow(gram_sums(ring, late_grams, late_cap))
    while sweep < NEWTON_STEPS:
        state = newton_sweep(state, sweep)
        sweep += 1
        state = stage([late_gram_flow, gain_flow], state)
    factor_flow = Flow(all_factors(ring, state[1]))
    while late_gram_flow.sends is not None:
        stage([late_gram_flow, factor_flow, gain_flow])
    (late_factors,) = stage([factor_flow, gain_flow], [newton_factor(late_gram_flow.value, growth)])
    late_factor_flow = Flow(all_factors(ring, late_factors))
    stage([late_factor_flow, factor_flow])
    finish(factor_flow)
    factors = factor_flow.value

    threes = main // TRIO
    early_spots = [(gate_mark // TRIO + k, [TRIO * k + i for i in range(TRIO)]) for k in range(threes)]
    new_weights = []
    for k in range(0, threes, 3):
        new_weights = stage(
            [late_factor_flow, gain_flow],
            [renew(weights, new_momentum, factors, early_spots[k : k + 3], new_weights)],
        )
    finish(late_factor_flow, gain_flow)
    gain_grads = gain_flow.value
    rest = jnp.concatenate([late_factor_flow.value[:late_count], factors[TRIO * threes : main]], axis=0)
    blocks_of = [2 * pair + i for pair in pairs for i in range(2)] + list(range(query_heads, out_mark))
    blocks_of += [gate_mark + main + k for k in range(late)] + [gate_mark + k for k in range(TRIO * threes, main)]
    late_spots = [
        (spot, [blocks_of.index(TRIO * spot + i) for i in range(TRIO)])
        for spot in sorted({block // TRIO for block in blocks_of})
    ]
    new_weights = renew(weights, new_momentum, rest, late_spots, new_weights)

    new_gain_first = BETA_ONE * gain_first + (1.0 - BETA_ONE) * gain_grads
    new_gain_second = BETA_TWO * gain_second + (1.0 - BETA_TWO) * gain_grads * gain_grads
    first_hat = new_gain_first / (1.0 - BETA_ONE**UPDATE_STEP)
    second_hat = new_gain_second / (1.0 - BETA_TWO**UPDATE_STEP)
    new_gains = gains - ADAM_RATE * first_hat / (jnp.sqrt(second_hat) + ADAM_EPS)
    back = lambda array: jnp.transpose(array, (1, 0, 2))
    return (
        block_out,
        grad_input,
        back(weight_grads),
        back(new_momentum),
        back(new_weights),
        gain_grads,
        new_gain_first,
        new_gain_second,
        new_gains,
    )


def solution(mesh):
    return jax.shard_map(
        on_device,
        mesh=mesh,
        in_specs=(
            P(("dp", "head"), None),
            P(("dp", "head"), None),
            P(("dp", "head")),
            P("dp", "head", None),
            P("dp", "head", None),
            P(),
            P(),
            P(),
        ),
        out_specs=(
            P(("dp", "head"), None),
            P(("dp", "head"), None),
            P("dp", "head", None),
            P("dp", "head", None),
            P("dp", "head", None),
            P(),
            P(),
            P(),
            P(),
        ),
        check_vma=False,
    )
```

```python
import functools
import math

import jax
import jax.numpy as jnp
from jax import lax
from jax.experimental import pallas as pl
from jax.experimental.pallas import tpu as pltpu
from jax.sharding import PartitionSpec as P

H = 8
KV = 4
FF = 9216
NEWTON_STEPS = 5
UPDATE_STEP = 10

NORM_EPS = 1e-06
SOFT_CAP = 50.0
MUON_RATE = 0.2
MUON_DECAY = 0.01
MUON_BETA = 0.95
ADAM_RATE = 0.3
BETA_ONE = 0.9
BETA_TWO = 0.95
ADAM_EPS = 1e-08
NEWTON_LINEAR = 3.4445
NEWTON_SQUARE = -4.775
NEWTON_CUBIC = 2.0315
TOP_PRECISION = lax.Precision.HIGHEST

BF16 = jnp.bfloat16
F32 = jnp.float32
VMEM_LIMIT = 62 * 1024 * 1024
NN = (((1,), (0,)), ((), ()))
NT = (((1,), (1,)), ((), ()))
TN = (((0,), (0,)), ((), ()))


def mm(a, b, dims):
    return lax.dot_general(a, b, dims, preferred_element_type=F32)


def rms_scale(rows, gain):
    inverse = lax.rsqrt(jnp.mean(rows * rows, axis=-1, keepdims=True) + NORM_EPS)
    return rows * inverse * gain


class Flow:
    def __init__(self, steps):
        self.steps = steps
        self.value = None
        self.sends = None
        self.advance(None)

    def advance(self, arrived):
        try:
            self.sends = self.steps.send(arrived)
        except StopIteration as stop:
            self.sends = None
            self.value = stop.value


def stage(flows, extra=(), idle=()):
    flows = [flow for flow in flows if flow.sends is not None]
    idle = [flow for flow in idle if flow.sends is not None and flow not in flows]
    arrived = [[lax.ppermute(*send) for send in flow.sends] for flow in flows]
    held = [[send[0] for send in flow.sends] for flow in idle]
    arrived, held, extra = lax.optimization_barrier((arrived, held, list(extra)))
    for flow, got in zip(flows, arrived):
        flow.advance(got)
    for flow, kept in zip(idle, held):
        flow.sends = [(value,) + send[1:] for value, send in zip(kept, flow.sends)]
    return extra


def run(steps):
    flow = Flow(steps)
    while flow.sends is not None:
        flow.advance([lax.ppermute(*send) for send in flow.sends])
    return flow.value


def finish(*flows):
    while any(flow.sends is not None for flow in flows):
        stage(flows)


def swap(value, axis, mask):
    size = lax.axis_size(axis)
    return (value, axis, [(i, i ^ mask) for i in range(size)])


def head_gather(rows):
    (other,) = yield [swap(rows, "head", 2)]
    pair = jnp.concatenate([rows, other], axis=0)
    (other,) = yield [swap(pair, "head", 1)]
    return jnp.concatenate([pair, other], axis=0)


def wide_gather(rows):
    (other,) = yield [swap(rows, "dp", 4)]
    both = jnp.concatenate([rows, other], axis=0)
    (other,) = yield [swap(both, "head", 2)]
    pair = jnp.concatenate([both, other], axis=0)
    (other,) = yield [swap(pair, "head", 1)]
    return [pair, other]


def add_low(kept, other):
    return (kept.astype(F32) + other.astype(F32)).astype(BF16)


def scatter_rows(kept, sent, moves):
    for k, (axis, mask) in enumerate(moves):
        (other,) = yield [swap(sent, axis, mask)]
        part = kept.astype(F32) + other.astype(F32)
        if k < len(moves) - 1:
            half = part.shape[0] // 2
            kept, sent = part[:half], part[half:].astype(BF16)
    return part


HEAD_MOVES = (("head", 1), ("head", 2))
WIDE_MOVES = (("head", 1), ("head", 2), ("dp", 4))


def total_sum(value):
    for axis in ("head", "dp"):
        mask = 1
        while mask < lax.axis_size(axis):
            (other,) = yield [swap(value, axis, mask)]
            value = value + other
            mask *= 2
    return value


class Ring:
    def __init__(self):
        size = lax.axis_size("dp")
        order = list(range(0, size, 2)) + list(range(size - 1, 0, -2))
        around = [[order[(order.index(i) + offset) % size] for offset in range(size)] for i in range(size)]
        self.size = size
        self.around = jnp.array(around, jnp.int32)[lax.axis_index("dp")]
        self.up = [(order[k], order[(k + 1) % size]) for k in range(size)]
        self.down = [(order[(k + 1) % size], order[k]) for k in range(size)]

    def index(self, offset):
        return self.around[offset % self.size]

    def gather(self, value, mid):
        half = self.size // 2
        zeros = (0,) * (value.ndim - 1)
        out = jnp.zeros((self.size,) + value.shape, value.dtype)
        out = lax.dynamic_update_index_in_dim(out, value, self.index(0), 0)
        ahead, back = value, value
        for step in range(1, half):
            ahead, back = yield [(ahead, "dp", self.up), (back, "dp", self.down)]
            out = lax.dynamic_update_index_in_dim(out, ahead, self.index(-step), 0)
            out = lax.dynamic_update_index_in_dim(out, back, self.index(step), 0)
        first, second = yield [(ahead[:mid], "dp", self.up), (back[mid:], "dp", self.down)]
        far = self.index(half)
        out = lax.dynamic_update_slice(out, first[None], (far, 0) + zeros)
        return lax.dynamic_update_slice(out, second[None], (far, mid) + zeros)

    def scatter(self, take, mid):
        half = self.size // 2
        far = take(self.index(half))
        kind = far.dtype
        up, down = yield [(far[:mid], "dp", self.up), (far[mid:], "dp", self.down)]
        for step in range(half - 1, 0, -1):
            part = take(self.index(step)).astype(F32)
            ahead = jnp.concatenate([part[:mid] + up, part[mid:]]) if step == half - 1 else part + up
            part = take(self.index(-step)).astype(F32)
            back = jnp.concatenate([part[:mid], part[mid:] + down]) if step == half - 1 else part + down
            up, down = yield [(ahead.astype(kind), "dp", self.up), (back.astype(kind), "dp", self.down)]
        return take(self.index(0)).astype(F32) + up.astype(F32) + down.astype(F32)


def once(sends, take):
    def steps():
        take((yield sends))

    return Flow(steps())


SIDE_BIT = 2


def plane_classes():
    planes = range(lax.axis_size("dp") // 2)
    kept = [m for m in planes if m & 1 == 0]
    passed = [m for m in planes if m & 1 == 1]
    return {0: [0], 1: [1], 2: [m for m in passed if m != 1], 3: [m for m in kept if m]}


class Spread:
    def __init__(self, mine, other):
        self.mine, self.other = mine, other
        self.pieces = {0: mine}

    def move(self, moves):
        def take(arrived):
            for (_, _, _, number), piece in zip(moves, arrived):
                self.pieces[number] = piece

        return once([swap(value, "dp", offset << 1 | bit) for value, offset, bit, _ in moves], take)

    def cross(self):
        group = plane_classes()[3]
        return self.move([(self.other if m & SIDE_BIT else self.mine, m, 0, m << 1) for m in group])

    def near(self, key):
        group = plane_classes()[key]
        return self.move([(self.pieces[m << 1], 1, 0, (m ^ 1) << 1) for m in group])

    def y(self, key):
        group = plane_classes()[key]
        return self.move([(self.pieces[m << 1], 0, 1, m << 1 | 1) for m in group])

    def value(self):
        return [self.pieces[k] for k in range(lax.axis_size("dp"))]


class Reduce:
    def __init__(self, rows):
        self.rows = rows
        self.parts = {}
        self.sums = [None, None]

    def part(self, offset):
        terms = [term.astype(F32) for term in self.parts[offset]]
        return functools.reduce(jnp.add, terms)

    def hold(self, offset, *terms):
        self.parts.setdefault(offset, []).extend(terms)

    def y(self, key):
        group = plane_classes()[key]

        def take(arrived):
            for offset, got in zip(group, arrived):
                self.hold(offset, self.rows(offset << 1), got)

        return once([swap(self.rows(offset << 1 | 1), "dp", 1) for offset in group], take)

    def near(self, key):
        group = plane_classes()[key]

        def take(arrived):
            for offset, got in zip(group, arrived):
                self.hold(offset ^ 1, got)

        return once([swap(self.part(offset).astype(BF16), "dp", 2) for offset in group], take)

    def cross(self):
        group = plane_classes()[3]

        def take(arrived):
            for offset, got in zip(group, arrived):
                self.add(1 if offset & SIDE_BIT else 0, got.astype(F32))

        return once([swap(self.part(offset).astype(BF16), "dp", offset << 1) for offset in group], take)

    def add(self, side, value):
        self.sums[side] = value if self.sums[side] is None else self.sums[side] + value

    def value(self):
        self.add(0, self.part(0))
        return self.sums


def params(**more):
    return pltpu.CompilerParams(vmem_limit_bytes=VMEM_LIMIT, **more)


TRIO = 3


def cast_blocks(blocks, count):
    _, r, c = blocks.shape

    def body(x_ref, o_ref):
        o_ref[...] = x_ref[...].astype(BF16)

    spec = pl.BlockSpec((TRIO, r, c), lambda k: (k, 0, 0))
    return pl.pallas_call(
        body,
        grid=(count // TRIO,),
        in_specs=[spec],
        out_specs=spec,
        out_shape=jax.ShapeDtypeStruct((count, r, c), BF16),
        compiler_params=params(),
        cost_estimate=pl.CostEstimate(flops=0, bytes_accessed=6 * count * r * c, transcendentals=0),
    )(blocks)


def pack_units(parity, blocks, first, kind_blocks, early):
    _, r, c = blocks.shape
    h = c // 2
    full = kind_blocks // 2
    each = kind_blocks // TRIO
    u, v = early * c, (full - early) * c + h

    def body(s_ref, *refs):
        parts, outs = refs[:each], refs[each:]

        def tile(f):
            return parts[f // TRIO].at[f % TRIO]

        for turn in range(2):

            @pl.when(s_ref[0] == turn)
            def _():
                for k in range(2):
                    side = turn ^ k
                    for i in range(full):
                        value = tile(side * full + i)[...].astype(BF16)
                        if i < early:
                            outs[2 * k][:, i * c : (i + 1) * c] = value
                        else:
                            outs[2 * k + 1][:, (i - early) * c : (i - early + 1) * c] = value
                    rest = tile(2 * full)[:, side * h : (side + 1) * h]
                    outs[2 * k + 1][:, v - h :] = rest.astype(BF16)

    def part(i):
        return pl.BlockSpec((TRIO, r, c), lambda k, s: (first // TRIO + each * k + i, 0, 0))

    wide = pl.BlockSpec((None, r, u), lambda k, s: (k, 0, 0))
    slim = pl.BlockSpec((None, r, v), lambda k, s: (k, 0, 0))
    shapes = [jax.ShapeDtypeStruct((3, r, u), BF16), jax.ShapeDtypeStruct((3, r, v), BF16)]
    return pl.pallas_call(
        body,
        grid_spec=pltpu.PrefetchScalarGridSpec(
            num_scalar_prefetch=1,
            grid=(3,),
            in_specs=[part(i) for i in range(each)],
            out_specs=[wide, slim, wide, slim],
        ),
        out_shape=shapes + shapes,
        compiler_params=params(),
        cost_estimate=pl.CostEstimate(flops=0, bytes_accessed=18 * kind_blocks * r * c, transcendentals=0),
    )(parity, *([blocks] * each))


def block_project(rows, blocks):
    t = rows.shape[0]
    count, d, c = blocks.shape

    def body(x_ref, w_ref, o_ref):
        o_ref[...] = mm(x_ref[...], w_ref[...], NN).astype(BF16)

    return pl.pallas_call(
        body,
        grid=(count,),
        in_specs=[
            pl.BlockSpec((t, d), lambda b: (0, 0)),
            pl.BlockSpec((None, d, c), lambda b: (b, 0, 0)),
        ],
        out_specs=pl.BlockSpec((None, t, c), lambda b: (b, 0, 0)),
        out_shape=jax.ShapeDtypeStruct((count, t, c), BF16),
        compiler_params=params(),
        cost_estimate=pl.CostEstimate(
            flops=2 * count * t * d * c, bytes_accessed=2 * (t * d + count * (d * c + t * c)), transcendentals=0
        ),
    )(rows, blocks)


def block_back(cols, blocks):
    count, t, c = cols.shape
    d = blocks.shape[1]
    half = t // 2

    def body(x_ref, w_ref, o_ref, p_ref, acc_ref):
        b = pl.program_id(0)

        @pl.when(b == 0)
        def _():
            acc_ref[...] = jnp.zeros_like(acc_ref)

        acc_ref[...] += mm(x_ref[...], w_ref[...], NT)

        @pl.when(b == count - 1)
        def _():
            o_ref[...] = acc_ref[:half, :].astype(BF16)
            p_ref[...] = acc_ref[half:, :].astype(BF16)

    result = pl.BlockSpec((half, d), lambda b: (0, 0))
    return pl.pallas_call(
        body,
        grid=(count,),
        in_specs=[
            pl.BlockSpec((None, t, c), lambda b: (b, 0, 0)),
            pl.BlockSpec((None, d, c), lambda b: (b, 0, 0)),
        ],
        out_specs=[result, result],
        out_shape=[jax.ShapeDtypeStruct((half, d), BF16)] * 2,
        scratch_shapes=[pltpu.VMEM((t, d), F32)],
        compiler_params=params(),
        cost_estimate=pl.CostEstimate(
            flops=2 * count * t * d * c, bytes_accessed=2 * (t * d + count * (d * c + t * c)), transcendentals=0
        ),
    )(cols, blocks)


def block_outer(rows, cols, d):
    t = rows[0].shape[0]
    c = cols[0].shape[2]
    starts = [0]
    for col in cols:
        starts.append(starts[-1] + col.shape[0])
    count = len(rows)
    total = starts[-1]

    def body(*refs):
        o_ref, t_ref = refs[2 * count :]
        b = pl.program_id(0)
        for k in range(count):

            @pl.when(b == starts[k])
            def _():
                t_ref[...] = refs[k][...].T

            @pl.when((b >= starts[k]) & (b < starts[k + 1]))
            def _():
                o_ref[...] = mm(t_ref[...], refs[count + k][...], NN).astype(BF16)

    def col_at(k):
        return pl.BlockSpec((None, t, c), lambda b: (jnp.clip(b - starts[k], 0, starts[k + 1] - starts[k] - 1), 0, 0))

    return pl.pallas_call(
        body,
        grid=(total,),
        in_specs=[pl.BlockSpec((t, d), lambda b: (0, 0))] * count + [col_at(k) for k in range(count)],
        out_specs=pl.BlockSpec((None, d, c), lambda b: (b, 0, 0)),
        out_shape=jax.ShapeDtypeStruct((total, d, c), BF16),
        scratch_shapes=[pltpu.VMEM((d, t), BF16)],
        compiler_params=params(),
        cost_estimate=pl.CostEstimate(
            flops=2 * total * t * d * c,
            bytes_accessed=2 * (count * t * d + total * (d * c + t * c)),
            transcendentals=0,
        ),
    )(*rows, *cols)


def in_group(local, width, head_shift):
    quarter = width // 4
    low = jnp.bitwise_and(local, quarter - 1)
    one = jnp.where(jnp.bitwise_and(local, quarter) != 0, 2 * quarter, 0)
    two = jnp.where(jnp.bitwise_and(local, 2 * quarter) != 0, quarter, 0)
    return jnp.bitwise_xor(low + one + two, head_shift)


def key_position(block, width, head_shift, shape, axis):
    local = lax.broadcasted_iota(jnp.int32, shape, axis)
    return block * width + in_group(local, width, head_shift)


def attend(place, queries, keys_values, query_pos, first_pos, scale, p):
    m, e = queries.shape
    n = keys_values.shape[0]
    step = 256

    def body(place_ref, q_ref, kv_ref, pos_ref, first_ref, low_ref, full_ref, sum_ref, acc_ref, tot_ref):
        j = pl.program_id(0)

        @pl.when(j == 0)
        def _():
            acc_ref[...] = jnp.zeros_like(acc_ref)
            tot_ref[...] = jnp.zeros_like(tot_ref)

        @pl.when(j <= place_ref[0])
        def _():
            key_pos = key_position(j, p, place_ref[1], (1, p), 1)
            for r in range(0, m, step):
                rows = pl.ds(r, step)
                raw = mm(q_ref[rows, :], kv_ref[:p, :], NT)
                soft = SOFT_CAP * jnp.tanh(raw * (scale / SOFT_CAP))
                seen = (key_pos >= first_ref[rows, :]) & (key_pos <= pos_ref[rows, :])
                terms = jnp.where(seen, jnp.exp(soft), 0.0)
                tot_ref[rows, :] += jnp.sum(terms, axis=1, keepdims=True)
                acc_ref[rows, :] += mm(terms.astype(BF16), kv_ref[p:, :], NN)

        @pl.when(j == n - 1)
        def _():
            total = tot_ref[...]
            mixed = acc_ref[...] / total
            full_ref[...] = mixed
            low_ref[...] = mixed.astype(BF16)
            sum_ref[...] = total

    whole = lambda shape: pl.BlockSpec(shape, lambda j, s: (0, 0))
    return pl.pallas_call(
        body,
        grid_spec=pltpu.PrefetchScalarGridSpec(
            num_scalar_prefetch=1,
            grid=(n,),
            in_specs=[
                whole((m, e)),
                pl.BlockSpec((None, 2 * p, e), lambda j, s: (jnp.minimum(j, s[0]), 0, 0)),
                whole((m, 1)),
                whole((m, 1)),
            ],
            out_specs=[whole((m, e)), whole((m, e)), whole((m, 1))],
            scratch_shapes=[pltpu.VMEM((m, e), F32), pltpu.VMEM((m, 1), F32)],
        ),
        out_shape=[
            jax.ShapeDtypeStruct((m, e), BF16),
            jax.ShapeDtypeStruct((m, e), F32),
            jax.ShapeDtypeStruct((m, 1), F32),
        ],
        compiler_params=params(),
        cost_estimate=pl.CostEstimate(
            flops=4 * m * n * p * e, bytes_accessed=4 * n * p * e, transcendentals=2 * m * n * p
        ),
    )(place, queries, keys_values, query_pos, first_pos)


def attend_back(place, queries, grads, keys_values, inverse, delta, query_pos, first_pos, scale, p):
    m, e = queries.shape
    n = keys_values.shape[0]
    step = 256

    def body(
        place_ref, q_ref, g_ref, kv_ref, inv_ref, delta_ref, pos_ref, first_ref, dq_ref, dkv_ref, acc_ref, dk_ref, dv_ref
    ):
        j = pl.program_id(0)

        @pl.when(j == 0)
        def _():
            acc_ref[...] = jnp.zeros_like(acc_ref)

        @pl.when(j <= place_ref[0])
        def _():
            key_pos = key_position(j, p, place_ref[1], (p, 1), 0)
            for r in range(0, m, step):
                rows = pl.ds(r, step)
                raw = mm(kv_ref[:p, :], q_ref[rows, :], NT)
                capped = jnp.tanh(raw * (scale / SOFT_CAP))
                seen = (key_pos >= first_ref[:, rows]) & (key_pos <= pos_ref[:, rows])
                probs = jnp.where(seen, jnp.exp(SOFT_CAP * capped), 0.0) * inv_ref[:, rows]
                grad_probs = mm(kv_ref[p:, :], g_ref[rows, :], NT)
                grad_raw = probs * (grad_probs - delta_ref[:, rows]) * (1.0 - capped * capped)
                grad_low = grad_raw.astype(BF16)
                value_part = mm(probs.astype(BF16), g_ref[rows, :], NN)
                key_part = mm(grad_low, q_ref[rows, :], NN)
                if r == 0:
                    dv_ref[...] = value_part
                    dk_ref[...] = key_part
                else:
                    dv_ref[...] += value_part
                    dk_ref[...] += key_part
                acc_ref[rows, :] += mm(grad_low, kv_ref[:p, :], TN)
            dkv_ref[0] = dk_ref[...].astype(BF16)
            dkv_ref[1] = dv_ref[...].astype(BF16)

        @pl.when(j > place_ref[0])
        def _():
            dkv_ref[...] = jnp.zeros_like(dkv_ref)

        @pl.when(j == n - 1)
        def _():
            dq_ref[...] = (acc_ref[...] * scale).astype(BF16)

    whole = lambda shape: pl.BlockSpec(shape, lambda j, s: (0, 0))
    return pl.pallas_call(
        body,
        grid_spec=pltpu.PrefetchScalarGridSpec(
            num_scalar_prefetch=1,
            grid=(n,),
            in_specs=[
                whole((m, e)),
                whole((m, e)),
                pl.BlockSpec((None, 2 * p, e), lambda j, s: (jnp.minimum(j, s[0]), 0, 0)),
                whole((1, m)),
                whole((1, m)),
                whole((1, m)),
                whole((1, m)),
            ],
            out_specs=[whole((m, e)), pl.BlockSpec((None, 2, p, e), lambda j, s: (j, 0, 0, 0))],
            scratch_shapes=[pltpu.VMEM((m, e), F32), pltpu.VMEM((p, e), F32), pltpu.VMEM((p, e), F32)],
        ),
        out_shape=[jax.ShapeDtypeStruct((m, e), BF16), jax.ShapeDtypeStruct((n, 2, p, e), BF16)],
        compiler_params=params(),
        cost_estimate=pl.CostEstimate(
            flops=10 * m * n * p * e, bytes_accessed=8 * n * p * e, transcendentals=2 * m * n * p
        ),
    )(place, queries, grads, keys_values, inverse, delta, query_pos, first_pos)


def gelu_pair(gate):
    outer = math.sqrt(2.0 / math.pi)
    square = gate * gate
    bent = jnp.tanh(outer * gate * (1.0 + 0.044715 * square))
    half = 0.5 * (1.0 + bent)
    slope = half + 0.5 * gate * (1.0 - bent * bent) * outer * (1.0 + 3.0 * 0.044715 * square)
    return gate * half, slope


def ffn_front(place, rows, cots, early, late):
    part_rows, d = rows[0].shape
    t = 2 * part_rows
    count = len(early)
    r = early[0].shape[1]
    u, v = early[0].shape[2], late[0].shape[2]
    tall = min(512, t)
    wide = d // 3
    cuts = [(k, min(256, u + v - k)) for k in range(0, u + v, 256)]

    def body(place_ref, x0, x1, y0, y1, *refs):
        early_refs, late_refs = refs[:count], refs[count : 2 * count]
        refs = refs[2 * count :]
        hs_ref, w_out = refs[:2]
        grad_refs = refs[2 : 2 + count], refs[2 + count : 2 + 2 * count]
        x, y, w, xt, yt, hs, row_sems, sems, out_sems, grad_sems = refs[2 + 2 * count :]
        row_copies = []
        for k, (source, target) in enumerate(((x0, x), (x1, x), (y0, y), (y1, y))):
            target = target.at[pl.ds((k % 2) * part_rows, part_rows), :]
            row_copies.append(pltpu.make_async_copy(source, target, row_sems.at[k]))
            row_copies[k].start()
        copies = []
        chunks = ((early_refs, pl.ds(0, u)), (late_refs, pl.ds(u, v)))

        def spot(k):
            return pl.ds(pl.multiple_of(jnp.bitwise_xor(place_ref[0], k) * r, 16) if count > 1 else 0, r)

        for k in range(count):
            for way, (sources, lanes) in enumerate(chunks):
                copy = pltpu.make_async_copy(sources[k], w.at[:, spot(k), lanes], sems.at[way, k])
                copy.start()
                copies.append(copy)
        for copy in row_copies:
            copy.wait()

        @pl.loop(0, d // 256)
        def _(k):
            cols = pl.ds(pl.multiple_of(k * 256, 256), 256)
            xt[cols, :] = x[:, cols].T
            yt[cols, :] = y[:, cols].T

        for copy in copies:
            copy.wait()
        kept = pltpu.make_async_copy(w, w_out, out_sems.at[0])
        kept.start()

        @pl.loop(0, t // tall)
        def _(i):
            part = pl.ds(pl.multiple_of(i * tall, tall), tall)
            for start, size in cuts:
                units = pl.ds(start, size)
                gate = mm(x[part, :], w[0, :, units], NN)
                up = mm(x[part, :], w[1, :, units], NN)
                grad = mm(y[part, :], w[2, :, units], NN)
                active, slope = gelu_pair(gate)
                hs[0, part, units] = (active * up).astype(BF16)
                hs[1, part, units] = (grad * up * slope).astype(BF16)
                hs[2, part, units] = (grad * active).astype(BF16)

        sides = pltpu.make_async_copy(hs, hs_ref, out_sems.at[1])
        sides.start()
        kept.wait()
        copies = []
        for kind, (left, right) in enumerate(((xt, 1), (xt, 2), (yt, 0))):

            @pl.loop(0, d // wide)
            def _(k):
                cols = pl.ds(pl.multiple_of(k * wide, wide), wide)
                w[kind, cols, :] = mm(left[cols, :], hs[right], NN).astype(BF16)

            for k in range(count):
                for way, (_, lanes) in enumerate(chunks):
                    target = grad_refs[way][k].at[kind]
                    copy = pltpu.make_async_copy(w.at[kind, spot(k), lanes], target, grad_sems.at[kind, way, k])
                    copy.start()
                    copies.append(copy)
        sides.wait()
        for copy in copies:
            copy.wait()

    apart = pl.BlockSpec(memory_space=pl.ANY)
    return pl.pallas_call(
        body,
        grid_spec=pltpu.PrefetchScalarGridSpec(
            num_scalar_prefetch=1,
            grid=(1,),
            in_specs=[apart] * (4 + 2 * count),
            out_specs=[apart] * (2 + 2 * count),
            scratch_shapes=[
                pltpu.VMEM((t, d), BF16),
                pltpu.VMEM((t, d), BF16),
                pltpu.VMEM((3, d, u + v), BF16),
                pltpu.VMEM((d, t), BF16),
                pltpu.VMEM((d, t), BF16),
                pltpu.VMEM((3, t, u + v), BF16),
                pltpu.SemaphoreType.DMA((4,)),
                pltpu.SemaphoreType.DMA((2, count)),
                pltpu.SemaphoreType.DMA((2,)),
                pltpu.SemaphoreType.DMA((3, 2, count)),
            ],
        ),
        out_shape=[
            jax.ShapeDtypeStruct((3, t, u + v), BF16),
            jax.ShapeDtypeStruct((3, d, u + v), BF16),
            *[jax.ShapeDtypeStruct((3, r, u), BF16)] * count,
            *[jax.ShapeDtypeStruct((3, r, v), BF16)] * count,
        ],
        compiler_params=params(),
        cost_estimate=pl.CostEstimate(
            flops=12 * t * d * (u + v), bytes_accessed=12 * d * (u + v) + 4 * t * d, transcendentals=t * (u + v)
        ),
    )(place, *rows, *cots, *early, *late)


def ffn_back(sides, blocks):
    _, t, u = sides.shape
    d = blocks.shape[1]
    wide = 256
    half = t // 2

    def body(s_ref, w_ref, *refs):
        for k in range(2):
            part = pl.ds(k * half, half)
            refs[k][...] = mm(s_ref[0, part, :], w_ref[2], NT).astype(BF16)
            refs[2 + k][...] = (mm(s_ref[1, part, :], w_ref[0], NT) + mm(s_ref[2, part, :], w_ref[1], NT)).astype(BF16)

    return pl.pallas_call(
        body,
        grid=(d // wide,),
        in_specs=[
            pl.BlockSpec((3, t, u), lambda k: (0, 0, 0), pipeline_mode=pl.Buffered(1)),
            pl.BlockSpec((3, wide, u), lambda k: (0, k, 0)),
        ],
        out_specs=[pl.BlockSpec((half, wide), lambda k: (0, k))] * 4,
        out_shape=[jax.ShapeDtypeStruct((half, d), BF16)] * 4,
        compiler_params=params(),
        cost_estimate=pl.CostEstimate(
            flops=6 * t * d * u, bytes_accessed=6 * d * u + 6 * t * u + 4 * t * d, transcendentals=0
        ),
    )(sides, blocks)


def gram_parts(m):
    h = m.shape[1] // 2
    high = m.astype(BF16)
    low = (m - high.astype(F32)).astype(BF16)
    mixed = mm(high, low, TN)
    gram = mm(high, high, TN) + mm(low, low, TN) + mixed + mixed.T
    return gram[:h, :h], gram[:h, h:], gram[h:, h:]


def ffn_moment(low_early, low_late, high_early, high_late, momentum, first, blocks, places):
    total, r, c = momentum.shape
    early = low_early.shape[2] // c
    h = c // 2
    full = early + 1
    each = blocks // TRIO

    def body(le_ref, ll_ref, he_ref, hl_ref, m_ref, wg_ref, nm_ref, gram_ref):
        j = pl.program_id(0)

        @pl.when(j >= TRIO * each)
        def _():
            gram_ref[...] = jnp.zeros_like(gram_ref)

        for turn in range(each):

            @pl.when((j < TRIO * each) & (lax.rem(j, each) == turn))
            def _():
                for i in range(TRIO):
                    side, f = divmod(turn * TRIO + i, full)
                    if side == 2:
                        wg_ref[i, :, :h] = ll_ref[:, c:]
                        wg_ref[i, :, h:] = hl_ref[:, c:]
                    elif f < early:
                        wg_ref[i] = (le_ref, he_ref)[side][:, f * c : (f + 1) * c]
                    else:
                        wg_ref[i] = (ll_ref, hl_ref)[side][:, :c]

        @pl.when(j < TRIO * each)
        def _():
            for i in range(TRIO):
                new = MUON_BETA * m_ref[i] + wg_ref[i]
                nm_ref[i] = new
                gram_ref[i, 0], gram_ref[i, 1], gram_ref[i, 2] = gram_parts(new)

    kind = lambda j: (jnp.minimum(j // each, 2), 0, 0)
    block = lambda j: (first // TRIO + jnp.minimum(j, TRIO * each - 1), 0, 0)
    u, v = low_early.shape[2], low_late.shape[2]
    return pl.pallas_call(
        body,
        grid=(places // TRIO,),
        in_specs=[
            pl.BlockSpec((None, r, u), kind),
            pl.BlockSpec((None, r, v), kind),
            pl.BlockSpec((None, r, u), kind),
            pl.BlockSpec((None, r, v), kind),
            pl.BlockSpec((TRIO, r, c), block),
        ],
        out_specs=[
            pl.BlockSpec((TRIO, r, c), block),
            pl.BlockSpec((TRIO, r, c), block),
            pl.BlockSpec((TRIO, 3, h, h), lambda j: (j, 0, 0, 0)),
        ],
        out_shape=[
            jax.ShapeDtypeStruct((total, r, c), F32),
            jax.ShapeDtypeStruct((total, r, c), F32),
            jax.ShapeDtypeStruct((places, 3, h, h), F32),
        ],
        compiler_params=params(),
        cost_estimate=pl.CostEstimate(
            flops=6 * 3 * blocks * r * c * c, bytes_accessed=16 * 3 * blocks * r * c, transcendentals=0
        ),
    )(low_early, low_late, high_early, high_late, momentum)


def attn_moment(grads, pairs, momentum, weight_grads, new_momentum):
    count, r, c = grads.shape
    h = c // 2

    def body(s_ref, g_ref, m_ref, wg_in, nm_in, wg_ref, nm_ref, gram_ref):
        for i in range(2):
            new = MUON_BETA * m_ref[i] + g_ref[i]
            wg_ref[i] = g_ref[i]
            nm_ref[i] = new
            gram_ref[i, 0], gram_ref[i, 1], gram_ref[i, 2] = gram_parts(new)

    block = pl.BlockSpec((2, r, c), lambda j, s: (s[j], 0, 0))
    apart = pl.BlockSpec(memory_space=pl.ANY)
    return pl.pallas_call(
        body,
        grid_spec=pltpu.PrefetchScalarGridSpec(
            num_scalar_prefetch=1,
            grid=(count // 2,),
            in_specs=[pl.BlockSpec((2, r, c), lambda j, s: (j, 0, 0)), block, apart, apart],
            out_specs=[block, block, pl.BlockSpec((2, 3, h, h), lambda j, s: (j, 0, 0, 0))],
        ),
        out_shape=[
            jax.ShapeDtypeStruct(momentum.shape, F32),
            jax.ShapeDtypeStruct(momentum.shape, F32),
            jax.ShapeDtypeStruct((count, 3, h, h), F32),
        ],
        input_output_aliases={3: 0, 4: 1},
        compiler_params=params(),
        cost_estimate=pl.CostEstimate(
            flops=6 * count * r * c * c, bytes_accessed=16 * count * r * c, transcendentals=0
        ),
    )(jnp.array(pairs, jnp.int32), grads, momentum, weight_grads, new_momentum)


def renew(weights, momentum, factors, spots, updated):
    _, r, c = weights.shape
    h = c // 2
    steps = len(spots)
    table = jnp.array([spot for spot, _ in spots] + [f for _, places in spots for f in places], jnp.int32)

    def body(s_ref, w_ref, m_ref, *refs):
        factor_refs, o_ref = refs[:TRIO], refs[-1]
        for i in range(TRIO):
            left = m_ref[i, :, :h].astype(BF16)
            right = m_ref[i, :, h:].astype(BF16)
            first, off, last = factor_refs[i][0], factor_refs[i][1], factor_refs[i][2]
            start = mm(left, first, NN) + mm(right, off, NT)
            rest = mm(left, off, NN) + mm(right, last, NN)
            keep = 1.0 - MUON_RATE * MUON_DECAY
            o_ref[i, :, :h] = w_ref[i, :, :h] * keep - MUON_RATE * start
            o_ref[i, :, h:] = w_ref[i, :, h:] * keep - MUON_RATE * rest

    block = pl.BlockSpec((TRIO, r, c), lambda j, s: (s[j], 0, 0))

    def factor_at(i):
        return pl.BlockSpec((None, 3, h, h), lambda j, s: (s[steps + TRIO * j + i], 0, 0, 0))

    apart = [pl.BlockSpec(memory_space=pl.ANY)] * len(updated)
    return pl.pallas_call(
        body,
        grid_spec=pltpu.PrefetchScalarGridSpec(
            num_scalar_prefetch=1,
            grid=(steps,),
            in_specs=[block, block] + [factor_at(i) for i in range(TRIO)] + apart,
            out_specs=block,
        ),
        out_shape=jax.ShapeDtypeStruct(weights.shape, F32),
        input_output_aliases={3 + TRIO: 0} if updated else {},
        compiler_params=params(),
        cost_estimate=pl.CostEstimate(
            flops=2 * TRIO * steps * r * c * c, bytes_accessed=12 * TRIO * steps * r * c, transcendentals=0
        ),
    )(table, weights, momentum, *([factors] * TRIO), *updated)


def top(spec, a, b):
    return jnp.einsum(spec, a, b, precision=TOP_PRECISION)


def newton_start(grams, growth):
    eye = jnp.eye(grams.shape[-1], dtype=F32)
    norm = jnp.sqrt(jnp.sum(grams * eye, axis=(1, 2), keepdims=True))
    inverse = 1.0 / (norm + 1e-07)
    return [grams * (inverse * inverse), growth * inverse]


def newton_sweep(state, sweep):
    gram, factor = state
    eye = jnp.eye(gram.shape[-1], dtype=F32)
    square = top("bij,bjk->bik", gram, gram)
    poly = NEWTON_LINEAR * eye + NEWTON_SQUARE * gram + NEWTON_CUBIC * square
    factor = poly * factor if sweep == 0 else top("bij,bjk->bik", factor, poly)
    if sweep < NEWTON_STEPS - 1:
        gram = top("bij,bjk->bik", top("bij,bjk->bik", gram, poly), poly)
    return [gram, factor]


def newton_factor(grams, growth):
    state = newton_start(grams, growth)
    for sweep in range(NEWTON_STEPS):
        state = newton_sweep(state, sweep)
    return state[1]


def fold(squares):
    h = squares.shape[1] // 2
    return jnp.stack([squares[:, :h, :h], squares[:, :h, h:], squares[:, h:, h:]], axis=1)


def unfold(parts):
    first, off, last = parts[:, 0], parts[:, 1], parts[:, 2]
    upper = jnp.concatenate([first, off], axis=2)
    lower = jnp.concatenate([jnp.swapaxes(off, 1, 2), last], axis=2)
    return jnp.concatenate([upper, lower], axis=1)


def gram_sums(ring, parts, cap):
    h = parts.shape[2]
    parts = parts.reshape(-1, h, h)
    rows = 3 * cap
    mine = yield from ring.scatter(lambda i: lax.dynamic_slice_in_dim(parts, i * rows, rows, 0), rows // 2)
    return unfold(mine.reshape(cap, 3, h, h))


def all_factors(ring, factors):
    cap, c, _ = factors.shape
    parts = fold(factors.astype(BF16)).reshape(3 * cap, c // 2, c // 2)
    parts = yield from ring.gather(parts, 3 * cap // 2)
    return parts.reshape(ring.size * cap, 3, c // 2, c // 2)


def on_device(block_in, cotangent, seq_ids, weights, momentum, gains, gain_first, gain_second):
    tok_rows, model_width = block_in.shape
    rows_dp, group_blocks, head_dim = weights.shape
    head_count = lax.axis_size("head")
    data_count = lax.axis_size("dp")
    group_rows = tok_rows * head_count
    key_heads = KV // head_count
    query_heads = H // head_count
    ffn_blocks = FF // (head_dim * head_count)
    out_mark = query_heads + 2 * key_heads
    gate_mark = out_mark + query_heads
    half_dim = head_dim // 2
    full = ffn_blocks // 2
    scale = head_dim ** (-0.5)
    growth = math.sqrt(max(1.0, model_width / head_dim))
    data_index = lax.axis_index("dp")
    head_index = lax.axis_index("head")
    parity = (data_index >> 2) & 1
    ring = Ring()

    weights = jnp.transpose(weights, (1, 0, 2))
    momentum = jnp.transpose(momentum, (1, 0, 2))
    attn_low = cast_blocks(weights, gate_mark)
    inputs = block_in.astype(F32)
    normed_one, norm_one_back = jax.vjp(rms_scale, inputs, gains[0])
    ids_column = jnp.pad(seq_ids.astype(BF16)[:, None], ((0, 0), (0, 127)))

    early = full - 1
    mine_early, mine_late, other_early, other_late = pack_units(
        jnp.reshape(parity, (1,)), weights, gate_mark, ffn_blocks, early
    )
    spread = [Spread(mine_early, other_early), Spread(mine_late, other_late)]

    group_in = run(head_gather(jnp.concatenate([normed_one.astype(BF16), ids_column], axis=1)))
    qkv_parts = run(ring.gather(attn_low[:out_mark], out_mark // 2))
    qkv_blocks = jnp.transpose(qkv_parts, (1, 0, 2, 3)).reshape(out_mark, model_width, head_dim)
    cot_flow = Flow(wide_gather(cotangent))
    held = {"near0": spread[0].near(0), "cross": spread[1].cross(), "y0": spread[1].y(0), "near": spread[1].near(0)}
    group_in, qkv_blocks, attn_low = stage(
        [spread[0].cross(), spread[0].y(0)], [group_in, qkv_blocks, attn_low], idle=[cot_flow, *held.values()]
    )
    projected = block_project(group_in, qkv_blocks)
    queries = projected[:query_heads].reshape(query_heads * group_rows, head_dim)
    group_ids = group_in[:, model_width]
    kv_rows = 2 * key_heads * group_rows
    out_rows = query_heads * rows_dp
    id_rows = group_rows // head_dim
    packed = jnp.concatenate(
        [
            projected[query_heads:].reshape(kv_rows, head_dim),
            attn_low[out_mark:].reshape(out_rows, head_dim),
            jnp.pad(group_ids.reshape(id_rows, head_dim), ((0, 16 - id_rows), (0, 0))),
        ],
        axis=0,
    )
    keys_values = run(ring.gather(packed, packed.shape[0] // 32 * 16))
    out_blocks = keys_values[:, kv_rows : kv_rows + out_rows].reshape(data_count, query_heads, rows_dp, head_dim)
    out_blocks = jnp.transpose(out_blocks, (1, 0, 2, 3)).reshape(query_heads, model_width, head_dim)
    queries, keys_values, out_blocks = stage(
        [cot_flow, held.pop("near0"), spread[0].y(3)], [queries, keys_values, out_blocks], idle=held.values()
    )
    all_ids = keys_values[:, kv_rows + out_rows : kv_rows + out_rows + id_rows].reshape(-1)

    local = in_group(jnp.arange(group_rows, dtype=jnp.int32), group_rows, head_index * tok_rows)
    query_pos = data_index * group_rows + local
    first_pos = jnp.sum((all_ids[None, :] < group_ids[:, None]).astype(jnp.int32), axis=1)
    query_pos = jnp.tile(query_pos, query_heads)
    first_pos = jnp.tile(first_pos, query_heads)
    place = jnp.stack([data_index, head_index * tok_rows]).astype(jnp.int32)
    mixed_low, mixed_full, totals = attend(
        place, queries, keys_values, query_pos[:, None], first_pos[:, None], scale, group_rows
    )
    mixed_heads = mixed_low.reshape(query_heads, group_rows, head_dim)
    attn_add = run(scatter_rows(*block_back(mixed_heads, out_blocks), HEAD_MOVES))
    mixed_heads, mixed_full, totals, attn_add = stage(
        [spread[0].near(3), spread[0].y(1), held.pop("cross"), held.pop("y0"), cot_flow],
        [mixed_heads, mixed_full, totals, attn_add],
        idle=held.values(),
    )
    residual = inputs + attn_add
    normed_two, norm_two_back = jax.vjp(rms_scale, residual, gains[1])
    wide_flow = Flow(wide_gather(normed_two.astype(BF16)))
    stage([wide_flow, spread[0].y(2), held.pop("near"), spread[1].near(3), spread[1].y(3)], idle=[cot_flow])
    stage([wide_flow, spread[1].y(1), spread[1].y(2)], idle=[cot_flow])
    stage([wide_flow, cot_flow])
    finish(wide_flow, cot_flow)

    def whole_rows(pieces):
        if rows_dp % 16 == 0:
            return pieces
        out = jnp.zeros((3, data_count) + pieces[0].shape[1:], BF16)
        for k, piece in enumerate(pieces):
            out = lax.dynamic_update_index_in_dim(out, piece, data_index ^ k, 1)
        return [out.reshape(3, model_width, -1)]

    ffn_sides, ffn_full, *ffn_grads = ffn_front(
        place, wide_flow.value, cot_flow.value, whole_rows(spread[0].value()), whole_rows(spread[1].value())
    )

    def taker(pieces):
        if len(pieces) > 1:
            return lambda k: pieces[k]
        cut = pieces[0].reshape(3, data_count, rows_dp, pieces[0].shape[2])
        return lambda k: lax.dynamic_index_in_dim(cut, data_index ^ k, 1, keepdims=False)

    pieces = len(ffn_grads) // 2
    reduce = [Reduce(taker(ffn_grads[:pieces])), Reduce(taker(ffn_grads[pieces:]))]
    first, second = ({key: part.y(key) for key in (0, 1, 2, 3)} for part in reduce)

    def waiting():
        return [*first.values(), *second.values()]

    starts = [second.pop(2), second.pop(3)]
    *down_part, dx_kept, dx_sent = stage(starts, ffn_back(ffn_sides, ffn_full), idle=waiting())
    out_flow = Flow(scatter_rows(*down_part, WIDE_MOVES))
    dx_flow = Flow(scatter_rows(dx_kept, dx_sent, WIDE_MOVES))
    dx_flow.advance([lax.ppermute(*send) for send in dx_flow.sends])
    starts = [reduce[1].near(2), first.pop(2), second.pop(1)]
    stage([dx_flow, *starts], idle=waiting() + [out_flow])
    starts = [reduce[0].near(2), first.pop(3)]
    stage([dx_flow, *starts, out_flow], idle=waiting())
    grad_residual_norm, grad_gain_two = norm_two_back(dx_flow.value)
    grad_residual = cotangent.astype(F32) + grad_residual_norm
    grad_flow = Flow(head_gather(grad_residual.astype(BF16)))
    starts = [reduce[1].cross(), first.pop(1)]
    stage([grad_flow, *starts], idle=waiting() + [out_flow])
    grad_flow.advance([lax.ppermute(*send) for send in grad_flow.sends])
    group_grad = grad_flow.value

    grad_heads = block_project(group_grad, out_blocks)
    grad_mixed = grad_heads.reshape(query_heads * group_rows, head_dim)
    delta = jnp.sum(grad_mixed.astype(F32) * mixed_full, axis=1)
    grad_queries, grad_keys_values = attend_back(
        place,
        queries,
        grad_mixed,
        keys_values,
        1.0 / totals.reshape(1, -1),
        delta[None, :],
        query_pos[None, :],
        first_pos[None, :],
        scale,
        group_rows,
    )
    group_grad, grad_queries, grad_keys_values = stage(
        [reduce[0].cross(), reduce[0].near(1), first.pop(0), second.pop(0)],
        [group_grad, grad_queries, grad_keys_values],
        idle=[out_flow],
    )
    grad_queries = grad_queries.reshape(query_heads, group_rows, head_dim)

    late = 2
    main = 3 * ffn_blocks - late
    cap = -(-main // data_count)
    places = -(-max(cap * data_count, 3 * ffn_blocks) // TRIO) * TRIO
    def weight_sums(outer):
        cut = outer.reshape(outer.shape[0], data_count, rows_dp, head_dim)
        return Flow(ring.scatter(lambda i: lax.dynamic_index_in_dim(cut, i, 1, keepdims=False), outer.shape[0] // 2))

    key_flow = Flow(
        ring.scatter(lambda i: lax.dynamic_index_in_dim(grad_keys_values, i, 0, keepdims=False), key_heads)
    )
    pick = lambda own, other: (jnp.where(parity == 1, other, own), jnp.where(parity == 1, own, other))
    low_early, high_early = pick(*reduce[0].value())
    outer, low_early, high_early = stage(
        [key_flow, reduce[1].near(1), out_flow],
        [block_outer([group_in, group_grad], [grad_queries, mixed_heads], model_width), low_early, high_early],
    )
    low_late, high_late = pick(*reduce[1].value())
    first_flow = weight_sums(outer)
    weight_grads, new_momentum, grams = stage(
        [key_flow, first_flow],
        ffn_moment(low_early, low_late, high_early, high_late, momentum, gate_mark, ffn_blocks, places),
    )
    gram_flow = Flow(gram_sums(ring, grams, cap))
    stage([key_flow, first_flow, gram_flow])
    while key_flow.sends is not None:
        stage([key_flow, first_flow, gram_flow])
    key_value_sums = key_flow.value
    grad_keys = (key_value_sums[:key_heads] * scale).astype(BF16)
    grad_values = key_value_sums[key_heads:].astype(BF16)
    grad_keys_values = jnp.concatenate([grad_keys, grad_values], axis=0)
    (outer,) = stage([first_flow, gram_flow], [block_outer([group_in], [grad_keys_values], model_width)])
    finish(first_flow)
    second_flow = weight_sums(outer)
    pairs = [k for k in range(gate_mark // 2) if not query_heads <= 2 * k < out_mark]
    grad_projected = jnp.concatenate([grad_queries, grad_keys_values], axis=0)
    *attn_dx, weight_grads, new_momentum, first_grams = stage(
        [second_flow, gram_flow],
        [
            *block_back(grad_projected, qkv_blocks),
            *attn_moment(first_flow.value, pairs, momentum, weight_grads, new_momentum),
        ],
    )
    last_flow = Flow(scatter_rows(*attn_dx, HEAD_MOVES))
    finish(gram_flow)
    gram_value = gram_flow.value
    while second_flow.sends is not None:
        (gram_value,) = stage([second_flow, last_flow, out_flow], [gram_value])
    finish(last_flow, out_flow)
    block_out = (residual + out_flow.value).astype(BF16)
    grad_input_norm, grad_gain_one = norm_one_back(last_flow.value)
    grad_input = grad_residual + grad_input_norm
    gain_flow = Flow(total_sum(jnp.stack([grad_gain_one, grad_gain_two])))
    weight_grads, new_momentum, second_grams = attn_moment(
        second_flow.value, list(range(query_heads // 2, out_mark // 2)), momentum, weight_grads, new_momentum
    )
    late_count = gate_mark + late
    late_cap = -(-late_count // data_count)
    late_grams = jnp.concatenate([first_grams, second_grams, grams[main : main + late]], axis=0)
    late_grams = jnp.pad(late_grams, ((0, late_cap * data_count - late_count), (0, 0), (0, 0), (0, 0)))
    late_gram_flow = Flow(gram_sums(ring, late_grams, late_cap))
    state, sweep = newton_start(gram_value, growth), 0
    while late_gram_flow.sends is not None:
        if sweep < NEWTON_STEPS - 1:
            state = newton_sweep(state, sweep)
            sweep += 1
        state = stage([late_gram_flow, gain_flow], state)
    while sweep < NEWTON_STEPS:
        state = newton_sweep(state, sweep)
        sweep += 1
    factor_flow = Flow(all_factors(ring, state[1]))
    state = newton_start(late_gram_flow.value, growth)
    for sweeps in (range(2), range(2, NEWTON_STEPS)):
        for sweep in sweeps:
            state = newton_sweep(state, sweep)
        state = stage([factor_flow, gain_flow], state)
    late_factor_flow = Flow(all_factors(ring, state[1]))
    while factor_flow.sends is not None:
        stage([factor_flow, late_factor_flow])
    factors = factor_flow.value

    threes = main // TRIO
    early_spots = [(gate_mark // TRIO + k, [TRIO * k + i for i in range(TRIO)]) for k in range(threes)]
    new_weights = []
    for k in range(0, threes, 4):
        new_weights = stage(
            [late_factor_flow, gain_flow],
            [renew(weights, new_momentum, factors, early_spots[k : k + 4], new_weights)],
        )
    finish(late_factor_flow, gain_flow)
    gain_grads = gain_flow.value
    rest = jnp.concatenate([late_factor_flow.value[:late_count], factors[TRIO * threes : main]], axis=0)
    blocks_of = [2 * pair + i for pair in pairs for i in range(2)] + list(range(query_heads, out_mark))
    blocks_of += [gate_mark + main + k for k in range(late)] + [gate_mark + k for k in range(TRIO * threes, main)]
    late_spots = [
        (spot, [blocks_of.index(TRIO * spot + i) for i in range(TRIO)])
        for spot in sorted({block // TRIO for block in blocks_of})
    ]
    new_weights = renew(weights, new_momentum, rest, late_spots, new_weights)

    new_gain_first = BETA_ONE * gain_first + (1.0 - BETA_ONE) * gain_grads
    new_gain_second = BETA_TWO * gain_second + (1.0 - BETA_TWO) * gain_grads * gain_grads
    first_hat = new_gain_first / (1.0 - BETA_ONE**UPDATE_STEP)
    second_hat = new_gain_second / (1.0 - BETA_TWO**UPDATE_STEP)
    new_gains = gains - ADAM_RATE * first_hat / (jnp.sqrt(second_hat) + ADAM_EPS)
    back = lambda array: jnp.transpose(array, (1, 0, 2))
    return (
        block_out,
        grad_input,
        back(weight_grads),
        back(new_momentum),
        back(new_weights),
        gain_grads,
        new_gain_first,
        new_gain_second,
        new_gains,
    )


def solution(mesh):
    return jax.shard_map(
        on_device,
        mesh=mesh,
        in_specs=(
            P(("dp", "head"), None),
            P(("dp", "head"), None),
            P(("dp", "head")),
            P("dp", "head", None),
            P("dp", "head", None),
            P(),
            P(),
            P(),
        ),
        out_specs=(
            P(("dp", "head"), None),
            P(("dp", "head"), None),
            P("dp", "head", None),
            P("dp", "head", None),
            P("dp", "head", None),
            P(),
            P(),
            P(),
            P(),
        ),
        check_vma=False,
    )
```

```python
import functools
import math

import jax
import jax.numpy as jnp
from jax import lax
from jax.experimental import pallas as pl
from jax.experimental.pallas import tpu as pltpu
from jax.sharding import PartitionSpec as P

H = 8
KV = 4
FF = 9216
NEWTON_STEPS = 5
UPDATE_STEP = 10

NORM_EPS = 1e-06
SOFT_CAP = 50.0
MUON_RATE = 0.2
MUON_DECAY = 0.01
MUON_BETA = 0.95
ADAM_RATE = 0.3
BETA_ONE = 0.9
BETA_TWO = 0.95
ADAM_EPS = 1e-08
NEWTON_LINEAR = 3.4445
NEWTON_SQUARE = -4.775
NEWTON_CUBIC = 2.0315
TOP_PRECISION = lax.Precision.HIGHEST

BF16 = jnp.bfloat16
F32 = jnp.float32
VMEM_LIMIT = 62 * 1024 * 1024
NN = (((1,), (0,)), ((), ()))
NT = (((1,), (1,)), ((), ()))
TN = (((0,), (0,)), ((), ()))


def mm(a, b, dims):
    return lax.dot_general(a, b, dims, preferred_element_type=F32)


def rms_scale(rows, gain):
    inverse = lax.rsqrt(jnp.mean(rows * rows, axis=-1, keepdims=True) + NORM_EPS)
    return rows * inverse * gain


class Flow:
    def __init__(self, steps):
        self.steps = steps
        self.value = None
        self.sends = None
        self.advance(None)

    def advance(self, arrived):
        try:
            self.sends = self.steps.send(arrived)
        except StopIteration as stop:
            self.sends = None
            self.value = stop.value


def stage(flows, extra=(), idle=()):
    flows = [flow for flow in flows if flow.sends is not None]
    idle = [flow for flow in idle if flow.sends is not None and flow not in flows]
    arrived = [[lax.ppermute(*send) for send in flow.sends] for flow in flows]
    held = [[send[0] for send in flow.sends] for flow in idle]
    arrived, held, extra = lax.optimization_barrier((arrived, held, list(extra)))
    for flow, got in zip(flows, arrived):
        flow.advance(got)
    for flow, kept in zip(idle, held):
        flow.sends = [(value,) + send[1:] for value, send in zip(kept, flow.sends)]
    return extra


def run(steps):
    flow = Flow(steps)
    while flow.sends is not None:
        flow.advance([lax.ppermute(*send) for send in flow.sends])
    return flow.value


def finish(*flows):
    while any(flow.sends is not None for flow in flows):
        stage(flows)


def swap(value, axis, mask):
    size = lax.axis_size(axis)
    return (value, axis, [(i, i ^ mask) for i in range(size)])


def head_gather(rows):
    (other,) = yield [swap(rows, "head", 2)]
    pair = jnp.concatenate([rows, other], axis=0)
    (other,) = yield [swap(pair, "head", 1)]
    return jnp.concatenate([pair, other], axis=0)


def wide_gather(rows):
    (other,) = yield [swap(rows, "dp", 4)]
    both = jnp.concatenate([rows, other], axis=0)
    (other,) = yield [swap(both, "head", 2)]
    pair = jnp.concatenate([both, other], axis=0)
    (other,) = yield [swap(pair, "head", 1)]
    return [pair, other]


def add_low(kept, other):
    return (kept.astype(F32) + other.astype(F32)).astype(BF16)


def scatter_rows(kept, sent, moves):
    for k, (axis, mask) in enumerate(moves):
        (other,) = yield [swap(sent, axis, mask)]
        part = kept.astype(F32) + other.astype(F32)
        if k < len(moves) - 1:
            half = part.shape[0] // 2
            kept, sent = part[:half], part[half:].astype(BF16)
    return part


HEAD_MOVES = (("head", 1), ("head", 2))
WIDE_MOVES = (("head", 1), ("head", 2), ("dp", 4))


def total_sum(value):
    for axis in ("head", "dp"):
        mask = 1
        while mask < lax.axis_size(axis):
            (other,) = yield [swap(value, axis, mask)]
            value = value + other
            mask *= 2
    return value


class Ring:
    def __init__(self):
        size = lax.axis_size("dp")
        order = list(range(0, size, 2)) + list(range(size - 1, 0, -2))
        around = [[order[(order.index(i) + offset) % size] for offset in range(size)] for i in range(size)]
        self.size = size
        self.around = jnp.array(around, jnp.int32)[lax.axis_index("dp")]
        self.up = [(order[k], order[(k + 1) % size]) for k in range(size)]
        self.down = [(order[(k + 1) % size], order[k]) for k in range(size)]

    def index(self, offset, scale=1):
        return (self.around * scale)[offset % self.size]

    def gather(self, value, mid):
        half = self.size // 2
        out = jnp.zeros((self.size,) + value.shape, value.dtype)

        def put(out, piece, offset, start=0):
            spot = (self.index(offset), start) + (0,) * (value.ndim - 1)
            return lax.dynamic_update_slice(out, piece[None], spot, allow_negative_indices=False)

        out = put(out, value, 0)
        ahead, back = value, value
        for step in range(1, half):
            ahead, back = yield [(ahead, "dp", self.up), (back, "dp", self.down)]
            out = put(put(out, ahead, -step), back, step)
        if mid is None:
            (last,) = yield [(ahead, "dp", self.up)]
            return put(out, last, half)
        first, second = yield [(ahead[:mid], "dp", self.up), (back[mid:], "dp", self.down)]
        return put(put(out, first, half), second, half, mid)

    def part(self, array, axis, size=None):
        if size is None:
            return lambda offset: lax.dynamic_index_in_dim(
                array, self.index(offset), axis, keepdims=False, allow_negative_indices=False
            )
        return lambda offset: lax.dynamic_slice_in_dim(
            array, self.index(offset, size), size, axis, allow_negative_indices=False
        )

    def scatter(self, take, mid):
        half = self.size // 2
        far = take(half)
        kind = far.dtype
        if mid is None:
            (up,) = yield [(far, "dp", self.up)]
            down = None
        else:
            up, down = yield [(far[:mid], "dp", self.up), (far[mid:], "dp", self.down)]
        for step in range(half - 1, 0, -1):
            ahead, back = take(step).astype(F32), take(-step).astype(F32)
            if mid is None or step < half - 1:
                ahead = ahead + up
                back = back if down is None else back + down
            else:
                ahead = jnp.concatenate([ahead[:mid] + up, ahead[mid:]])
                back = jnp.concatenate([back[:mid], back[mid:] + down])
            up, down = yield [(ahead.astype(kind), "dp", self.up), (back.astype(kind), "dp", self.down)]
        return take(0).astype(F32) + up.astype(F32) + down.astype(F32)


def once(sends, take):
    def steps():
        take((yield sends))

    return Flow(steps())


SIDE_BIT = 2


def plane_classes():
    planes = range(lax.axis_size("dp") // 2)
    kept = [m for m in planes if m & 3 in (0, 3)]
    passed = [m for m in planes if m & 3 in (1, 2)]
    return {0: [0], 1: [1], 2: [m for m in passed if m != 1], 3: [m for m in kept if m]}


class Spread:
    def __init__(self, mine, other):
        self.mine, self.other = mine, other
        self.pieces = {0: mine}

    def move(self, moves):
        def take(arrived):
            for (_, _, _, number), piece in zip(moves, arrived):
                self.pieces[number] = piece

        return once([swap(value, "dp", offset << 1 | bit) for value, offset, bit, _ in moves], take)

    def cross(self):
        group = plane_classes()[3]
        return self.move([(self.other if m & SIDE_BIT else self.mine, m, 0, m << 1) for m in group])

    def near(self, key):
        group = plane_classes()[key]
        return self.move([(self.pieces[m << 1], 1, 0, (m ^ 1) << 1) for m in group])

    def y(self, key):
        group = plane_classes()[key]
        return self.move([(self.pieces[m << 1], 0, 1, m << 1 | 1) for m in group])

    def value(self):
        return [self.pieces[k] for k in range(lax.axis_size("dp"))]


class Reduce:
    def __init__(self, rows):
        self.rows = rows
        self.parts = {}
        self.sums = [[], []]

    def part(self, offset):
        terms = [term.astype(F32) for term in self.parts[offset]]
        return functools.reduce(jnp.add, terms)

    def hold(self, offset, *terms):
        self.parts.setdefault(offset, []).extend(terms)

    def y(self, key):
        group = plane_classes()[key]

        def take(arrived):
            for offset, got in zip(group, arrived):
                self.hold(offset, self.rows(offset << 1), got)

        return once([swap(self.rows(offset << 1 | 1), "dp", 1) for offset in group], take)

    def near(self, key):
        group = plane_classes()[key]

        def take(arrived):
            for offset, got in zip(group, arrived):
                self.hold(offset ^ 1, got)

        return once([swap(self.part(offset).astype(BF16), "dp", 2) for offset in group], take)

    def cross(self):
        group = plane_classes()[3]

        def take(arrived):
            for offset, got in zip(group, arrived):
                self.sums[1 if offset & SIDE_BIT else 0].append(got)

        return once([swap(self.part(offset).astype(BF16), "dp", offset << 1) for offset in group], take)

    def value(self):
        return self.parts[0] + self.sums[0], self.sums[1]


def params(**more):
    return pltpu.CompilerParams(vmem_limit_bytes=VMEM_LIMIT, **more)


TRIO = 3


def cast_blocks(blocks, count):
    _, r, c = blocks.shape

    def body(x_ref, o_ref):
        o_ref[...] = x_ref[...].astype(BF16)

    spec = pl.BlockSpec((TRIO, r, c), lambda k: (k, 0, 0))
    return pl.pallas_call(
        body,
        grid=(count // TRIO,),
        in_specs=[spec],
        out_specs=spec,
        out_shape=jax.ShapeDtypeStruct((count, r, c), BF16),
        compiler_params=params(),
        cost_estimate=pl.CostEstimate(flops=0, bytes_accessed=6 * count * r * c, transcendentals=0),
    )(blocks)


def pack_units(parity, blocks, first, kind_blocks, early):
    _, r, c = blocks.shape
    h = c // 2
    full = kind_blocks // 2
    each = kind_blocks // TRIO
    u, v = early * c, (full - early) * c + h

    def body(s_ref, *refs):
        parts, outs = refs[:each], refs[each:]

        def tile(f):
            return parts[f // TRIO].at[f % TRIO]

        for turn in range(2):

            @pl.when(s_ref[0] == turn)
            def _():
                for k in range(2):
                    side = turn ^ k
                    for i in range(full):
                        value = tile(side * full + i)[...].astype(BF16)
                        if i < early:
                            outs[2 * k][:, i * c : (i + 1) * c] = value
                        else:
                            outs[2 * k + 1][:, (i - early) * c : (i - early + 1) * c] = value
                    rest = tile(2 * full)[:, side * h : (side + 1) * h]
                    outs[2 * k + 1][:, v - h :] = rest.astype(BF16)

    def part(i):
        return pl.BlockSpec((TRIO, r, c), lambda k, s: (first // TRIO + each * k + i, 0, 0))

    wide = pl.BlockSpec((None, r, u), lambda k, s: (k, 0, 0))
    slim = pl.BlockSpec((None, r, v), lambda k, s: (k, 0, 0))
    shapes = [jax.ShapeDtypeStruct((3, r, u), BF16), jax.ShapeDtypeStruct((3, r, v), BF16)]
    return pl.pallas_call(
        body,
        grid_spec=pltpu.PrefetchScalarGridSpec(
            num_scalar_prefetch=1,
            grid=(3,),
            in_specs=[part(i) for i in range(each)],
            out_specs=[wide, slim, wide, slim],
        ),
        out_shape=shapes + shapes,
        compiler_params=params(),
        cost_estimate=pl.CostEstimate(flops=0, bytes_accessed=18 * kind_blocks * r * c, transcendentals=0),
    )(parity, *([blocks] * each))


def block_project(rows, blocks):
    t = rows.shape[0]
    count, d, c = blocks.shape

    def body(x_ref, w_ref, o_ref):
        o_ref[...] = mm(x_ref[...], w_ref[...], NN).astype(BF16)

    return pl.pallas_call(
        body,
        grid=(count,),
        in_specs=[
            pl.BlockSpec((t, d), lambda b: (0, 0)),
            pl.BlockSpec((None, d, c), lambda b: (b, 0, 0)),
        ],
        out_specs=pl.BlockSpec((None, t, c), lambda b: (b, 0, 0)),
        out_shape=jax.ShapeDtypeStruct((count, t, c), BF16),
        compiler_params=params(),
        cost_estimate=pl.CostEstimate(
            flops=2 * count * t * d * c, bytes_accessed=2 * (t * d + count * (d * c + t * c)), transcendentals=0
        ),
    )(rows, blocks)


def block_back(cols, blocks):
    count, t, c = cols.shape
    d = blocks.shape[1]
    half = t // 2

    def body(x_ref, w_ref, o_ref, p_ref, acc_ref):
        b = pl.program_id(0)

        @pl.when(b == 0)
        def _():
            acc_ref[...] = jnp.zeros_like(acc_ref)

        acc_ref[...] += mm(x_ref[...], w_ref[...], NT)

        @pl.when(b == count - 1)
        def _():
            o_ref[...] = acc_ref[:half, :].astype(BF16)
            p_ref[...] = acc_ref[half:, :].astype(BF16)

    result = pl.BlockSpec((half, d), lambda b: (0, 0))
    return pl.pallas_call(
        body,
        grid=(count,),
        in_specs=[
            pl.BlockSpec((None, t, c), lambda b: (b, 0, 0)),
            pl.BlockSpec((None, d, c), lambda b: (b, 0, 0)),
        ],
        out_specs=[result, result],
        out_shape=[jax.ShapeDtypeStruct((half, d), BF16)] * 2,
        scratch_shapes=[pltpu.VMEM((t, d), F32)],
        compiler_params=params(),
        cost_estimate=pl.CostEstimate(
            flops=2 * count * t * d * c, bytes_accessed=2 * (t * d + count * (d * c + t * c)), transcendentals=0
        ),
    )(cols, blocks)


def block_outer(rows, cols, d):
    t = rows[0].shape[0]
    c = cols[0].shape[2]
    starts = [0]
    for col in cols:
        starts.append(starts[-1] + col.shape[0])
    count = len(rows)
    total = starts[-1]

    def body(*refs):
        o_ref, t_ref = refs[2 * count :]
        b = pl.program_id(0)
        for k in range(count):

            @pl.when(b == starts[k])
            def _():
                t_ref[...] = refs[k][...].T

            @pl.when((b >= starts[k]) & (b < starts[k + 1]))
            def _():
                o_ref[...] = mm(t_ref[...], refs[count + k][...], NN).astype(BF16)

    def col_at(k):
        return pl.BlockSpec((None, t, c), lambda b: (jnp.clip(b - starts[k], 0, starts[k + 1] - starts[k] - 1), 0, 0))

    return pl.pallas_call(
        body,
        grid=(total,),
        in_specs=[pl.BlockSpec((t, d), lambda b: (0, 0))] * count + [col_at(k) for k in range(count)],
        out_specs=pl.BlockSpec((None, d, c), lambda b: (b, 0, 0)),
        out_shape=jax.ShapeDtypeStruct((total, d, c), BF16),
        scratch_shapes=[pltpu.VMEM((d, t), BF16)],
        compiler_params=params(),
        cost_estimate=pl.CostEstimate(
            flops=2 * total * t * d * c,
            bytes_accessed=2 * (count * t * d + total * (d * c + t * c)),
            transcendentals=0,
        ),
    )(*rows, *cols)


def in_group(local, width, head_shift):
    quarter = width // 4
    low = jnp.bitwise_and(local, quarter - 1)
    one = jnp.where(jnp.bitwise_and(local, quarter) != 0, 2 * quarter, 0)
    two = jnp.where(jnp.bitwise_and(local, 2 * quarter) != 0, quarter, 0)
    return jnp.bitwise_xor(low + one + two, head_shift)


def key_position(block, width, head_shift, shape, axis):
    local = lax.broadcasted_iota(jnp.int32, shape, axis)
    return block * width + in_group(local, width, head_shift)


def attend(place, queries, keys_values, query_pos, first_pos, scale, p):
    m, e = queries.shape
    n = keys_values.shape[0]
    step = 256

    def body(place_ref, q_ref, kv_ref, pos_ref, first_ref, low_ref, full_ref, sum_ref, acc_ref, tot_ref):
        j = pl.program_id(0)

        @pl.when(j == 0)
        def _():
            acc_ref[...] = jnp.zeros_like(acc_ref)
            tot_ref[...] = jnp.zeros_like(tot_ref)

        @pl.when(j <= place_ref[0])
        def _():
            key_pos = key_position(j, p, place_ref[1], (1, p), 1)
            for r in range(0, m, step):
                rows = pl.ds(r, step)
                raw = mm(q_ref[rows, :], kv_ref[:p, :], NT)
                soft = SOFT_CAP * jnp.tanh(raw * (scale / SOFT_CAP))
                seen = (key_pos >= first_ref[rows, :]) & (key_pos <= pos_ref[rows, :])
                terms = jnp.where(seen, jnp.exp(soft), 0.0)
                tot_ref[rows, :] += jnp.sum(terms, axis=1, keepdims=True)
                acc_ref[rows, :] += mm(terms.astype(BF16), kv_ref[p:, :], NN)

        @pl.when(j == n - 1)
        def _():
            total = tot_ref[...]
            mixed = acc_ref[...] / total
            full_ref[...] = mixed
            low_ref[...] = mixed.astype(BF16)
            sum_ref[...] = total

    whole = lambda shape: pl.BlockSpec(shape, lambda j, s: (0, 0))
    return pl.pallas_call(
        body,
        grid_spec=pltpu.PrefetchScalarGridSpec(
            num_scalar_prefetch=1,
            grid=(n,),
            in_specs=[
                whole((m, e)),
                pl.BlockSpec((None, 2 * p, e), lambda j, s: (jnp.minimum(j, s[0]), 0, 0)),
                whole((m, 1)),
                whole((m, 1)),
            ],
            out_specs=[whole((m, e)), whole((m, e)), whole((m, 1))],
            scratch_shapes=[pltpu.VMEM((m, e), F32), pltpu.VMEM((m, 1), F32)],
        ),
        out_shape=[
            jax.ShapeDtypeStruct((m, e), BF16),
            jax.ShapeDtypeStruct((m, e), F32),
            jax.ShapeDtypeStruct((m, 1), F32),
        ],
        compiler_params=params(),
        cost_estimate=pl.CostEstimate(
            flops=4 * m * n * p * e, bytes_accessed=4 * n * p * e, transcendentals=2 * m * n * p
        ),
    )(place, queries, keys_values, query_pos, first_pos)


def attend_back(place, queries, grads, keys_values, inverse, delta, query_pos, first_pos, scale, p):
    m, e = queries.shape
    n = keys_values.shape[0]
    step = 256

    def body(
        place_ref, q_ref, g_ref, kv_ref, inv_ref, delta_ref, pos_ref, first_ref, dq_ref, dkv_ref, acc_ref, dk_ref, dv_ref
    ):
        j = pl.program_id(0)

        @pl.when(j == 0)
        def _():
            acc_ref[...] = jnp.zeros_like(acc_ref)

        @pl.when(j <= place_ref[0])
        def _():
            key_pos = key_position(j, p, place_ref[1], (p, 1), 0)
            for r in range(0, m, step):
                rows = pl.ds(r, step)
                raw = mm(kv_ref[:p, :], q_ref[rows, :], NT)
                capped = jnp.tanh(raw * (scale / SOFT_CAP))
                seen = (key_pos >= first_ref[:, rows]) & (key_pos <= pos_ref[:, rows])
                probs = jnp.where(seen, jnp.exp(SOFT_CAP * capped), 0.0) * inv_ref[:, rows]
                grad_probs = mm(kv_ref[p:, :], g_ref[rows, :], NT)
                grad_raw = probs * (grad_probs - delta_ref[:, rows]) * (1.0 - capped * capped)
                grad_low = grad_raw.astype(BF16)
                value_part = mm(probs.astype(BF16), g_ref[rows, :], NN)
                key_part = mm(grad_low, q_ref[rows, :], NN)
                if r == 0:
                    dv_ref[...] = value_part
                    dk_ref[...] = key_part
                else:
                    dv_ref[...] += value_part
                    dk_ref[...] += key_part
                acc_ref[rows, :] += mm(grad_low, kv_ref[:p, :], TN)
            dkv_ref[0] = dk_ref[...].astype(BF16)
            dkv_ref[1] = dv_ref[...].astype(BF16)

        @pl.when(j > place_ref[0])
        def _():
            dkv_ref[...] = jnp.zeros_like(dkv_ref)

        @pl.when(j == n - 1)
        def _():
            dq_ref[...] = (acc_ref[...] * scale).astype(BF16)

    whole = lambda shape: pl.BlockSpec(shape, lambda j, s: (0, 0))
    return pl.pallas_call(
        body,
        grid_spec=pltpu.PrefetchScalarGridSpec(
            num_scalar_prefetch=1,
            grid=(n,),
            in_specs=[
                whole((m, e)),
                whole((m, e)),
                pl.BlockSpec((None, 2 * p, e), lambda j, s: (jnp.minimum(j, s[0]), 0, 0)),
                whole((1, m)),
                whole((1, m)),
                whole((1, m)),
                whole((1, m)),
            ],
            out_specs=[whole((m, e)), pl.BlockSpec((None, 2, p, e), lambda j, s: (j, 0, 0, 0))],
            scratch_shapes=[pltpu.VMEM((m, e), F32), pltpu.VMEM((p, e), F32), pltpu.VMEM((p, e), F32)],
        ),
        out_shape=[jax.ShapeDtypeStruct((m, e), BF16), jax.ShapeDtypeStruct((n, 2, p, e), BF16)],
        compiler_params=params(),
        cost_estimate=pl.CostEstimate(
            flops=10 * m * n * p * e, bytes_accessed=8 * n * p * e, transcendentals=2 * m * n * p
        ),
    )(place, queries, grads, keys_values, inverse, delta, query_pos, first_pos)


def gelu_pair(gate):
    outer = math.sqrt(2.0 / math.pi)
    square = gate * gate
    bent = jnp.tanh(outer * gate * (1.0 + 0.044715 * square))
    half = 0.5 * (1.0 + bent)
    slope = half + 0.5 * gate * (1.0 - bent * bent) * outer * (1.0 + 3.0 * 0.044715 * square)
    return gate * half, slope


def ffn_front(place, rows, cots, early, late):
    part_rows, d = rows[0].shape
    t = 2 * part_rows
    count = len(early)
    r = early[0].shape[1]
    u, v = early[0].shape[2], late[0].shape[2]
    tall = min(512, t)
    wide = d // 3
    cuts = [(k, min(256, u + v - k)) for k in range(0, u + v, 256)]

    def body(place_ref, x0, x1, y0, y1, *refs):
        early_refs, late_refs = refs[:count], refs[count : 2 * count]
        refs = refs[2 * count :]
        hs_ref, w_out = refs[:2]
        grad_refs = refs[2 : 2 + count], refs[2 + count : 2 + 2 * count]
        x, y, w, xt, yt, hs, row_sems, sems, out_sems, grad_sems = refs[2 + 2 * count :]
        row_copies = []
        for k, (source, target) in enumerate(((x0, x), (x1, x), (y0, y), (y1, y))):
            target = target.at[pl.ds((k % 2) * part_rows, part_rows), :]
            row_copies.append(pltpu.make_async_copy(source, target, row_sems.at[k]))
            row_copies[k].start()
        copies = []
        chunks = ((early_refs, pl.ds(0, u)), (late_refs, pl.ds(u, v)))

        def spot(k):
            return pl.ds(pl.multiple_of(jnp.bitwise_xor(place_ref[0], k) * r, 16) if count > 1 else 0, r)

        for k in range(count):
            for way, (sources, lanes) in enumerate(chunks):
                copy = pltpu.make_async_copy(sources[k], w.at[:, spot(k), lanes], sems.at[way, k])
                copy.start()
                copies.append(copy)
        for copy in row_copies:
            copy.wait()

        @pl.loop(0, d // 256)
        def _(k):
            cols = pl.ds(pl.multiple_of(k * 256, 256), 256)
            xt[cols, :] = x[:, cols].T
            yt[cols, :] = y[:, cols].T

        for copy in copies:
            copy.wait()
        kept = pltpu.make_async_copy(w, w_out, out_sems.at[0])
        kept.start()

        @pl.loop(0, t // tall)
        def _(i):
            part = pl.ds(pl.multiple_of(i * tall, tall), tall)
            for start, size in cuts:
                units = pl.ds(start, size)
                gate = mm(x[part, :], w[0, :, units], NN)
                up = mm(x[part, :], w[1, :, units], NN)
                grad = mm(y[part, :], w[2, :, units], NN)
                active, slope = gelu_pair(gate)
                hs[0, part, units] = (active * up).astype(BF16)
                hs[1, part, units] = (grad * up * slope).astype(BF16)
                hs[2, part, units] = (grad * active).astype(BF16)

        sides = pltpu.make_async_copy(hs, hs_ref, out_sems.at[1])
        sides.start()
        kept.wait()
        copies = []
        for kind, (left, right) in enumerate(((xt, 1), (xt, 2), (yt, 0))):

            @pl.loop(0, d // wide)
            def _(k):
                cols = pl.ds(pl.multiple_of(k * wide, wide), wide)
                w[kind, cols, :] = mm(left[cols, :], hs[right], NN).astype(BF16)

            for k in range(count):
                for way, (_, lanes) in enumerate(chunks):
                    target = grad_refs[way][k].at[kind]
                    copy = pltpu.make_async_copy(w.at[kind, spot(k), lanes], target, grad_sems.at[kind, way, k])
                    copy.start()
                    copies.append(copy)
        sides.wait()
        for copy in copies:
            copy.wait()

    apart = pl.BlockSpec(memory_space=pl.ANY)
    return pl.pallas_call(
        body,
        grid_spec=pltpu.PrefetchScalarGridSpec(
            num_scalar_prefetch=1,
            grid=(1,),
            in_specs=[apart] * (4 + 2 * count),
            out_specs=[apart] * (2 + 2 * count),
            scratch_shapes=[
                pltpu.VMEM((t, d), BF16),
                pltpu.VMEM((t, d), BF16),
                pltpu.VMEM((3, d, u + v), BF16),
                pltpu.VMEM((d, t), BF16),
                pltpu.VMEM((d, t), BF16),
                pltpu.VMEM((3, t, u + v), BF16),
                pltpu.SemaphoreType.DMA((4,)),
                pltpu.SemaphoreType.DMA((2, count)),
                pltpu.SemaphoreType.DMA((2,)),
                pltpu.SemaphoreType.DMA((3, 2, count)),
            ],
        ),
        out_shape=[
            jax.ShapeDtypeStruct((3, t, u + v), BF16),
            jax.ShapeDtypeStruct((3, d, u + v), BF16),
            *[jax.ShapeDtypeStruct((3, r, u), BF16)] * count,
            *[jax.ShapeDtypeStruct((3, r, v), BF16)] * count,
        ],
        compiler_params=params(),
        cost_estimate=pl.CostEstimate(
            flops=12 * t * d * (u + v), bytes_accessed=12 * d * (u + v) + 4 * t * d, transcendentals=t * (u + v)
        ),
    )(place, *rows, *cots, *early, *late)


def ffn_back(sides, blocks):
    _, t, u = sides.shape
    d = blocks.shape[1]
    wide = 256
    half = t // 2

    def body(s_ref, w_ref, *refs):
        for k in range(2):
            part = pl.ds(k * half, half)
            refs[k][...] = mm(s_ref[0, part, :], w_ref[2], NT).astype(BF16)
            refs[2 + k][...] = (mm(s_ref[1, part, :], w_ref[0], NT) + mm(s_ref[2, part, :], w_ref[1], NT)).astype(BF16)

    return pl.pallas_call(
        body,
        grid=(d // wide,),
        in_specs=[
            pl.BlockSpec((3, t, u), lambda k: (0, 0, 0), pipeline_mode=pl.Buffered(1)),
            pl.BlockSpec((3, wide, u), lambda k: (0, k, 0)),
        ],
        out_specs=[pl.BlockSpec((half, wide), lambda k: (0, k))] * 4,
        out_shape=[jax.ShapeDtypeStruct((half, d), BF16)] * 4,
        compiler_params=params(),
        cost_estimate=pl.CostEstimate(
            flops=6 * t * d * u, bytes_accessed=6 * d * u + 6 * t * u + 4 * t * d, transcendentals=0
        ),
    )(sides, blocks)


def gram_parts(m):
    h = m.shape[1] // 2
    high = m.astype(BF16)
    low = (m - high.astype(F32)).astype(BF16)
    mixed = mm(high, low, TN)
    gram = mm(high, high, TN) + mm(low, low, TN) + mixed + mixed.T
    return gram[:h, :h], gram[:h, h:], gram[h:, h:]


def ffn_moment(parity, own, other, momentum, first, blocks, places):
    total, r, c = momentum.shape
    terms = [*own, *other]
    counts = [len(group) for group in terms]
    u, v = own[0][0].shape[2], own[1][0].shape[2]
    early = u // c
    h = c // 2
    full = early + 1
    each = blocks // TRIO

    def body(s_ref, *refs):
        groups = []
        for count in counts:
            groups.append(refs[:count])
            refs = refs[count:]
        m_ref, wg_ref, nm_ref, gram_ref = refs
        j = pl.program_id(0)

        def total_of(group, start, size):
            lanes = pl.ds(start, size)
            return functools.reduce(jnp.add, [ref[:, lanes].astype(F32) for ref in group])

        @pl.when(j >= TRIO * each)
        def _():
            gram_ref[...] = jnp.zeros_like(gram_ref)

        for turn in range(each):
            for mine in range(2):

                @pl.when((j < TRIO * each) & (lax.rem(j, each) == turn) & (s_ref[0] == mine))
                def _():
                    for i in range(TRIO):
                        side, f = divmod(turn * TRIO + i, full)
                        if side == 2:
                            for k in range(2):
                                group = groups[1 if k == mine else 3]
                                wg_ref[i, :, k * h : (k + 1) * h] = total_of(group, c, h)
                        elif f < early:
                            wg_ref[i] = total_of(groups[0 if side == mine else 2], f * c, c)
                        else:
                            wg_ref[i] = total_of(groups[1 if side == mine else 3], 0, c)

        @pl.when(j < TRIO * each)
        def _():
            for i in range(TRIO):
                new = MUON_BETA * m_ref[i] + wg_ref[i]
                nm_ref[i] = new
                gram_ref[i, 0], gram_ref[i, 1], gram_ref[i, 2] = gram_parts(new)

    kind = lambda j, s: (jnp.minimum(j // each, 2), 0, 0)
    block = lambda j, s: (first // TRIO + jnp.minimum(j, TRIO * each - 1), 0, 0)
    arrays = [array for group in terms for array in group]
    return pl.pallas_call(
        body,
        grid_spec=pltpu.PrefetchScalarGridSpec(
            num_scalar_prefetch=1,
            grid=(places // TRIO,),
            in_specs=[pl.BlockSpec((None,) + array.shape[1:], kind) for array in arrays]
            + [pl.BlockSpec((TRIO, r, c), block)],
            out_specs=[
                pl.BlockSpec((TRIO, r, c), block),
                pl.BlockSpec((TRIO, r, c), block),
                pl.BlockSpec((TRIO, 3, h, h), lambda j, s: (j, 0, 0, 0)),
            ],
        ),
        out_shape=[
            jax.ShapeDtypeStruct((total, r, c), F32),
            jax.ShapeDtypeStruct((total, r, c), F32),
            jax.ShapeDtypeStruct((places, 3, h, h), F32),
        ],
        compiler_params=params(),
        cost_estimate=pl.CostEstimate(
            flops=6 * 3 * blocks * r * c * c, bytes_accessed=16 * 3 * blocks * r * c, transcendentals=0
        ),
    )(parity, *arrays, momentum)


def attn_moment(grads, pairs, momentum, weight_grads, new_momentum):
    count, r, c = grads.shape
    h = c // 2

    def body(s_ref, g_ref, m_ref, wg_in, nm_in, wg_ref, nm_ref, gram_ref):
        for i in range(2):
            new = MUON_BETA * m_ref[i] + g_ref[i]
            wg_ref[i] = g_ref[i]
            nm_ref[i] = new
            gram_ref[i, 0], gram_ref[i, 1], gram_ref[i, 2] = gram_parts(new)

    block = pl.BlockSpec((2, r, c), lambda j, s: (s[j], 0, 0))
    apart = pl.BlockSpec(memory_space=pl.ANY)
    return pl.pallas_call(
        body,
        grid_spec=pltpu.PrefetchScalarGridSpec(
            num_scalar_prefetch=1,
            grid=(count // 2,),
            in_specs=[pl.BlockSpec((2, r, c), lambda j, s: (j, 0, 0)), block, apart, apart],
            out_specs=[block, block, pl.BlockSpec((2, 3, h, h), lambda j, s: (j, 0, 0, 0))],
        ),
        out_shape=[
            jax.ShapeDtypeStruct(momentum.shape, F32),
            jax.ShapeDtypeStruct(momentum.shape, F32),
            jax.ShapeDtypeStruct((count, 3, h, h), F32),
        ],
        input_output_aliases={3: 0, 4: 1},
        compiler_params=params(),
        cost_estimate=pl.CostEstimate(
            flops=6 * count * r * c * c, bytes_accessed=16 * count * r * c, transcendentals=0
        ),
    )(jnp.array(pairs, jnp.int32), grads, momentum, weight_grads, new_momentum)


def renew(weights, momentum, factors, spots, updated):
    _, r, c = weights.shape
    h = c // 2
    steps = len(spots)
    table = jnp.array([spot for spot, _ in spots] + [f for _, places in spots for f in places], jnp.int32)

    def body(s_ref, w_ref, m_ref, *refs):
        factor_refs, o_ref = refs[:TRIO], refs[-1]
        for i in range(TRIO):
            left = m_ref[i, :, :h].astype(BF16)
            right = m_ref[i, :, h:].astype(BF16)
            first, off, last = factor_refs[i][0], factor_refs[i][1], factor_refs[i][2]
            start = mm(left, first, NN) + mm(right, off, NT)
            rest = mm(left, off, NN) + mm(right, last, NN)
            keep = 1.0 - MUON_RATE * MUON_DECAY
            o_ref[i, :, :h] = w_ref[i, :, :h] * keep - MUON_RATE * start
            o_ref[i, :, h:] = w_ref[i, :, h:] * keep - MUON_RATE * rest

    block = pl.BlockSpec((TRIO, r, c), lambda j, s: (s[j], 0, 0))

    def factor_at(i):
        return pl.BlockSpec((None, 3, h, h), lambda j, s: (s[steps + TRIO * j + i], 0, 0, 0))

    apart = [pl.BlockSpec(memory_space=pl.ANY)] * len(updated)
    return pl.pallas_call(
        body,
        grid_spec=pltpu.PrefetchScalarGridSpec(
            num_scalar_prefetch=1,
            grid=(steps,),
            in_specs=[block, block] + [factor_at(i) for i in range(TRIO)] + apart,
            out_specs=block,
        ),
        out_shape=jax.ShapeDtypeStruct(weights.shape, F32),
        input_output_aliases={3 + TRIO: 0} if updated else {},
        compiler_params=params(),
        cost_estimate=pl.CostEstimate(
            flops=2 * TRIO * steps * r * c * c, bytes_accessed=12 * TRIO * steps * r * c, transcendentals=0
        ),
    )(table, weights, momentum, *([factors] * TRIO), *updated)


def top(spec, a, b):
    return jnp.einsum(spec, a, b, precision=TOP_PRECISION)


def newton_factor(grams, growth):
    size = grams.shape[-1]
    eye = jnp.eye(size, dtype=F32)
    norm = jnp.sqrt(jnp.sum(grams * eye, axis=(1, 2), keepdims=True))
    inverse = 1.0 / (norm + 1e-07)
    gram = grams * (inverse * inverse)
    factor = None
    for sweep in range(NEWTON_STEPS):
        square = top("bij,bjk->bik", gram, gram)
        poly = NEWTON_LINEAR * eye + NEWTON_SQUARE * gram + NEWTON_CUBIC * square
        factor = poly if sweep == 0 else top("bij,bjk->bik", factor, poly)
        if sweep < NEWTON_STEPS - 1:
            gram = top("bij,bjk->bik", top("bij,bjk->bik", gram, poly), poly)
    return factor * (growth * inverse)


def fold(squares):
    h = squares.shape[1] // 2
    return jnp.stack([squares[:, :h, :h], squares[:, :h, h:], squares[:, h:, h:]], axis=1)


def unfold(parts):
    first, off, last = parts[:, 0], parts[:, 1], parts[:, 2]
    upper = jnp.concatenate([first, off], axis=2)
    lower = jnp.concatenate([jnp.swapaxes(off, 1, 2), last], axis=2)
    return jnp.concatenate([upper, lower], axis=1)


def gram_sums(ring, parts, cap):
    h = parts.shape[2]
    parts = parts.reshape(-1, h, h)
    rows = 3 * cap
    mine = yield from ring.scatter(ring.part(parts, 0, rows), rows // 2 if cap > 1 else None)
    return unfold(mine.reshape(cap, 3, h, h))


def all_factors(ring, factors):
    cap, c, _ = factors.shape
    parts = fold(factors.astype(BF16)).reshape(3 * cap, c // 2, c // 2)
    parts = yield from ring.gather(parts, 3 * cap // 2 if cap > 1 else None)
    return parts.reshape(ring.size * cap, 3, c // 2, c // 2)


def on_device(block_in, cotangent, seq_ids, weights, momentum, gains, gain_first, gain_second):
    tok_rows, model_width = block_in.shape
    rows_dp, group_blocks, head_dim = weights.shape
    head_count = lax.axis_size("head")
    data_count = lax.axis_size("dp")
    group_rows = tok_rows * head_count
    key_heads = KV // head_count
    query_heads = H // head_count
    ffn_blocks = FF // (head_dim * head_count)
    out_mark = query_heads + 2 * key_heads
    gate_mark = out_mark + query_heads
    half_dim = head_dim // 2
    full = ffn_blocks // 2
    scale = head_dim ** (-0.5)
    growth = math.sqrt(max(1.0, model_width / head_dim))
    data_index = lax.axis_index("dp")
    head_index = lax.axis_index("head")
    parity = (data_index >> 2) & 1
    ring = Ring()

    weights = jnp.transpose(weights, (1, 0, 2))
    momentum = jnp.transpose(momentum, (1, 0, 2))
    attn_low = cast_blocks(weights, gate_mark)
    inputs = block_in.astype(F32)
    normed_one, norm_one_back = jax.vjp(rms_scale, inputs, gains[0])
    ids_column = jnp.pad(seq_ids.astype(BF16)[:, None], ((0, 0), (0, 127)))

    early = full - 1
    mine_early, mine_late, other_early, other_late = pack_units(
        jnp.reshape(parity, (1,)), weights, gate_mark, ffn_blocks, early
    )
    spread = [Spread(mine_early, other_early), Spread(mine_late, other_late)]

    group_in = run(head_gather(jnp.concatenate([normed_one.astype(BF16), ids_column], axis=1)))
    qkv_parts = run(ring.gather(attn_low[:out_mark], out_mark // 2))
    qkv_blocks = jnp.transpose(qkv_parts, (1, 0, 2, 3)).reshape(out_mark, model_width, head_dim)
    cot_flow = Flow(wide_gather(cotangent))
    group_in, qkv_blocks, attn_low = stage(
        [spread[0].near(0), spread[0].y(0)], [group_in, qkv_blocks, attn_low], idle=[cot_flow]
    )
    projected = block_project(group_in, qkv_blocks)
    queries = projected[:query_heads].reshape(query_heads * group_rows, head_dim)
    group_ids = group_in[:, model_width]
    kv_rows = 2 * key_heads * group_rows
    out_rows = query_heads * rows_dp
    id_rows = group_rows // head_dim
    packed = jnp.concatenate(
        [
            projected[query_heads:].reshape(kv_rows, head_dim),
            attn_low[out_mark:].reshape(out_rows, head_dim),
            jnp.pad(group_ids.reshape(id_rows, head_dim), ((0, 16 - id_rows), (0, 0))),
        ],
        axis=0,
    )
    keys_values = run(ring.gather(packed, packed.shape[0] // 32 * 16))
    out_blocks = keys_values[:, kv_rows : kv_rows + out_rows].reshape(data_count, query_heads, rows_dp, head_dim)
    out_blocks = jnp.transpose(out_blocks, (1, 0, 2, 3)).reshape(query_heads, model_width, head_dim)
    queries, keys_values, out_blocks = stage(
        [cot_flow, spread[0].y(1), spread[1].near(0)], [queries, keys_values, out_blocks]
    )
    all_ids = keys_values[:, kv_rows + out_rows : kv_rows + out_rows + id_rows].reshape(-1)

    local = in_group(jnp.arange(group_rows, dtype=jnp.int32), group_rows, head_index * tok_rows)
    query_pos = data_index * group_rows + local
    first_pos = jnp.sum((all_ids[None, :] < group_ids[:, None]).astype(jnp.int32), axis=1)
    query_pos = jnp.tile(query_pos, query_heads)
    first_pos = jnp.tile(first_pos, query_heads)
    place = jnp.stack([data_index, head_index * tok_rows]).astype(jnp.int32)
    mixed_low, mixed_full, totals = attend(
        place, queries, keys_values, query_pos[:, None], first_pos[:, None], scale, group_rows
    )
    mixed_heads = mixed_low.reshape(query_heads, group_rows, head_dim)
    mixed_heads, mixed_full, totals, attn_part = stage(
        [spread[0].cross(), spread[1].y(0), spread[1].y(1), cot_flow],
        [mixed_heads, mixed_full, totals, block_back(mixed_heads, out_blocks)],
    )
    attn_flow = Flow(scatter_rows(*attn_part, HEAD_MOVES))
    attn_flow.advance([lax.ppermute(*send) for send in attn_flow.sends])
    stage([attn_flow, spread[0].near(3), spread[0].y(3), spread[1].cross()], idle=[cot_flow])
    residual = inputs + attn_flow.value
    normed_two, norm_two_back = jax.vjp(rms_scale, residual, gains[1])
    wide_flow = Flow(wide_gather(normed_two.astype(BF16)))
    stage([wide_flow, spread[0].y(2), spread[1].near(3), spread[1].y(3)], idle=[cot_flow])
    stage([wide_flow, spread[1].y(2), cot_flow])
    stage([wide_flow])
    finish(wide_flow, cot_flow)

    def whole_rows(pieces):
        if rows_dp % 16 == 0:
            return pieces
        out = jnp.zeros((3, data_count) + pieces[0].shape[1:], BF16)
        for k, piece in enumerate(pieces):
            out = lax.dynamic_update_index_in_dim(out, piece, data_index ^ k, 1)
        return [out.reshape(3, model_width, -1)]

    ffn_sides, ffn_full, *ffn_grads = ffn_front(
        place, wide_flow.value, cot_flow.value, whole_rows(spread[0].value()), whole_rows(spread[1].value())
    )

    def taker(pieces):
        if len(pieces) > 1:
            return lambda k: pieces[k]
        cut = pieces[0].reshape(3, data_count, rows_dp, pieces[0].shape[2])
        return lambda k: lax.dynamic_index_in_dim(cut, data_index ^ k, 1, keepdims=False)

    pieces = len(ffn_grads) // 2
    reduce = [Reduce(taker(ffn_grads[:pieces])), Reduce(taker(ffn_grads[pieces:]))]
    *down_part, dx_kept, dx_sent = stage([reduce[0].y(2)], ffn_back(ffn_sides, ffn_full))
    out_flow = Flow(scatter_rows(*down_part, WIDE_MOVES))
    dx_flow = Flow(scatter_rows(dx_kept, dx_sent, WIDE_MOVES))
    dx_flow.advance([lax.ppermute(*send) for send in dx_flow.sends])
    stage([dx_flow, reduce[0].near(2), reduce[0].y(3), reduce[1].y(2)])
    stage([dx_flow, reduce[0].y(1), reduce[1].near(2), out_flow])
    grad_residual_norm, grad_gain_two = norm_two_back(dx_flow.value)
    grad_residual = cotangent.astype(F32) + grad_residual_norm
    grad_flow = Flow(head_gather(grad_residual.astype(BF16)))
    stage([grad_flow, reduce[0].near(1), reduce[1].y(1), reduce[1].y(3)])
    grad_flow.advance([lax.ppermute(*send) for send in grad_flow.sends])
    group_grad = grad_flow.value

    grad_heads = block_project(group_grad, out_blocks)
    grad_mixed = grad_heads.reshape(query_heads * group_rows, head_dim)
    delta = jnp.sum(grad_mixed.astype(F32) * mixed_full, axis=1)
    grad_queries, grad_keys_values = attend_back(
        place,
        queries,
        grad_mixed,
        keys_values,
        1.0 / totals.reshape(1, -1),
        delta[None, :],
        query_pos[None, :],
        first_pos[None, :],
        scale,
        group_rows,
    )
    group_grad, grad_queries, grad_keys_values = stage(
        [reduce[0].cross(), reduce[1].near(1), reduce[0].y(0), reduce[1].y(0)],
        [group_grad, grad_queries, grad_keys_values],
    )
    grad_queries = grad_queries.reshape(query_heads, group_rows, head_dim)

    late = 2
    main = 3 * ffn_blocks - late
    cap = -(-main // data_count)
    places = -(-max(cap * data_count, 3 * ffn_blocks) // TRIO) * TRIO
    def weight_sums(outer):
        cut = outer.reshape(outer.shape[0], data_count, rows_dp, head_dim)
        return Flow(ring.scatter(ring.part(cut, 1), outer.shape[0] // 2 if outer.shape[0] > 2 else None))

    key_flow = Flow(ring.scatter(ring.part(grad_keys_values, 0), key_heads))
    (outer,) = stage(
        [key_flow, reduce[1].cross(), out_flow],
        [block_outer([group_in, group_grad], [grad_queries, mixed_heads], model_width)],
    )
    (own_early, other_early), (own_late, other_late) = (part.value() for part in reduce)
    first_flow = weight_sums(outer)
    weight_grads, new_momentum, grams = stage(
        [key_flow, first_flow],
        ffn_moment(
            jnp.reshape(parity, (1,)),
            [own_early, own_late],
            [other_early, other_late],
            momentum,
            gate_mark,
            ffn_blocks,
            places,
        ),
    )
    gram_flow = Flow(gram_sums(ring, grams, cap))
    stage([key_flow, first_flow, gram_flow])
    while key_flow.sends is not None:
        stage([key_flow, first_flow, gram_flow])
    key_value_sums = key_flow.value
    grad_keys = (key_value_sums[:key_heads] * scale).astype(BF16)
    grad_values = key_value_sums[key_heads:].astype(BF16)
    grad_keys_values = jnp.concatenate([grad_keys, grad_values], axis=0)
    (outer,) = stage([first_flow, gram_flow], [block_outer([group_in], [grad_keys_values], model_width)])
    finish(first_flow)
    second_flow = weight_sums(outer)
    pairs = [k for k in range(gate_mark // 2) if not query_heads <= 2 * k < out_mark]
    grad_projected = jnp.concatenate([grad_queries, grad_keys_values], axis=0)
    *attn_dx, weight_grads, new_momentum, first_grams = stage(
        [second_flow, gram_flow],
        [
            *block_back(grad_projected, qkv_blocks),
            *attn_moment(first_flow.value, pairs, momentum, weight_grads, new_momentum),
        ],
    )
    last_flow = Flow(scatter_rows(*attn_dx, HEAD_MOVES))
    finish(gram_flow)
    gram_value = gram_flow.value
    while second_flow.sends is not None:
        (gram_value,) = stage([second_flow, last_flow, out_flow], [gram_value])
    finish(last_flow, out_flow)
    block_out = (residual + out_flow.value).astype(BF16)
    grad_input_norm, grad_gain_one = norm_one_back(last_flow.value)
    grad_input = grad_residual + grad_input_norm
    gain_flow = Flow(total_sum(jnp.stack([grad_gain_one, grad_gain_two])))
    weight_grads, new_momentum, second_grams = attn_moment(
        second_flow.value, list(range(query_heads // 2, out_mark // 2)), momentum, weight_grads, new_momentum
    )
    late_count = gate_mark + late
    late_cap = -(-late_count // data_count)
    late_grams = jnp.concatenate([first_grams, second_grams, grams[main : main + late]], axis=0)
    late_grams = jnp.pad(late_grams, ((0, late_cap * data_count - late_count), (0, 0), (0, 0), (0, 0)))
    factors = newton_factor(gram_value, growth)
    factors = run(all_factors(ring, factors))

    threes = main // TRIO
    early_spots = [(gate_mark // TRIO + k, [TRIO * k + i for i in range(TRIO)]) for k in range(threes)]
    late_sums, factors = stage([gain_flow], [run(gram_sums(ring, late_grams, late_cap)), factors])
    (late_factors,) = stage([gain_flow], [newton_factor(late_sums, growth)])
    late_factor_flow = Flow(all_factors(ring, late_factors))
    new_weights = []
    for k in range(0, threes, 2):
        new_weights = stage(
            [late_factor_flow, gain_flow],
            [renew(weights, new_momentum, factors, early_spots[k : k + 2], new_weights)],
        )

    finish(late_factor_flow, gain_flow)
    gain_grads = gain_flow.value
    rest = jnp.concatenate([late_factor_flow.value[:late_count], factors[TRIO * threes : main]], axis=0)
    blocks_of = [2 * pair + i for pair in pairs for i in range(2)] + list(range(query_heads, out_mark))
    blocks_of += [gate_mark + main + k for k in range(late)] + [gate_mark + k for k in range(TRIO * threes, main)]
    late_spots = [
        (spot, [blocks_of.index(TRIO * spot + i) for i in range(TRIO)])
        for spot in sorted({block // TRIO for block in blocks_of})
    ]
    new_weights = renew(weights, new_momentum, rest, late_spots, new_weights)

    new_gain_first = BETA_ONE * gain_first + (1.0 - BETA_ONE) * gain_grads
    new_gain_second = BETA_TWO * gain_second + (1.0 - BETA_TWO) * gain_grads * gain_grads
    first_hat = new_gain_first / (1.0 - BETA_ONE**UPDATE_STEP)
    second_hat = new_gain_second / (1.0 - BETA_TWO**UPDATE_STEP)
    new_gains = gains - ADAM_RATE * first_hat / (jnp.sqrt(second_hat) + ADAM_EPS)
    back = lambda array: jnp.transpose(array, (1, 0, 2))
    return (
        block_out,
        grad_input,
        back(weight_grads),
        back(new_momentum),
        back(new_weights),
        gain_grads,
        new_gain_first,
        new_gain_second,
        new_gains,
    )


def solution(mesh):
    return jax.shard_map(
        on_device,
        mesh=mesh,
        in_specs=(
            P(("dp", "head"), None),
            P(("dp", "head"), None),
            P(("dp", "head")),
            P("dp", "head", None),
            P("dp", "head", None),
            P(),
            P(),
            P(),
        ),
        out_specs=(
            P(("dp", "head"), None),
            P(("dp", "head"), None),
            P("dp", "head", None),
            P("dp", "head", None),
            P("dp", "head", None),
            P(),
            P(),
            P(),
            P(),
        ),
        check_vma=False,
    )
```

```python
import functools
import math

import jax
import jax.numpy as jnp
from jax import lax
from jax.experimental import pallas as pl
from jax.experimental.pallas import tpu as pltpu
from jax.sharding import PartitionSpec as P

H = 8
KV = 4
FF = 9216
NEWTON_STEPS = 5
UPDATE_STEP = 10

NORM_EPS = 1e-06
SOFT_CAP = 50.0
MUON_RATE = 0.2
MUON_DECAY = 0.01
MUON_BETA = 0.95
ADAM_RATE = 0.3
BETA_ONE = 0.9
BETA_TWO = 0.95
ADAM_EPS = 1e-08
NEWTON_LINEAR = 3.4445
NEWTON_SQUARE = -4.775
NEWTON_CUBIC = 2.0315
NEWTON_PRECISION = lax.Precision.HIGH

BF16 = jnp.bfloat16
F32 = jnp.float32
VMEM_LIMIT = 62 * 1024 * 1024
NN = (((1,), (0,)), ((), ()))
NT = (((1,), (1,)), ((), ()))
TN = (((0,), (0,)), ((), ()))


def mm(a, b, dims):
    return lax.dot_general(a, b, dims, preferred_element_type=F32)


def rms_scale(rows, gain):
    inverse = lax.rsqrt(jnp.mean(rows * rows, axis=-1, keepdims=True) + NORM_EPS)
    return rows * inverse * gain


class Flow:
    def __init__(self, steps):
        self.steps = steps
        self.value = None
        self.sends = None
        self.advance(None)

    def advance(self, arrived):
        try:
            self.sends = self.steps.send(arrived)
        except StopIteration as stop:
            self.sends = None
            self.value = stop.value


def stage(flows, extra=(), idle=()):
    flows = [flow for flow in flows if flow.sends is not None]
    idle = [flow for flow in idle if flow.sends is not None and flow not in flows]
    arrived = [[lax.ppermute(*send) for send in flow.sends] for flow in flows]
    held = [[send[0] for send in flow.sends] for flow in idle]
    arrived, held, extra = lax.optimization_barrier((arrived, held, list(extra)))
    for flow, got in zip(flows, arrived):
        flow.advance(got)
    for flow, kept in zip(idle, held):
        flow.sends = [(value,) + send[1:] for value, send in zip(kept, flow.sends)]
    return extra


def run(steps):
    flow = Flow(steps)
    while flow.sends is not None:
        flow.advance([lax.ppermute(*send) for send in flow.sends])
    return flow.value


def finish(*flows):
    while any(flow.sends is not None for flow in flows):
        stage(flows)


def swap(value, axis, mask):
    size = lax.axis_size(axis)
    return (value, axis, [(i, i ^ mask) for i in range(size)])


def head_gather(rows):
    (other,) = yield [swap(rows, "head", 2)]
    pair = jnp.concatenate([rows, other], axis=0)
    (other,) = yield [swap(pair, "head", 1)]
    return jnp.concatenate([pair, other], axis=0)


def wide_gather(rows):
    (other,) = yield [swap(rows, "dp", 4)]
    both = jnp.concatenate([rows, other], axis=0)
    (other,) = yield [swap(both, "head", 2)]
    pair = jnp.concatenate([both, other], axis=0)
    (other,) = yield [swap(pair, "head", 1)]
    return [pair, other]


def add_low(kept, other):
    return (kept.astype(F32) + other.astype(F32)).astype(BF16)


def scatter_rows(kept, sent, moves):
    for k, (axis, mask) in enumerate(moves):
        (other,) = yield [swap(sent, axis, mask)]
        part = kept.astype(F32) + other.astype(F32)
        if k < len(moves) - 1:
            half = part.shape[0] // 2
            kept, sent = part[:half], part[half:].astype(BF16)
    return part


HEAD_MOVES = (("head", 1), ("head", 2))
WIDE_MOVES = (("head", 1), ("head", 2), ("dp", 4))


def total_sum(value):
    for axis in ("head", "dp"):
        mask = 1
        while mask < lax.axis_size(axis):
            (other,) = yield [swap(value, axis, mask)]
            value = value + other
            mask *= 2
    return value


class Ring:
    def __init__(self):
        size = lax.axis_size("dp")
        order = list(range(0, size, 2)) + list(range(size - 1, 0, -2))
        around = [[order[(order.index(i) + offset) % size] for offset in range(size)] for i in range(size)]
        self.size = size
        row = jnp.array(around, jnp.int32)[lax.axis_index("dp")]
        self.around = lax.optimization_barrier([row[k] for k in range(size)])
        self.up = [(order[k], order[(k + 1) % size]) for k in range(size)]
        self.down = [(order[(k + 1) % size], order[k]) for k in range(size)]

    def index(self, offset, scale=1):
        return self.around[offset % self.size] * scale

    def gather(self, value, mid):
        half = self.size // 2
        out = jnp.zeros((self.size,) + value.shape, value.dtype)

        def put(out, piece, offset, start=0):
            spot = (self.index(offset), start) + (0,) * (value.ndim - 1)
            return lax.dynamic_update_slice(out, piece[None], spot, allow_negative_indices=False)

        out = put(out, value, 0)
        ahead, back = value, value
        for step in range(1, half):
            ahead, back = yield [(ahead, "dp", self.up), (back, "dp", self.down)]
            out = put(put(out, ahead, -step), back, step)
        if mid is None:
            (last,) = yield [(ahead, "dp", self.up)]
            return put(out, last, half)
        first, second = yield [(ahead[:mid], "dp", self.up), (back[mid:], "dp", self.down)]
        return put(put(out, first, half), second, half, mid)

    def part(self, array, axis, size=None):
        if size is None:
            return lambda offset: lax.dynamic_index_in_dim(
                array, self.index(offset), axis, keepdims=False, allow_negative_indices=False
            )
        return lambda offset: lax.dynamic_slice_in_dim(
            array, self.index(offset, size), size, axis, allow_negative_indices=False
        )

    def scatter(self, take, mid):
        half = self.size // 2
        far = take(half)
        kind = far.dtype
        if mid is None:
            (up,) = yield [(far, "dp", self.up)]
            down = None
        else:
            up, down = yield [(far[:mid], "dp", self.up), (far[mid:], "dp", self.down)]
        for step in range(half - 1, 0, -1):
            ahead, back = take(step).astype(F32), take(-step).astype(F32)
            if mid is None or step < half - 1:
                ahead = ahead + up
                back = back if down is None else back + down
            else:
                ahead = jnp.concatenate([ahead[:mid] + up, ahead[mid:]])
                back = jnp.concatenate([back[:mid], back[mid:] + down])
            up, down = yield [(ahead.astype(kind), "dp", self.up), (back.astype(kind), "dp", self.down)]
        return take(0).astype(F32) + up.astype(F32) + down.astype(F32)


def once(sends, take):
    def steps():
        take((yield sends))

    return Flow(steps())


SIDE_BIT = 2


def plane_classes():
    planes = range(lax.axis_size("dp") // 2)
    kept = [m for m in planes if m & 3 in (0, 3)]
    passed = [m for m in planes if m & 3 in (1, 2)]
    return {0: [0], 1: [1], 2: [m for m in passed if m != 1], 3: [m for m in kept if m]}


class Spread:
    def __init__(self, mine, other):
        self.mine, self.other = mine, other
        self.pieces = {0: mine}

    def move(self, moves):
        def take(arrived):
            for (_, _, _, number), piece in zip(moves, arrived):
                self.pieces[number] = piece

        return once([swap(value, "dp", offset << 1 | bit) for value, offset, bit, _ in moves], take)

    def cross(self):
        group = plane_classes()[3]
        return self.move([(self.other if m & SIDE_BIT else self.mine, m, 0, m << 1) for m in group])

    def near(self, key):
        group = plane_classes()[key]
        return self.move([(self.pieces[m << 1], 1, 0, (m ^ 1) << 1) for m in group])

    def y(self, key):
        group = plane_classes()[key]
        return self.move([(self.pieces[m << 1], 0, 1, m << 1 | 1) for m in group])

    def value(self):
        return [self.pieces[k] for k in range(lax.axis_size("dp"))]


class Reduce:
    def __init__(self, rows):
        self.rows = rows
        self.parts = {}
        self.sums = [[], []]

    def part(self, offset):
        terms = [term.astype(F32) for term in self.parts[offset]]
        return functools.reduce(jnp.add, terms)

    def hold(self, offset, *terms):
        self.parts.setdefault(offset, []).extend(terms)

    def y(self, key):
        group = plane_classes()[key]

        def take(arrived):
            for offset, got in zip(group, arrived):
                self.hold(offset, self.rows(offset << 1), got)

        return once([swap(self.rows(offset << 1 | 1), "dp", 1) for offset in group], take)

    def near(self, key):
        group = plane_classes()[key]

        def take(arrived):
            for offset, got in zip(group, arrived):
                self.hold(offset ^ 1, got)

        return once([swap(self.part(offset).astype(BF16), "dp", 2) for offset in group], take)

    def cross(self):
        group = plane_classes()[3]

        def take(arrived):
            for offset, got in zip(group, arrived):
                self.sums[1 if offset & SIDE_BIT else 0].append(got)

        return once([swap(self.part(offset).astype(BF16), "dp", offset << 1) for offset in group], take)

    def value(self):
        return self.parts[0] + self.sums[0], self.sums[1]


def params(**more):
    return pltpu.CompilerParams(vmem_limit_bytes=VMEM_LIMIT, **more)


TRIO = 3


def cast_blocks(blocks, count):
    _, r, c = blocks.shape

    def body(x_ref, o_ref):
        o_ref[...] = x_ref[...].astype(BF16)

    spec = pl.BlockSpec((TRIO, r, c), lambda k: (k, 0, 0))
    return pl.pallas_call(
        body,
        grid=(count // TRIO,),
        in_specs=[spec],
        out_specs=spec,
        out_shape=jax.ShapeDtypeStruct((count, r, c), BF16),
        compiler_params=params(),
        cost_estimate=pl.CostEstimate(flops=0, bytes_accessed=6 * count * r * c, transcendentals=0),
    )(blocks)


def pack_units(parity, blocks, first, kind_blocks, early):
    _, r, c = blocks.shape
    h = c // 2
    full = kind_blocks // 2
    each = kind_blocks // TRIO
    u, v = early * c, (full - early) * c + h

    def body(s_ref, *refs):
        parts, outs = refs[:each], refs[each:]

        def tile(f):
            return parts[f // TRIO].at[f % TRIO]

        for turn in range(2):

            @pl.when(s_ref[0] == turn)
            def _():
                for k in range(2):
                    side = turn ^ k
                    for i in range(full):
                        value = tile(side * full + i)[...].astype(BF16)
                        if i < early:
                            outs[2 * k][:, i * c : (i + 1) * c] = value
                        else:
                            outs[2 * k + 1][:, (i - early) * c : (i - early + 1) * c] = value
                    rest = tile(2 * full)[:, side * h : (side + 1) * h]
                    outs[2 * k + 1][:, v - h :] = rest.astype(BF16)

    def part(i):
        return pl.BlockSpec((TRIO, r, c), lambda k, s: (first // TRIO + each * k + i, 0, 0))

    wide = pl.BlockSpec((None, r, u), lambda k, s: (k, 0, 0))
    slim = pl.BlockSpec((None, r, v), lambda k, s: (k, 0, 0))
    shapes = [jax.ShapeDtypeStruct((3, r, u), BF16), jax.ShapeDtypeStruct((3, r, v), BF16)]
    return pl.pallas_call(
        body,
        grid_spec=pltpu.PrefetchScalarGridSpec(
            num_scalar_prefetch=1,
            grid=(3,),
            in_specs=[part(i) for i in range(each)],
            out_specs=[wide, slim, wide, slim],
        ),
        out_shape=shapes + shapes,
        compiler_params=params(),
        cost_estimate=pl.CostEstimate(flops=0, bytes_accessed=18 * kind_blocks * r * c, transcendentals=0),
    )(parity, *([blocks] * each))


def block_project(rows, blocks):
    t = rows.shape[0]
    count, d, c = blocks.shape

    def body(x_ref, w_ref, o_ref):
        o_ref[...] = mm(x_ref[...], w_ref[...], NN).astype(BF16)

    return pl.pallas_call(
        body,
        grid=(count,),
        in_specs=[
            pl.BlockSpec((t, d), lambda b: (0, 0)),
            pl.BlockSpec((None, d, c), lambda b: (b, 0, 0)),
        ],
        out_specs=pl.BlockSpec((None, t, c), lambda b: (b, 0, 0)),
        out_shape=jax.ShapeDtypeStruct((count, t, c), BF16),
        compiler_params=params(),
        cost_estimate=pl.CostEstimate(
            flops=2 * count * t * d * c, bytes_accessed=2 * (t * d + count * (d * c + t * c)), transcendentals=0
        ),
    )(rows, blocks)


def block_back(cols, blocks):
    count, t, c = cols.shape
    d = blocks.shape[1]
    half = t // 2

    def body(x_ref, w_ref, o_ref, p_ref, acc_ref):
        b = pl.program_id(0)

        @pl.when(b == 0)
        def _():
            acc_ref[...] = jnp.zeros_like(acc_ref)

        acc_ref[...] += mm(x_ref[...], w_ref[...], NT)

        @pl.when(b == count - 1)
        def _():
            o_ref[...] = acc_ref[:half, :].astype(BF16)
            p_ref[...] = acc_ref[half:, :].astype(BF16)

    result = pl.BlockSpec((half, d), lambda b: (0, 0))
    return pl.pallas_call(
        body,
        grid=(count,),
        in_specs=[
            pl.BlockSpec((None, t, c), lambda b: (b, 0, 0)),
            pl.BlockSpec((None, d, c), lambda b: (b, 0, 0)),
        ],
        out_specs=[result, result],
        out_shape=[jax.ShapeDtypeStruct((half, d), BF16)] * 2,
        scratch_shapes=[pltpu.VMEM((t, d), F32)],
        compiler_params=params(),
        cost_estimate=pl.CostEstimate(
            flops=2 * count * t * d * c, bytes_accessed=2 * (t * d + count * (d * c + t * c)), transcendentals=0
        ),
    )(cols, blocks)


def block_outer(rows, cols, d):
    t = rows[0].shape[0]
    c = cols[0].shape[2]
    starts = [0]
    for col in cols:
        starts.append(starts[-1] + col.shape[0])
    count = len(rows)
    total = starts[-1]

    def body(*refs):
        o_ref, t_ref = refs[2 * count :]
        b = pl.program_id(0)
        for k in range(count):

            @pl.when(b == starts[k])
            def _():
                t_ref[...] = refs[k][...].T

            @pl.when((b >= starts[k]) & (b < starts[k + 1]))
            def _():
                o_ref[...] = mm(t_ref[...], refs[count + k][...], NN).astype(BF16)

    def col_at(k):
        return pl.BlockSpec((None, t, c), lambda b: (jnp.clip(b - starts[k], 0, starts[k + 1] - starts[k] - 1), 0, 0))

    return pl.pallas_call(
        body,
        grid=(total,),
        in_specs=[pl.BlockSpec((t, d), lambda b: (0, 0))] * count + [col_at(k) for k in range(count)],
        out_specs=pl.BlockSpec((None, d, c), lambda b: (b, 0, 0)),
        out_shape=jax.ShapeDtypeStruct((total, d, c), BF16),
        scratch_shapes=[pltpu.VMEM((d, t), BF16)],
        compiler_params=params(),
        cost_estimate=pl.CostEstimate(
            flops=2 * total * t * d * c,
            bytes_accessed=2 * (count * t * d + total * (d * c + t * c)),
            transcendentals=0,
        ),
    )(*rows, *cols)


def in_group(local, width, head_shift):
    quarter = width // 4
    low = jnp.bitwise_and(local, quarter - 1)
    one = jnp.where(jnp.bitwise_and(local, quarter) != 0, 2 * quarter, 0)
    two = jnp.where(jnp.bitwise_and(local, 2 * quarter) != 0, quarter, 0)
    return jnp.bitwise_xor(low + one + two, head_shift)


def key_position(block, width, head_shift, shape, axis):
    local = lax.broadcasted_iota(jnp.int32, shape, axis)
    return block * width + in_group(local, width, head_shift)


def attend(place, queries, keys_values, query_pos, first_pos, scale, p):
    m, e = queries.shape
    n = keys_values.shape[0]
    step = 256

    def body(place_ref, q_ref, kv_ref, pos_ref, first_ref, low_ref, full_ref, sum_ref, acc_ref, tot_ref):
        j = pl.program_id(0)

        @pl.when(j == 0)
        def _():
            acc_ref[...] = jnp.zeros_like(acc_ref)
            tot_ref[...] = jnp.zeros_like(tot_ref)

        @pl.when(j <= place_ref[0])
        def _():
            key_pos = key_position(j, p, place_ref[1], (1, p), 1)
            for r in range(0, m, step):
                rows = pl.ds(r, step)
                raw = mm(q_ref[rows, :], kv_ref[:p, :], NT)
                soft = SOFT_CAP * jnp.tanh(raw * (scale / SOFT_CAP))
                seen = (key_pos >= first_ref[rows, :]) & (key_pos <= pos_ref[rows, :])
                terms = jnp.where(seen, jnp.exp(soft), 0.0)
                tot_ref[rows, :] += jnp.sum(terms, axis=1, keepdims=True)
                acc_ref[rows, :] += mm(terms.astype(BF16), kv_ref[p:, :], NN)

        @pl.when(j == n - 1)
        def _():
            total = tot_ref[...]
            mixed = acc_ref[...] / total
            full_ref[...] = mixed
            low_ref[...] = mixed.astype(BF16)
            sum_ref[...] = total

    whole = lambda shape: pl.BlockSpec(shape, lambda j, s: (0, 0))
    return pl.pallas_call(
        body,
        grid_spec=pltpu.PrefetchScalarGridSpec(
            num_scalar_prefetch=1,
            grid=(n,),
            in_specs=[
                whole((m, e)),
                pl.BlockSpec((None, 2 * p, e), lambda j, s: (jnp.minimum(j, s[0]), 0, 0)),
                whole((m, 1)),
                whole((m, 1)),
            ],
            out_specs=[whole((m, e)), whole((m, e)), whole((m, 1))],
            scratch_shapes=[pltpu.VMEM((m, e), F32), pltpu.VMEM((m, 1), F32)],
        ),
        out_shape=[
            jax.ShapeDtypeStruct((m, e), BF16),
            jax.ShapeDtypeStruct((m, e), F32),
            jax.ShapeDtypeStruct((m, 1), F32),
        ],
        compiler_params=params(),
        cost_estimate=pl.CostEstimate(
            flops=4 * m * n * p * e, bytes_accessed=4 * n * p * e, transcendentals=2 * m * n * p
        ),
    )(place, queries, keys_values, query_pos, first_pos)


def attend_back(place, queries, grads, keys_values, inverse, delta, query_pos, first_pos, scale, p):
    m, e = queries.shape
    n = keys_values.shape[0]
    step = 256

    def body(
        place_ref, q_ref, g_ref, kv_ref, inv_ref, delta_ref, pos_ref, first_ref, dq_ref, dkv_ref, acc_ref, dk_ref, dv_ref
    ):
        j = pl.program_id(0)

        @pl.when(j == 0)
        def _():
            acc_ref[...] = jnp.zeros_like(acc_ref)

        @pl.when(j <= place_ref[0])
        def _():
            key_pos = key_position(j, p, place_ref[1], (p, 1), 0)
            for r in range(0, m, step):
                rows = pl.ds(r, step)
                raw = mm(kv_ref[:p, :], q_ref[rows, :], NT)
                capped = jnp.tanh(raw * (scale / SOFT_CAP))
                seen = (key_pos >= first_ref[:, rows]) & (key_pos <= pos_ref[:, rows])
                probs = jnp.where(seen, jnp.exp(SOFT_CAP * capped), 0.0) * inv_ref[:, rows]
                grad_probs = mm(kv_ref[p:, :], g_ref[rows, :], NT)
                grad_raw = probs * (grad_probs - delta_ref[:, rows]) * (1.0 - capped * capped)
                grad_low = grad_raw.astype(BF16)
                value_part = mm(probs.astype(BF16), g_ref[rows, :], NN)
                key_part = mm(grad_low, q_ref[rows, :], NN)
                if r == 0:
                    dv_ref[...] = value_part
                    dk_ref[...] = key_part
                else:
                    dv_ref[...] += value_part
                    dk_ref[...] += key_part
                acc_ref[rows, :] += mm(grad_low, kv_ref[:p, :], TN)
            dkv_ref[0] = dk_ref[...].astype(BF16)
            dkv_ref[1] = dv_ref[...].astype(BF16)

        @pl.when(j > place_ref[0])
        def _():
            dkv_ref[...] = jnp.zeros_like(dkv_ref)

        @pl.when(j == n - 1)
        def _():
            dq_ref[...] = (acc_ref[...] * scale).astype(BF16)

    whole = lambda shape: pl.BlockSpec(shape, lambda j, s: (0, 0))
    return pl.pallas_call(
        body,
        grid_spec=pltpu.PrefetchScalarGridSpec(
            num_scalar_prefetch=1,
            grid=(n,),
            in_specs=[
                whole((m, e)),
                whole((m, e)),
                pl.BlockSpec((None, 2 * p, e), lambda j, s: (jnp.minimum(j, s[0]), 0, 0)),
                whole((1, m)),
                whole((1, m)),
                whole((1, m)),
                whole((1, m)),
            ],
            out_specs=[whole((m, e)), pl.BlockSpec((None, 2, p, e), lambda j, s: (j, 0, 0, 0))],
            scratch_shapes=[pltpu.VMEM((m, e), F32), pltpu.VMEM((p, e), F32), pltpu.VMEM((p, e), F32)],
        ),
        out_shape=[jax.ShapeDtypeStruct((m, e), BF16), jax.ShapeDtypeStruct((n, 2, p, e), BF16)],
        compiler_params=params(),
        cost_estimate=pl.CostEstimate(
            flops=10 * m * n * p * e, bytes_accessed=8 * n * p * e, transcendentals=2 * m * n * p
        ),
    )(place, queries, grads, keys_values, inverse, delta, query_pos, first_pos)


def gelu_pair(gate):
    outer = math.sqrt(2.0 / math.pi)
    square = gate * gate
    bent = jnp.tanh(outer * gate * (1.0 + 0.044715 * square))
    half = 0.5 * (1.0 + bent)
    slope = half + 0.5 * gate * (1.0 - bent * bent) * outer * (1.0 + 3.0 * 0.044715 * square)
    return gate * half, slope


def ffn_front(place, rows, cots, early, late):
    part_rows, d = rows[0].shape
    t = 2 * part_rows
    count = len(early)
    r = early[0].shape[1]
    u, v = early[0].shape[2], late[0].shape[2]
    tall = min(512, t)
    wide = d // 3
    cuts = [(k, min(256, u + v - k)) for k in range(0, u + v, 256)]

    def body(place_ref, x0, x1, y0, y1, *refs):
        early_refs, late_refs = refs[:count], refs[count : 2 * count]
        refs = refs[2 * count :]
        hs_ref, w_out = refs[:2]
        grad_refs = refs[2 : 2 + count], refs[2 + count : 2 + 2 * count]
        x, y, w, xt, yt, hs, row_sems, sems, out_sems, grad_sems = refs[2 + 2 * count :]
        row_copies = []
        for k, (source, target) in enumerate(((x0, x), (x1, x), (y0, y), (y1, y))):
            target = target.at[pl.ds((k % 2) * part_rows, part_rows), :]
            row_copies.append(pltpu.make_async_copy(source, target, row_sems.at[k]))
            row_copies[k].start()
        copies = []
        chunks = ((early_refs, pl.ds(0, u)), (late_refs, pl.ds(u, v)))

        def spot(k):
            return pl.ds(pl.multiple_of(jnp.bitwise_xor(place_ref[0], k) * r, 16) if count > 1 else 0, r)

        for k in range(count):
            for way, (sources, lanes) in enumerate(chunks):
                copy = pltpu.make_async_copy(sources[k], w.at[:, spot(k), lanes], sems.at[way, k])
                copy.start()
                copies.append(copy)
        for copy in row_copies:
            copy.wait()

        @pl.loop(0, d // 256)
        def _(k):
            cols = pl.ds(pl.multiple_of(k * 256, 256), 256)
            xt[cols, :] = x[:, cols].T
            yt[cols, :] = y[:, cols].T

        for copy in copies:
            copy.wait()
        kept = pltpu.make_async_copy(w, w_out, out_sems.at[0])
        kept.start()

        @pl.loop(0, t // tall)
        def _(i):
            part = pl.ds(pl.multiple_of(i * tall, tall), tall)
            for start, size in cuts:
                units = pl.ds(start, size)
                gate = mm(x[part, :], w[0, :, units], NN)
                up = mm(x[part, :], w[1, :, units], NN)
                grad = mm(y[part, :], w[2, :, units], NN)
                active, slope = gelu_pair(gate)
                hs[0, part, units] = (active * up).astype(BF16)
                hs[1, part, units] = (grad * up * slope).astype(BF16)
                hs[2, part, units] = (grad * active).astype(BF16)

        sides = pltpu.make_async_copy(hs, hs_ref, out_sems.at[1])
        sides.start()
        kept.wait()
        copies = []
        for kind, (left, right) in enumerate(((xt, 1), (xt, 2), (yt, 0))):

            @pl.loop(0, d // wide)
            def _(k):
                cols = pl.ds(pl.multiple_of(k * wide, wide), wide)
                w[kind, cols, :] = mm(left[cols, :], hs[right], NN).astype(BF16)

            for k in range(count):
                for way, (_, lanes) in enumerate(chunks):
                    target = grad_refs[way][k].at[kind]
                    copy = pltpu.make_async_copy(w.at[kind, spot(k), lanes], target, grad_sems.at[kind, way, k])
                    copy.start()
                    copies.append(copy)
        sides.wait()
        for copy in copies:
            copy.wait()

    apart = pl.BlockSpec(memory_space=pl.ANY)
    return pl.pallas_call(
        body,
        grid_spec=pltpu.PrefetchScalarGridSpec(
            num_scalar_prefetch=1,
            grid=(1,),
            in_specs=[apart] * (4 + 2 * count),
            out_specs=[apart] * (2 + 2 * count),
            scratch_shapes=[
                pltpu.VMEM((t, d), BF16),
                pltpu.VMEM((t, d), BF16),
                pltpu.VMEM((3, d, u + v), BF16),
                pltpu.VMEM((d, t), BF16),
                pltpu.VMEM((d, t), BF16),
                pltpu.VMEM((3, t, u + v), BF16),
                pltpu.SemaphoreType.DMA((4,)),
                pltpu.SemaphoreType.DMA((2, count)),
                pltpu.SemaphoreType.DMA((2,)),
                pltpu.SemaphoreType.DMA((3, 2, count)),
            ],
        ),
        out_shape=[
            jax.ShapeDtypeStruct((3, t, u + v), BF16),
            jax.ShapeDtypeStruct((3, d, u + v), BF16),
            *[jax.ShapeDtypeStruct((3, r, u), BF16)] * count,
            *[jax.ShapeDtypeStruct((3, r, v), BF16)] * count,
        ],
        compiler_params=params(),
        cost_estimate=pl.CostEstimate(
            flops=12 * t * d * (u + v), bytes_accessed=12 * d * (u + v) + 4 * t * d, transcendentals=t * (u + v)
        ),
    )(place, *rows, *cots, *early, *late)


def ffn_back(sides, blocks):
    _, t, u = sides.shape
    d = blocks.shape[1]
    wide = 256
    half = t // 2

    def body(s_ref, w_ref, *refs):
        for k in range(2):
            part = pl.ds(k * half, half)
            refs[k][...] = mm(s_ref[0, part, :], w_ref[2], NT).astype(BF16)
            refs[2 + k][...] = (mm(s_ref[1, part, :], w_ref[0], NT) + mm(s_ref[2, part, :], w_ref[1], NT)).astype(BF16)

    return pl.pallas_call(
        body,
        grid=(d // wide,),
        in_specs=[
            pl.BlockSpec((3, t, u), lambda k: (0, 0, 0), pipeline_mode=pl.Buffered(1)),
            pl.BlockSpec((3, wide, u), lambda k: (0, k, 0)),
        ],
        out_specs=[pl.BlockSpec((half, wide), lambda k: (0, k))] * 4,
        out_shape=[jax.ShapeDtypeStruct((half, d), BF16)] * 4,
        compiler_params=params(),
        cost_estimate=pl.CostEstimate(
            flops=6 * t * d * u, bytes_accessed=6 * d * u + 6 * t * u + 4 * t * d, transcendentals=0
        ),
    )(sides, blocks)


def gram_parts(m):
    h = m.shape[1] // 2
    high = m.astype(BF16)
    low = (m - high.astype(F32)).astype(BF16)
    mixed = mm(high, low, TN)
    gram = mm(high, high, TN) + mm(low, low, TN) + mixed + mixed.T
    return gram[:h, :h], gram[:h, h:], gram[h:, h:]


def ffn_moment(parity, own, other, momentum, first, blocks, places):
    total, r, c = momentum.shape
    terms = [*own, *other]
    counts = [len(group) for group in terms]
    u, v = own[0][0].shape[2], own[1][0].shape[2]
    early = u // c
    h = c // 2
    full = early + 1
    each = blocks // TRIO

    def body(s_ref, *refs):
        groups = []
        for count in counts:
            groups.append(refs[:count])
            refs = refs[count:]
        m_ref, wg_ref, nm_ref, gram_ref = refs
        j = pl.program_id(0)

        def total_of(group, start, size):
            lanes = pl.ds(start, size)
            return functools.reduce(jnp.add, [ref[:, lanes].astype(F32) for ref in group])

        @pl.when(j >= TRIO * each)
        def _():
            gram_ref[...] = jnp.zeros_like(gram_ref)

        for turn in range(each):
            for mine in range(2):

                @pl.when((j < TRIO * each) & (lax.rem(j, each) == turn) & (s_ref[0] == mine))
                def _():
                    for i in range(TRIO):
                        side, f = divmod(turn * TRIO + i, full)
                        if side == 2:
                            for k in range(2):
                                group = groups[1 if k == mine else 3]
                                wg_ref[i, :, k * h : (k + 1) * h] = total_of(group, c, h)
                        elif f < early:
                            wg_ref[i] = total_of(groups[0 if side == mine else 2], f * c, c)
                        else:
                            wg_ref[i] = total_of(groups[1 if side == mine else 3], 0, c)

        @pl.when(j < TRIO * each)
        def _():
            for i in range(TRIO):
                new = MUON_BETA * m_ref[i] + wg_ref[i]
                nm_ref[i] = new
                gram_ref[i, 0], gram_ref[i, 1], gram_ref[i, 2] = gram_parts(new)

    kind = lambda j, s: (jnp.minimum(j // each, 2), 0, 0)
    block = lambda j, s: (first // TRIO + jnp.minimum(j, TRIO * each - 1), 0, 0)
    arrays = [array for group in terms for array in group]
    return pl.pallas_call(
        body,
        grid_spec=pltpu.PrefetchScalarGridSpec(
            num_scalar_prefetch=1,
            grid=(places // TRIO,),
            in_specs=[pl.BlockSpec((None,) + array.shape[1:], kind) for array in arrays]
            + [pl.BlockSpec((TRIO, r, c), block)],
            out_specs=[
                pl.BlockSpec((TRIO, r, c), block),
                pl.BlockSpec((TRIO, r, c), block),
                pl.BlockSpec((TRIO, 3, h, h), lambda j, s: (j, 0, 0, 0)),
            ],
        ),
        out_shape=[
            jax.ShapeDtypeStruct((total, r, c), F32),
            jax.ShapeDtypeStruct((total, r, c), F32),
            jax.ShapeDtypeStruct((places, 3, h, h), F32),
        ],
        compiler_params=params(),
        cost_estimate=pl.CostEstimate(
            flops=6 * 3 * blocks * r * c * c, bytes_accessed=16 * 3 * blocks * r * c, transcendentals=0
        ),
    )(parity, *arrays, momentum)


def attn_moment(grads, pairs, momentum, weight_grads, new_momentum):
    count, r, c = grads.shape
    h = c // 2

    def body(s_ref, g_ref, m_ref, wg_in, nm_in, wg_ref, nm_ref, gram_ref):
        for i in range(2):
            new = MUON_BETA * m_ref[i] + g_ref[i]
            wg_ref[i] = g_ref[i]
            nm_ref[i] = new
            gram_ref[i, 0], gram_ref[i, 1], gram_ref[i, 2] = gram_parts(new)

    block = pl.BlockSpec((2, r, c), lambda j, s: (s[j], 0, 0))
    apart = pl.BlockSpec(memory_space=pl.ANY)
    return pl.pallas_call(
        body,
        grid_spec=pltpu.PrefetchScalarGridSpec(
            num_scalar_prefetch=1,
            grid=(count // 2,),
            in_specs=[pl.BlockSpec((2, r, c), lambda j, s: (j, 0, 0)), block, apart, apart],
            out_specs=[block, block, pl.BlockSpec((2, 3, h, h), lambda j, s: (j, 0, 0, 0))],
        ),
        out_shape=[
            jax.ShapeDtypeStruct(momentum.shape, F32),
            jax.ShapeDtypeStruct(momentum.shape, F32),
            jax.ShapeDtypeStruct((count, 3, h, h), F32),
        ],
        input_output_aliases={3: 0, 4: 1},
        compiler_params=params(),
        cost_estimate=pl.CostEstimate(
            flops=6 * count * r * c * c, bytes_accessed=16 * count * r * c, transcendentals=0
        ),
    )(jnp.array(pairs, jnp.int32), grads, momentum, weight_grads, new_momentum)


def renew(weights, momentum, factors, spots, updated):
    _, r, c = weights.shape
    h = c // 2
    steps = len(spots)
    table = jnp.array([spot for spot, _ in spots] + [f for _, places in spots for f in places], jnp.int32)

    def body(s_ref, w_ref, m_ref, *refs):
        factor_refs, o_ref = refs[:TRIO], refs[-1]
        for i in range(TRIO):
            left = m_ref[i, :, :h].astype(BF16)
            right = m_ref[i, :, h:].astype(BF16)
            first, off, last = factor_refs[i][0], factor_refs[i][1], factor_refs[i][2]
            start = mm(left, first, NN) + mm(right, off, NT)
            rest = mm(left, off, NN) + mm(right, last, NN)
            keep = 1.0 - MUON_RATE * MUON_DECAY
            o_ref[i, :, :h] = w_ref[i, :, :h] * keep - MUON_RATE * start
            o_ref[i, :, h:] = w_ref[i, :, h:] * keep - MUON_RATE * rest

    block = pl.BlockSpec((TRIO, r, c), lambda j, s: (s[j], 0, 0))

    def factor_at(i):
        return pl.BlockSpec((None, 3, h, h), lambda j, s: (s[steps + TRIO * j + i], 0, 0, 0))

    apart = [pl.BlockSpec(memory_space=pl.ANY)] * len(updated)
    return pl.pallas_call(
        body,
        grid_spec=pltpu.PrefetchScalarGridSpec(
            num_scalar_prefetch=1,
            grid=(steps,),
            in_specs=[block, block] + [factor_at(i) for i in range(TRIO)] + apart,
            out_specs=block,
        ),
        out_shape=jax.ShapeDtypeStruct(weights.shape, F32),
        input_output_aliases={3 + TRIO: 0} if updated else {},
        compiler_params=params(),
        cost_estimate=pl.CostEstimate(
            flops=2 * TRIO * steps * r * c * c, bytes_accessed=12 * TRIO * steps * r * c, transcendentals=0
        ),
    )(table, weights, momentum, *([factors] * TRIO), *updated)


def top(spec, a, b):
    return jnp.einsum(spec, a, b, precision=NEWTON_PRECISION)


def newton_factor(grams, growth):
    size = grams.shape[-1]
    eye = jnp.eye(size, dtype=F32)
    norm = jnp.sqrt(jnp.sum(grams * eye, axis=(1, 2), keepdims=True))
    inverse = 1.0 / (norm + 1e-07)
    gram = grams * (inverse * inverse)
    factor = None
    for sweep in range(NEWTON_STEPS):
        square = top("bij,bjk->bik", gram, gram)
        poly = NEWTON_LINEAR * eye + NEWTON_SQUARE * gram + NEWTON_CUBIC * square
        factor = poly if sweep == 0 else top("bij,bjk->bik", factor, poly)
        if sweep < NEWTON_STEPS - 1:
            gram = top("bij,bjk->bik", top("bij,bjk->bik", gram, poly), poly)
    return factor * (growth * inverse)


def fold(squares):
    h = squares.shape[1] // 2
    return jnp.stack([squares[:, :h, :h], squares[:, :h, h:], squares[:, h:, h:]], axis=1)


def unfold(parts):
    first, off, last = parts[:, 0], parts[:, 1], parts[:, 2]
    upper = jnp.concatenate([first, off], axis=2)
    lower = jnp.concatenate([jnp.swapaxes(off, 1, 2), last], axis=2)
    return jnp.concatenate([upper, lower], axis=1)


def gram_sums(ring, parts, cap):
    h = parts.shape[2]
    parts = parts.reshape(-1, h, h)
    rows = 3 * cap
    mine = yield from ring.scatter(ring.part(parts, 0, rows), rows // 2 if cap > 1 else None)
    return unfold(mine.reshape(cap, 3, h, h))


def all_factors(ring, factors):
    cap, c, _ = factors.shape
    parts = fold(factors.astype(BF16)).reshape(3 * cap, c // 2, c // 2)
    parts = yield from ring.gather(parts, 3 * cap // 2 if cap > 1 else None)
    return parts.reshape(ring.size * cap, 3, c // 2, c // 2)


def on_device(block_in, cotangent, seq_ids, weights, momentum, gains, gain_first, gain_second):
    tok_rows, model_width = block_in.shape
    rows_dp, group_blocks, head_dim = weights.shape
    head_count = lax.axis_size("head")
    data_count = lax.axis_size("dp")
    group_rows = tok_rows * head_count
    key_heads = KV // head_count
    query_heads = H // head_count
    ffn_blocks = FF // (head_dim * head_count)
    out_mark = query_heads + 2 * key_heads
    gate_mark = out_mark + query_heads
    half_dim = head_dim // 2
    full = ffn_blocks // 2
    scale = head_dim ** (-0.5)
    growth = math.sqrt(max(1.0, model_width / head_dim))
    data_index = lax.axis_index("dp")
    head_index = lax.axis_index("head")
    parity = (data_index >> 2) & 1
    ring = Ring()

    weights = jnp.transpose(weights, (1, 0, 2))
    momentum = jnp.transpose(momentum, (1, 0, 2))
    attn_low = cast_blocks(weights, gate_mark)
    inputs = block_in.astype(F32)
    normed_one, norm_one_back = jax.vjp(rms_scale, inputs, gains[0])
    ids_column = jnp.pad(seq_ids.astype(BF16)[:, None], ((0, 0), (0, 127)))

    early = full - 1
    mine_early, mine_late, other_early, other_late = pack_units(
        jnp.reshape(parity, (1,)), weights, gate_mark, ffn_blocks, early
    )
    spread = [Spread(mine_early, other_early), Spread(mine_late, other_late)]

    group_in = run(head_gather(jnp.concatenate([normed_one.astype(BF16), ids_column], axis=1)))
    qkv_parts = run(ring.gather(attn_low[:out_mark], out_mark // 2))
    qkv_blocks = jnp.transpose(qkv_parts, (1, 0, 2, 3)).reshape(out_mark, model_width, head_dim)
    cot_flow = Flow(wide_gather(cotangent))
    group_in, qkv_blocks, attn_low = stage(
        [spread[0].near(0), spread[0].y(0)], [group_in, qkv_blocks, attn_low], idle=[cot_flow]
    )
    projected = block_project(group_in, qkv_blocks)
    queries = projected[:query_heads].reshape(query_heads * group_rows, head_dim)
    group_ids = group_in[:, model_width]
    kv_rows = 2 * key_heads * group_rows
    out_rows = query_heads * rows_dp
    id_rows = group_rows // head_dim
    packed = jnp.concatenate(
        [
            projected[query_heads:].reshape(kv_rows, head_dim),
            attn_low[out_mark:].reshape(out_rows, head_dim),
            jnp.pad(group_ids.reshape(id_rows, head_dim), ((0, 16 - id_rows), (0, 0))),
        ],
        axis=0,
    )
    keys_values = run(ring.gather(packed, packed.shape[0] // 32 * 16))
    out_blocks = keys_values[:, kv_rows : kv_rows + out_rows].reshape(data_count, query_heads, rows_dp, head_dim)
    out_blocks = jnp.transpose(out_blocks, (1, 0, 2, 3)).reshape(query_heads, model_width, head_dim)
    queries, keys_values, out_blocks = stage(
        [cot_flow, spread[0].y(1), spread[1].near(0)], [queries, keys_values, out_blocks]
    )
    all_ids = keys_values[:, kv_rows + out_rows : kv_rows + out_rows + id_rows].reshape(-1)

    local = in_group(jnp.arange(group_rows, dtype=jnp.int32), group_rows, head_index * tok_rows)
    query_pos = data_index * group_rows + local
    first_pos = jnp.sum((all_ids[None, :] < group_ids[:, None]).astype(jnp.int32), axis=1)
    query_pos = jnp.tile(query_pos, query_heads)
    first_pos = jnp.tile(first_pos, query_heads)
    place = jnp.stack([data_index, head_index * tok_rows]).astype(jnp.int32)
    mixed_low, mixed_full, totals = attend(
        place, queries, keys_values, query_pos[:, None], first_pos[:, None], scale, group_rows
    )
    mixed_heads = mixed_low.reshape(query_heads, group_rows, head_dim)
    mixed_heads, mixed_full, totals, attn_part = stage(
        [spread[0].cross(), spread[1].y(0), spread[1].y(1), cot_flow],
        [mixed_heads, mixed_full, totals, block_back(mixed_heads, out_blocks)],
    )
    attn_flow = Flow(scatter_rows(*attn_part, HEAD_MOVES))
    attn_flow.advance([lax.ppermute(*send) for send in attn_flow.sends])
    stage([attn_flow, spread[0].near(3), spread[0].y(3), spread[1].cross()], idle=[cot_flow])
    residual = inputs + attn_flow.value
    normed_two, norm_two_back = jax.vjp(rms_scale, residual, gains[1])
    wide_flow = Flow(wide_gather(normed_two.astype(BF16)))
    stage([wide_flow, spread[0].y(2), spread[1].near(3), spread[1].y(3)], idle=[cot_flow])
    stage([wide_flow, spread[1].y(2), cot_flow])
    stage([wide_flow])
    finish(wide_flow, cot_flow)

    def whole_rows(pieces):
        if rows_dp % 16 == 0:
            return pieces
        out = jnp.zeros((3, data_count) + pieces[0].shape[1:], BF16)
        for k, piece in enumerate(pieces):
            out = lax.dynamic_update_index_in_dim(out, piece, data_index ^ k, 1)
        return [out.reshape(3, model_width, -1)]

    ffn_sides, ffn_full, *ffn_grads = ffn_front(
        place, wide_flow.value, cot_flow.value, whole_rows(spread[0].value()), whole_rows(spread[1].value())
    )

    def taker(pieces):
        if len(pieces) > 1:
            return lambda k: pieces[k]
        cut = pieces[0].reshape(3, data_count, rows_dp, pieces[0].shape[2])
        return lambda k: lax.dynamic_index_in_dim(cut, data_index ^ k, 1, keepdims=False)

    pieces = len(ffn_grads) // 2
    reduce = [Reduce(taker(ffn_grads[:pieces])), Reduce(taker(ffn_grads[pieces:]))]
    *down_part, dx_kept, dx_sent = stage([reduce[0].y(2)], ffn_back(ffn_sides, ffn_full))
    out_flow = Flow(scatter_rows(*down_part, WIDE_MOVES))
    dx_flow = Flow(scatter_rows(dx_kept, dx_sent, WIDE_MOVES))
    dx_flow.advance([lax.ppermute(*send) for send in dx_flow.sends])
    stage([dx_flow, reduce[0].near(2), reduce[0].y(3), reduce[1].y(2)])
    stage([dx_flow, reduce[0].y(1), reduce[1].near(2), out_flow])
    grad_residual_norm, grad_gain_two = norm_two_back(dx_flow.value)
    grad_residual = cotangent.astype(F32) + grad_residual_norm
    grad_flow = Flow(head_gather(grad_residual.astype(BF16)))
    stage([grad_flow, reduce[0].near(1), reduce[1].y(1), reduce[1].y(3)])
    grad_flow.advance([lax.ppermute(*send) for send in grad_flow.sends])
    group_grad = grad_flow.value

    grad_heads = block_project(group_grad, out_blocks)
    grad_mixed = grad_heads.reshape(query_heads * group_rows, head_dim)
    delta = jnp.sum(grad_mixed.astype(F32) * mixed_full, axis=1)
    grad_queries, grad_keys_values = attend_back(
        place,
        queries,
        grad_mixed,
        keys_values,
        1.0 / totals.reshape(1, -1),
        delta[None, :],
        query_pos[None, :],
        first_pos[None, :],
        scale,
        group_rows,
    )
    group_grad, grad_queries, grad_keys_values = stage(
        [reduce[0].cross(), reduce[0].y(0), reduce[1].y(0)],
        [group_grad, grad_queries, grad_keys_values],
    )
    grad_queries = grad_queries.reshape(query_heads, group_rows, head_dim)

    late = 2
    main = 3 * ffn_blocks - late
    cap = -(-main // data_count)
    places = -(-max(cap * data_count, 3 * ffn_blocks) // TRIO) * TRIO
    def weight_sums(outer):
        cut = outer.reshape(outer.shape[0], data_count, rows_dp, head_dim)
        return Flow(ring.scatter(ring.part(cut, 1), outer.shape[0] // 2 if outer.shape[0] > 2 else None))

    key_flow = Flow(ring.scatter(ring.part(grad_keys_values, 0), key_heads))
    (outer,) = stage(
        [key_flow, reduce[1].cross(), reduce[1].near(1), out_flow],
        [block_outer([group_in, group_grad], [grad_queries, mixed_heads], model_width)],
    )
    (own_early, other_early), (own_late, other_late) = (part.value() for part in reduce)
    first_flow = weight_sums(outer)
    weight_grads, new_momentum, grams = stage(
        [key_flow, first_flow],
        ffn_moment(
            jnp.reshape(parity, (1,)),
            [own_early, own_late],
            [other_early, other_late],
            momentum,
            gate_mark,
            ffn_blocks,
            places,
        ),
    )
    gram_flow = Flow(gram_sums(ring, grams, cap))
    stage([key_flow, first_flow, gram_flow])
    while key_flow.sends is not None:
        stage([key_flow, first_flow, gram_flow])
    key_value_sums = key_flow.value
    grad_keys = (key_value_sums[:key_heads] * scale).astype(BF16)
    grad_values = key_value_sums[key_heads:].astype(BF16)
    grad_keys_values = jnp.concatenate([grad_keys, grad_values], axis=0)
    (outer,) = stage([first_flow, gram_flow], [block_outer([group_in], [grad_keys_values], model_width)])
    finish(first_flow)
    second_flow = weight_sums(outer)
    pairs = [k for k in range(gate_mark // 2) if not query_heads <= 2 * k < out_mark]
    grad_projected = jnp.concatenate([grad_queries, grad_keys_values], axis=0)
    *attn_dx, weight_grads, new_momentum, first_grams = stage(
        [second_flow, gram_flow],
        [
            *block_back(grad_projected, qkv_blocks),
            *attn_moment(first_flow.value, pairs, momentum, weight_grads, new_momentum),
        ],
    )
    last_flow = Flow(scatter_rows(*attn_dx, HEAD_MOVES))
    finish(gram_flow)
    gram_value = gram_flow.value
    while second_flow.sends is not None:
        (gram_value,) = stage([second_flow, last_flow], [gram_value], idle=[out_flow])
    finish(last_flow)
    grad_input_norm, grad_gain_one = norm_one_back(last_flow.value)
    grad_input = grad_residual + grad_input_norm
    gain_flow = Flow(total_sum(jnp.stack([grad_gain_one, grad_gain_two])))
    weight_grads, new_momentum, second_grams = attn_moment(
        second_flow.value, list(range(query_heads // 2, out_mark // 2)), momentum, weight_grads, new_momentum
    )
    late_count = gate_mark + late
    late_cap = -(-late_count // data_count)
    late_grams = jnp.concatenate([first_grams, second_grams, grams[main : main + late]], axis=0)
    late_grams = jnp.pad(late_grams, ((0, late_cap * data_count - late_count), (0, 0), (0, 0), (0, 0)))
    late_gram_flow = Flow(gram_sums(ring, late_grams, late_cap))
    for turn in range(2):
        (gram_value,) = stage([late_gram_flow, gain_flow] + [out_flow] * turn, [gram_value], idle=[out_flow])
    while late_gram_flow.sends is not None:
        late_gram_flow.advance([lax.ppermute(*send) for send in late_gram_flow.sends])
    late_sums, factors = stage([gain_flow, out_flow], [late_gram_flow.value, newton_factor(gram_value, growth)])
    block_out = (residual + out_flow.value).astype(BF16)
    factor_flow = Flow(all_factors(ring, factors))
    (late_factors,) = stage([factor_flow, gain_flow], [newton_factor(late_sums, growth)])
    late_factor_flow = Flow(all_factors(ring, late_factors))
    while factor_flow.sends is not None:
        stage([factor_flow, late_factor_flow, gain_flow])
    factors = factor_flow.value

    threes = main // TRIO
    early_spots = [(gate_mark // TRIO + k, [TRIO * k + i for i in range(TRIO)]) for k in range(threes)]
    new_weights = []
    for k in range(0, threes, 4):
        new_weights = stage(
            [late_factor_flow, gain_flow],
            [renew(weights, new_momentum, factors, early_spots[k : k + 4], new_weights)],
        )

    finish(late_factor_flow, gain_flow)
    gain_grads = gain_flow.value
    rest = jnp.concatenate([late_factor_flow.value[:late_count], factors[TRIO * threes : main]], axis=0)
    blocks_of = [2 * pair + i for pair in pairs for i in range(2)] + list(range(query_heads, out_mark))
    blocks_of += [gate_mark + main + k for k in range(late)] + [gate_mark + k for k in range(TRIO * threes, main)]
    late_spots = [
        (spot, [blocks_of.index(TRIO * spot + i) for i in range(TRIO)])
        for spot in sorted({block // TRIO for block in blocks_of})
    ]
    new_weights = renew(weights, new_momentum, rest, late_spots, new_weights)

    new_gain_first = BETA_ONE * gain_first + (1.0 - BETA_ONE) * gain_grads
    new_gain_second = BETA_TWO * gain_second + (1.0 - BETA_TWO) * gain_grads * gain_grads
    first_hat = new_gain_first / (1.0 - BETA_ONE**UPDATE_STEP)
    second_hat = new_gain_second / (1.0 - BETA_TWO**UPDATE_STEP)
    new_gains = gains - ADAM_RATE * first_hat / (jnp.sqrt(second_hat) + ADAM_EPS)
    back = lambda array: jnp.transpose(array, (1, 0, 2))
    return (
        block_out,
        grad_input,
        back(weight_grads),
        back(new_momentum),
        back(new_weights),
        gain_grads,
        new_gain_first,
        new_gain_second,
        new_gains,
    )


def solution(mesh):
    return jax.shard_map(
        on_device,
        mesh=mesh,
        in_specs=(
            P(("dp", "head"), None),
            P(("dp", "head"), None),
            P(("dp", "head")),
            P("dp", "head", None),
            P("dp", "head", None),
            P(),
            P(),
            P(),
        ),
        out_specs=(
            P(("dp", "head"), None),
            P(("dp", "head"), None),
            P("dp", "head", None),
            P("dp", "head", None),
            P("dp", "head", None),
            P(),
            P(),
            P(),
            P(),
        ),
        check_vma=False,
    )
```

```python
import functools
import math

import jax
import jax.numpy as jnp
from jax import lax
from jax.experimental import pallas as pl
from jax.experimental.pallas import tpu as pltpu
from jax.sharding import PartitionSpec as P

H = 8
KV = 4
FF = 9216
NEWTON_STEPS = 5
UPDATE_STEP = 10

NORM_EPS = 1e-06
SOFT_CAP = 50.0
MUON_RATE = 0.2
MUON_DECAY = 0.01
MUON_BETA = 0.95
ADAM_RATE = 0.3
BETA_ONE = 0.9
BETA_TWO = 0.95
ADAM_EPS = 1e-08
NEWTON_LINEAR = 3.4445
NEWTON_SQUARE = -4.775
NEWTON_CUBIC = 2.0315
NEWTON_PRECISION = lax.Precision.HIGH

BF16 = jnp.bfloat16
F32 = jnp.float32
VMEM_LIMIT = 62 * 1024 * 1024
NN = (((1,), (0,)), ((), ()))
NT = (((1,), (1,)), ((), ()))
TN = (((0,), (0,)), ((), ()))


def mm(a, b, dims):
    return lax.dot_general(a, b, dims, preferred_element_type=F32)


def rms_scale(rows, gain):
    inverse = lax.rsqrt(jnp.mean(rows * rows, axis=-1, keepdims=True) + NORM_EPS)
    return rows * inverse * gain


class Flow:
    def __init__(self, steps):
        self.steps = steps
        self.value = None
        self.sends = None
        self.advance(None)

    def advance(self, arrived):
        try:
            self.sends = self.steps.send(arrived)
        except StopIteration as stop:
            self.sends = None
            self.value = stop.value


def stage(flows, extra=(), idle=()):
    flows = [flow for flow in flows if flow.sends is not None]
    idle = [flow for flow in idle if flow.sends is not None and flow not in flows]
    arrived = [[lax.ppermute(*send) for send in flow.sends] for flow in flows]
    held = [[send[0] for send in flow.sends] for flow in idle]
    arrived, held, extra = lax.optimization_barrier((arrived, held, list(extra)))
    for flow, got in zip(flows, arrived):
        flow.advance(got)
    for flow, kept in zip(idle, held):
        flow.sends = [(value,) + send[1:] for value, send in zip(kept, flow.sends)]
    return extra


def run(steps):
    flow = Flow(steps)
    while flow.sends is not None:
        flow.advance([lax.ppermute(*send) for send in flow.sends])
    return flow.value


def finish(*flows):
    while any(flow.sends is not None for flow in flows):
        stage(flows)


def swap(value, axis, mask):
    size = lax.axis_size(axis)
    return (value, axis, [(i, i ^ mask) for i in range(size)])


def head_gather(rows):
    (other,) = yield [swap(rows, "head", 2)]
    pair = jnp.concatenate([rows, other], axis=0)
    (other,) = yield [swap(pair, "head", 1)]
    return jnp.concatenate([pair, other], axis=0)


def wide_gather(rows):
    (other,) = yield [swap(rows, "dp", 4)]
    both = jnp.concatenate([rows, other], axis=0)
    (other,) = yield [swap(both, "head", 2)]
    pair = jnp.concatenate([both, other], axis=0)
    (other,) = yield [swap(pair, "head", 1)]
    return [pair, other]


def add_low(kept, other):
    return (kept.astype(F32) + other.astype(F32)).astype(BF16)


def scatter_rows(kept, sent, moves, cuts=1):
    for k, (axis, mask) in enumerate(moves):
        last = k == len(moves) - 1
        others = []
        for piece in jnp.split(sent, cuts if last else 1):
            others += yield [swap(piece, axis, mask)]
        other = jnp.concatenate(others, axis=0) if len(others) > 1 else others[0]
        part = kept.astype(F32) + other.astype(F32)
        if not last:
            half = part.shape[0] // 2
            kept, sent = part[:half], part[half:].astype(BF16)
    return part


HEAD_MOVES = (("head", 1), ("head", 2))
WIDE_MOVES = (("head", 1), ("head", 2), ("dp", 4))


def total_sum(value):
    for axis in ("head", "dp"):
        mask = 1
        while mask < lax.axis_size(axis):
            (other,) = yield [swap(value, axis, mask)]
            value = value + other
            mask *= 2
    return value


class Ring:
    def __init__(self):
        size = lax.axis_size("dp")
        order = list(range(0, size, 2)) + list(range(size - 1, 0, -2))
        around = [[order[(order.index(i) + offset) % size] for offset in range(size)] for i in range(size)]
        self.size = size
        row = jnp.array(around, jnp.int32)[lax.axis_index("dp")]
        zero = jnp.zeros((), jnp.int32)
        self.around = [lax.select(lax.lt(row[k], zero), row[k] + size, row[k]) for k in range(size)]
        self.up = [(order[k], order[(k + 1) % size]) for k in range(size)]
        self.down = [(order[(k + 1) % size], order[k]) for k in range(size)]

    def index(self, offset, scale=1):
        return self.around[offset % self.size] * scale

    def gather(self, value, mid):
        half = self.size // 2
        out = jnp.zeros((self.size,) + value.shape, value.dtype)

        def put(out, piece, offset, start=0):
            spot = (self.index(offset), start) + (0,) * (value.ndim - 1)
            return lax.dynamic_update_slice(out, piece[None], spot, allow_negative_indices=False)

        out = put(out, value, 0)
        ahead, back = value, value
        for step in range(1, half):
            ahead, back = yield [(ahead, "dp", self.up), (back, "dp", self.down)]
            out = put(put(out, ahead, -step), back, step)
        if mid is None:
            (last,) = yield [(ahead, "dp", self.up)]
            return put(out, last, half)
        first, second = yield [(ahead[:mid], "dp", self.up), (back[mid:], "dp", self.down)]
        return put(put(out, first, half), second, half, mid)

    def part(self, array, axis, size=None):
        if size is None:
            return lambda offset: lax.dynamic_index_in_dim(
                array, self.index(offset), axis, keepdims=False, allow_negative_indices=False
            )
        return lambda offset: lax.dynamic_slice_in_dim(
            array, self.index(offset, size), size, axis, allow_negative_indices=False
        )

    def scatter(self, take, mid):
        half = self.size // 2
        far = take(half)
        kind = far.dtype
        if mid is None:
            (up,) = yield [(far, "dp", self.up)]
            down = None
        else:
            up, down = yield [(far[:mid], "dp", self.up), (far[mid:], "dp", self.down)]
        for step in range(half - 1, 0, -1):
            ahead, back = take(step).astype(F32), take(-step).astype(F32)
            if mid is None or step < half - 1:
                ahead = ahead + up
                back = back if down is None else back + down
            else:
                ahead = jnp.concatenate([ahead[:mid] + up, ahead[mid:]])
                back = jnp.concatenate([back[:mid], back[mid:] + down])
            up, down = yield [(ahead.astype(kind), "dp", self.up), (back.astype(kind), "dp", self.down)]
        return take(0).astype(F32) + up.astype(F32) + down.astype(F32)


def once(sends, take):
    def steps():
        take((yield sends))

    return Flow(steps())


SIDE_BIT = 2


def plane_classes():
    planes = range(lax.axis_size("dp") // 2)
    kept = [m for m in planes if m & 3 in (0, 3)]
    passed = [m for m in planes if m & 3 in (1, 2)]
    return {0: [0], 1: [1], 2: [m for m in passed if m != 1], 3: [m for m in kept if m]}


class Spread:
    def __init__(self, mine, other):
        self.mine, self.other = mine, other
        self.pieces = {0: mine}

    def move(self, moves):
        def take(arrived):
            for (_, _, _, number), piece in zip(moves, arrived):
                self.pieces[number] = piece

        return once([swap(value, "dp", offset << 1 | bit) for value, offset, bit, _ in moves], take)

    def cross(self):
        group = plane_classes()[3]
        return self.move([(self.other if m & SIDE_BIT else self.mine, m, 0, m << 1) for m in group])

    def near(self, key):
        group = plane_classes()[key]
        return self.move([(self.pieces[m << 1], 1, 0, (m ^ 1) << 1) for m in group])

    def y(self, key):
        group = plane_classes()[key]
        return self.move([(self.pieces[m << 1], 0, 1, m << 1 | 1) for m in group])

    def value(self):
        return [self.pieces[k] for k in range(lax.axis_size("dp"))]


class Reduce:
    def __init__(self, rows):
        self.rows = rows
        self.parts = {}
        self.sums = [[], []]

    def part(self, offset):
        terms = [term.astype(F32) for term in self.parts[offset]]
        return functools.reduce(jnp.add, terms)

    def hold(self, offset, *terms):
        self.parts.setdefault(offset, []).extend(terms)

    def y(self, key):
        group = plane_classes()[key]

        def take(arrived):
            for offset, got in zip(group, arrived):
                self.hold(offset, self.rows(offset << 1), got)

        return once([swap(self.rows(offset << 1 | 1), "dp", 1) for offset in group], take)

    def near(self, key):
        group = plane_classes()[key]

        def take(arrived):
            for offset, got in zip(group, arrived):
                self.hold(offset ^ 1, got)

        return once([swap(self.part(offset).astype(BF16), "dp", 2) for offset in group], take)

    def cross(self):
        group = plane_classes()[3]

        def take(arrived):
            for offset, got in zip(group, arrived):
                self.sums[1 if offset & SIDE_BIT else 0].append(got)

        return once([swap(self.part(offset).astype(BF16), "dp", offset << 1) for offset in group], take)

    def value(self):
        return self.parts[0] + self.sums[0], self.sums[1]


def params(**more):
    return pltpu.CompilerParams(vmem_limit_bytes=VMEM_LIMIT, **more)


TRIO = 3


def cast_blocks(blocks, count):
    _, r, c = blocks.shape

    def body(x_ref, o_ref):
        o_ref[...] = x_ref[...].astype(BF16)

    spec = pl.BlockSpec((TRIO, r, c), lambda k: (k, 0, 0))
    return pl.pallas_call(
        body,
        grid=(count // TRIO,),
        in_specs=[spec],
        out_specs=spec,
        out_shape=jax.ShapeDtypeStruct((count, r, c), BF16),
        compiler_params=params(),
        cost_estimate=pl.CostEstimate(flops=0, bytes_accessed=6 * count * r * c, transcendentals=0),
    )(blocks)


def pack_units(parity, blocks, first, kind_blocks, early):
    _, r, c = blocks.shape
    h = c // 2
    full = kind_blocks // 2
    each = kind_blocks // TRIO
    u, v = early * c, (full - early) * c + h

    def body(s_ref, *refs):
        parts, outs = refs[:each], refs[each:]

        def tile(f):
            return parts[f // TRIO].at[f % TRIO]

        for turn in range(2):

            @pl.when(s_ref[0] == turn)
            def _():
                for k in range(2):
                    side = turn ^ k
                    for i in range(full):
                        value = tile(side * full + i)[...].astype(BF16)
                        if i < early:
                            outs[2 * k][:, i * c : (i + 1) * c] = value
                        else:
                            outs[2 * k + 1][:, (i - early) * c : (i - early + 1) * c] = value
                    rest = tile(2 * full)[:, side * h : (side + 1) * h]
                    outs[2 * k + 1][:, v - h :] = rest.astype(BF16)

    def part(i):
        return pl.BlockSpec((TRIO, r, c), lambda k, s: (first // TRIO + each * k + i, 0, 0))

    wide = pl.BlockSpec((None, r, u), lambda k, s: (k, 0, 0))
    slim = pl.BlockSpec((None, r, v), lambda k, s: (k, 0, 0))
    shapes = [jax.ShapeDtypeStruct((3, r, u), BF16), jax.ShapeDtypeStruct((3, r, v), BF16)]
    return pl.pallas_call(
        body,
        grid_spec=pltpu.PrefetchScalarGridSpec(
            num_scalar_prefetch=1,
            grid=(3,),
            in_specs=[part(i) for i in range(each)],
            out_specs=[wide, slim, wide, slim],
        ),
        out_shape=shapes + shapes,
        compiler_params=params(),
        cost_estimate=pl.CostEstimate(flops=0, bytes_accessed=18 * kind_blocks * r * c, transcendentals=0),
    )(parity, *([blocks] * each))


def block_project(rows, blocks):
    t = rows.shape[0]
    count, d, c = blocks.shape

    def body(x_ref, w_ref, o_ref):
        o_ref[...] = mm(x_ref[...], w_ref[...], NN).astype(BF16)

    return pl.pallas_call(
        body,
        grid=(count,),
        in_specs=[
            pl.BlockSpec((t, d), lambda b: (0, 0)),
            pl.BlockSpec((None, d, c), lambda b: (b, 0, 0)),
        ],
        out_specs=pl.BlockSpec((None, t, c), lambda b: (b, 0, 0)),
        out_shape=jax.ShapeDtypeStruct((count, t, c), BF16),
        compiler_params=params(),
        cost_estimate=pl.CostEstimate(
            flops=2 * count * t * d * c, bytes_accessed=2 * (t * d + count * (d * c + t * c)), transcendentals=0
        ),
    )(rows, blocks)


def block_back(cols, blocks):
    count, t, c = cols.shape
    d = blocks.shape[1]
    half = t // 2

    def body(x_ref, w_ref, o_ref, p_ref, acc_ref):
        b = pl.program_id(0)

        @pl.when(b == 0)
        def _():
            acc_ref[...] = jnp.zeros_like(acc_ref)

        acc_ref[...] += mm(x_ref[...], w_ref[...], NT)

        @pl.when(b == count - 1)
        def _():
            o_ref[...] = acc_ref[:half, :].astype(BF16)
            p_ref[...] = acc_ref[half:, :].astype(BF16)

    result = pl.BlockSpec((half, d), lambda b: (0, 0))
    return pl.pallas_call(
        body,
        grid=(count,),
        in_specs=[
            pl.BlockSpec((None, t, c), lambda b: (b, 0, 0)),
            pl.BlockSpec((None, d, c), lambda b: (b, 0, 0)),
        ],
        out_specs=[result, result],
        out_shape=[jax.ShapeDtypeStruct((half, d), BF16)] * 2,
        scratch_shapes=[pltpu.VMEM((t, d), F32)],
        compiler_params=params(),
        cost_estimate=pl.CostEstimate(
            flops=2 * count * t * d * c, bytes_accessed=2 * (t * d + count * (d * c + t * c)), transcendentals=0
        ),
    )(cols, blocks)


def block_outer(rows, cols, d):
    t = rows[0].shape[0]
    c = cols[0].shape[2]
    starts = [0]
    for col in cols:
        starts.append(starts[-1] + col.shape[0])
    count = len(rows)
    total = starts[-1]

    def body(*refs):
        o_ref, t_ref = refs[2 * count :]
        b = pl.program_id(0)
        for k in range(count):

            @pl.when(b == starts[k])
            def _():
                t_ref[...] = refs[k][...].T

            @pl.when((b >= starts[k]) & (b < starts[k + 1]))
            def _():
                o_ref[...] = mm(t_ref[...], refs[count + k][...], NN).astype(BF16)

    def col_at(k):
        return pl.BlockSpec((None, t, c), lambda b: (jnp.clip(b - starts[k], 0, starts[k + 1] - starts[k] - 1), 0, 0))

    return pl.pallas_call(
        body,
        grid=(total,),
        in_specs=[pl.BlockSpec((t, d), lambda b: (0, 0))] * count + [col_at(k) for k in range(count)],
        out_specs=pl.BlockSpec((None, d, c), lambda b: (b, 0, 0)),
        out_shape=jax.ShapeDtypeStruct((total, d, c), BF16),
        scratch_shapes=[pltpu.VMEM((d, t), BF16)],
        compiler_params=params(),
        cost_estimate=pl.CostEstimate(
            flops=2 * total * t * d * c,
            bytes_accessed=2 * (count * t * d + total * (d * c + t * c)),
            transcendentals=0,
        ),
    )(*rows, *cols)


def in_group(local, width, head_shift):
    quarter = width // 4
    low = jnp.bitwise_and(local, quarter - 1)
    one = jnp.where(jnp.bitwise_and(local, quarter) != 0, 2 * quarter, 0)
    two = jnp.where(jnp.bitwise_and(local, 2 * quarter) != 0, quarter, 0)
    return jnp.bitwise_xor(low + one + two, head_shift)


def key_position(block, width, head_shift, shape, axis):
    local = lax.broadcasted_iota(jnp.int32, shape, axis)
    return block * width + in_group(local, width, head_shift)


def attend(place, queries, keys_values, query_pos, first_pos, scale, p):
    m, e = queries.shape
    n = keys_values.shape[0]
    step = 256

    def body(place_ref, q_ref, kv_ref, pos_ref, first_ref, low_ref, full_ref, sum_ref, acc_ref, tot_ref):
        j = pl.program_id(0)

        @pl.when(j == 0)
        def _():
            acc_ref[...] = jnp.zeros_like(acc_ref)
            tot_ref[...] = jnp.zeros_like(tot_ref)

        @pl.when(j <= place_ref[0])
        def _():
            key_pos = key_position(j, p, place_ref[1], (1, p), 1)
            for r in range(0, m, step):
                rows = pl.ds(r, step)
                raw = mm(q_ref[rows, :], kv_ref[:p, :], NT)
                soft = SOFT_CAP * jnp.tanh(raw * (scale / SOFT_CAP))
                seen = (key_pos >= first_ref[rows, :]) & (key_pos <= pos_ref[rows, :])
                terms = jnp.where(seen, jnp.exp(soft), 0.0)
                tot_ref[rows, :] += jnp.sum(terms, axis=1, keepdims=True)
                acc_ref[rows, :] += mm(terms.astype(BF16), kv_ref[p:, :], NN)

        @pl.when(j == n - 1)
        def _():
            total = tot_ref[...]
            mixed = acc_ref[...] / total
            full_ref[...] = mixed
            low_ref[...] = mixed.astype(BF16)
            sum_ref[...] = total

    whole = lambda shape: pl.BlockSpec(shape, lambda j, s: (0, 0))
    return pl.pallas_call(
        body,
        grid_spec=pltpu.PrefetchScalarGridSpec(
            num_scalar_prefetch=1,
            grid=(n,),
            in_specs=[
                whole((m, e)),
                pl.BlockSpec((None, 2 * p, e), lambda j, s: (jnp.minimum(j, s[0]), 0, 0)),
                whole((m, 1)),
                whole((m, 1)),
            ],
            out_specs=[whole((m, e)), whole((m, e)), whole((m, 1))],
            scratch_shapes=[pltpu.VMEM((m, e), F32), pltpu.VMEM((m, 1), F32)],
        ),
        out_shape=[
            jax.ShapeDtypeStruct((m, e), BF16),
            jax.ShapeDtypeStruct((m, e), F32),
            jax.ShapeDtypeStruct((m, 1), F32),
        ],
        compiler_params=params(),
        cost_estimate=pl.CostEstimate(
            flops=4 * m * n * p * e, bytes_accessed=4 * n * p * e, transcendentals=2 * m * n * p
        ),
    )(place, queries, keys_values, query_pos, first_pos)


def attend_back(place, queries, grads, keys_values, inverse, delta, query_pos, first_pos, scale, p):
    m, e = queries.shape
    n = keys_values.shape[0]
    step = 256

    def body(
        place_ref, q_ref, g_ref, kv_ref, inv_ref, delta_ref, pos_ref, first_ref, dq_ref, dkv_ref, acc_ref, dk_ref, dv_ref
    ):
        j = pl.program_id(0)

        @pl.when(j == 0)
        def _():
            acc_ref[...] = jnp.zeros_like(acc_ref)

        @pl.when(j <= place_ref[0])
        def _():
            key_pos = key_position(j, p, place_ref[1], (p, 1), 0)
            for r in range(0, m, step):
                rows = pl.ds(r, step)
                raw = mm(kv_ref[:p, :], q_ref[rows, :], NT)
                capped = jnp.tanh(raw * (scale / SOFT_CAP))
                seen = (key_pos >= first_ref[:, rows]) & (key_pos <= pos_ref[:, rows])
                probs = jnp.where(seen, jnp.exp(SOFT_CAP * capped), 0.0) * inv_ref[:, rows]
                grad_probs = mm(kv_ref[p:, :], g_ref[rows, :], NT)
                grad_raw = probs * (grad_probs - delta_ref[:, rows]) * (1.0 - capped * capped)
                grad_low = grad_raw.astype(BF16)
                value_part = mm(probs.astype(BF16), g_ref[rows, :], NN)
                key_part = mm(grad_low, q_ref[rows, :], NN)
                if r == 0:
                    dv_ref[...] = value_part
                    dk_ref[...] = key_part
                else:
                    dv_ref[...] += value_part
                    dk_ref[...] += key_part
                acc_ref[rows, :] += mm(grad_low, kv_ref[:p, :], TN)
            dkv_ref[0] = dk_ref[...].astype(BF16)
            dkv_ref[1] = dv_ref[...].astype(BF16)

        @pl.when(j > place_ref[0])
        def _():
            dkv_ref[...] = jnp.zeros_like(dkv_ref)

        @pl.when(j == n - 1)
        def _():
            dq_ref[...] = (acc_ref[...] * scale).astype(BF16)

    whole = lambda shape: pl.BlockSpec(shape, lambda j, s: (0, 0))
    return pl.pallas_call(
        body,
        grid_spec=pltpu.PrefetchScalarGridSpec(
            num_scalar_prefetch=1,
            grid=(n,),
            in_specs=[
                whole((m, e)),
                whole((m, e)),
                pl.BlockSpec((None, 2 * p, e), lambda j, s: (jnp.minimum(j, s[0]), 0, 0)),
                whole((1, m)),
                whole((1, m)),
                whole((1, m)),
                whole((1, m)),
            ],
            out_specs=[whole((m, e)), pl.BlockSpec((None, 2, p, e), lambda j, s: (j, 0, 0, 0))],
            scratch_shapes=[pltpu.VMEM((m, e), F32), pltpu.VMEM((p, e), F32), pltpu.VMEM((p, e), F32)],
        ),
        out_shape=[jax.ShapeDtypeStruct((m, e), BF16), jax.ShapeDtypeStruct((n, 2, p, e), BF16)],
        compiler_params=params(),
        cost_estimate=pl.CostEstimate(
            flops=10 * m * n * p * e, bytes_accessed=8 * n * p * e, transcendentals=2 * m * n * p
        ),
    )(place, queries, grads, keys_values, inverse, delta, query_pos, first_pos)


def gelu_pair(gate):
    outer = math.sqrt(2.0 / math.pi)
    square = gate * gate
    bent = jnp.tanh(outer * gate * (1.0 + 0.044715 * square))
    half = 0.5 * (1.0 + bent)
    slope = half + 0.5 * gate * (1.0 - bent * bent) * outer * (1.0 + 3.0 * 0.044715 * square)
    return gate * half, slope


def ffn_front(place, rows, cots, early, late):
    part_rows, d = rows[0].shape
    t = 2 * part_rows
    count = len(early)
    r = early[0].shape[1]
    u, v = early[0].shape[2], late[0].shape[2]
    tall = min(512, t)
    wide = d // 3
    cuts = [(k, min(256, u + v - k)) for k in range(0, u + v, 256)]

    def body(place_ref, x0, x1, y0, y1, *refs):
        early_refs, late_refs = refs[:count], refs[count : 2 * count]
        refs = refs[2 * count :]
        hs_ref, w_out = refs[:2]
        grad_refs = refs[2 : 2 + count], refs[2 + count : 2 + 2 * count]
        x, y, w, xt, yt, hs, row_sems, sems, out_sems, grad_sems = refs[2 + 2 * count :]
        row_copies = []
        for k, (source, target) in enumerate(((x0, x), (x1, x), (y0, y), (y1, y))):
            target = target.at[pl.ds((k % 2) * part_rows, part_rows), :]
            row_copies.append(pltpu.make_async_copy(source, target, row_sems.at[k]))
            row_copies[k].start()
        copies = []
        chunks = ((early_refs, pl.ds(0, u)), (late_refs, pl.ds(u, v)))

        def spot(k):
            return pl.ds(pl.multiple_of(jnp.bitwise_xor(place_ref[0], k) * r, 16) if count > 1 else 0, r)

        for k in range(count):
            for way, (sources, lanes) in enumerate(chunks):
                copy = pltpu.make_async_copy(sources[k], w.at[:, spot(k), lanes], sems.at[way, k])
                copy.start()
                copies.append(copy)
        for copy in row_copies:
            copy.wait()

        @pl.loop(0, d // 256)
        def _(k):
            cols = pl.ds(pl.multiple_of(k * 256, 256), 256)
            xt[cols, :] = x[:, cols].T
            yt[cols, :] = y[:, cols].T

        for copy in copies:
            copy.wait()
        kept = pltpu.make_async_copy(w, w_out, out_sems.at[0])
        kept.start()

        @pl.loop(0, t // tall)
        def _(i):
            part = pl.ds(pl.multiple_of(i * tall, tall), tall)
            for start, size in cuts:
                units = pl.ds(start, size)
                gate = mm(x[part, :], w[0, :, units], NN)
                up = mm(x[part, :], w[1, :, units], NN)
                grad = mm(y[part, :], w[2, :, units], NN)
                active, slope = gelu_pair(gate)
                hs[0, part, units] = (active * up).astype(BF16)
                hs[1, part, units] = (grad * up * slope).astype(BF16)
                hs[2, part, units] = (grad * active).astype(BF16)

        sides = pltpu.make_async_copy(hs, hs_ref, out_sems.at[1])
        sides.start()
        kept.wait()
        copies = []
        for kind, (left, right) in enumerate(((xt, 1), (xt, 2), (yt, 0))):

            @pl.loop(0, d // wide)
            def _(k):
                cols = pl.ds(pl.multiple_of(k * wide, wide), wide)
                w[kind, cols, :] = mm(left[cols, :], hs[right], NN).astype(BF16)

            for k in range(count):
                for way, (_, lanes) in enumerate(chunks):
                    target = grad_refs[way][k].at[kind]
                    copy = pltpu.make_async_copy(w.at[kind, spot(k), lanes], target, grad_sems.at[kind, way, k])
                    copy.start()
                    copies.append(copy)
        sides.wait()
        for copy in copies:
            copy.wait()

    apart = pl.BlockSpec(memory_space=pl.ANY)
    return pl.pallas_call(
        body,
        grid_spec=pltpu.PrefetchScalarGridSpec(
            num_scalar_prefetch=1,
            grid=(1,),
            in_specs=[apart] * (4 + 2 * count),
            out_specs=[apart] * (2 + 2 * count),
            scratch_shapes=[
                pltpu.VMEM((t, d), BF16),
                pltpu.VMEM((t, d), BF16),
                pltpu.VMEM((3, d, u + v), BF16),
                pltpu.VMEM((d, t), BF16),
                pltpu.VMEM((d, t), BF16),
                pltpu.VMEM((3, t, u + v), BF16),
                pltpu.SemaphoreType.DMA((4,)),
                pltpu.SemaphoreType.DMA((2, count)),
                pltpu.SemaphoreType.DMA((2,)),
                pltpu.SemaphoreType.DMA((3, 2, count)),
            ],
        ),
        out_shape=[
            jax.ShapeDtypeStruct((3, t, u + v), BF16),
            jax.ShapeDtypeStruct((3, d, u + v), BF16),
            *[jax.ShapeDtypeStruct((3, r, u), BF16)] * count,
            *[jax.ShapeDtypeStruct((3, r, v), BF16)] * count,
        ],
        compiler_params=params(),
        cost_estimate=pl.CostEstimate(
            flops=12 * t * d * (u + v), bytes_accessed=12 * d * (u + v) + 4 * t * d, transcendentals=t * (u + v)
        ),
    )(place, *rows, *cots, *early, *late)


def ffn_back(sides, blocks):
    _, t, u = sides.shape
    d = blocks.shape[1]
    wide = 256
    half = t // 2

    def body(s_ref, w_ref, *refs):
        for k in range(2):
            part = pl.ds(k * half, half)
            refs[k][...] = mm(s_ref[0, part, :], w_ref[2], NT).astype(BF16)
            refs[2 + k][...] = (mm(s_ref[1, part, :], w_ref[0], NT) + mm(s_ref[2, part, :], w_ref[1], NT)).astype(BF16)

    return pl.pallas_call(
        body,
        grid=(d // wide,),
        in_specs=[
            pl.BlockSpec((3, t, u), lambda k: (0, 0, 0), pipeline_mode=pl.Buffered(1)),
            pl.BlockSpec((3, wide, u), lambda k: (0, k, 0)),
        ],
        out_specs=[pl.BlockSpec((half, wide), lambda k: (0, k))] * 4,
        out_shape=[jax.ShapeDtypeStruct((half, d), BF16)] * 4,
        compiler_params=params(),
        cost_estimate=pl.CostEstimate(
            flops=6 * t * d * u, bytes_accessed=6 * d * u + 6 * t * u + 4 * t * d, transcendentals=0
        ),
    )(sides, blocks)


def gram_parts(m):
    h = m.shape[1] // 2
    high = m.astype(BF16)
    low = (m - high.astype(F32)).astype(BF16)
    mixed = mm(high, low, TN)
    gram = mm(high, high, TN) + mm(low, low, TN) + mixed + mixed.T
    return gram[:h, :h], gram[:h, h:], gram[h:, h:]


def ffn_moment(parity, own, other, momentum, first, blocks, places):
    total, r, c = momentum.shape
    terms = [*own, *other]
    counts = [len(group) for group in terms]
    u, v = own[0][0].shape[2], own[1][0].shape[2]
    early = u // c
    h = c // 2
    full = early + 1
    each = blocks // TRIO

    def body(s_ref, *refs):
        groups = []
        for count in counts:
            groups.append(refs[:count])
            refs = refs[count:]
        m_ref, wg_ref, nm_ref, gram_ref = refs
        j = pl.program_id(0)

        def total_of(group, start, size):
            lanes = pl.ds(start, size)
            return functools.reduce(jnp.add, [ref[:, lanes].astype(F32) for ref in group])

        @pl.when(j >= TRIO * each)
        def _():
            gram_ref[...] = jnp.zeros_like(gram_ref)

        for turn in range(each):
            for mine in range(2):

                @pl.when((j < TRIO * each) & (lax.rem(j, each) == turn) & (s_ref[0] == mine))
                def _():
                    for i in range(TRIO):
                        side, f = divmod(turn * TRIO + i, full)
                        if side == 2:
                            for k in range(2):
                                group = groups[1 if k == mine else 3]
                                wg_ref[i, :, k * h : (k + 1) * h] = total_of(group, c, h)
                        elif f < early:
                            wg_ref[i] = total_of(groups[0 if side == mine else 2], f * c, c)
                        else:
                            wg_ref[i] = total_of(groups[1 if side == mine else 3], 0, c)

        @pl.when(j < TRIO * each)
        def _():
            for i in range(TRIO):
                new = MUON_BETA * m_ref[i] + wg_ref[i]
                nm_ref[i] = new
                gram_ref[i, 0], gram_ref[i, 1], gram_ref[i, 2] = gram_parts(new)

    kind = lambda j, s: (jnp.minimum(j // each, 2), 0, 0)
    block = lambda j, s: (first // TRIO + jnp.minimum(j, TRIO * each - 1), 0, 0)
    arrays = [array for group in terms for array in group]
    return pl.pallas_call(
        body,
        grid_spec=pltpu.PrefetchScalarGridSpec(
            num_scalar_prefetch=1,
            grid=(places // TRIO,),
            in_specs=[pl.BlockSpec((None,) + array.shape[1:], kind) for array in arrays]
            + [pl.BlockSpec((TRIO, r, c), block)],
            out_specs=[
                pl.BlockSpec((TRIO, r, c), block),
                pl.BlockSpec((TRIO, r, c), block),
                pl.BlockSpec((TRIO, 3, h, h), lambda j, s: (j, 0, 0, 0)),
            ],
        ),
        out_shape=[
            jax.ShapeDtypeStruct((total, r, c), F32),
            jax.ShapeDtypeStruct((total, r, c), F32),
            jax.ShapeDtypeStruct((places, 3, h, h), F32),
        ],
        compiler_params=params(),
        cost_estimate=pl.CostEstimate(
            flops=6 * 3 * blocks * r * c * c, bytes_accessed=16 * 3 * blocks * r * c, transcendentals=0
        ),
    )(parity, *arrays, momentum)


def attn_moment(grads, pairs, momentum, weight_grads, new_momentum):
    count, r, c = grads.shape
    h = c // 2

    def body(s_ref, g_ref, m_ref, wg_in, nm_in, wg_ref, nm_ref, gram_ref):
        for i in range(2):
            new = MUON_BETA * m_ref[i] + g_ref[i]
            wg_ref[i] = g_ref[i]
            nm_ref[i] = new
            gram_ref[i, 0], gram_ref[i, 1], gram_ref[i, 2] = gram_parts(new)

    block = pl.BlockSpec((2, r, c), lambda j, s: (s[j], 0, 0))
    apart = pl.BlockSpec(memory_space=pl.ANY)
    return pl.pallas_call(
        body,
        grid_spec=pltpu.PrefetchScalarGridSpec(
            num_scalar_prefetch=1,
            grid=(count // 2,),
            in_specs=[pl.BlockSpec((2, r, c), lambda j, s: (j, 0, 0)), block, apart, apart],
            out_specs=[block, block, pl.BlockSpec((2, 3, h, h), lambda j, s: (j, 0, 0, 0))],
        ),
        out_shape=[
            jax.ShapeDtypeStruct(momentum.shape, F32),
            jax.ShapeDtypeStruct(momentum.shape, F32),
            jax.ShapeDtypeStruct((count, 3, h, h), F32),
        ],
        input_output_aliases={3: 0, 4: 1},
        compiler_params=params(),
        cost_estimate=pl.CostEstimate(
            flops=6 * count * r * c * c, bytes_accessed=16 * count * r * c, transcendentals=0
        ),
    )(jnp.array(pairs, jnp.int32), grads, momentum, weight_grads, new_momentum)


def renew(weights, momentum, factors, spots, updated):
    _, r, c = weights.shape
    h = c // 2
    steps = len(spots)
    table = jnp.array([spot for spot, _ in spots] + [f for _, places in spots for f in places], jnp.int32)

    def body(s_ref, w_ref, m_ref, *refs):
        factor_refs, o_ref = refs[:TRIO], refs[-1]
        for i in range(TRIO):
            left = m_ref[i, :, :h].astype(BF16)
            right = m_ref[i, :, h:].astype(BF16)
            first, off, last = factor_refs[i][0], factor_refs[i][1], factor_refs[i][2]
            start = mm(left, first, NN) + mm(right, off, NT)
            rest = mm(left, off, NN) + mm(right, last, NN)
            keep = 1.0 - MUON_RATE * MUON_DECAY
            o_ref[i, :, :h] = w_ref[i, :, :h] * keep - MUON_RATE * start
            o_ref[i, :, h:] = w_ref[i, :, h:] * keep - MUON_RATE * rest

    block = pl.BlockSpec((TRIO, r, c), lambda j, s: (s[j], 0, 0))

    def factor_at(i):
        return pl.BlockSpec((None, 3, h, h), lambda j, s: (s[steps + TRIO * j + i], 0, 0, 0))

    apart = [pl.BlockSpec(memory_space=pl.ANY)] * len(updated)
    return pl.pallas_call(
        body,
        grid_spec=pltpu.PrefetchScalarGridSpec(
            num_scalar_prefetch=1,
            grid=(steps,),
            in_specs=[block, block] + [factor_at(i) for i in range(TRIO)] + apart,
            out_specs=block,
        ),
        out_shape=jax.ShapeDtypeStruct(weights.shape, F32),
        input_output_aliases={3 + TRIO: 0} if updated else {},
        compiler_params=params(),
        cost_estimate=pl.CostEstimate(
            flops=2 * TRIO * steps * r * c * c, bytes_accessed=12 * TRIO * steps * r * c, transcendentals=0
        ),
    )(table, weights, momentum, *([factors] * TRIO), *updated)


def top(spec, a, b):
    return jnp.einsum(spec, a, b, precision=NEWTON_PRECISION)


def newton_factor(grams, growth):
    size = grams.shape[-1]
    eye = jnp.eye(size, dtype=F32)
    norm = jnp.sqrt(jnp.sum(grams * eye, axis=(1, 2), keepdims=True))
    inverse = 1.0 / (norm + 1e-07)
    gram = grams * (inverse * inverse)
    factor = None
    for sweep in range(NEWTON_STEPS):
        square = top("bij,bjk->bik", gram, gram)
        poly = NEWTON_LINEAR * eye + NEWTON_SQUARE * gram + NEWTON_CUBIC * square
        factor = poly if sweep == 0 else top("bij,bjk->bik", factor, poly)
        if sweep < NEWTON_STEPS - 1:
            gram = top("bij,bjk->bik", top("bij,bjk->bik", gram, poly), poly)
    return factor * (growth * inverse)


def fold(squares):
    h = squares.shape[1] // 2
    return jnp.stack([squares[:, :h, :h], squares[:, :h, h:], squares[:, h:, h:]], axis=1)


def unfold(parts):
    first, off, last = parts[:, 0], parts[:, 1], parts[:, 2]
    upper = jnp.concatenate([first, off], axis=2)
    lower = jnp.concatenate([jnp.swapaxes(off, 1, 2), last], axis=2)
    return jnp.concatenate([upper, lower], axis=1)


def gram_sums(ring, parts, cap):
    h = parts.shape[2]
    parts = parts.reshape(-1, h, h)
    rows = 3 * cap
    mine = yield from ring.scatter(ring.part(parts, 0, rows), rows // 2 if cap > 1 else None)
    return unfold(mine.reshape(cap, 3, h, h))


def all_factors(ring, factors):
    cap, c, _ = factors.shape
    parts = fold(factors.astype(BF16)).reshape(3 * cap, c // 2, c // 2)
    parts = yield from ring.gather(parts, 3 * cap // 2 if cap > 1 else None)
    return parts.reshape(ring.size * cap, 3, c // 2, c // 2)


def on_device(block_in, cotangent, seq_ids, weights, momentum, gains, gain_first, gain_second):
    tok_rows, model_width = block_in.shape
    rows_dp, group_blocks, head_dim = weights.shape
    head_count = lax.axis_size("head")
    data_count = lax.axis_size("dp")
    group_rows = tok_rows * head_count
    key_heads = KV // head_count
    query_heads = H // head_count
    ffn_blocks = FF // (head_dim * head_count)
    out_mark = query_heads + 2 * key_heads
    gate_mark = out_mark + query_heads
    half_dim = head_dim // 2
    full = ffn_blocks // 2
    scale = head_dim ** (-0.5)
    growth = math.sqrt(max(1.0, model_width / head_dim))
    data_index = lax.axis_index("dp")
    head_index = lax.axis_index("head")
    parity = (data_index >> 2) & 1
    ring = Ring()

    weights = jnp.transpose(weights, (1, 0, 2))
    momentum = jnp.transpose(momentum, (1, 0, 2))
    attn_low = cast_blocks(weights, gate_mark)
    inputs = block_in.astype(F32)
    normed_one, norm_one_back = jax.vjp(rms_scale, inputs, gains[0])
    ids_column = jnp.pad(seq_ids.astype(BF16)[:, None], ((0, 0), (0, 127)))

    early = full - 1
    mine_early, mine_late, other_early, other_late = pack_units(
        jnp.reshape(parity, (1,)), weights, gate_mark, ffn_blocks, early
    )
    spread = [Spread(mine_early, other_early), Spread(mine_late, other_late)]

    group_in = run(head_gather(jnp.concatenate([normed_one.astype(BF16), ids_column], axis=1)))
    qkv_parts = run(ring.gather(attn_low[:out_mark], out_mark // 2))
    qkv_blocks = jnp.transpose(qkv_parts, (1, 0, 2, 3)).reshape(out_mark, model_width, head_dim)
    cot_flow = Flow(wide_gather(cotangent))
    group_in, qkv_blocks, attn_low = stage(
        [spread[0].near(0), spread[0].y(0)], [group_in, qkv_blocks, attn_low], idle=[cot_flow]
    )
    projected = block_project(group_in, qkv_blocks)
    queries = projected[:query_heads].reshape(query_heads * group_rows, head_dim)
    group_ids = group_in[:, model_width]
    kv_rows = 2 * key_heads * group_rows
    out_rows = query_heads * rows_dp
    id_rows = group_rows // head_dim
    packed = jnp.concatenate(
        [
            projected[query_heads:].reshape(kv_rows, head_dim),
            attn_low[out_mark:].reshape(out_rows, head_dim),
            jnp.pad(group_ids.reshape(id_rows, head_dim), ((0, 16 - id_rows), (0, 0))),
        ],
        axis=0,
    )
    keys_values = run(ring.gather(packed, packed.shape[0] // 32 * 16))
    out_blocks = keys_values[:, kv_rows : kv_rows + out_rows].reshape(data_count, query_heads, rows_dp, head_dim)
    out_blocks = jnp.transpose(out_blocks, (1, 0, 2, 3)).reshape(query_heads, model_width, head_dim)
    queries, keys_values, out_blocks = stage(
        [cot_flow, spread[0].y(1), spread[1].near(0)], [queries, keys_values, out_blocks]
    )
    all_ids = keys_values[:, kv_rows + out_rows : kv_rows + out_rows + id_rows].reshape(-1)

    local = in_group(jnp.arange(group_rows, dtype=jnp.int32), group_rows, head_index * tok_rows)
    query_pos = data_index * group_rows + local
    first_pos = jnp.sum((all_ids[None, :] < group_ids[:, None]).astype(jnp.int32), axis=1)
    query_pos = jnp.tile(query_pos, query_heads)
    first_pos = jnp.tile(first_pos, query_heads)
    place = jnp.stack([data_index, head_index * tok_rows]).astype(jnp.int32)
    mixed_low, mixed_full, totals = attend(
        place, queries, keys_values, query_pos[:, None], first_pos[:, None], scale, group_rows
    )
    mixed_heads = mixed_low.reshape(query_heads, group_rows, head_dim)
    mixed_heads, mixed_full, totals, attn_part = stage(
        [spread[0].cross(), spread[1].y(0), spread[1].y(1), cot_flow],
        [mixed_heads, mixed_full, totals, block_back(mixed_heads, out_blocks)],
    )
    attn_flow = Flow(scatter_rows(*attn_part, HEAD_MOVES))
    attn_flow.advance([lax.ppermute(*send) for send in attn_flow.sends])
    stage([attn_flow, spread[0].near(3), spread[0].y(3), spread[1].cross()], idle=[cot_flow])
    residual = inputs + attn_flow.value
    normed_two, norm_two_back = jax.vjp(rms_scale, residual, gains[1])
    wide_flow = Flow(wide_gather(normed_two.astype(BF16)))
    stage([wide_flow, spread[0].y(2), spread[1].near(3), spread[1].y(3)], idle=[cot_flow])
    stage([wide_flow, spread[1].y(2), cot_flow])
    stage([wide_flow])
    finish(wide_flow, cot_flow)

    def whole_rows(pieces):
        if rows_dp % 16 == 0:
            return pieces
        out = jnp.zeros((3, data_count) + pieces[0].shape[1:], BF16)
        for k, piece in enumerate(pieces):
            out = lax.dynamic_update_index_in_dim(out, piece, data_index ^ k, 1)
        return [out.reshape(3, model_width, -1)]

    ffn_sides, ffn_full, *ffn_grads = ffn_front(
        place, wide_flow.value, cot_flow.value, whole_rows(spread[0].value()), whole_rows(spread[1].value())
    )

    def taker(pieces):
        if len(pieces) > 1:
            return lambda k: pieces[k]
        cut = pieces[0].reshape(3, data_count, rows_dp, pieces[0].shape[2])
        return lambda k: lax.dynamic_index_in_dim(cut, data_index ^ k, 1, keepdims=False)

    pieces = len(ffn_grads) // 2
    reduce = [Reduce(taker(ffn_grads[:pieces])), Reduce(taker(ffn_grads[pieces:]))]
    *down_part, dx_kept, dx_sent = stage([reduce[0].y(2)], ffn_back(ffn_sides, ffn_full))
    out_flow = Flow(scatter_rows(*down_part, WIDE_MOVES, 4))
    dx_flow = Flow(scatter_rows(dx_kept, dx_sent, WIDE_MOVES))
    dx_flow.advance([lax.ppermute(*send) for send in dx_flow.sends])
    stage([dx_flow, reduce[0].near(2), reduce[0].y(3), reduce[1].y(2)])
    stage([dx_flow, reduce[0].y(1), reduce[1].near(2), out_flow])
    grad_residual_norm, grad_gain_two = norm_two_back(dx_flow.value)
    grad_residual = cotangent.astype(F32) + grad_residual_norm
    grad_flow = Flow(head_gather(grad_residual.astype(BF16)))
    stage([grad_flow, reduce[0].near(1), reduce[1].y(1), reduce[1].y(3)])
    grad_flow.advance([lax.ppermute(*send) for send in grad_flow.sends])
    group_grad = grad_flow.value

    grad_heads = block_project(group_grad, out_blocks)
    grad_mixed = grad_heads.reshape(query_heads * group_rows, head_dim)
    delta = jnp.sum(grad_mixed.astype(F32) * mixed_full, axis=1)
    grad_queries, grad_keys_values = attend_back(
        place,
        queries,
        grad_mixed,
        keys_values,
        1.0 / totals.reshape(1, -1),
        delta[None, :],
        query_pos[None, :],
        first_pos[None, :],
        scale,
        group_rows,
    )
    late_cross = reduce[1].cross()
    group_grad, grad_queries, grad_keys_values = stage(
        [reduce[0].cross(), reduce[0].y(0), reduce[1].y(0)],
        [group_grad, grad_queries, grad_keys_values],
        idle=[late_cross],
    )
    grad_queries = grad_queries.reshape(query_heads, group_rows, head_dim)

    late = 2
    main = 3 * ffn_blocks - late
    cap = -(-main // data_count)
    places = -(-max(cap * data_count, 3 * ffn_blocks) // TRIO) * TRIO
    def weight_sums(outer):
        cut = outer.reshape(outer.shape[0], data_count, rows_dp, head_dim)
        return Flow(ring.scatter(ring.part(cut, 1), outer.shape[0] // 2 if outer.shape[0] > 2 else None))

    key_flow = Flow(ring.scatter(ring.part(grad_keys_values, 0), key_heads))
    (outer,) = stage(
        [key_flow, late_cross, reduce[1].near(1), out_flow],
        [block_outer([group_in, group_grad], [grad_queries, mixed_heads], model_width)],
    )
    (own_early, other_early), (own_late, other_late) = (part.value() for part in reduce)
    first_flow = weight_sums(outer)
    weight_grads, new_momentum, grams = stage(
        [key_flow, first_flow],
        ffn_moment(
            jnp.reshape(parity, (1,)),
            [own_early, own_late],
            [other_early, other_late],
            momentum,
            gate_mark,
            ffn_blocks,
            places,
        ),
    )
    gram_flow = Flow(gram_sums(ring, grams, cap))
    stage([key_flow, first_flow, gram_flow])
    while key_flow.sends is not None:
        stage([key_flow, first_flow, gram_flow])
    key_value_sums = key_flow.value
    grad_keys = (key_value_sums[:key_heads] * scale).astype(BF16)
    grad_values = key_value_sums[key_heads:].astype(BF16)
    grad_keys_values = jnp.concatenate([grad_keys, grad_values], axis=0)
    (outer,) = stage([first_flow, gram_flow, out_flow], [block_outer([group_in], [grad_keys_values], model_width)])
    finish(first_flow)
    second_flow = weight_sums(outer)
    pairs = [k for k in range(gate_mark // 2) if not query_heads <= 2 * k < out_mark]
    grad_projected = jnp.concatenate([grad_queries, grad_keys_values], axis=0)
    *attn_dx, weight_grads, new_momentum, first_grams = stage(
        [second_flow, gram_flow],
        [
            *block_back(grad_projected, qkv_blocks),
            *attn_moment(first_flow.value, pairs, momentum, weight_grads, new_momentum),
        ],
    )
    last_flow = Flow(scatter_rows(*attn_dx, HEAD_MOVES))
    finish(gram_flow)
    gram_value = gram_flow.value
    while second_flow.sends is not None:
        (gram_value,) = stage([second_flow, last_flow, out_flow], [gram_value])
    finish(last_flow, out_flow)
    block_out = (residual + out_flow.value).astype(BF16)
    grad_input_norm, grad_gain_one = norm_one_back(last_flow.value)
    grad_input = grad_residual + grad_input_norm
    gain_flow = Flow(total_sum(jnp.stack([grad_gain_one, grad_gain_two])))
    weight_grads, new_momentum, second_grams = attn_moment(
        second_flow.value, list(range(query_heads // 2, out_mark // 2)), momentum, weight_grads, new_momentum
    )
    late_count = gate_mark + late
    late_cap = -(-late_count // data_count)
    late_grams = jnp.concatenate([first_grams, second_grams, grams[main : main + late]], axis=0)
    late_grams = jnp.pad(late_grams, ((0, late_cap * data_count - late_count), (0, 0), (0, 0), (0, 0)))
    late_gram_flow = Flow(gram_sums(ring, late_grams, late_cap))
    (gram_value,) = stage([late_gram_flow, gain_flow], [gram_value])
    (factors,) = stage([late_gram_flow, gain_flow], [newton_factor(gram_value, growth)])
    factor_flow = Flow(all_factors(ring, factors))
    while late_gram_flow.sends is not None:
        stage([late_gram_flow, factor_flow, gain_flow])
    (late_factors,) = stage([factor_flow, gain_flow], [newton_factor(late_gram_flow.value, growth)])
    late_factor_flow = Flow(all_factors(ring, late_factors))
    while factor_flow.sends is not None:
        stage([factor_flow, late_factor_flow, gain_flow])
    factors = factor_flow.value

    threes = main // TRIO
    early_spots = [(gate_mark // TRIO + k, [TRIO * k + i for i in range(TRIO)]) for k in range(threes)]
    new_weights = []
    for k in range(0, threes, 3):
        new_weights = stage(
            [late_factor_flow, gain_flow],
            [renew(weights, new_momentum, factors, early_spots[k : k + 3], new_weights)],
        )

    finish(late_factor_flow, gain_flow)
    gain_grads = gain_flow.value
    rest = jnp.concatenate([late_factor_flow.value[:late_count], factors[TRIO * threes : main]], axis=0)
    blocks_of = [2 * pair + i for pair in pairs for i in range(2)] + list(range(query_heads, out_mark))
    blocks_of += [gate_mark + main + k for k in range(late)] + [gate_mark + k for k in range(TRIO * threes, main)]
    late_spots = [
        (spot, [blocks_of.index(TRIO * spot + i) for i in range(TRIO)])
        for spot in sorted({block // TRIO for block in blocks_of})
    ]
    new_weights = renew(weights, new_momentum, rest, late_spots, new_weights)

    new_gain_first = BETA_ONE * gain_first + (1.0 - BETA_ONE) * gain_grads
    new_gain_second = BETA_TWO * gain_second + (1.0 - BETA_TWO) * gain_grads * gain_grads
    first_hat = new_gain_first / (1.0 - BETA_ONE**UPDATE_STEP)
    second_hat = new_gain_second / (1.0 - BETA_TWO**UPDATE_STEP)
    new_gains = gains - ADAM_RATE * first_hat / (jnp.sqrt(second_hat) + ADAM_EPS)
    back = lambda array: jnp.transpose(array, (1, 0, 2))
    return (
        block_out,
        grad_input,
        back(weight_grads),
        back(new_momentum),
        back(new_weights),
        gain_grads,
        new_gain_first,
        new_gain_second,
        new_gains,
    )


def solution(mesh):
    return jax.shard_map(
        on_device,
        mesh=mesh,
        in_specs=(
            P(("dp", "head"), None),
            P(("dp", "head"), None),
            P(("dp", "head")),
            P("dp", "head", None),
            P("dp", "head", None),
            P(),
            P(),
            P(),
        ),
        out_specs=(
            P(("dp", "head"), None),
            P(("dp", "head"), None),
            P("dp", "head", None),
            P("dp", "head", None),
            P("dp", "head", None),
            P(),
            P(),
            P(),
            P(),
        ),
        check_vma=False,
    )
```

```python
import functools
import math

import jax
import jax.numpy as jnp
from jax import lax
from jax.experimental import pallas as pl
from jax.experimental.pallas import tpu as pltpu
from jax.sharding import PartitionSpec as P

H = 8
KV = 4
FF = 9216
NEWTON_STEPS = 5
UPDATE_STEP = 10

NORM_EPS = 1e-06
SOFT_CAP = 50.0
MUON_RATE = 0.2
MUON_DECAY = 0.01
MUON_BETA = 0.95
ADAM_RATE = 0.3
BETA_ONE = 0.9
BETA_TWO = 0.95
ADAM_EPS = 1e-08
NEWTON_LINEAR = 3.4445
NEWTON_SQUARE = -4.775
NEWTON_CUBIC = 2.0315
NEWTON_PRECISION = lax.Precision.HIGH

BF16 = jnp.bfloat16
F32 = jnp.float32
VMEM_LIMIT = 62 * 1024 * 1024
NN = (((1,), (0,)), ((), ()))
NT = (((1,), (1,)), ((), ()))
TN = (((0,), (0,)), ((), ()))


def mm(a, b, dims):
    return lax.dot_general(a, b, dims, preferred_element_type=F32)


def rms_scale(rows, gain):
    inverse = lax.rsqrt(jnp.mean(rows * rows, axis=-1, keepdims=True) + NORM_EPS)
    return rows * inverse * gain


class Flow:
    def __init__(self, steps):
        self.steps = steps
        self.value = None
        self.sends = None
        self.advance(None)

    def advance(self, arrived):
        try:
            self.sends = self.steps.send(arrived)
        except StopIteration as stop:
            self.sends = None
            self.value = stop.value


def stage(flows, extra=(), idle=()):
    flows = [flow for flow in flows if flow.sends is not None]
    idle = [flow for flow in idle if flow.sends is not None and flow not in flows]
    arrived = [[lax.ppermute(*send) for send in flow.sends] for flow in flows]
    held = [[send[0] for send in flow.sends] for flow in idle]
    arrived, held, extra = lax.optimization_barrier((arrived, held, list(extra)))
    for flow, got in zip(flows, arrived):
        flow.advance(got)
    for flow, kept in zip(idle, held):
        flow.sends = [(value,) + send[1:] for value, send in zip(kept, flow.sends)]
    return extra


def run(steps):
    flow = Flow(steps)
    while flow.sends is not None:
        flow.advance([lax.ppermute(*send) for send in flow.sends])
    return flow.value


def finish(*flows):
    while any(flow.sends is not None for flow in flows):
        stage(flows)


def swap(value, axis, mask):
    size = lax.axis_size(axis)
    return (value, axis, [(i, i ^ mask) for i in range(size)])


def head_gather(rows):
    (other,) = yield [swap(rows, "head", 2)]
    pair = jnp.concatenate([rows, other], axis=0)
    (other,) = yield [swap(pair, "head", 1)]
    return jnp.concatenate([pair, other], axis=0)


def wide_gather(rows):
    (other,) = yield [swap(rows, "dp", 4)]
    both = jnp.concatenate([rows, other], axis=0)
    (other,) = yield [swap(both, "head", 2)]
    pair = jnp.concatenate([both, other], axis=0)
    (other,) = yield [swap(pair, "head", 1)]
    return [pair, other]


def add_low(kept, other):
    return (kept.astype(F32) + other.astype(F32)).astype(BF16)


def scatter_rows(kept, sent, moves, cuts=1):
    for k, (axis, mask) in enumerate(moves):
        last = k == len(moves) - 1
        others = []
        for piece in jnp.split(sent, cuts if last else 1):
            others += yield [swap(piece, axis, mask)]
        other = jnp.concatenate(others, axis=0) if len(others) > 1 else others[0]
        part = kept.astype(F32) + other.astype(F32)
        if not last:
            half = part.shape[0] // 2
            kept, sent = part[:half], part[half:].astype(BF16)
    return part


HEAD_MOVES = (("head", 1), ("head", 2))
WIDE_MOVES = (("head", 1), ("head", 2), ("dp", 4))


def total_sum(value):
    for axis in ("head", "dp"):
        mask = 1
        while mask < lax.axis_size(axis):
            (other,) = yield [swap(value, axis, mask)]
            value = value + other
            mask *= 2
    return value


class Ring:
    def __init__(self):
        size = lax.axis_size("dp")
        order = list(range(0, size, 2)) + list(range(size - 1, 0, -2))
        around = [[order[(order.index(i) + offset) % size] for offset in range(size)] for i in range(size)]
        self.size = size
        row = jnp.array(around, jnp.int32)[lax.axis_index("dp")]
        zero = jnp.zeros((), jnp.int32)
        self.around = [lax.select(lax.lt(row[k], zero), row[k] + size, row[k]) for k in range(size)]
        self.up = [(order[k], order[(k + 1) % size]) for k in range(size)]
        self.down = [(order[(k + 1) % size], order[k]) for k in range(size)]

    def index(self, offset, scale=1):
        return self.around[offset % self.size] * scale

    def gather(self, value, mid):
        half = self.size // 2
        out = jnp.zeros((self.size,) + value.shape, value.dtype)

        def put(out, piece, offset, start=0):
            spot = (self.index(offset), start) + (0,) * (value.ndim - 1)
            return lax.dynamic_update_slice(out, piece[None], spot, allow_negative_indices=False)

        out = put(out, value, 0)
        ahead, back = value, value
        for step in range(1, half):
            ahead, back = yield [(ahead, "dp", self.up), (back, "dp", self.down)]
            out = put(put(out, ahead, -step), back, step)
        if mid is None:
            (last,) = yield [(ahead, "dp", self.up)]
            return put(out, last, half)
        first, second = yield [(ahead[:mid], "dp", self.up), (back[mid:], "dp", self.down)]
        return put(put(out, first, half), second, half, mid)

    def part(self, array, axis, size=None):
        if size is None:
            return lambda offset: lax.dynamic_index_in_dim(
                array, self.index(offset), axis, keepdims=False, allow_negative_indices=False
            )
        return lambda offset: lax.dynamic_slice_in_dim(
            array, self.index(offset, size), size, axis, allow_negative_indices=False
        )

    def scatter(self, take, mid):
        half = self.size // 2
        far = take(half)
        kind = far.dtype
        if mid is None:
            (up,) = yield [(far, "dp", self.up)]
            down = None
        else:
            up, down = yield [(far[:mid], "dp", self.up), (far[mid:], "dp", self.down)]
        for step in range(half - 1, 0, -1):
            ahead, back = take(step).astype(F32), take(-step).astype(F32)
            if mid is None or step < half - 1:
                ahead = ahead + up
                back = back if down is None else back + down
            else:
                ahead = jnp.concatenate([ahead[:mid] + up, ahead[mid:]])
                back = jnp.concatenate([back[:mid], back[mid:] + down])
            up, down = yield [(ahead.astype(kind), "dp", self.up), (back.astype(kind), "dp", self.down)]
        return take(0).astype(F32) + up.astype(F32) + down.astype(F32)


def once(sends, take):
    def steps():
        take((yield sends))

    return Flow(steps())


SIDE_BIT = 2


def plane_classes():
    planes = range(lax.axis_size("dp") // 2)
    kept = [m for m in planes if m & 1 == 0]
    passed = [m for m in planes if m & 1 == 1]
    return {0: [0], 1: [1], 2: [m for m in passed if m != 1], 3: [m for m in kept if m]}


class Spread:
    def __init__(self, mine, other):
        self.mine, self.other = mine, other
        self.pieces = {0: mine}

    def move(self, moves):
        def take(arrived):
            for (_, _, _, number), piece in zip(moves, arrived):
                self.pieces[number] = piece

        return once([swap(value, "dp", offset << 1 | bit) for value, offset, bit, _ in moves], take)

    def cross(self):
        group = plane_classes()[3]
        return self.move([(self.other if m & SIDE_BIT else self.mine, m, 0, m << 1) for m in group])

    def near(self, key):
        group = plane_classes()[key]
        return self.move([(self.pieces[m << 1], 1, 0, (m ^ 1) << 1) for m in group])

    def y(self, key):
        group = plane_classes()[key]
        return self.move([(self.pieces[m << 1], 0, 1, m << 1 | 1) for m in group])

    def value(self):
        return [self.pieces[k] for k in range(lax.axis_size("dp"))]


class Reduce:
    def __init__(self, rows):
        self.rows = rows
        self.parts = {}
        self.sums = [[], []]

    def part(self, offset):
        terms = [term.astype(F32) for term in self.parts[offset]]
        return functools.reduce(jnp.add, terms)

    def hold(self, offset, *terms):
        self.parts.setdefault(offset, []).extend(terms)

    def y(self, key):
        group = plane_classes()[key]

        def take(arrived):
            for offset, got in zip(group, arrived):
                self.hold(offset, self.rows(offset << 1), got)

        return once([swap(self.rows(offset << 1 | 1), "dp", 1) for offset in group], take)

    def near(self, key):
        group = plane_classes()[key]

        def take(arrived):
            for offset, got in zip(group, arrived):
                self.hold(offset ^ 1, got)

        return once([swap(self.part(offset).astype(BF16), "dp", 2) for offset in group], take)

    def cross(self):
        group = plane_classes()[3]

        def take(arrived):
            for offset, got in zip(group, arrived):
                self.sums[1 if offset & SIDE_BIT else 0].append(got)

        return once([swap(self.part(offset).astype(BF16), "dp", offset << 1) for offset in group], take)

    def value(self):
        return self.parts[0] + self.sums[0], self.sums[1]


def params(**more):
    return pltpu.CompilerParams(vmem_limit_bytes=VMEM_LIMIT, **more)


TRIO = 3


def cast_blocks(blocks, count):
    _, r, c = blocks.shape

    def body(x_ref, o_ref):
        o_ref[...] = x_ref[...].astype(BF16)

    spec = pl.BlockSpec((TRIO, r, c), lambda k: (k, 0, 0))
    return pl.pallas_call(
        body,
        grid=(count // TRIO,),
        in_specs=[spec],
        out_specs=spec,
        out_shape=jax.ShapeDtypeStruct((count, r, c), BF16),
        compiler_params=params(),
        cost_estimate=pl.CostEstimate(flops=0, bytes_accessed=6 * count * r * c, transcendentals=0),
    )(blocks)


def pack_units(parity, blocks, first, kind_blocks, early):
    _, r, c = blocks.shape
    h = c // 2
    full = kind_blocks // 2
    each = kind_blocks // TRIO
    u, v = early * c, (full - early) * c + h

    def body(s_ref, *refs):
        parts, outs = refs[:each], refs[each:]

        def tile(f):
            return parts[f // TRIO].at[f % TRIO]

        for turn in range(2):

            @pl.when(s_ref[0] == turn)
            def _():
                for k in range(2):
                    side = turn ^ k
                    for i in range(full):
                        value = tile(side * full + i)[...].astype(BF16)
                        if i < early:
                            outs[2 * k][:, i * c : (i + 1) * c] = value
                        else:
                            outs[2 * k + 1][:, (i - early) * c : (i - early + 1) * c] = value
                    rest = tile(2 * full)[:, side * h : (side + 1) * h]
                    outs[2 * k + 1][:, v - h :] = rest.astype(BF16)

    def part(i):
        return pl.BlockSpec((TRIO, r, c), lambda k, s: (first // TRIO + each * k + i, 0, 0))

    wide = pl.BlockSpec((None, r, u), lambda k, s: (k, 0, 0))
    slim = pl.BlockSpec((None, r, v), lambda k, s: (k, 0, 0))
    shapes = [jax.ShapeDtypeStruct((3, r, u), BF16), jax.ShapeDtypeStruct((3, r, v), BF16)]
    return pl.pallas_call(
        body,
        grid_spec=pltpu.PrefetchScalarGridSpec(
            num_scalar_prefetch=1,
            grid=(3,),
            in_specs=[part(i) for i in range(each)],
            out_specs=[wide, slim, wide, slim],
        ),
        out_shape=shapes + shapes,
        compiler_params=params(),
        cost_estimate=pl.CostEstimate(flops=0, bytes_accessed=18 * kind_blocks * r * c, transcendentals=0),
    )(parity, *([blocks] * each))


def block_project(rows, blocks):
    t = rows.shape[0]
    count, d, c = blocks.shape

    def body(x_ref, w_ref, o_ref):
        o_ref[...] = mm(x_ref[...], w_ref[...], NN).astype(BF16)

    return pl.pallas_call(
        body,
        grid=(count,),
        in_specs=[
            pl.BlockSpec((t, d), lambda b: (0, 0)),
            pl.BlockSpec((None, d, c), lambda b: (b, 0, 0)),
        ],
        out_specs=pl.BlockSpec((None, t, c), lambda b: (b, 0, 0)),
        out_shape=jax.ShapeDtypeStruct((count, t, c), BF16),
        compiler_params=params(),
        cost_estimate=pl.CostEstimate(
            flops=2 * count * t * d * c, bytes_accessed=2 * (t * d + count * (d * c + t * c)), transcendentals=0
        ),
    )(rows, blocks)


def block_back(cols, blocks):
    count, t, c = cols.shape
    d = blocks.shape[1]
    half = t // 2

    def body(x_ref, w_ref, o_ref, p_ref, acc_ref):
        b = pl.program_id(0)

        @pl.when(b == 0)
        def _():
            acc_ref[...] = jnp.zeros_like(acc_ref)

        acc_ref[...] += mm(x_ref[...], w_ref[...], NT)

        @pl.when(b == count - 1)
        def _():
            o_ref[...] = acc_ref[:half, :].astype(BF16)
            p_ref[...] = acc_ref[half:, :].astype(BF16)

    result = pl.BlockSpec((half, d), lambda b: (0, 0))
    return pl.pallas_call(
        body,
        grid=(count,),
        in_specs=[
            pl.BlockSpec((None, t, c), lambda b: (b, 0, 0)),
            pl.BlockSpec((None, d, c), lambda b: (b, 0, 0)),
        ],
        out_specs=[result, result],
        out_shape=[jax.ShapeDtypeStruct((half, d), BF16)] * 2,
        scratch_shapes=[pltpu.VMEM((t, d), F32)],
        compiler_params=params(),
        cost_estimate=pl.CostEstimate(
            flops=2 * count * t * d * c, bytes_accessed=2 * (t * d + count * (d * c + t * c)), transcendentals=0
        ),
    )(cols, blocks)


def block_outer(rows, cols, d):
    t = rows[0].shape[0]
    c = cols[0].shape[2]
    starts = [0]
    for col in cols:
        starts.append(starts[-1] + col.shape[0])
    count = len(rows)
    total = starts[-1]

    def body(*refs):
        o_ref, t_ref = refs[2 * count :]
        b = pl.program_id(0)
        for k in range(count):

            @pl.when(b == starts[k])
            def _():
                t_ref[...] = refs[k][...].T

            @pl.when((b >= starts[k]) & (b < starts[k + 1]))
            def _():
                o_ref[...] = mm(t_ref[...], refs[count + k][...], NN).astype(BF16)

    def col_at(k):
        return pl.BlockSpec((None, t, c), lambda b: (jnp.clip(b - starts[k], 0, starts[k + 1] - starts[k] - 1), 0, 0))

    return pl.pallas_call(
        body,
        grid=(total,),
        in_specs=[pl.BlockSpec((t, d), lambda b: (0, 0))] * count + [col_at(k) for k in range(count)],
        out_specs=pl.BlockSpec((None, d, c), lambda b: (b, 0, 0)),
        out_shape=jax.ShapeDtypeStruct((total, d, c), BF16),
        scratch_shapes=[pltpu.VMEM((d, t), BF16)],
        compiler_params=params(),
        cost_estimate=pl.CostEstimate(
            flops=2 * total * t * d * c,
            bytes_accessed=2 * (count * t * d + total * (d * c + t * c)),
            transcendentals=0,
        ),
    )(*rows, *cols)


def in_group(local, width, head_shift):
    quarter = width // 4
    low = jnp.bitwise_and(local, quarter - 1)
    one = jnp.where(jnp.bitwise_and(local, quarter) != 0, 2 * quarter, 0)
    two = jnp.where(jnp.bitwise_and(local, 2 * quarter) != 0, quarter, 0)
    return jnp.bitwise_xor(low + one + two, head_shift)


def key_position(block, width, head_shift, shape, axis):
    local = lax.broadcasted_iota(jnp.int32, shape, axis)
    return block * width + in_group(local, width, head_shift)


def attend(place, queries, keys_values, query_pos, first_pos, scale, p):
    m, e = queries.shape
    n = keys_values.shape[0]
    step = 256

    def body(place_ref, q_ref, kv_ref, pos_ref, first_ref, low_ref, full_ref, sum_ref, acc_ref, tot_ref):
        j = pl.program_id(0)

        @pl.when(j == 0)
        def _():
            acc_ref[...] = jnp.zeros_like(acc_ref)
            tot_ref[...] = jnp.zeros_like(tot_ref)

        @pl.when(j <= place_ref[0])
        def _():
            key_pos = key_position(j, p, place_ref[1], (1, p), 1)
            for r in range(0, m, step):
                rows = pl.ds(r, step)
                raw = mm(q_ref[rows, :], kv_ref[:p, :], NT)
                soft = SOFT_CAP * jnp.tanh(raw * (scale / SOFT_CAP))
                seen = (key_pos >= first_ref[rows, :]) & (key_pos <= pos_ref[rows, :])
                terms = jnp.where(seen, jnp.exp(soft), 0.0)
                tot_ref[rows, :] += jnp.sum(terms, axis=1, keepdims=True)
                acc_ref[rows, :] += mm(terms.astype(BF16), kv_ref[p:, :], NN)

        @pl.when(j == n - 1)
        def _():
            total = tot_ref[...]
            mixed = acc_ref[...] / total
            full_ref[...] = mixed
            low_ref[...] = mixed.astype(BF16)
            sum_ref[...] = total

    whole = lambda shape: pl.BlockSpec(shape, lambda j, s: (0, 0))
    return pl.pallas_call(
        body,
        grid_spec=pltpu.PrefetchScalarGridSpec(
            num_scalar_prefetch=1,
            grid=(n,),
            in_specs=[
                whole((m, e)),
                pl.BlockSpec((None, 2 * p, e), lambda j, s: (jnp.minimum(j, s[0]), 0, 0)),
                whole((m, 1)),
                whole((m, 1)),
            ],
            out_specs=[whole((m, e)), whole((m, e)), whole((m, 1))],
            scratch_shapes=[pltpu.VMEM((m, e), F32), pltpu.VMEM((m, 1), F32)],
        ),
        out_shape=[
            jax.ShapeDtypeStruct((m, e), BF16),
            jax.ShapeDtypeStruct((m, e), F32),
            jax.ShapeDtypeStruct((m, 1), F32),
        ],
        compiler_params=params(),
        cost_estimate=pl.CostEstimate(
            flops=4 * m * n * p * e, bytes_accessed=4 * n * p * e, transcendentals=2 * m * n * p
        ),
    )(place, queries, keys_values, query_pos, first_pos)


def attend_back(place, queries, grads, keys_values, inverse, delta, query_pos, first_pos, scale, p):
    m, e = queries.shape
    n = keys_values.shape[0]
    step = 256

    def body(
        place_ref, q_ref, g_ref, kv_ref, inv_ref, delta_ref, pos_ref, first_ref, dq_ref, dkv_ref, acc_ref, dk_ref, dv_ref
    ):
        j = pl.program_id(0)

        @pl.when(j == 0)
        def _():
            acc_ref[...] = jnp.zeros_like(acc_ref)

        @pl.when(j <= place_ref[0])
        def _():
            key_pos = key_position(j, p, place_ref[1], (p, 1), 0)
            for r in range(0, m, step):
                rows = pl.ds(r, step)
                raw = mm(kv_ref[:p, :], q_ref[rows, :], NT)
                capped = jnp.tanh(raw * (scale / SOFT_CAP))
                seen = (key_pos >= first_ref[:, rows]) & (key_pos <= pos_ref[:, rows])
                probs = jnp.where(seen, jnp.exp(SOFT_CAP * capped), 0.0) * inv_ref[:, rows]
                grad_probs = mm(kv_ref[p:, :], g_ref[rows, :], NT)
                grad_raw = probs * (grad_probs - delta_ref[:, rows]) * (1.0 - capped * capped)
                grad_low = grad_raw.astype(BF16)
                value_part = mm(probs.astype(BF16), g_ref[rows, :], NN)
                key_part = mm(grad_low, q_ref[rows, :], NN)
                if r == 0:
                    dv_ref[...] = value_part
                    dk_ref[...] = key_part
                else:
                    dv_ref[...] += value_part
                    dk_ref[...] += key_part
                acc_ref[rows, :] += mm(grad_low, kv_ref[:p, :], TN)
            dkv_ref[0] = dk_ref[...].astype(BF16)
            dkv_ref[1] = dv_ref[...].astype(BF16)

        @pl.when(j > place_ref[0])
        def _():
            dkv_ref[...] = jnp.zeros_like(dkv_ref)

        @pl.when(j == n - 1)
        def _():
            dq_ref[...] = (acc_ref[...] * scale).astype(BF16)

    whole = lambda shape: pl.BlockSpec(shape, lambda j, s: (0, 0))
    return pl.pallas_call(
        body,
        grid_spec=pltpu.PrefetchScalarGridSpec(
            num_scalar_prefetch=1,
            grid=(n,),
            in_specs=[
                whole((m, e)),
                whole((m, e)),
                pl.BlockSpec((None, 2 * p, e), lambda j, s: (jnp.minimum(j, s[0]), 0, 0)),
                whole((1, m)),
                whole((1, m)),
                whole((1, m)),
                whole((1, m)),
            ],
            out_specs=[whole((m, e)), pl.BlockSpec((None, 2, p, e), lambda j, s: (j, 0, 0, 0))],
            scratch_shapes=[pltpu.VMEM((m, e), F32), pltpu.VMEM((p, e), F32), pltpu.VMEM((p, e), F32)],
        ),
        out_shape=[jax.ShapeDtypeStruct((m, e), BF16), jax.ShapeDtypeStruct((n, 2, p, e), BF16)],
        compiler_params=params(),
        cost_estimate=pl.CostEstimate(
            flops=10 * m * n * p * e, bytes_accessed=8 * n * p * e, transcendentals=2 * m * n * p
        ),
    )(place, queries, grads, keys_values, inverse, delta, query_pos, first_pos)


def gelu_pair(gate):
    outer = math.sqrt(2.0 / math.pi)
    square = gate * gate
    bent = jnp.tanh(outer * gate * (1.0 + 0.044715 * square))
    half = 0.5 * (1.0 + bent)
    slope = half + 0.5 * gate * (1.0 - bent * bent) * outer * (1.0 + 3.0 * 0.044715 * square)
    return gate * half, slope


def ffn_front(place, rows, cots, early, late):
    part_rows, d = rows[0].shape
    t = 2 * part_rows
    count = len(early)
    r = early[0].shape[1]
    u, v = early[0].shape[2], late[0].shape[2]
    tall = min(512, t)
    wide = d // 3
    cuts = [(k, min(256, u + v - k)) for k in range(0, u + v, 256)]

    def body(place_ref, x0, x1, y0, y1, *refs):
        early_refs, late_refs = refs[:count], refs[count : 2 * count]
        refs = refs[2 * count :]
        hs_ref, w_out = refs[:2]
        grad_refs = refs[2 : 2 + count], refs[2 + count : 2 + 2 * count]
        x, y, w, xt, yt, hs, row_sems, sems, out_sems, grad_sems = refs[2 + 2 * count :]
        row_copies = []
        for k, (source, target) in enumerate(((x0, x), (x1, x), (y0, y), (y1, y))):
            target = target.at[pl.ds((k % 2) * part_rows, part_rows), :]
            row_copies.append(pltpu.make_async_copy(source, target, row_sems.at[k]))
            row_copies[k].start()
        copies = []
        chunks = ((early_refs, pl.ds(0, u)), (late_refs, pl.ds(u, v)))

        def spot(k):
            return pl.ds(pl.multiple_of(jnp.bitwise_xor(place_ref[0], k) * r, 16) if count > 1 else 0, r)

        for k in range(count):
            for way, (sources, lanes) in enumerate(chunks):
                copy = pltpu.make_async_copy(sources[k], w.at[:, spot(k), lanes], sems.at[way, k])
                copy.start()
                copies.append(copy)
        for copy in row_copies:
            copy.wait()

        @pl.loop(0, d // 256)
        def _(k):
            cols = pl.ds(pl.multiple_of(k * 256, 256), 256)
            xt[cols, :] = x[:, cols].T
            yt[cols, :] = y[:, cols].T

        for copy in copies:
            copy.wait()
        kept = pltpu.make_async_copy(w, w_out, out_sems.at[0])
        kept.start()

        @pl.loop(0, t // tall)
        def _(i):
            part = pl.ds(pl.multiple_of(i * tall, tall), tall)
            for start, size in cuts:
                units = pl.ds(start, size)
                gate = mm(x[part, :], w[0, :, units], NN)
                up = mm(x[part, :], w[1, :, units], NN)
                grad = mm(y[part, :], w[2, :, units], NN)
                active, slope = gelu_pair(gate)
                hs[0, part, units] = (active * up).astype(BF16)
                hs[1, part, units] = (grad * up * slope).astype(BF16)
                hs[2, part, units] = (grad * active).astype(BF16)

        sides = pltpu.make_async_copy(hs, hs_ref, out_sems.at[1])
        sides.start()
        kept.wait()
        copies = []
        for kind, (left, right) in enumerate(((xt, 1), (xt, 2), (yt, 0))):

            @pl.loop(0, d // wide)
            def _(k):
                cols = pl.ds(pl.multiple_of(k * wide, wide), wide)
                w[kind, cols, :] = mm(left[cols, :], hs[right], NN).astype(BF16)

            for k in range(count):
                for way, (_, lanes) in enumerate(chunks):
                    target = grad_refs[way][k].at[kind]
                    copy = pltpu.make_async_copy(w.at[kind, spot(k), lanes], target, grad_sems.at[kind, way, k])
                    copy.start()
                    copies.append(copy)
        sides.wait()
        for copy in copies:
            copy.wait()

    apart = pl.BlockSpec(memory_space=pl.ANY)
    return pl.pallas_call(
        body,
        grid_spec=pltpu.PrefetchScalarGridSpec(
            num_scalar_prefetch=1,
            grid=(1,),
            in_specs=[apart] * (4 + 2 * count),
            out_specs=[apart] * (2 + 2 * count),
            scratch_shapes=[
                pltpu.VMEM((t, d), BF16),
                pltpu.VMEM((t, d), BF16),
                pltpu.VMEM((3, d, u + v), BF16),
                pltpu.VMEM((d, t), BF16),
                pltpu.VMEM((d, t), BF16),
                pltpu.VMEM((3, t, u + v), BF16),
                pltpu.SemaphoreType.DMA((4,)),
                pltpu.SemaphoreType.DMA((2, count)),
                pltpu.SemaphoreType.DMA((2,)),
                pltpu.SemaphoreType.DMA((3, 2, count)),
            ],
        ),
        out_shape=[
            jax.ShapeDtypeStruct((3, t, u + v), BF16),
            jax.ShapeDtypeStruct((3, d, u + v), BF16),
            *[jax.ShapeDtypeStruct((3, r, u), BF16)] * count,
            *[jax.ShapeDtypeStruct((3, r, v), BF16)] * count,
        ],
        compiler_params=params(),
        cost_estimate=pl.CostEstimate(
            flops=12 * t * d * (u + v), bytes_accessed=12 * d * (u + v) + 4 * t * d, transcendentals=t * (u + v)
        ),
    )(place, *rows, *cots, *early, *late)


def ffn_back(sides, blocks):
    _, t, u = sides.shape
    d = blocks.shape[1]
    wide = 256
    half = t // 2

    def body(s_ref, w_ref, *refs):
        for k in range(2):
            part = pl.ds(k * half, half)
            refs[k][...] = mm(s_ref[0, part, :], w_ref[2], NT).astype(BF16)
            refs[2 + k][...] = (mm(s_ref[1, part, :], w_ref[0], NT) + mm(s_ref[2, part, :], w_ref[1], NT)).astype(BF16)

    return pl.pallas_call(
        body,
        grid=(d // wide,),
        in_specs=[
            pl.BlockSpec((3, t, u), lambda k: (0, 0, 0), pipeline_mode=pl.Buffered(1)),
            pl.BlockSpec((3, wide, u), lambda k: (0, k, 0)),
        ],
        out_specs=[pl.BlockSpec((half, wide), lambda k: (0, k))] * 4,
        out_shape=[jax.ShapeDtypeStruct((half, d), BF16)] * 4,
        compiler_params=params(),
        cost_estimate=pl.CostEstimate(
            flops=6 * t * d * u, bytes_accessed=6 * d * u + 6 * t * u + 4 * t * d, transcendentals=0
        ),
    )(sides, blocks)


def gram_parts(m):
    h = m.shape[1] // 2
    high = m.astype(BF16)
    low = (m - high.astype(F32)).astype(BF16)
    mixed = mm(high, low, TN)
    gram = mm(high, high, TN) + mm(low, low, TN) + mixed + mixed.T
    return gram[:h, :h], gram[:h, h:], gram[h:, h:]


def ffn_moment(parity, own, other, momentum, first, blocks, places):
    total, r, c = momentum.shape
    terms = [*own, *other]
    counts = [len(group) for group in terms]
    u, v = own[0][0].shape[2], own[1][0].shape[2]
    early = u // c
    h = c // 2
    full = early + 1
    each = blocks // TRIO

    def body(s_ref, *refs):
        groups = []
        for count in counts:
            groups.append(refs[:count])
            refs = refs[count:]
        m_ref, wg_ref, nm_ref, gram_ref = refs
        j = pl.program_id(0)

        def total_of(group, start, size):
            lanes = pl.ds(start, size)
            return functools.reduce(jnp.add, [ref[:, lanes].astype(F32) for ref in group])

        @pl.when(j >= TRIO * each)
        def _():
            gram_ref[...] = jnp.zeros_like(gram_ref)

        for turn in range(each):
            for mine in range(2):

                @pl.when((j < TRIO * each) & (lax.rem(j, each) == turn) & (s_ref[0] == mine))
                def _():
                    for i in range(TRIO):
                        side, f = divmod(turn * TRIO + i, full)
                        if side == 2:
                            for k in range(2):
                                group = groups[1 if k == mine else 3]
                                wg_ref[i, :, k * h : (k + 1) * h] = total_of(group, c, h)
                        elif f < early:
                            wg_ref[i] = total_of(groups[0 if side == mine else 2], f * c, c)
                        else:
                            wg_ref[i] = total_of(groups[1 if side == mine else 3], 0, c)

        @pl.when(j < TRIO * each)
        def _():
            for i in range(TRIO):
                new = MUON_BETA * m_ref[i] + wg_ref[i]
                nm_ref[i] = new
                gram_ref[i, 0], gram_ref[i, 1], gram_ref[i, 2] = gram_parts(new)

    kind = lambda j, s: (jnp.minimum(j // each, 2), 0, 0)
    block = lambda j, s: (first // TRIO + jnp.minimum(j, TRIO * each - 1), 0, 0)
    arrays = [array for group in terms for array in group]
    return pl.pallas_call(
        body,
        grid_spec=pltpu.PrefetchScalarGridSpec(
            num_scalar_prefetch=1,
            grid=(places // TRIO,),
            in_specs=[pl.BlockSpec((None,) + array.shape[1:], kind) for array in arrays]
            + [pl.BlockSpec((TRIO, r, c), block)],
            out_specs=[
                pl.BlockSpec((TRIO, r, c), block),
                pl.BlockSpec((TRIO, r, c), block),
                pl.BlockSpec((TRIO, 3, h, h), lambda j, s: (j, 0, 0, 0)),
            ],
        ),
        out_shape=[
            jax.ShapeDtypeStruct((total, r, c), F32),
            jax.ShapeDtypeStruct((total, r, c), F32),
            jax.ShapeDtypeStruct((places, 3, h, h), F32),
        ],
        compiler_params=params(),
        cost_estimate=pl.CostEstimate(
            flops=6 * 3 * blocks * r * c * c, bytes_accessed=16 * 3 * blocks * r * c, transcendentals=0
        ),
    )(parity, *arrays, momentum)


def attn_moment(grads, pairs, momentum, weight_grads, new_momentum):
    count, r, c = grads.shape
    h = c // 2

    def body(s_ref, g_ref, m_ref, wg_in, nm_in, wg_ref, nm_ref, gram_ref):
        for i in range(2):
            new = MUON_BETA * m_ref[i] + g_ref[i]
            wg_ref[i] = g_ref[i]
            nm_ref[i] = new
            gram_ref[i, 0], gram_ref[i, 1], gram_ref[i, 2] = gram_parts(new)

    block = pl.BlockSpec((2, r, c), lambda j, s: (s[j], 0, 0))
    apart = pl.BlockSpec(memory_space=pl.ANY)
    return pl.pallas_call(
        body,
        grid_spec=pltpu.PrefetchScalarGridSpec(
            num_scalar_prefetch=1,
            grid=(count // 2,),
            in_specs=[pl.BlockSpec((2, r, c), lambda j, s: (j, 0, 0)), block, apart, apart],
            out_specs=[block, block, pl.BlockSpec((2, 3, h, h), lambda j, s: (j, 0, 0, 0))],
        ),
        out_shape=[
            jax.ShapeDtypeStruct(momentum.shape, F32),
            jax.ShapeDtypeStruct(momentum.shape, F32),
            jax.ShapeDtypeStruct((count, 3, h, h), F32),
        ],
        input_output_aliases={3: 0, 4: 1},
        compiler_params=params(),
        cost_estimate=pl.CostEstimate(
            flops=6 * count * r * c * c, bytes_accessed=16 * count * r * c, transcendentals=0
        ),
    )(jnp.array(pairs, jnp.int32), grads, momentum, weight_grads, new_momentum)


def renew(weights, momentum, factors, spots, updated):
    _, r, c = weights.shape
    h = c // 2
    steps = len(spots)
    table = jnp.array([spot for spot, _ in spots] + [f for _, places in spots for f in places], jnp.int32)

    def body(s_ref, w_ref, m_ref, *refs):
        factor_refs, o_ref = refs[:TRIO], refs[-1]
        for i in range(TRIO):
            left = m_ref[i, :, :h].astype(BF16)
            right = m_ref[i, :, h:].astype(BF16)
            first, off, last = factor_refs[i][0], factor_refs[i][1], factor_refs[i][2]
            start = mm(left, first, NN) + mm(right, off, NT)
            rest = mm(left, off, NN) + mm(right, last, NN)
            keep = 1.0 - MUON_RATE * MUON_DECAY
            o_ref[i, :, :h] = w_ref[i, :, :h] * keep - MUON_RATE * start
            o_ref[i, :, h:] = w_ref[i, :, h:] * keep - MUON_RATE * rest

    block = pl.BlockSpec((TRIO, r, c), lambda j, s: (s[j], 0, 0))

    def factor_at(i):
        return pl.BlockSpec((None, 3, h, h), lambda j, s: (s[steps + TRIO * j + i], 0, 0, 0))

    apart = [pl.BlockSpec(memory_space=pl.ANY)] * len(updated)
    return pl.pallas_call(
        body,
        grid_spec=pltpu.PrefetchScalarGridSpec(
            num_scalar_prefetch=1,
            grid=(steps,),
            in_specs=[block, block] + [factor_at(i) for i in range(TRIO)] + apart,
            out_specs=block,
        ),
        out_shape=jax.ShapeDtypeStruct(weights.shape, F32),
        input_output_aliases={3 + TRIO: 0} if updated else {},
        compiler_params=params(),
        cost_estimate=pl.CostEstimate(
            flops=2 * TRIO * steps * r * c * c, bytes_accessed=12 * TRIO * steps * r * c, transcendentals=0
        ),
    )(table, weights, momentum, *([factors] * TRIO), *updated)


def top(spec, a, b):
    return jnp.einsum(spec, a, b, precision=NEWTON_PRECISION)


def newton_factor(grams, growth):
    size = grams.shape[-1]
    eye = jnp.eye(size, dtype=F32)
    norm = jnp.sqrt(jnp.sum(grams * eye, axis=(1, 2), keepdims=True))
    inverse = 1.0 / (norm + 1e-07)
    gram = grams * (inverse * inverse)
    factor = None
    for sweep in range(NEWTON_STEPS):
        square = top("bij,bjk->bik", gram, gram)
        poly = NEWTON_LINEAR * eye + NEWTON_SQUARE * gram + NEWTON_CUBIC * square
        factor = poly if sweep == 0 else top("bij,bjk->bik", factor, poly)
        if sweep < NEWTON_STEPS - 1:
            gram = top("bij,bjk->bik", top("bij,bjk->bik", gram, poly), poly)
    return factor * (growth * inverse)


def fold(squares):
    h = squares.shape[1] // 2
    return jnp.stack([squares[:, :h, :h], squares[:, :h, h:], squares[:, h:, h:]], axis=1)


def unfold(parts):
    first, off, last = parts[:, 0], parts[:, 1], parts[:, 2]
    upper = jnp.concatenate([first, off], axis=2)
    lower = jnp.concatenate([jnp.swapaxes(off, 1, 2), last], axis=2)
    return jnp.concatenate([upper, lower], axis=1)


def gram_sums(ring, parts, cap):
    h = parts.shape[2]
    parts = parts.reshape(-1, h, h)
    rows = 3 * cap
    mine = yield from ring.scatter(ring.part(parts, 0, rows), rows // 2 if cap > 1 else None)
    return unfold(mine.reshape(cap, 3, h, h))


def all_factors(ring, factors):
    cap, c, _ = factors.shape
    parts = fold(factors.astype(BF16)).reshape(3 * cap, c // 2, c // 2)
    parts = yield from ring.gather(parts, 3 * cap // 2 if cap > 1 else None)
    return parts.reshape(ring.size * cap, 3, c // 2, c // 2)


def on_device(block_in, cotangent, seq_ids, weights, momentum, gains, gain_first, gain_second):
    tok_rows, model_width = block_in.shape
    rows_dp, group_blocks, head_dim = weights.shape
    head_count = lax.axis_size("head")
    data_count = lax.axis_size("dp")
    group_rows = tok_rows * head_count
    key_heads = KV // head_count
    query_heads = H // head_count
    ffn_blocks = FF // (head_dim * head_count)
    out_mark = query_heads + 2 * key_heads
    gate_mark = out_mark + query_heads
    half_dim = head_dim // 2
    full = ffn_blocks // 2
    scale = head_dim ** (-0.5)
    growth = math.sqrt(max(1.0, model_width / head_dim))
    data_index = lax.axis_index("dp")
    head_index = lax.axis_index("head")
    parity = (data_index >> 2) & 1
    ring = Ring()

    weights = jnp.transpose(weights, (1, 0, 2))
    momentum = jnp.transpose(momentum, (1, 0, 2))
    attn_low = cast_blocks(weights, gate_mark)
    inputs = block_in.astype(F32)
    normed_one, norm_one_back = jax.vjp(rms_scale, inputs, gains[0])
    ids_column = jnp.pad(seq_ids.astype(BF16)[:, None], ((0, 0), (0, 127)))

    early = full - 1
    mine_early, mine_late, other_early, other_late = pack_units(
        jnp.reshape(parity, (1,)), weights, gate_mark, ffn_blocks, early
    )
    spread = [Spread(mine_early, other_early), Spread(mine_late, other_late)]

    group_in = run(head_gather(jnp.concatenate([normed_one.astype(BF16), ids_column], axis=1)))
    qkv_parts = run(ring.gather(attn_low[:out_mark], out_mark // 2))
    qkv_blocks = jnp.transpose(qkv_parts, (1, 0, 2, 3)).reshape(out_mark, model_width, head_dim)
    cot_flow = Flow(wide_gather(cotangent))
    group_in, qkv_blocks, attn_low = stage(
        [spread[0].near(0), spread[0].y(0)], [group_in, qkv_blocks, attn_low], idle=[cot_flow]
    )
    projected = block_project(group_in, qkv_blocks)
    queries = projected[:query_heads].reshape(query_heads * group_rows, head_dim)
    group_ids = group_in[:, model_width]
    kv_rows = 2 * key_heads * group_rows
    out_rows = query_heads * rows_dp
    id_rows = group_rows // head_dim
    packed = jnp.concatenate(
        [
            projected[query_heads:].reshape(kv_rows, head_dim),
            attn_low[out_mark:].reshape(out_rows, head_dim),
            jnp.pad(group_ids.reshape(id_rows, head_dim), ((0, 16 - id_rows), (0, 0))),
        ],
        axis=0,
    )
    keys_values = run(ring.gather(packed, packed.shape[0] // 32 * 16))
    out_blocks = keys_values[:, kv_rows : kv_rows + out_rows].reshape(data_count, query_heads, rows_dp, head_dim)
    out_blocks = jnp.transpose(out_blocks, (1, 0, 2, 3)).reshape(query_heads, model_width, head_dim)
    queries, keys_values, out_blocks = stage(
        [cot_flow, spread[0].y(1), spread[1].near(0)], [queries, keys_values, out_blocks]
    )
    all_ids = keys_values[:, kv_rows + out_rows : kv_rows + out_rows + id_rows].reshape(-1)

    local = in_group(jnp.arange(group_rows, dtype=jnp.int32), group_rows, head_index * tok_rows)
    query_pos = data_index * group_rows + local
    first_pos = jnp.sum((all_ids[None, :] < group_ids[:, None]).astype(jnp.int32), axis=1)
    query_pos = jnp.tile(query_pos, query_heads)
    first_pos = jnp.tile(first_pos, query_heads)
    place = jnp.stack([data_index, head_index * tok_rows]).astype(jnp.int32)
    mixed_low, mixed_full, totals = attend(
        place, queries, keys_values, query_pos[:, None], first_pos[:, None], scale, group_rows
    )
    mixed_heads = mixed_low.reshape(query_heads, group_rows, head_dim)
    mixed_heads, mixed_full, totals, attn_part = stage(
        [spread[0].cross(), spread[1].y(0), spread[1].y(1), cot_flow],
        [mixed_heads, mixed_full, totals, block_back(mixed_heads, out_blocks)],
    )
    attn_flow = Flow(scatter_rows(*attn_part, HEAD_MOVES))
    attn_flow.advance([lax.ppermute(*send) for send in attn_flow.sends])
    stage([attn_flow, spread[0].near(3), spread[0].y(3), spread[1].cross()], idle=[cot_flow])
    residual = inputs + attn_flow.value
    normed_two, norm_two_back = jax.vjp(rms_scale, residual, gains[1])
    wide_flow = Flow(wide_gather(normed_two.astype(BF16)))
    stage([wide_flow, spread[0].y(2), spread[1].near(3), spread[1].y(3)], idle=[cot_flow])
    stage([wide_flow, spread[1].y(2), cot_flow])
    stage([wide_flow])
    finish(wide_flow, cot_flow)

    def whole_rows(pieces):
        if rows_dp % 16 == 0:
            return pieces
        out = jnp.zeros((3, data_count) + pieces[0].shape[1:], BF16)
        for k, piece in enumerate(pieces):
            out = lax.dynamic_update_index_in_dim(out, piece, data_index ^ k, 1)
        return [out.reshape(3, model_width, -1)]

    ffn_sides, ffn_full, *ffn_grads = ffn_front(
        place, wide_flow.value, cot_flow.value, whole_rows(spread[0].value()), whole_rows(spread[1].value())
    )

    def taker(pieces):
        if len(pieces) > 1:
            return lambda k: pieces[k]
        cut = pieces[0].reshape(3, data_count, rows_dp, pieces[0].shape[2])
        return lambda k: lax.dynamic_index_in_dim(cut, data_index ^ k, 1, keepdims=False)

    pieces = len(ffn_grads) // 2
    reduce = [Reduce(taker(ffn_grads[:pieces])), Reduce(taker(ffn_grads[pieces:]))]
    *down_part, dx_kept, dx_sent = stage([reduce[0].y(2)], ffn_back(ffn_sides, ffn_full))
    out_flow = Flow(scatter_rows(*down_part, WIDE_MOVES, 4))
    dx_flow = Flow(scatter_rows(dx_kept, dx_sent, WIDE_MOVES))
    dx_flow.advance([lax.ppermute(*send) for send in dx_flow.sends])
    stage([dx_flow, reduce[0].near(2), reduce[0].y(3), reduce[1].y(2)])
    stage([dx_flow, reduce[0].y(1), reduce[1].near(2), out_flow])
    grad_residual_norm, grad_gain_two = norm_two_back(dx_flow.value)
    grad_residual = cotangent.astype(F32) + grad_residual_norm
    grad_flow = Flow(head_gather(grad_residual.astype(BF16)))
    stage([grad_flow, reduce[0].near(1), reduce[1].y(1), reduce[1].y(3)])
    grad_flow.advance([lax.ppermute(*send) for send in grad_flow.sends])
    group_grad = grad_flow.value

    grad_heads = block_project(group_grad, out_blocks)
    grad_mixed = grad_heads.reshape(query_heads * group_rows, head_dim)
    delta = jnp.sum(grad_mixed.astype(F32) * mixed_full, axis=1)
    grad_queries, grad_keys_values = attend_back(
        place,
        queries,
        grad_mixed,
        keys_values,
        1.0 / totals.reshape(1, -1),
        delta[None, :],
        query_pos[None, :],
        first_pos[None, :],
        scale,
        group_rows,
    )
    late_cross = reduce[1].cross()
    group_grad, grad_queries, grad_keys_values = stage(
        [reduce[0].cross(), reduce[0].y(0), reduce[1].y(0)],
        [group_grad, grad_queries, grad_keys_values],
        idle=[late_cross],
    )
    grad_queries = grad_queries.reshape(query_heads, group_rows, head_dim)

    late = 2
    main = 3 * ffn_blocks - late
    cap = -(-main // data_count)
    places = -(-max(cap * data_count, 3 * ffn_blocks) // TRIO) * TRIO
    def weight_sums(outer):
        cut = outer.reshape(outer.shape[0], data_count, rows_dp, head_dim)
        return Flow(ring.scatter(ring.part(cut, 1), outer.shape[0] // 2 if outer.shape[0] > 2 else None))

    key_flow = Flow(ring.scatter(ring.part(grad_keys_values, 0), key_heads))
    (outer,) = stage(
        [key_flow, late_cross, reduce[1].near(1), out_flow],
        [block_outer([group_in, group_grad], [grad_queries, mixed_heads], model_width)],
    )
    (own_early, other_early), (own_late, other_late) = (part.value() for part in reduce)
    first_flow = weight_sums(outer)
    weight_grads, new_momentum, grams = stage(
        [key_flow, first_flow],
        ffn_moment(
            jnp.reshape(parity, (1,)),
            [own_early, own_late],
            [other_early, other_late],
            momentum,
            gate_mark,
            ffn_blocks,
            places,
        ),
    )
    gram_flow = Flow(gram_sums(ring, grams, cap))
    stage([key_flow, first_flow, gram_flow])
    while key_flow.sends is not None:
        stage([key_flow, first_flow, gram_flow])
    key_value_sums = key_flow.value
    grad_keys = (key_value_sums[:key_heads] * scale).astype(BF16)
    grad_values = key_value_sums[key_heads:].astype(BF16)
    grad_keys_values = jnp.concatenate([grad_keys, grad_values], axis=0)
    (outer,) = stage([first_flow, gram_flow, out_flow], [block_outer([group_in], [grad_keys_values], model_width)])
    finish(first_flow)
    second_flow = weight_sums(outer)
    pairs = [k for k in range(gate_mark // 2) if not query_heads <= 2 * k < out_mark]
    grad_projected = jnp.concatenate([grad_queries, grad_keys_values], axis=0)
    *attn_dx, weight_grads, new_momentum, first_grams = stage(
        [second_flow, gram_flow],
        [
            *block_back(grad_projected, qkv_blocks),
            *attn_moment(first_flow.value, pairs, momentum, weight_grads, new_momentum),
        ],
    )
    last_flow = Flow(scatter_rows(*attn_dx, HEAD_MOVES))
    finish(gram_flow)
    gram_value = gram_flow.value
    while second_flow.sends is not None:
        (gram_value,) = stage([second_flow, last_flow, out_flow], [gram_value])
    finish(last_flow, out_flow)
    block_out = (residual + out_flow.value).astype(BF16)
    grad_input_norm, grad_gain_one = norm_one_back(last_flow.value)
    grad_input = grad_residual + grad_input_norm
    gain_flow = Flow(total_sum(jnp.stack([grad_gain_one, grad_gain_two])))
    weight_grads, new_momentum, second_grams = attn_moment(
        second_flow.value, list(range(query_heads // 2, out_mark // 2)), momentum, weight_grads, new_momentum
    )
    late_count = gate_mark + late
    late_cap = -(-late_count // data_count)
    late_grams = jnp.concatenate([first_grams, second_grams, grams[main : main + late]], axis=0)
    late_grams = jnp.pad(late_grams, ((0, late_cap * data_count - late_count), (0, 0), (0, 0), (0, 0)))
    late_gram_flow = Flow(gram_sums(ring, late_grams, late_cap))
    (gram_value,) = stage([late_gram_flow, gain_flow], [gram_value])
    (factors,) = stage([late_gram_flow, gain_flow], [newton_factor(gram_value, growth)])
    factor_flow = Flow(all_factors(ring, factors))
    while late_gram_flow.sends is not None:
        stage([late_gram_flow, factor_flow, gain_flow])
    (late_factors,) = stage([factor_flow, gain_flow], [newton_factor(late_gram_flow.value, growth)])
    late_factor_flow = Flow(all_factors(ring, late_factors))
    while factor_flow.sends is not None:
        stage([factor_flow, late_factor_flow, gain_flow])
    factors = factor_flow.value

    threes = main // TRIO
    early_spots = [(gate_mark // TRIO + k, [TRIO * k + i for i in range(TRIO)]) for k in range(threes)]
    new_weights = []
    for k in range(0, threes, 3):
        new_weights = stage(
            [late_factor_flow, gain_flow],
            [renew(weights, new_momentum, factors, early_spots[k : k + 3], new_weights)],
        )

    finish(late_factor_flow, gain_flow)
    gain_grads = gain_flow.value
    rest = jnp.concatenate([late_factor_flow.value[:late_count], factors[TRIO * threes : main]], axis=0)
    blocks_of = [2 * pair + i for pair in pairs for i in range(2)] + list(range(query_heads, out_mark))
    blocks_of += [gate_mark + main + k for k in range(late)] + [gate_mark + k for k in range(TRIO * threes, main)]
    late_spots = [
        (spot, [blocks_of.index(TRIO * spot + i) for i in range(TRIO)])
        for spot in sorted({block // TRIO for block in blocks_of})
    ]
    new_weights = renew(weights, new_momentum, rest, late_spots, new_weights)

    new_gain_first = BETA_ONE * gain_first + (1.0 - BETA_ONE) * gain_grads
    new_gain_second = BETA_TWO * gain_second + (1.0 - BETA_TWO) * gain_grads * gain_grads
    first_hat = new_gain_first / (1.0 - BETA_ONE**UPDATE_STEP)
    second_hat = new_gain_second / (1.0 - BETA_TWO**UPDATE_STEP)
    new_gains = gains - ADAM_RATE * first_hat / (jnp.sqrt(second_hat) + ADAM_EPS)
    back = lambda array: jnp.transpose(array, (1, 0, 2))
    return (
        block_out,
        grad_input,
        back(weight_grads),
        back(new_momentum),
        back(new_weights),
        gain_grads,
        new_gain_first,
        new_gain_second,
        new_gains,
    )


def solution(mesh):
    return jax.shard_map(
        on_device,
        mesh=mesh,
        in_specs=(
            P(("dp", "head"), None),
            P(("dp", "head"), None),
            P(("dp", "head")),
            P("dp", "head", None),
            P("dp", "head", None),
            P(),
            P(),
            P(),
        ),
        out_specs=(
            P(("dp", "head"), None),
            P(("dp", "head"), None),
            P("dp", "head", None),
            P("dp", "head", None),
            P("dp", "head", None),
            P(),
            P(),
            P(),
            P(),
        ),
        check_vma=False,
    )
```

```python
import functools
import math

import jax
import jax.numpy as jnp
from jax import lax
from jax.experimental import pallas as pl
from jax.experimental.pallas import tpu as pltpu
from jax.sharding import PartitionSpec as P

H = 8
KV = 4
FF = 9216
NEWTON_STEPS = 5
UPDATE_STEP = 10

NORM_EPS = 1e-06
SOFT_CAP = 50.0
MUON_RATE = 0.2
MUON_DECAY = 0.01
MUON_BETA = 0.95
ADAM_RATE = 0.3
BETA_ONE = 0.9
BETA_TWO = 0.95
ADAM_EPS = 1e-08
NEWTON_LINEAR = 3.4445
NEWTON_SQUARE = -4.775
NEWTON_CUBIC = 2.0315
NEWTON_PRECISION = lax.Precision.HIGH

BF16 = jnp.bfloat16
F32 = jnp.float32
VMEM_LIMIT = 62 * 1024 * 1024
NN = (((1,), (0,)), ((), ()))
NT = (((1,), (1,)), ((), ()))
TN = (((0,), (0,)), ((), ()))


def mm(a, b, dims):
    return lax.dot_general(a, b, dims, preferred_element_type=F32)


def rms_scale(rows, gain):
    inverse = lax.rsqrt(jnp.mean(rows * rows, axis=-1, keepdims=True) + NORM_EPS)
    return rows * inverse * gain


class Flow:
    def __init__(self, steps):
        self.steps = steps
        self.value = None
        self.sends = None
        self.advance(None)

    def advance(self, arrived):
        try:
            self.sends = self.steps.send(arrived)
        except StopIteration as stop:
            self.sends = None
            self.value = stop.value


def stage(flows, extra=(), idle=()):
    flows = [flow for flow in flows if flow.sends is not None]
    idle = [flow for flow in idle if flow.sends is not None and flow not in flows]
    arrived = [[lax.ppermute(*send) for send in flow.sends] for flow in flows]
    held = [[send[0] for send in flow.sends] for flow in idle]
    arrived, held, extra = lax.optimization_barrier((arrived, held, list(extra)))
    for flow, got in zip(flows, arrived):
        flow.advance(got)
    for flow, kept in zip(idle, held):
        flow.sends = [(value,) + send[1:] for value, send in zip(kept, flow.sends)]
    return extra


def run(steps):
    flow = Flow(steps)
    while flow.sends is not None:
        flow.advance([lax.ppermute(*send) for send in flow.sends])
    return flow.value


def finish(*flows):
    while any(flow.sends is not None for flow in flows):
        stage(flows)


def swap(value, axis, mask):
    size = lax.axis_size(axis)
    return (value, axis, [(i, i ^ mask) for i in range(size)])


def head_gather(rows):
    (other,) = yield [swap(rows, "head", 2)]
    pair = jnp.concatenate([rows, other], axis=0)
    (other,) = yield [swap(pair, "head", 1)]
    return jnp.concatenate([pair, other], axis=0)


def wide_gather(rows):
    (other,) = yield [swap(rows, "dp", 4)]
    both = jnp.concatenate([rows, other], axis=0)
    (other,) = yield [swap(both, "head", 2)]
    pair = jnp.concatenate([both, other], axis=0)
    (other,) = yield [swap(pair, "head", 1)]
    return [pair, other]


def add_low(kept, other):
    return (kept.astype(F32) + other.astype(F32)).astype(BF16)


def scatter_rows(kept, sent, moves, cuts=1):
    for k, (axis, mask) in enumerate(moves):
        last = k == len(moves) - 1
        others = []
        for piece in jnp.split(sent, cuts if last else 1):
            others += yield [swap(piece, axis, mask)]
        other = jnp.concatenate(others, axis=0) if len(others) > 1 else others[0]
        part = kept.astype(F32) + other.astype(F32)
        if not last:
            half = part.shape[0] // 2
            kept, sent = part[:half], part[half:].astype(BF16)
    return part


HEAD_MOVES = (("head", 1), ("head", 2))
WIDE_MOVES = (("head", 1), ("head", 2), ("dp", 4))


def total_sum(value):
    for axis in ("head", "dp"):
        mask = 1
        while mask < lax.axis_size(axis):
            (other,) = yield [swap(value, axis, mask)]
            value = value + other
            mask *= 2
    return value


class Ring:
    def __init__(self):
        size = lax.axis_size("dp")
        order = list(range(0, size, 2)) + list(range(size - 1, 0, -2))
        around = [[order[(order.index(i) + offset) % size] for offset in range(size)] for i in range(size)]
        self.size = size
        row = jnp.array(around, jnp.int32)[lax.axis_index("dp")]
        zero = jnp.zeros((), jnp.int32)
        self.around = [lax.select(lax.lt(row[k], zero), row[k] + size, row[k]) for k in range(size)]
        self.up = [(order[k], order[(k + 1) % size]) for k in range(size)]
        self.down = [(order[(k + 1) % size], order[k]) for k in range(size)]

    def index(self, offset, scale=1):
        return self.around[offset % self.size] * scale

    def gather(self, value, mid):
        half = self.size // 2
        out = jnp.zeros((self.size,) + value.shape, value.dtype)

        def put(out, piece, offset, start=0):
            spot = (self.index(offset), start) + (0,) * (value.ndim - 1)
            return lax.dynamic_update_slice(out, piece[None], spot, allow_negative_indices=False)

        out = put(out, value, 0)
        ahead, back = value, value
        for step in range(1, half):
            ahead, back = yield [(ahead, "dp", self.up), (back, "dp", self.down)]
            out = put(put(out, ahead, -step), back, step)
        if mid is None:
            (last,) = yield [(ahead, "dp", self.up)]
            return put(out, last, half)
        first, second = yield [(ahead[:mid], "dp", self.up), (back[mid:], "dp", self.down)]
        return put(put(out, first, half), second, half, mid)

    def part(self, array, axis, size=None):
        if size is None:
            return lambda offset: lax.dynamic_index_in_dim(
                array, self.index(offset), axis, keepdims=False, allow_negative_indices=False
            )
        return lambda offset: lax.dynamic_slice_in_dim(
            array, self.index(offset, size), size, axis, allow_negative_indices=False
        )

    def scatter(self, take, mid):
        half = self.size // 2
        far = take(half)
        kind = far.dtype
        if mid is None:
            (up,) = yield [(far, "dp", self.up)]
            down = None
        else:
            up, down = yield [(far[:mid], "dp", self.up), (far[mid:], "dp", self.down)]
        for step in range(half - 1, 0, -1):
            ahead, back = take(step).astype(F32), take(-step).astype(F32)
            if mid is None or step < half - 1:
                ahead = ahead + up
                back = back if down is None else back + down
            else:
                ahead = jnp.concatenate([ahead[:mid] + up, ahead[mid:]])
                back = jnp.concatenate([back[:mid], back[mid:] + down])
            up, down = yield [(ahead.astype(kind), "dp", self.up), (back.astype(kind), "dp", self.down)]
        return take(0).astype(F32) + up.astype(F32) + down.astype(F32)


def once(sends, take):
    def steps():
        take((yield sends))

    return Flow(steps())


SIDE_BIT = 2


def plane_classes():
    planes = range(lax.axis_size("dp") // 2)
    kept = [m for m in planes if m & 1 == 0]
    passed = [m for m in planes if m & 1 == 1]
    return {0: [0], 1: [1], 2: [m for m in passed if m != 1], 3: [m for m in kept if m]}


class Spread:
    def __init__(self, mine, other):
        self.mine, self.other = mine, other
        self.pieces = {0: mine}

    def move(self, moves):
        def take(arrived):
            for (_, _, _, number), piece in zip(moves, arrived):
                self.pieces[number] = piece

        return once([swap(value, "dp", offset << 1 | bit) for value, offset, bit, _ in moves], take)

    def cross(self):
        group = plane_classes()[3]
        return self.move([(self.other if m & SIDE_BIT else self.mine, m, 0, m << 1) for m in group])

    def near(self, key):
        group = plane_classes()[key]
        return self.move([(self.pieces[m << 1], 1, 0, (m ^ 1) << 1) for m in group])

    def y(self, key):
        group = plane_classes()[key]
        return self.move([(self.pieces[m << 1], 0, 1, m << 1 | 1) for m in group])

    def value(self):
        return [self.pieces[k] for k in range(lax.axis_size("dp"))]


class Reduce:
    def __init__(self, rows):
        self.rows = rows
        self.parts = {}
        self.sums = [[], []]

    def part(self, offset):
        terms = [term.astype(F32) for term in self.parts[offset]]
        return functools.reduce(jnp.add, terms)

    def hold(self, offset, *terms):
        self.parts.setdefault(offset, []).extend(terms)

    def y(self, key):
        group = plane_classes()[key]

        def take(arrived):
            for offset, got in zip(group, arrived):
                self.hold(offset, self.rows(offset << 1), got)

        return once([swap(self.rows(offset << 1 | 1), "dp", 1) for offset in group], take)

    def near(self, key):
        group = plane_classes()[key]

        def take(arrived):
            for offset, got in zip(group, arrived):
                self.hold(offset ^ 1, got)

        return once([swap(self.part(offset).astype(BF16), "dp", 2) for offset in group], take)

    def cross(self):
        group = plane_classes()[3]

        def take(arrived):
            for offset, got in zip(group, arrived):
                self.sums[1 if offset & SIDE_BIT else 0].append(got)

        return once([swap(self.part(offset).astype(BF16), "dp", offset << 1) for offset in group], take)

    def value(self):
        return self.parts[0] + self.sums[0], self.sums[1]


def params(**more):
    return pltpu.CompilerParams(vmem_limit_bytes=VMEM_LIMIT, **more)


TRIO = 3


def cast_blocks(blocks, count):
    _, r, c = blocks.shape

    def body(x_ref, o_ref):
        o_ref[...] = x_ref[...].astype(BF16)

    spec = pl.BlockSpec((TRIO, r, c), lambda k: (k, 0, 0))
    return pl.pallas_call(
        body,
        grid=(count // TRIO,),
        in_specs=[spec],
        out_specs=spec,
        out_shape=jax.ShapeDtypeStruct((count, r, c), BF16),
        compiler_params=params(),
        cost_estimate=pl.CostEstimate(flops=0, bytes_accessed=6 * count * r * c, transcendentals=0),
    )(blocks)


def pack_units(parity, blocks, first, kind_blocks, early):
    _, r, c = blocks.shape
    h = c // 2
    full = kind_blocks // 2
    each = kind_blocks // TRIO
    u, v = early * c, (full - early) * c + h

    def body(s_ref, *refs):
        parts, outs = refs[:each], refs[each:]

        def tile(f):
            return parts[f // TRIO].at[f % TRIO]

        for turn in range(2):

            @pl.when(s_ref[0] == turn)
            def _():
                for k in range(2):
                    side = turn ^ k
                    for i in range(full):
                        value = tile(side * full + i)[...].astype(BF16)
                        if i < early:
                            outs[2 * k][:, i * c : (i + 1) * c] = value
                        else:
                            outs[2 * k + 1][:, (i - early) * c : (i - early + 1) * c] = value
                    rest = tile(2 * full)[:, side * h : (side + 1) * h]
                    outs[2 * k + 1][:, v - h :] = rest.astype(BF16)

    def part(i):
        return pl.BlockSpec((TRIO, r, c), lambda k, s: (first // TRIO + each * k + i, 0, 0))

    wide = pl.BlockSpec((None, r, u), lambda k, s: (k, 0, 0))
    slim = pl.BlockSpec((None, r, v), lambda k, s: (k, 0, 0))
    shapes = [jax.ShapeDtypeStruct((3, r, u), BF16), jax.ShapeDtypeStruct((3, r, v), BF16)]
    return pl.pallas_call(
        body,
        grid_spec=pltpu.PrefetchScalarGridSpec(
            num_scalar_prefetch=1,
            grid=(3,),
            in_specs=[part(i) for i in range(each)],
            out_specs=[wide, slim, wide, slim],
        ),
        out_shape=shapes + shapes,
        compiler_params=params(),
        cost_estimate=pl.CostEstimate(flops=0, bytes_accessed=18 * kind_blocks * r * c, transcendentals=0),
    )(parity, *([blocks] * each))


def block_project(rows, blocks):
    t = rows.shape[0]
    count, d, c = blocks.shape

    def body(x_ref, w_ref, o_ref):
        o_ref[...] = mm(x_ref[...], w_ref[...], NN).astype(BF16)

    return pl.pallas_call(
        body,
        grid=(count,),
        in_specs=[
            pl.BlockSpec((t, d), lambda b: (0, 0)),
            pl.BlockSpec((None, d, c), lambda b: (b, 0, 0)),
        ],
        out_specs=pl.BlockSpec((None, t, c), lambda b: (b, 0, 0)),
        out_shape=jax.ShapeDtypeStruct((count, t, c), BF16),
        compiler_params=params(),
        cost_estimate=pl.CostEstimate(
            flops=2 * count * t * d * c, bytes_accessed=2 * (t * d + count * (d * c + t * c)), transcendentals=0
        ),
    )(rows, blocks)


def block_back(cols, blocks):
    count, t, c = cols.shape
    d = blocks.shape[1]
    half = t // 2

    def body(x_ref, w_ref, o_ref, p_ref, acc_ref):
        b = pl.program_id(0)

        @pl.when(b == 0)
        def _():
            acc_ref[...] = jnp.zeros_like(acc_ref)

        acc_ref[...] += mm(x_ref[...], w_ref[...], NT)

        @pl.when(b == count - 1)
        def _():
            o_ref[...] = acc_ref[:half, :].astype(BF16)
            p_ref[...] = acc_ref[half:, :].astype(BF16)

    result = pl.BlockSpec((half, d), lambda b: (0, 0))
    return pl.pallas_call(
        body,
        grid=(count,),
        in_specs=[
            pl.BlockSpec((None, t, c), lambda b: (b, 0, 0)),
            pl.BlockSpec((None, d, c), lambda b: (b, 0, 0)),
        ],
        out_specs=[result, result],
        out_shape=[jax.ShapeDtypeStruct((half, d), BF16)] * 2,
        scratch_shapes=[pltpu.VMEM((t, d), F32)],
        compiler_params=params(),
        cost_estimate=pl.CostEstimate(
            flops=2 * count * t * d * c, bytes_accessed=2 * (t * d + count * (d * c + t * c)), transcendentals=0
        ),
    )(cols, blocks)


def block_outer(rows, cols, d):
    t = rows[0].shape[0]
    c = cols[0].shape[2]
    starts = [0]
    for col in cols:
        starts.append(starts[-1] + col.shape[0])
    count = len(rows)
    total = starts[-1]

    def body(*refs):
        o_ref, t_ref = refs[2 * count :]
        b = pl.program_id(0)
        for k in range(count):

            @pl.when(b == starts[k])
            def _():
                t_ref[...] = refs[k][...].T

            @pl.when((b >= starts[k]) & (b < starts[k + 1]))
            def _():
                o_ref[...] = mm(t_ref[...], refs[count + k][...], NN).astype(BF16)

    def col_at(k):
        return pl.BlockSpec((None, t, c), lambda b: (jnp.clip(b - starts[k], 0, starts[k + 1] - starts[k] - 1), 0, 0))

    return pl.pallas_call(
        body,
        grid=(total,),
        in_specs=[pl.BlockSpec((t, d), lambda b: (0, 0))] * count + [col_at(k) for k in range(count)],
        out_specs=pl.BlockSpec((None, d, c), lambda b: (b, 0, 0)),
        out_shape=jax.ShapeDtypeStruct((total, d, c), BF16),
        scratch_shapes=[pltpu.VMEM((d, t), BF16)],
        compiler_params=params(),
        cost_estimate=pl.CostEstimate(
            flops=2 * total * t * d * c,
            bytes_accessed=2 * (count * t * d + total * (d * c + t * c)),
            transcendentals=0,
        ),
    )(*rows, *cols)


def in_group(local, width, head_shift):
    quarter = width // 4
    low = jnp.bitwise_and(local, quarter - 1)
    one = jnp.where(jnp.bitwise_and(local, quarter) != 0, 2 * quarter, 0)
    two = jnp.where(jnp.bitwise_and(local, 2 * quarter) != 0, quarter, 0)
    return jnp.bitwise_xor(low + one + two, head_shift)


def key_position(block, width, head_shift, shape, axis):
    local = lax.broadcasted_iota(jnp.int32, shape, axis)
    return block * width + in_group(local, width, head_shift)


def attend(place, queries, keys_values, query_pos, first_pos, scale, p):
    m, e = queries.shape
    n = keys_values.shape[0]
    step = 256

    def body(place_ref, q_ref, kv_ref, pos_ref, first_ref, low_ref, full_ref, sum_ref, acc_ref, tot_ref):
        j = pl.program_id(0)

        @pl.when(j == 0)
        def _():
            acc_ref[...] = jnp.zeros_like(acc_ref)
            tot_ref[...] = jnp.zeros_like(tot_ref)

        @pl.when(j <= place_ref[0])
        def _():
            key_pos = key_position(j, p, place_ref[1], (1, p), 1)
            for r in range(0, m, step):
                rows = pl.ds(r, step)
                raw = mm(q_ref[rows, :], kv_ref[:p, :], NT)
                soft = SOFT_CAP * jnp.tanh(raw * (scale / SOFT_CAP))
                seen = (key_pos >= first_ref[rows, :]) & (key_pos <= pos_ref[rows, :])
                terms = jnp.where(seen, jnp.exp(soft), 0.0)
                tot_ref[rows, :] += jnp.sum(terms, axis=1, keepdims=True)
                acc_ref[rows, :] += mm(terms.astype(BF16), kv_ref[p:, :], NN)

        @pl.when(j == n - 1)
        def _():
            total = tot_ref[...]
            mixed = acc_ref[...] / total
            full_ref[...] = mixed
            low_ref[...] = mixed.astype(BF16)
            sum_ref[...] = total

    whole = lambda shape: pl.BlockSpec(shape, lambda j, s: (0, 0))
    return pl.pallas_call(
        body,
        grid_spec=pltpu.PrefetchScalarGridSpec(
            num_scalar_prefetch=1,
            grid=(n,),
            in_specs=[
                whole((m, e)),
                pl.BlockSpec((None, 2 * p, e), lambda j, s: (jnp.minimum(j, s[0]), 0, 0)),
                whole((m, 1)),
                whole((m, 1)),
            ],
            out_specs=[whole((m, e)), whole((m, e)), whole((m, 1))],
            scratch_shapes=[pltpu.VMEM((m, e), F32), pltpu.VMEM((m, 1), F32)],
        ),
        out_shape=[
            jax.ShapeDtypeStruct((m, e), BF16),
            jax.ShapeDtypeStruct((m, e), F32),
            jax.ShapeDtypeStruct((m, 1), F32),
        ],
        compiler_params=params(),
        cost_estimate=pl.CostEstimate(
            flops=4 * m * n * p * e, bytes_accessed=4 * n * p * e, transcendentals=2 * m * n * p
        ),
    )(place, queries, keys_values, query_pos, first_pos)


def attend_back(place, queries, grads, keys_values, inverse, delta, query_pos, first_pos, scale, p):
    m, e = queries.shape
    n = keys_values.shape[0]
    step = 256

    def body(
        place_ref, q_ref, g_ref, kv_ref, inv_ref, delta_ref, pos_ref, first_ref, dq_ref, dkv_ref, acc_ref, dk_ref, dv_ref
    ):
        j = pl.program_id(0)

        @pl.when(j == 0)
        def _():
            acc_ref[...] = jnp.zeros_like(acc_ref)

        @pl.when(j <= place_ref[0])
        def _():
            key_pos = key_position(j, p, place_ref[1], (p, 1), 0)
            for r in range(0, m, step):
                rows = pl.ds(r, step)
                raw = mm(kv_ref[:p, :], q_ref[rows, :], NT)
                capped = jnp.tanh(raw * (scale / SOFT_CAP))
                seen = (key_pos >= first_ref[:, rows]) & (key_pos <= pos_ref[:, rows])
                probs = jnp.where(seen, jnp.exp(SOFT_CAP * capped), 0.0) * inv_ref[:, rows]
                grad_probs = mm(kv_ref[p:, :], g_ref[rows, :], NT)
                grad_raw = probs * (grad_probs - delta_ref[:, rows]) * (1.0 - capped * capped)
                grad_low = grad_raw.astype(BF16)
                value_part = mm(probs.astype(BF16), g_ref[rows, :], NN)
                key_part = mm(grad_low, q_ref[rows, :], NN)
                if r == 0:
                    dv_ref[...] = value_part
                    dk_ref[...] = key_part
                else:
                    dv_ref[...] += value_part
                    dk_ref[...] += key_part
                acc_ref[rows, :] += mm(grad_low, kv_ref[:p, :], TN)
            dkv_ref[0] = dk_ref[...].astype(BF16)
            dkv_ref[1] = dv_ref[...].astype(BF16)

        @pl.when(j > place_ref[0])
        def _():
            dkv_ref[...] = jnp.zeros_like(dkv_ref)

        @pl.when(j == n - 1)
        def _():
            dq_ref[...] = (acc_ref[...] * scale).astype(BF16)

    whole = lambda shape: pl.BlockSpec(shape, lambda j, s: (0, 0))
    return pl.pallas_call(
        body,
        grid_spec=pltpu.PrefetchScalarGridSpec(
            num_scalar_prefetch=1,
            grid=(n,),
            in_specs=[
                whole((m, e)),
                whole((m, e)),
                pl.BlockSpec((None, 2 * p, e), lambda j, s: (jnp.minimum(j, s[0]), 0, 0)),
                whole((1, m)),
                whole((1, m)),
                whole((1, m)),
                whole((1, m)),
            ],
            out_specs=[whole((m, e)), pl.BlockSpec((None, 2, p, e), lambda j, s: (j, 0, 0, 0))],
            scratch_shapes=[pltpu.VMEM((m, e), F32), pltpu.VMEM((p, e), F32), pltpu.VMEM((p, e), F32)],
        ),
        out_shape=[jax.ShapeDtypeStruct((m, e), BF16), jax.ShapeDtypeStruct((n, 2, p, e), BF16)],
        compiler_params=params(),
        cost_estimate=pl.CostEstimate(
            flops=10 * m * n * p * e, bytes_accessed=8 * n * p * e, transcendentals=2 * m * n * p
        ),
    )(place, queries, grads, keys_values, inverse, delta, query_pos, first_pos)


def gelu_pair(gate):
    outer = math.sqrt(2.0 / math.pi)
    square = gate * gate
    bent = jnp.tanh(outer * gate * (1.0 + 0.044715 * square))
    half = 0.5 * (1.0 + bent)
    slope = half + 0.5 * gate * (1.0 - bent * bent) * outer * (1.0 + 3.0 * 0.044715 * square)
    return gate * half, slope


def ffn_front(place, rows, cots, early, late):
    part_rows, d = rows[0].shape
    t = 2 * part_rows
    count = len(early)
    r = early[0].shape[1]
    u, v = early[0].shape[2], late[0].shape[2]
    tall = min(512, t)
    wide = d // 3
    cuts = [(k, min(256, u + v - k)) for k in range(0, u + v, 256)]

    def body(place_ref, x0, x1, y0, y1, *refs):
        early_refs, late_refs = refs[:count], refs[count : 2 * count]
        refs = refs[2 * count :]
        hs_ref, w_out = refs[:2]
        grad_refs = refs[2 : 2 + count], refs[2 + count : 2 + 2 * count]
        x, y, w, xt, yt, hs, row_sems, sems, out_sems, grad_sems = refs[2 + 2 * count :]
        row_copies = []
        for k, (source, target) in enumerate(((x0, x), (x1, x), (y0, y), (y1, y))):
            target = target.at[pl.ds((k % 2) * part_rows, part_rows), :]
            row_copies.append(pltpu.make_async_copy(source, target, row_sems.at[k]))
            row_copies[k].start()
        copies = []
        chunks = ((early_refs, pl.ds(0, u)), (late_refs, pl.ds(u, v)))

        def spot(k):
            return pl.ds(pl.multiple_of(jnp.bitwise_xor(place_ref[0], k) * r, 16) if count > 1 else 0, r)

        for k in range(count):
            for way, (sources, lanes) in enumerate(chunks):
                copy = pltpu.make_async_copy(sources[k], w.at[:, spot(k), lanes], sems.at[way, k])
                copy.start()
                copies.append(copy)
        for copy in row_copies:
            copy.wait()

        @pl.loop(0, d // 256)
        def _(k):
            cols = pl.ds(pl.multiple_of(k * 256, 256), 256)
            xt[cols, :] = x[:, cols].T
            yt[cols, :] = y[:, cols].T

        for copy in copies:
            copy.wait()
        kept = pltpu.make_async_copy(w, w_out, out_sems.at[0])
        kept.start()

        @pl.loop(0, t // tall)
        def _(i):
            part = pl.ds(pl.multiple_of(i * tall, tall), tall)
            for start, size in cuts:
                units = pl.ds(start, size)
                gate = mm(x[part, :], w[0, :, units], NN)
                up = mm(x[part, :], w[1, :, units], NN)
                grad = mm(y[part, :], w[2, :, units], NN)
                active, slope = gelu_pair(gate)
                hs[0, part, units] = (active * up).astype(BF16)
                hs[1, part, units] = (grad * up * slope).astype(BF16)
                hs[2, part, units] = (grad * active).astype(BF16)

        sides = pltpu.make_async_copy(hs, hs_ref, out_sems.at[1])
        sides.start()
        kept.wait()
        copies = []
        for kind, (left, right) in enumerate(((xt, 1), (xt, 2), (yt, 0))):

            @pl.loop(0, d // wide)
            def _(k):
                cols = pl.ds(pl.multiple_of(k * wide, wide), wide)
                w[kind, cols, :] = mm(left[cols, :], hs[right], NN).astype(BF16)

            for k in range(count):
                for way, (_, lanes) in enumerate(chunks):
                    target = grad_refs[way][k].at[kind]
                    copy = pltpu.make_async_copy(w.at[kind, spot(k), lanes], target, grad_sems.at[kind, way, k])
                    copy.start()
                    copies.append(copy)
        sides.wait()
        for copy in copies:
            copy.wait()

    apart = pl.BlockSpec(memory_space=pl.ANY)
    return pl.pallas_call(
        body,
        grid_spec=pltpu.PrefetchScalarGridSpec(
            num_scalar_prefetch=1,
            grid=(1,),
            in_specs=[apart] * (4 + 2 * count),
            out_specs=[apart] * (2 + 2 * count),
            scratch_shapes=[
                pltpu.VMEM((t, d), BF16),
                pltpu.VMEM((t, d), BF16),
                pltpu.VMEM((3, d, u + v), BF16),
                pltpu.VMEM((d, t), BF16),
                pltpu.VMEM((d, t), BF16),
                pltpu.VMEM((3, t, u + v), BF16),
                pltpu.SemaphoreType.DMA((4,)),
                pltpu.SemaphoreType.DMA((2, count)),
                pltpu.SemaphoreType.DMA((2,)),
                pltpu.SemaphoreType.DMA((3, 2, count)),
            ],
        ),
        out_shape=[
            jax.ShapeDtypeStruct((3, t, u + v), BF16),
            jax.ShapeDtypeStruct((3, d, u + v), BF16),
            *[jax.ShapeDtypeStruct((3, r, u), BF16)] * count,
            *[jax.ShapeDtypeStruct((3, r, v), BF16)] * count,
        ],
        compiler_params=params(),
        cost_estimate=pl.CostEstimate(
            flops=12 * t * d * (u + v), bytes_accessed=12 * d * (u + v) + 4 * t * d, transcendentals=t * (u + v)
        ),
    )(place, *rows, *cots, *early, *late)


def ffn_back(sides, blocks):
    _, t, u = sides.shape
    d = blocks.shape[1]
    wide = 256
    half = t // 2

    def body(s_ref, w_ref, *refs):
        for k in range(2):
            part = pl.ds(k * half, half)
            refs[k][...] = mm(s_ref[0, part, :], w_ref[2], NT).astype(BF16)
            refs[2 + k][...] = (mm(s_ref[1, part, :], w_ref[0], NT) + mm(s_ref[2, part, :], w_ref[1], NT)).astype(BF16)

    return pl.pallas_call(
        body,
        grid=(d // wide,),
        in_specs=[
            pl.BlockSpec((3, t, u), lambda k: (0, 0, 0), pipeline_mode=pl.Buffered(1)),
            pl.BlockSpec((3, wide, u), lambda k: (0, k, 0)),
        ],
        out_specs=[pl.BlockSpec((half, wide), lambda k: (0, k))] * 4,
        out_shape=[jax.ShapeDtypeStruct((half, d), BF16)] * 4,
        compiler_params=params(),
        cost_estimate=pl.CostEstimate(
            flops=6 * t * d * u, bytes_accessed=6 * d * u + 6 * t * u + 4 * t * d, transcendentals=0
        ),
    )(sides, blocks)


def gram_parts(m):
    h = m.shape[1] // 2
    high = m.astype(BF16)
    low = (m - high.astype(F32)).astype(BF16)
    mixed = mm(high, low, TN)
    gram = mm(high, high, TN) + mm(low, low, TN) + mixed + mixed.T
    return gram[:h, :h], gram[:h, h:], gram[h:, h:]


def ffn_moment(parity, own, other, momentum, first, blocks, places):
    total, r, c = momentum.shape
    terms = [*own, *other]
    counts = [len(group) for group in terms]
    u, v = own[0][0].shape[2], own[1][0].shape[2]
    early = u // c
    h = c // 2
    full = early + 1
    each = blocks // TRIO

    def body(s_ref, *refs):
        groups = []
        for count in counts:
            groups.append(refs[:count])
            refs = refs[count:]
        m_ref, wg_ref, nm_ref, gram_ref = refs
        j = pl.program_id(0)

        def total_of(group, start, size):
            lanes = pl.ds(start, size)
            return functools.reduce(jnp.add, [ref[:, lanes].astype(F32) for ref in group])

        @pl.when(j >= TRIO * each)
        def _():
            gram_ref[...] = jnp.zeros_like(gram_ref)

        for turn in range(each):
            for mine in range(2):

                @pl.when((j < TRIO * each) & (lax.rem(j, each) == turn) & (s_ref[0] == mine))
                def _():
                    for i in range(TRIO):
                        side, f = divmod(turn * TRIO + i, full)
                        if side == 2:
                            for k in range(2):
                                group = groups[1 if k == mine else 3]
                                wg_ref[i, :, k * h : (k + 1) * h] = total_of(group, c, h)
                        elif f < early:
                            wg_ref[i] = total_of(groups[0 if side == mine else 2], f * c, c)
                        else:
                            wg_ref[i] = total_of(groups[1 if side == mine else 3], 0, c)

        @pl.when(j < TRIO * each)
        def _():
            for i in range(TRIO):
                new = MUON_BETA * m_ref[i] + wg_ref[i]
                nm_ref[i] = new
                gram_ref[i, 0], gram_ref[i, 1], gram_ref[i, 2] = gram_parts(new)

    kind = lambda j, s: (jnp.minimum(j // each, 2), 0, 0)
    block = lambda j, s: (first // TRIO + jnp.minimum(j, TRIO * each - 1), 0, 0)
    arrays = [array for group in terms for array in group]
    return pl.pallas_call(
        body,
        grid_spec=pltpu.PrefetchScalarGridSpec(
            num_scalar_prefetch=1,
            grid=(places // TRIO,),
            in_specs=[pl.BlockSpec((None,) + array.shape[1:], kind) for array in arrays]
            + [pl.BlockSpec((TRIO, r, c), block)],
            out_specs=[
                pl.BlockSpec((TRIO, r, c), block),
                pl.BlockSpec((TRIO, r, c), block),
                pl.BlockSpec((TRIO, 3, h, h), lambda j, s: (j, 0, 0, 0)),
            ],
        ),
        out_shape=[
            jax.ShapeDtypeStruct((total, r, c), F32),
            jax.ShapeDtypeStruct((total, r, c), F32),
            jax.ShapeDtypeStruct((places, 3, h, h), F32),
        ],
        compiler_params=params(),
        cost_estimate=pl.CostEstimate(
            flops=6 * 3 * blocks * r * c * c, bytes_accessed=16 * 3 * blocks * r * c, transcendentals=0
        ),
    )(parity, *arrays, momentum)


def attn_moment(grads, pairs, momentum, weight_grads, new_momentum):
    count, r, c = grads.shape
    h = c // 2

    def body(s_ref, g_ref, m_ref, wg_in, nm_in, wg_ref, nm_ref, gram_ref):
        for i in range(2):
            new = MUON_BETA * m_ref[i] + g_ref[i]
            wg_ref[i] = g_ref[i]
            nm_ref[i] = new
            gram_ref[i, 0], gram_ref[i, 1], gram_ref[i, 2] = gram_parts(new)

    block = pl.BlockSpec((2, r, c), lambda j, s: (s[j], 0, 0))
    apart = pl.BlockSpec(memory_space=pl.ANY)
    return pl.pallas_call(
        body,
        grid_spec=pltpu.PrefetchScalarGridSpec(
            num_scalar_prefetch=1,
            grid=(count // 2,),
            in_specs=[pl.BlockSpec((2, r, c), lambda j, s: (j, 0, 0)), block, apart, apart],
            out_specs=[block, block, pl.BlockSpec((2, 3, h, h), lambda j, s: (j, 0, 0, 0))],
        ),
        out_shape=[
            jax.ShapeDtypeStruct(momentum.shape, F32),
            jax.ShapeDtypeStruct(momentum.shape, F32),
            jax.ShapeDtypeStruct((count, 3, h, h), F32),
        ],
        input_output_aliases={3: 0, 4: 1},
        compiler_params=params(),
        cost_estimate=pl.CostEstimate(
            flops=6 * count * r * c * c, bytes_accessed=16 * count * r * c, transcendentals=0
        ),
    )(jnp.array(pairs, jnp.int32), grads, momentum, weight_grads, new_momentum)


def renew(weights, momentum, factors, spots, updated):
    _, r, c = weights.shape
    h = c // 2
    steps = len(spots)
    table = jnp.array([spot for spot, _ in spots] + [f for _, places in spots for f in places], jnp.int32)

    def body(s_ref, w_ref, m_ref, *refs):
        factor_refs, o_ref = refs[:TRIO], refs[-1]
        for i in range(TRIO):
            left = m_ref[i, :, :h].astype(BF16)
            right = m_ref[i, :, h:].astype(BF16)
            first, off, last = factor_refs[i][0], factor_refs[i][1], factor_refs[i][2]
            start = mm(left, first, NN) + mm(right, off, NT)
            rest = mm(left, off, NN) + mm(right, last, NN)
            keep = 1.0 - MUON_RATE * MUON_DECAY
            o_ref[i, :, :h] = w_ref[i, :, :h] * keep - MUON_RATE * start
            o_ref[i, :, h:] = w_ref[i, :, h:] * keep - MUON_RATE * rest

    block = pl.BlockSpec((TRIO, r, c), lambda j, s: (s[j], 0, 0))

    def factor_at(i):
        return pl.BlockSpec((None, 3, h, h), lambda j, s: (s[steps + TRIO * j + i], 0, 0, 0))

    apart = [pl.BlockSpec(memory_space=pl.ANY)] * len(updated)
    return pl.pallas_call(
        body,
        grid_spec=pltpu.PrefetchScalarGridSpec(
            num_scalar_prefetch=1,
            grid=(steps,),
            in_specs=[block, block] + [factor_at(i) for i in range(TRIO)] + apart,
            out_specs=block,
        ),
        out_shape=jax.ShapeDtypeStruct(weights.shape, F32),
        input_output_aliases={3 + TRIO: 0} if updated else {},
        compiler_params=params(),
        cost_estimate=pl.CostEstimate(
            flops=2 * TRIO * steps * r * c * c, bytes_accessed=12 * TRIO * steps * r * c, transcendentals=0
        ),
    )(table, weights, momentum, *([factors] * TRIO), *updated)


def top(spec, a, b):
    return jnp.einsum(spec, a, b, precision=NEWTON_PRECISION)


def newton_factor(grams, growth):
    size = grams.shape[-1]
    eye = jnp.eye(size, dtype=F32)
    norm = jnp.sqrt(jnp.sum(grams * eye, axis=(1, 2), keepdims=True))
    inverse = 1.0 / (norm + 1e-07)
    gram = grams * (inverse * inverse)
    factor = None
    for sweep in range(NEWTON_STEPS):
        square = top("bij,bjk->bik", gram, gram)
        poly = NEWTON_LINEAR * eye + NEWTON_SQUARE * gram + NEWTON_CUBIC * square
        factor = poly if sweep == 0 else top("bij,bjk->bik", factor, poly)
        if sweep < NEWTON_STEPS - 1:
            gram = top("bij,bjk->bik", top("bij,bjk->bik", gram, poly), poly)
    return factor * (growth * inverse)


def fold(squares):
    h = squares.shape[1] // 2
    return jnp.stack([squares[:, :h, :h], squares[:, :h, h:], squares[:, h:, h:]], axis=1)


def unfold(parts):
    first, off, last = parts[:, 0], parts[:, 1], parts[:, 2]
    upper = jnp.concatenate([first, off], axis=2)
    lower = jnp.concatenate([jnp.swapaxes(off, 1, 2), last], axis=2)
    return jnp.concatenate([upper, lower], axis=1)


def gram_sums(ring, parts, cap):
    h = parts.shape[2]
    parts = parts.reshape(-1, h, h)
    rows = 3 * cap
    mine = yield from ring.scatter(ring.part(parts, 0, rows), rows // 2 if cap > 1 else None)
    return unfold(mine.reshape(cap, 3, h, h))


def all_factors(ring, factors):
    cap, c, _ = factors.shape
    parts = fold(factors.astype(BF16)).reshape(3 * cap, c // 2, c // 2)
    parts = yield from ring.gather(parts, 3 * cap // 2 if cap > 1 else None)
    return parts.reshape(ring.size * cap, 3, c // 2, c // 2)


def on_device(block_in, cotangent, seq_ids, weights, momentum, gains, gain_first, gain_second):
    tok_rows, model_width = block_in.shape
    rows_dp, group_blocks, head_dim = weights.shape
    head_count = lax.axis_size("head")
    data_count = lax.axis_size("dp")
    group_rows = tok_rows * head_count
    key_heads = KV // head_count
    query_heads = H // head_count
    ffn_blocks = FF // (head_dim * head_count)
    out_mark = query_heads + 2 * key_heads
    gate_mark = out_mark + query_heads
    half_dim = head_dim // 2
    full = ffn_blocks // 2
    scale = head_dim ** (-0.5)
    growth = math.sqrt(max(1.0, model_width / head_dim))
    data_index = lax.axis_index("dp")
    head_index = lax.axis_index("head")
    parity = (data_index >> 2) & 1
    ring = Ring()

    weights = jnp.transpose(weights, (1, 0, 2))
    momentum = jnp.transpose(momentum, (1, 0, 2))
    attn_low = cast_blocks(weights, gate_mark)
    inputs = block_in.astype(F32)
    normed_one, norm_one_back = jax.vjp(rms_scale, inputs, gains[0])
    ids_column = jnp.pad(seq_ids.astype(BF16)[:, None], ((0, 0), (0, 127)))

    early = full - 1
    mine_early, mine_late, other_early, other_late = pack_units(
        jnp.reshape(parity, (1,)), weights, gate_mark, ffn_blocks, early
    )
    spread = [Spread(mine_early, other_early), Spread(mine_late, other_late)]

    group_in = run(head_gather(jnp.concatenate([normed_one.astype(BF16), ids_column], axis=1)))
    qkv_parts = run(ring.gather(attn_low[:out_mark], out_mark // 2))
    qkv_blocks = jnp.transpose(qkv_parts, (1, 0, 2, 3)).reshape(out_mark, model_width, head_dim)
    cot_flow = Flow(wide_gather(cotangent))
    group_in, qkv_blocks, attn_low = stage(
        [spread[0].near(0), spread[0].y(0)], [group_in, qkv_blocks, attn_low], idle=[cot_flow]
    )
    projected = block_project(group_in, qkv_blocks)
    queries = projected[:query_heads].reshape(query_heads * group_rows, head_dim)
    group_ids = group_in[:, model_width]
    kv_rows = 2 * key_heads * group_rows
    out_rows = query_heads * rows_dp
    id_rows = group_rows // head_dim
    packed = jnp.concatenate(
        [
            projected[query_heads:].reshape(kv_rows, head_dim),
            attn_low[out_mark:].reshape(out_rows, head_dim),
            jnp.pad(group_ids.reshape(id_rows, head_dim), ((0, 16 - id_rows), (0, 0))),
        ],
        axis=0,
    )
    keys_values = run(ring.gather(packed, packed.shape[0] // 32 * 16))
    out_blocks = keys_values[:, kv_rows : kv_rows + out_rows].reshape(data_count, query_heads, rows_dp, head_dim)
    out_blocks = jnp.transpose(out_blocks, (1, 0, 2, 3)).reshape(query_heads, model_width, head_dim)
    queries, keys_values, out_blocks = stage(
        [cot_flow, spread[0].y(1), spread[1].near(0)], [queries, keys_values, out_blocks]
    )
    all_ids = keys_values[:, kv_rows + out_rows : kv_rows + out_rows + id_rows].reshape(-1)

    local = in_group(jnp.arange(group_rows, dtype=jnp.int32), group_rows, head_index * tok_rows)
    query_pos = data_index * group_rows + local
    first_pos = jnp.sum((all_ids[None, :] < group_ids[:, None]).astype(jnp.int32), axis=1)
    query_pos = jnp.tile(query_pos, query_heads)
    first_pos = jnp.tile(first_pos, query_heads)
    place = jnp.stack([data_index, head_index * tok_rows]).astype(jnp.int32)
    mixed_low, mixed_full, totals = attend(
        place, queries, keys_values, query_pos[:, None], first_pos[:, None], scale, group_rows
    )
    mixed_heads = mixed_low.reshape(query_heads, group_rows, head_dim)
    mixed_heads, mixed_full, totals, attn_part = stage(
        [spread[0].cross(), spread[1].y(0), spread[1].y(1), cot_flow],
        [mixed_heads, mixed_full, totals, block_back(mixed_heads, out_blocks)],
    )
    attn_flow = Flow(scatter_rows(*attn_part, HEAD_MOVES))
    attn_flow.advance([lax.ppermute(*send) for send in attn_flow.sends])
    stage([attn_flow, spread[0].near(3), spread[0].y(3), spread[1].cross()], idle=[cot_flow])
    residual = inputs + attn_flow.value
    normed_two, norm_two_back = jax.vjp(rms_scale, residual, gains[1])
    wide_flow = Flow(wide_gather(normed_two.astype(BF16)))
    stage([wide_flow, spread[0].y(2), spread[1].near(3), spread[1].y(3)], idle=[cot_flow])
    stage([wide_flow, spread[1].y(2), cot_flow])
    stage([wide_flow])
    finish(wide_flow, cot_flow)

    def whole_rows(pieces):
        if rows_dp % 16 == 0:
            return pieces
        out = jnp.zeros((3, data_count) + pieces[0].shape[1:], BF16)
        for k, piece in enumerate(pieces):
            out = lax.dynamic_update_index_in_dim(out, piece, data_index ^ k, 1)
        return [out.reshape(3, model_width, -1)]

    ffn_sides, ffn_full, *ffn_grads = ffn_front(
        place, wide_flow.value, cot_flow.value, whole_rows(spread[0].value()), whole_rows(spread[1].value())
    )

    def taker(pieces):
        if len(pieces) > 1:
            return lambda k: pieces[k]
        cut = pieces[0].reshape(3, data_count, rows_dp, pieces[0].shape[2])
        return lambda k: lax.dynamic_index_in_dim(cut, data_index ^ k, 1, keepdims=False)

    pieces = len(ffn_grads) // 2
    reduce = [Reduce(taker(ffn_grads[:pieces])), Reduce(taker(ffn_grads[pieces:]))]
    *down_part, dx_kept, dx_sent = stage([reduce[0].y(2)], ffn_back(ffn_sides, ffn_full))
    out_flow = Flow(scatter_rows(*down_part, WIDE_MOVES, 4))
    dx_flow = Flow(scatter_rows(dx_kept, dx_sent, WIDE_MOVES))
    dx_flow.advance([lax.ppermute(*send) for send in dx_flow.sends])
    stage([dx_flow, reduce[0].near(2), reduce[0].y(3), reduce[1].y(2)])
    stage([dx_flow, reduce[1].y(3), reduce[1].y(1), reduce[1].near(2), out_flow])
    grad_residual_norm, grad_gain_two = norm_two_back(dx_flow.value)
    grad_residual = cotangent.astype(F32) + grad_residual_norm
    grad_flow = Flow(head_gather(grad_residual.astype(BF16)))
    stage([grad_flow, reduce[1].cross(), reduce[0].y(1)])
    grad_flow.advance([lax.ppermute(*send) for send in grad_flow.sends])
    group_grad = grad_flow.value

    grad_heads = block_project(group_grad, out_blocks)
    grad_mixed = grad_heads.reshape(query_heads * group_rows, head_dim)
    delta = jnp.sum(grad_mixed.astype(F32) * mixed_full, axis=1)
    grad_queries, grad_keys_values = attend_back(
        place,
        queries,
        grad_mixed,
        keys_values,
        1.0 / totals.reshape(1, -1),
        delta[None, :],
        query_pos[None, :],
        first_pos[None, :],
        scale,
        group_rows,
    )
    late_near = reduce[1].near(1)
    group_grad, grad_queries, grad_keys_values = stage(
        [reduce[0].cross(), reduce[0].near(1), reduce[0].y(0), reduce[1].y(0)],
        [group_grad, grad_queries, grad_keys_values],
        idle=[late_near, out_flow],
    )
    grad_queries = grad_queries.reshape(query_heads, group_rows, head_dim)

    late = 2
    main = 3 * ffn_blocks - late
    cap = -(-main // data_count)
    places = -(-max(cap * data_count, 3 * ffn_blocks) // TRIO) * TRIO
    def weight_sums(outer):
        cut = outer.reshape(outer.shape[0], data_count, rows_dp, head_dim)
        return Flow(ring.scatter(ring.part(cut, 1), outer.shape[0] // 2 if outer.shape[0] > 2 else None))

    key_flow = Flow(ring.scatter(ring.part(grad_keys_values, 0), key_heads))
    (outer,) = stage(
        [key_flow, late_near, out_flow],
        [block_outer([group_in, group_grad], [grad_queries, mixed_heads], model_width)],
    )
    (own_early, other_early), (own_late, other_late) = (part.value() for part in reduce)
    first_flow = weight_sums(outer)
    weight_grads, new_momentum, grams = stage(
        [key_flow, first_flow],
        ffn_moment(
            jnp.reshape(parity, (1,)),
            [own_early, own_late],
            [other_early, other_late],
            momentum,
            gate_mark,
            ffn_blocks,
            places,
        ),
    )
    gram_flow = Flow(gram_sums(ring, grams, cap))
    stage([key_flow, first_flow, gram_flow])
    while key_flow.sends is not None:
        stage([key_flow, first_flow, gram_flow])
    key_value_sums = key_flow.value
    grad_keys = (key_value_sums[:key_heads] * scale).astype(BF16)
    grad_values = key_value_sums[key_heads:].astype(BF16)
    grad_keys_values = jnp.concatenate([grad_keys, grad_values], axis=0)
    (outer,) = stage([first_flow, gram_flow, out_flow], [block_outer([group_in], [grad_keys_values], model_width)])
    finish(first_flow)
    second_flow = weight_sums(outer)
    pairs = [k for k in range(gate_mark // 2) if not query_heads <= 2 * k < out_mark]
    grad_projected = jnp.concatenate([grad_queries, grad_keys_values], axis=0)
    *attn_dx, weight_grads, new_momentum, first_grams = stage(
        [second_flow, gram_flow],
        [
            *block_back(grad_projected, qkv_blocks),
            *attn_moment(first_flow.value, pairs, momentum, weight_grads, new_momentum),
        ],
    )
    last_flow = Flow(scatter_rows(*attn_dx, HEAD_MOVES))
    finish(gram_flow)
    gram_value = gram_flow.value
    while second_flow.sends is not None:
        (gram_value,) = stage([second_flow, last_flow, out_flow], [gram_value])
    finish(last_flow, out_flow)
    block_out = (residual + out_flow.value).astype(BF16)
    grad_input_norm, grad_gain_one = norm_one_back(last_flow.value)
    grad_input = grad_residual + grad_input_norm
    gain_flow = Flow(total_sum(jnp.stack([grad_gain_one, grad_gain_two])))
    weight_grads, new_momentum, second_grams = attn_moment(
        second_flow.value, list(range(query_heads // 2, out_mark // 2)), momentum, weight_grads, new_momentum
    )
    late_count = gate_mark + late
    late_cap = -(-late_count // data_count)
    late_grams = jnp.concatenate([first_grams, second_grams, grams[main : main + late]], axis=0)
    late_grams = jnp.pad(late_grams, ((0, late_cap * data_count - late_count), (0, 0), (0, 0), (0, 0)))
    late_gram_flow = Flow(gram_sums(ring, late_grams, late_cap))
    (gram_value,) = stage([late_gram_flow, gain_flow], [gram_value])
    (factors,) = stage([late_gram_flow, gain_flow], [newton_factor(gram_value, growth)])
    factor_flow = Flow(all_factors(ring, factors))
    while late_gram_flow.sends is not None:
        stage([late_gram_flow, factor_flow, gain_flow])
    (late_factors,) = stage([factor_flow, gain_flow], [newton_factor(late_gram_flow.value, growth)])
    late_factor_flow = Flow(all_factors(ring, late_factors))
    while factor_flow.sends is not None:
        stage([factor_flow, late_factor_flow, gain_flow])
    factors = factor_flow.value

    threes = main // TRIO
    early_spots = [(gate_mark // TRIO + k, [TRIO * k + i for i in range(TRIO)]) for k in range(threes)]
    new_weights = []
    for k in range(0, threes, 3):
        new_weights = stage(
            [late_factor_flow, gain_flow],
            [renew(weights, new_momentum, factors, early_spots[k : k + 3], new_weights)],
        )

    finish(late_factor_flow, gain_flow)
    gain_grads = gain_flow.value
    rest = jnp.concatenate([late_factor_flow.value[:late_count], factors[TRIO * threes : main]], axis=0)
    blocks_of = [2 * pair + i for pair in pairs for i in range(2)] + list(range(query_heads, out_mark))
    blocks_of += [gate_mark + main + k for k in range(late)] + [gate_mark + k for k in range(TRIO * threes, main)]
    late_spots = [
        (spot, [blocks_of.index(TRIO * spot + i) for i in range(TRIO)])
        for spot in sorted({block // TRIO for block in blocks_of})
    ]
    new_weights = renew(weights, new_momentum, rest, late_spots, new_weights)

    new_gain_first = BETA_ONE * gain_first + (1.0 - BETA_ONE) * gain_grads
    new_gain_second = BETA_TWO * gain_second + (1.0 - BETA_TWO) * gain_grads * gain_grads
    first_hat = new_gain_first / (1.0 - BETA_ONE**UPDATE_STEP)
    second_hat = new_gain_second / (1.0 - BETA_TWO**UPDATE_STEP)
    new_gains = gains - ADAM_RATE * first_hat / (jnp.sqrt(second_hat) + ADAM_EPS)
    back = lambda array: jnp.transpose(array, (1, 0, 2))
    return (
        block_out,
        grad_input,
        back(weight_grads),
        back(new_momentum),
        back(new_weights),
        gain_grads,
        new_gain_first,
        new_gain_second,
        new_gains,
    )


def solution(mesh):
    return jax.shard_map(
        on_device,
        mesh=mesh,
        in_specs=(
            P(("dp", "head"), None),
            P(("dp", "head"), None),
            P(("dp", "head")),
            P("dp", "head", None),
            P("dp", "head", None),
            P(),
            P(),
            P(),
        ),
        out_specs=(
            P(("dp", "head"), None),
            P(("dp", "head"), None),
            P("dp", "head", None),
            P("dp", "head", None),
            P("dp", "head", None),
            P(),
            P(),
            P(),
            P(),
        ),
        check_vma=False,
    )
```

```python
import functools
import math

import jax
import jax.numpy as jnp
from jax import lax
from jax.experimental import pallas as pl
from jax.experimental.pallas import tpu as pltpu
from jax.sharding import PartitionSpec as P

H = 8
KV = 4
FF = 9216
NEWTON_STEPS = 5
UPDATE_STEP = 10

NORM_EPS = 1e-06
SOFT_CAP = 50.0
MUON_RATE = 0.2
MUON_DECAY = 0.01
MUON_BETA = 0.95
ADAM_RATE = 0.3
BETA_ONE = 0.9
BETA_TWO = 0.95
ADAM_EPS = 1e-08
NEWTON_LINEAR = 3.4445
NEWTON_SQUARE = -4.775
NEWTON_CUBIC = 2.0315
NEWTON_PRECISION = lax.Precision.HIGH

BF16 = jnp.bfloat16
F32 = jnp.float32
VMEM_LIMIT = 62 * 1024 * 1024
NN = (((1,), (0,)), ((), ()))
NT = (((1,), (1,)), ((), ()))
TN = (((0,), (0,)), ((), ()))


def mm(a, b, dims):
    return lax.dot_general(a, b, dims, preferred_element_type=F32)


def rms_scale(rows, gain):
    inverse = lax.rsqrt(jnp.mean(rows * rows, axis=-1, keepdims=True) + NORM_EPS)
    return rows * inverse * gain


class Flow:
    def __init__(self, steps):
        self.steps = steps
        self.value = None
        self.sends = None
        self.advance(None)

    def advance(self, arrived):
        try:
            self.sends = self.steps.send(arrived)
        except StopIteration as stop:
            self.sends = None
            self.value = stop.value


def stage(flows, extra=(), idle=()):
    flows = [flow for flow in flows if flow.sends is not None]
    idle = [flow for flow in idle if flow.sends is not None and flow not in flows]
    arrived = [[lax.ppermute(*send) for send in flow.sends] for flow in flows]
    held = [[send[0] for send in flow.sends] for flow in idle]
    arrived, held, extra = lax.optimization_barrier((arrived, held, list(extra)))
    for flow, got in zip(flows, arrived):
        flow.advance(got)
    for flow, kept in zip(idle, held):
        flow.sends = [(value,) + send[1:] for value, send in zip(kept, flow.sends)]
    return extra


def run(steps):
    flow = Flow(steps)
    while flow.sends is not None:
        flow.advance([lax.ppermute(*send) for send in flow.sends])
    return flow.value


def finish(*flows):
    while any(flow.sends is not None for flow in flows):
        stage(flows)


def swap(value, axis, mask):
    size = lax.axis_size(axis)
    return (value, axis, [(i, i ^ mask) for i in range(size)])


def head_gather(rows):
    (other,) = yield [swap(rows, "head", 2)]
    pair = jnp.concatenate([rows, other], axis=0)
    (other,) = yield [swap(pair, "head", 1)]
    return jnp.concatenate([pair, other], axis=0)


def wide_gather(rows):
    (other,) = yield [swap(rows, "dp", 4)]
    both = jnp.concatenate([rows, other], axis=0)
    (other,) = yield [swap(both, "head", 2)]
    pair = jnp.concatenate([both, other], axis=0)
    (other,) = yield [swap(pair, "head", 1)]
    return [pair, other]


def add_low(kept, other):
    return (kept.astype(F32) + other.astype(F32)).astype(BF16)


def scatter_rows(kept, sent, moves, cuts=1):
    for k, (axis, mask) in enumerate(moves):
        last = k == len(moves) - 1
        others = []
        for piece in jnp.split(sent, cuts if last else 1):
            others += yield [swap(piece, axis, mask)]
        other = jnp.concatenate(others, axis=0) if len(others) > 1 else others[0]
        part = kept.astype(F32) + other.astype(F32)
        if not last:
            half = part.shape[0] // 2
            kept, sent = part[:half], part[half:].astype(BF16)
    return part


HEAD_MOVES = (("head", 1), ("head", 2))
WIDE_MOVES = (("head", 1), ("head", 2), ("dp", 4))


def total_sum(value):
    for axis in ("head", "dp"):
        mask = 1
        while mask < lax.axis_size(axis):
            (other,) = yield [swap(value, axis, mask)]
            value = value + other
            mask *= 2
    return value


class Ring:
    def __init__(self):
        size = lax.axis_size("dp")
        order = list(range(0, size, 2)) + list(range(size - 1, 0, -2))
        around = [[order[(order.index(i) + offset) % size] for offset in range(size)] for i in range(size)]
        self.size = size
        row = jnp.array(around, jnp.int32)[lax.axis_index("dp")]
        zero = jnp.zeros((), jnp.int32)
        self.around = [lax.select(lax.lt(row[k], zero), row[k] + size, row[k]) for k in range(size)]
        self.up = [(order[k], order[(k + 1) % size]) for k in range(size)]
        self.down = [(order[(k + 1) % size], order[k]) for k in range(size)]

    def index(self, offset, scale=1):
        return self.around[offset % self.size] * scale

    def gather(self, value, mid):
        half = self.size // 2
        out = jnp.zeros((self.size,) + value.shape, value.dtype)

        def put(out, piece, offset, start=0):
            spot = (self.index(offset), start) + (0,) * (value.ndim - 1)
            return lax.dynamic_update_slice(out, piece[None], spot, allow_negative_indices=False)

        out = put(out, value, 0)
        ahead, back = value, value
        for step in range(1, half):
            ahead, back = yield [(ahead, "dp", self.up), (back, "dp", self.down)]
            out = put(put(out, ahead, -step), back, step)
        if mid is None:
            (last,) = yield [(ahead, "dp", self.up)]
            return put(out, last, half)
        first, second = yield [(ahead[:mid], "dp", self.up), (back[mid:], "dp", self.down)]
        return put(put(out, first, half), second, half, mid)

    def part(self, array, axis, size=None):
        if size is None:
            return lambda offset: lax.dynamic_index_in_dim(
                array, self.index(offset), axis, keepdims=False, allow_negative_indices=False
            )
        return lambda offset: lax.dynamic_slice_in_dim(
            array, self.index(offset, size), size, axis, allow_negative_indices=False
        )

    def scatter(self, take, mid):
        half = self.size // 2
        far = take(half)
        kind = far.dtype
        if mid is None:
            (up,) = yield [(far, "dp", self.up)]
            down = None
        else:
            up, down = yield [(far[:mid], "dp", self.up), (far[mid:], "dp", self.down)]
        for step in range(half - 1, 0, -1):
            ahead, back = take(step).astype(F32), take(-step).astype(F32)
            if mid is None or step < half - 1:
                ahead = ahead + up
                back = back if down is None else back + down
            else:
                ahead = jnp.concatenate([ahead[:mid] + up, ahead[mid:]])
                back = jnp.concatenate([back[:mid], back[mid:] + down])
            up, down = yield [(ahead.astype(kind), "dp", self.up), (back.astype(kind), "dp", self.down)]
        return take(0).astype(F32) + up.astype(F32) + down.astype(F32)


def once(sends, take):
    def steps():
        take((yield sends))

    return Flow(steps())


SIDE_BIT = 2


def plane_classes():
    planes = range(lax.axis_size("dp") // 2)
    kept = [m for m in planes if m & 1 == 0]
    passed = [m for m in planes if m & 1 == 1]
    return {0: [0], 1: [1], 2: [m for m in passed if m != 1], 3: [m for m in kept if m]}


class Spread:
    def __init__(self, mine, other):
        self.mine, self.other = mine, other
        self.pieces = {0: mine}

    def move(self, moves):
        def take(arrived):
            for (_, _, _, number), piece in zip(moves, arrived):
                self.pieces[number] = piece

        return once([swap(value, "dp", offset << 1 | bit) for value, offset, bit, _ in moves], take)

    def cross(self):
        group = plane_classes()[3]
        return self.move([(self.other if m & SIDE_BIT else self.mine, m, 0, m << 1) for m in group])

    def near(self, key):
        group = plane_classes()[key]
        return self.move([(self.pieces[m << 1], 1, 0, (m ^ 1) << 1) for m in group])

    def y(self, key):
        group = plane_classes()[key]
        return self.move([(self.pieces[m << 1], 0, 1, m << 1 | 1) for m in group])

    def value(self):
        return [self.pieces[k] for k in range(lax.axis_size("dp"))]


class Reduce:
    def __init__(self, rows):
        self.rows = rows
        self.parts = {}
        self.sums = [[], []]

    def part(self, offset):
        terms = [term.astype(F32) for term in self.parts[offset]]
        return functools.reduce(jnp.add, terms)

    def hold(self, offset, *terms):
        self.parts.setdefault(offset, []).extend(terms)

    def y(self, key):
        group = plane_classes()[key]

        def take(arrived):
            for offset, got in zip(group, arrived):
                self.hold(offset, self.rows(offset << 1), got)

        return once([swap(self.rows(offset << 1 | 1), "dp", 1) for offset in group], take)

    def near(self, key):
        group = plane_classes()[key]

        def take(arrived):
            for offset, got in zip(group, arrived):
                self.hold(offset ^ 1, got)

        return once([swap(self.part(offset).astype(BF16), "dp", 2) for offset in group], take)

    def cross(self):
        group = plane_classes()[3]

        def take(arrived):
            for offset, got in zip(group, arrived):
                self.sums[1 if offset & SIDE_BIT else 0].append(got)

        return once([swap(self.part(offset).astype(BF16), "dp", offset << 1) for offset in group], take)

    def value(self):
        return self.parts[0] + self.sums[0], self.sums[1]


def params(**more):
    return pltpu.CompilerParams(vmem_limit_bytes=VMEM_LIMIT, **more)


TRIO = 3


def cast_blocks(blocks, count):
    _, r, c = blocks.shape

    def body(x_ref, o_ref):
        o_ref[...] = x_ref[...].astype(BF16)

    spec = pl.BlockSpec((TRIO, r, c), lambda k: (k, 0, 0))
    return pl.pallas_call(
        body,
        grid=(count // TRIO,),
        in_specs=[spec],
        out_specs=spec,
        out_shape=jax.ShapeDtypeStruct((count, r, c), BF16),
        compiler_params=params(),
        cost_estimate=pl.CostEstimate(flops=0, bytes_accessed=6 * count * r * c, transcendentals=0),
    )(blocks)


def pack_units(parity, blocks, first, kind_blocks, early):
    _, r, c = blocks.shape
    h = c // 2
    full = kind_blocks // 2
    each = kind_blocks // TRIO
    u, v = early * c, (full - early) * c + h

    def body(s_ref, *refs):
        parts, outs = refs[:each], refs[each:]

        def tile(f):
            return parts[f // TRIO].at[f % TRIO]

        for turn in range(2):

            @pl.when(s_ref[0] == turn)
            def _():
                for k in range(2):
                    side = turn ^ k
                    for i in range(full):
                        value = tile(side * full + i)[...].astype(BF16)
                        if i < early:
                            outs[2 * k][:, i * c : (i + 1) * c] = value
                        else:
                            outs[2 * k + 1][:, (i - early) * c : (i - early + 1) * c] = value
                    rest = tile(2 * full)[:, side * h : (side + 1) * h]
                    outs[2 * k + 1][:, v - h :] = rest.astype(BF16)

    def part(i):
        return pl.BlockSpec((TRIO, r, c), lambda k, s: (first // TRIO + each * k + i, 0, 0))

    wide = pl.BlockSpec((None, r, u), lambda k, s: (k, 0, 0))
    slim = pl.BlockSpec((None, r, v), lambda k, s: (k, 0, 0))
    shapes = [jax.ShapeDtypeStruct((3, r, u), BF16), jax.ShapeDtypeStruct((3, r, v), BF16)]
    return pl.pallas_call(
        body,
        grid_spec=pltpu.PrefetchScalarGridSpec(
            num_scalar_prefetch=1,
            grid=(3,),
            in_specs=[part(i) for i in range(each)],
            out_specs=[wide, slim, wide, slim],
        ),
        out_shape=shapes + shapes,
        compiler_params=params(),
        cost_estimate=pl.CostEstimate(flops=0, bytes_accessed=18 * kind_blocks * r * c, transcendentals=0),
    )(parity, *([blocks] * each))


def block_project(rows, blocks):
    t = rows.shape[0]
    count, d, c = blocks.shape

    def body(x_ref, w_ref, o_ref):
        o_ref[...] = mm(x_ref[...], w_ref[...], NN).astype(BF16)

    return pl.pallas_call(
        body,
        grid=(count,),
        in_specs=[
            pl.BlockSpec((t, d), lambda b: (0, 0)),
            pl.BlockSpec((None, d, c), lambda b: (b, 0, 0)),
        ],
        out_specs=pl.BlockSpec((None, t, c), lambda b: (b, 0, 0)),
        out_shape=jax.ShapeDtypeStruct((count, t, c), BF16),
        compiler_params=params(),
        cost_estimate=pl.CostEstimate(
            flops=2 * count * t * d * c, bytes_accessed=2 * (t * d + count * (d * c + t * c)), transcendentals=0
        ),
    )(rows, blocks)


def block_back(cols, blocks):
    count, t, c = cols.shape
    d = blocks.shape[1]
    half = t // 2

    def body(x_ref, w_ref, o_ref, p_ref, acc_ref):
        b = pl.program_id(0)

        @pl.when(b == 0)
        def _():
            acc_ref[...] = jnp.zeros_like(acc_ref)

        acc_ref[...] += mm(x_ref[...], w_ref[...], NT)

        @pl.when(b == count - 1)
        def _():
            o_ref[...] = acc_ref[:half, :].astype(BF16)
            p_ref[...] = acc_ref[half:, :].astype(BF16)

    result = pl.BlockSpec((half, d), lambda b: (0, 0))
    return pl.pallas_call(
        body,
        grid=(count,),
        in_specs=[
            pl.BlockSpec((None, t, c), lambda b: (b, 0, 0)),
            pl.BlockSpec((None, d, c), lambda b: (b, 0, 0)),
        ],
        out_specs=[result, result],
        out_shape=[jax.ShapeDtypeStruct((half, d), BF16)] * 2,
        scratch_shapes=[pltpu.VMEM((t, d), F32)],
        compiler_params=params(),
        cost_estimate=pl.CostEstimate(
            flops=2 * count * t * d * c, bytes_accessed=2 * (t * d + count * (d * c + t * c)), transcendentals=0
        ),
    )(cols, blocks)


def block_outer(rows, cols, d):
    t = rows[0].shape[0]
    c = cols[0].shape[2]
    starts = [0]
    for col in cols:
        starts.append(starts[-1] + col.shape[0])
    count = len(rows)
    total = starts[-1]

    def body(*refs):
        o_ref, t_ref = refs[2 * count :]
        b = pl.program_id(0)
        for k in range(count):

            @pl.when(b == starts[k])
            def _():
                t_ref[...] = refs[k][...].T

            @pl.when((b >= starts[k]) & (b < starts[k + 1]))
            def _():
                o_ref[...] = mm(t_ref[...], refs[count + k][...], NN).astype(BF16)

    def col_at(k):
        return pl.BlockSpec((None, t, c), lambda b: (jnp.clip(b - starts[k], 0, starts[k + 1] - starts[k] - 1), 0, 0))

    return pl.pallas_call(
        body,
        grid=(total,),
        in_specs=[pl.BlockSpec((t, d), lambda b: (0, 0))] * count + [col_at(k) for k in range(count)],
        out_specs=pl.BlockSpec((None, d, c), lambda b: (b, 0, 0)),
        out_shape=jax.ShapeDtypeStruct((total, d, c), BF16),
        scratch_shapes=[pltpu.VMEM((d, t), BF16)],
        compiler_params=params(),
        cost_estimate=pl.CostEstimate(
            flops=2 * total * t * d * c,
            bytes_accessed=2 * (count * t * d + total * (d * c + t * c)),
            transcendentals=0,
        ),
    )(*rows, *cols)


def in_group(local, width, head_shift):
    quarter = width // 4
    low = jnp.bitwise_and(local, quarter - 1)
    one = jnp.where(jnp.bitwise_and(local, quarter) != 0, 2 * quarter, 0)
    two = jnp.where(jnp.bitwise_and(local, 2 * quarter) != 0, quarter, 0)
    return jnp.bitwise_xor(low + one + two, head_shift)


def key_position(block, width, head_shift, shape, axis):
    local = lax.broadcasted_iota(jnp.int32, shape, axis)
    return block * width + in_group(local, width, head_shift)


def attend(place, queries, keys_values, query_pos, first_pos, scale, p):
    m, e = queries.shape
    n = keys_values.shape[0]
    step = 256

    def body(place_ref, q_ref, kv_ref, pos_ref, first_ref, low_ref, full_ref, sum_ref, acc_ref, tot_ref):
        j = pl.program_id(0)

        @pl.when(j == 0)
        def _():
            acc_ref[...] = jnp.zeros_like(acc_ref)
            tot_ref[...] = jnp.zeros_like(tot_ref)

        @pl.when(j <= place_ref[0])
        def _():
            key_pos = key_position(j, p, place_ref[1], (1, p), 1)
            for r in range(0, m, step):
                rows = pl.ds(r, step)
                raw = mm(q_ref[rows, :], kv_ref[:p, :], NT)
                soft = SOFT_CAP * jnp.tanh(raw * (scale / SOFT_CAP))
                seen = (key_pos >= first_ref[rows, :]) & (key_pos <= pos_ref[rows, :])
                terms = jnp.where(seen, jnp.exp(soft), 0.0)
                tot_ref[rows, :] += jnp.sum(terms, axis=1, keepdims=True)
                acc_ref[rows, :] += mm(terms.astype(BF16), kv_ref[p:, :], NN)

        @pl.when(j == n - 1)
        def _():
            total = tot_ref[...]
            mixed = acc_ref[...] / total
            full_ref[...] = mixed
            low_ref[...] = mixed.astype(BF16)
            sum_ref[...] = total

    whole = lambda shape: pl.BlockSpec(shape, lambda j, s: (0, 0))
    return pl.pallas_call(
        body,
        grid_spec=pltpu.PrefetchScalarGridSpec(
            num_scalar_prefetch=1,
            grid=(n,),
            in_specs=[
                whole((m, e)),
                pl.BlockSpec((None, 2 * p, e), lambda j, s: (jnp.minimum(j, s[0]), 0, 0)),
                whole((m, 1)),
                whole((m, 1)),
            ],
            out_specs=[whole((m, e)), whole((m, e)), whole((m, 1))],
            scratch_shapes=[pltpu.VMEM((m, e), F32), pltpu.VMEM((m, 1), F32)],
        ),
        out_shape=[
            jax.ShapeDtypeStruct((m, e), BF16),
            jax.ShapeDtypeStruct((m, e), F32),
            jax.ShapeDtypeStruct((m, 1), F32),
        ],
        compiler_params=params(),
        cost_estimate=pl.CostEstimate(
            flops=4 * m * n * p * e, bytes_accessed=4 * n * p * e, transcendentals=2 * m * n * p
        ),
    )(place, queries, keys_values, query_pos, first_pos)


def attend_back(place, queries, grads, keys_values, inverse, delta, query_pos, first_pos, scale, p):
    m, e = queries.shape
    n = keys_values.shape[0]
    step = 256

    def body(
        place_ref, q_ref, g_ref, kv_ref, inv_ref, delta_ref, pos_ref, first_ref, dq_ref, dkv_ref, acc_ref, dk_ref, dv_ref
    ):
        j = pl.program_id(0)

        @pl.when(j == 0)
        def _():
            acc_ref[...] = jnp.zeros_like(acc_ref)

        @pl.when(j <= place_ref[0])
        def _():
            key_pos = key_position(j, p, place_ref[1], (p, 1), 0)
            for r in range(0, m, step):
                rows = pl.ds(r, step)
                raw = mm(kv_ref[:p, :], q_ref[rows, :], NT)
                capped = jnp.tanh(raw * (scale / SOFT_CAP))
                seen = (key_pos >= first_ref[:, rows]) & (key_pos <= pos_ref[:, rows])
                probs = jnp.where(seen, jnp.exp(SOFT_CAP * capped), 0.0) * inv_ref[:, rows]
                grad_probs = mm(kv_ref[p:, :], g_ref[rows, :], NT)
                grad_raw = probs * (grad_probs - delta_ref[:, rows]) * (1.0 - capped * capped)
                grad_low = grad_raw.astype(BF16)
                value_part = mm(probs.astype(BF16), g_ref[rows, :], NN)
                key_part = mm(grad_low, q_ref[rows, :], NN)
                if r == 0:
                    dv_ref[...] = value_part
                    dk_ref[...] = key_part
                else:
                    dv_ref[...] += value_part
                    dk_ref[...] += key_part
                acc_ref[rows, :] += mm(grad_low, kv_ref[:p, :], TN)
            dkv_ref[0] = dk_ref[...].astype(BF16)
            dkv_ref[1] = dv_ref[...].astype(BF16)

        @pl.when(j > place_ref[0])
        def _():
            dkv_ref[...] = jnp.zeros_like(dkv_ref)

        @pl.when(j == n - 1)
        def _():
            dq_ref[...] = (acc_ref[...] * scale).astype(BF16)

    whole = lambda shape: pl.BlockSpec(shape, lambda j, s: (0, 0))
    return pl.pallas_call(
        body,
        grid_spec=pltpu.PrefetchScalarGridSpec(
            num_scalar_prefetch=1,
            grid=(n,),
            in_specs=[
                whole((m, e)),
                whole((m, e)),
                pl.BlockSpec((None, 2 * p, e), lambda j, s: (jnp.minimum(j, s[0]), 0, 0)),
                whole((1, m)),
                whole((1, m)),
                whole((1, m)),
                whole((1, m)),
            ],
            out_specs=[whole((m, e)), pl.BlockSpec((None, 2, p, e), lambda j, s: (j, 0, 0, 0))],
            scratch_shapes=[pltpu.VMEM((m, e), F32), pltpu.VMEM((p, e), F32), pltpu.VMEM((p, e), F32)],
        ),
        out_shape=[jax.ShapeDtypeStruct((m, e), BF16), jax.ShapeDtypeStruct((n, 2, p, e), BF16)],
        compiler_params=params(),
        cost_estimate=pl.CostEstimate(
            flops=10 * m * n * p * e, bytes_accessed=8 * n * p * e, transcendentals=2 * m * n * p
        ),
    )(place, queries, grads, keys_values, inverse, delta, query_pos, first_pos)


def gelu_pair(gate):
    outer = math.sqrt(2.0 / math.pi)
    square = gate * gate
    bent = jnp.tanh(outer * gate * (1.0 + 0.044715 * square))
    half = 0.5 * (1.0 + bent)
    slope = half + 0.5 * gate * (1.0 - bent * bent) * outer * (1.0 + 3.0 * 0.044715 * square)
    return gate * half, slope


def ffn_front(place, rows, cots, early, late):
    part_rows, d = rows[0].shape
    t = 2 * part_rows
    count = len(early)
    r = early[0].shape[1]
    u, v = early[0].shape[2], late[0].shape[2]
    tall = min(512, t)
    wide = d // 3
    cuts = [(k, min(256, u + v - k)) for k in range(0, u + v, 256)]

    def body(place_ref, x0, x1, y0, y1, *refs):
        early_refs, late_refs = refs[:count], refs[count : 2 * count]
        refs = refs[2 * count :]
        hs_ref, w_out = refs[:2]
        grad_refs = refs[2 : 2 + count], refs[2 + count : 2 + 2 * count]
        x, y, w, xt, yt, hs, row_sems, sems, out_sems, grad_sems = refs[2 + 2 * count :]
        row_copies = []
        for k, (source, target) in enumerate(((x0, x), (x1, x), (y0, y), (y1, y))):
            target = target.at[pl.ds((k % 2) * part_rows, part_rows), :]
            row_copies.append(pltpu.make_async_copy(source, target, row_sems.at[k]))
            row_copies[k].start()
        copies = []
        chunks = ((early_refs, pl.ds(0, u)), (late_refs, pl.ds(u, v)))

        def spot(k):
            return pl.ds(pl.multiple_of(jnp.bitwise_xor(place_ref[0], k) * r, 16) if count > 1 else 0, r)

        for k in range(count):
            for way, (sources, lanes) in enumerate(chunks):
                copy = pltpu.make_async_copy(sources[k], w.at[:, spot(k), lanes], sems.at[way, k])
                copy.start()
                copies.append(copy)
        for copy in row_copies:
            copy.wait()

        @pl.loop(0, d // 256)
        def _(k):
            cols = pl.ds(pl.multiple_of(k * 256, 256), 256)
            xt[cols, :] = x[:, cols].T
            yt[cols, :] = y[:, cols].T

        for copy in copies:
            copy.wait()
        kept = pltpu.make_async_copy(w, w_out, out_sems.at[0])
        kept.start()

        @pl.loop(0, t // tall)
        def _(i):
            part = pl.ds(pl.multiple_of(i * tall, tall), tall)
            for start, size in cuts:
                units = pl.ds(start, size)
                gate = mm(x[part, :], w[0, :, units], NN)
                up = mm(x[part, :], w[1, :, units], NN)
                grad = mm(y[part, :], w[2, :, units], NN)
                active, slope = gelu_pair(gate)
                hs[0, part, units] = (active * up).astype(BF16)
                hs[1, part, units] = (grad * up * slope).astype(BF16)
                hs[2, part, units] = (grad * active).astype(BF16)

        sides = pltpu.make_async_copy(hs, hs_ref, out_sems.at[1])
        sides.start()
        kept.wait()
        copies = []
        for kind, (left, right) in enumerate(((xt, 1), (xt, 2), (yt, 0))):

            @pl.loop(0, d // wide)
            def _(k):
                cols = pl.ds(pl.multiple_of(k * wide, wide), wide)
                w[kind, cols, :] = mm(left[cols, :], hs[right], NN).astype(BF16)

            for k in range(count):
                for way, (_, lanes) in enumerate(chunks):
                    target = grad_refs[way][k].at[kind]
                    copy = pltpu.make_async_copy(w.at[kind, spot(k), lanes], target, grad_sems.at[kind, way, k])
                    copy.start()
                    copies.append(copy)
        sides.wait()
        for copy in copies:
            copy.wait()

    apart = pl.BlockSpec(memory_space=pl.ANY)
    return pl.pallas_call(
        body,
        grid_spec=pltpu.PrefetchScalarGridSpec(
            num_scalar_prefetch=1,
            grid=(1,),
            in_specs=[apart] * (4 + 2 * count),
            out_specs=[apart] * (2 + 2 * count),
            scratch_shapes=[
                pltpu.VMEM((t, d), BF16),
                pltpu.VMEM((t, d), BF16),
                pltpu.VMEM((3, d, u + v), BF16),
                pltpu.VMEM((d, t), BF16),
                pltpu.VMEM((d, t), BF16),
                pltpu.VMEM((3, t, u + v), BF16),
                pltpu.SemaphoreType.DMA((4,)),
                pltpu.SemaphoreType.DMA((2, count)),
                pltpu.SemaphoreType.DMA((2,)),
                pltpu.SemaphoreType.DMA((3, 2, count)),
            ],
        ),
        out_shape=[
            jax.ShapeDtypeStruct((3, t, u + v), BF16),
            jax.ShapeDtypeStruct((3, d, u + v), BF16),
            *[jax.ShapeDtypeStruct((3, r, u), BF16)] * count,
            *[jax.ShapeDtypeStruct((3, r, v), BF16)] * count,
        ],
        compiler_params=params(),
        cost_estimate=pl.CostEstimate(
            flops=12 * t * d * (u + v), bytes_accessed=12 * d * (u + v) + 4 * t * d, transcendentals=t * (u + v)
        ),
    )(place, *rows, *cots, *early, *late)


def ffn_back(sides, blocks):
    _, t, u = sides.shape
    d = blocks.shape[1]
    wide = 256
    half = t // 2

    def body(s_ref, w_ref, *refs):
        for k in range(2):
            part = pl.ds(k * half, half)
            refs[k][...] = mm(s_ref[0, part, :], w_ref[2], NT).astype(BF16)
            refs[2 + k][...] = (mm(s_ref[1, part, :], w_ref[0], NT) + mm(s_ref[2, part, :], w_ref[1], NT)).astype(BF16)

    return pl.pallas_call(
        body,
        grid=(d // wide,),
        in_specs=[
            pl.BlockSpec((3, t, u), lambda k: (0, 0, 0), pipeline_mode=pl.Buffered(1)),
            pl.BlockSpec((3, wide, u), lambda k: (0, k, 0)),
        ],
        out_specs=[pl.BlockSpec((half, wide), lambda k: (0, k))] * 4,
        out_shape=[jax.ShapeDtypeStruct((half, d), BF16)] * 4,
        compiler_params=params(),
        cost_estimate=pl.CostEstimate(
            flops=6 * t * d * u, bytes_accessed=6 * d * u + 6 * t * u + 4 * t * d, transcendentals=0
        ),
    )(sides, blocks)


def gram_parts(m):
    h = m.shape[1] // 2
    high = m.astype(BF16)
    low = (m - high.astype(F32)).astype(BF16)
    mixed = mm(high, low, TN)
    gram = mm(high, high, TN) + mm(low, low, TN) + mixed + mixed.T
    return gram[:h, :h], gram[:h, h:], gram[h:, h:]


def ffn_moment(parity, own, other, momentum, first, blocks, places):
    total, r, c = momentum.shape
    terms = [*own, *other]
    counts = [len(group) for group in terms]
    u, v = own[0][0].shape[2], own[1][0].shape[2]
    early = u // c
    h = c // 2
    full = early + 1
    each = blocks // TRIO

    def body(s_ref, *refs):
        groups = []
        for count in counts:
            groups.append(refs[:count])
            refs = refs[count:]
        m_ref, wg_ref, nm_ref, gram_ref = refs
        j = pl.program_id(0)

        def total_of(group, start, size):
            lanes = pl.ds(start, size)
            return functools.reduce(jnp.add, [ref[:, lanes].astype(F32) for ref in group])

        @pl.when(j >= TRIO * each)
        def _():
            gram_ref[...] = jnp.zeros_like(gram_ref)

        for turn in range(each):
            for mine in range(2):

                @pl.when((j < TRIO * each) & (lax.rem(j, each) == turn) & (s_ref[0] == mine))
                def _():
                    for i in range(TRIO):
                        side, f = divmod(turn * TRIO + i, full)
                        if side == 2:
                            for k in range(2):
                                group = groups[1 if k == mine else 3]
                                wg_ref[i, :, k * h : (k + 1) * h] = total_of(group, c, h)
                        elif f < early:
                            wg_ref[i] = total_of(groups[0 if side == mine else 2], f * c, c)
                        else:
                            wg_ref[i] = total_of(groups[1 if side == mine else 3], 0, c)

        @pl.when(j < TRIO * each)
        def _():
            for i in range(TRIO):
                new = MUON_BETA * m_ref[i] + wg_ref[i]
                nm_ref[i] = new
                gram_ref[i, 0], gram_ref[i, 1], gram_ref[i, 2] = gram_parts(new)

    kind = lambda j, s: (jnp.minimum(j // each, 2), 0, 0)
    block = lambda j, s: (first // TRIO + jnp.minimum(j, TRIO * each - 1), 0, 0)
    arrays = [array for group in terms for array in group]
    return pl.pallas_call(
        body,
        grid_spec=pltpu.PrefetchScalarGridSpec(
            num_scalar_prefetch=1,
            grid=(places // TRIO,),
            in_specs=[pl.BlockSpec((None,) + array.shape[1:], kind) for array in arrays]
            + [pl.BlockSpec((TRIO, r, c), block)],
            out_specs=[
                pl.BlockSpec((TRIO, r, c), block),
                pl.BlockSpec((TRIO, r, c), block),
                pl.BlockSpec((TRIO, 3, h, h), lambda j, s: (j, 0, 0, 0)),
            ],
        ),
        out_shape=[
            jax.ShapeDtypeStruct((total, r, c), F32),
            jax.ShapeDtypeStruct((total, r, c), F32),
            jax.ShapeDtypeStruct((places, 3, h, h), F32),
        ],
        compiler_params=params(),
        cost_estimate=pl.CostEstimate(
            flops=6 * 3 * blocks * r * c * c, bytes_accessed=16 * 3 * blocks * r * c, transcendentals=0
        ),
    )(parity, *arrays, momentum)


def attn_moment(grads, pairs, momentum, weight_grads, new_momentum):
    count, r, c = grads.shape
    h = c // 2

    def body(s_ref, g_ref, m_ref, wg_in, nm_in, wg_ref, nm_ref, gram_ref):
        for i in range(2):
            new = MUON_BETA * m_ref[i] + g_ref[i]
            wg_ref[i] = g_ref[i]
            nm_ref[i] = new
            gram_ref[i, 0], gram_ref[i, 1], gram_ref[i, 2] = gram_parts(new)

    block = pl.BlockSpec((2, r, c), lambda j, s: (s[j], 0, 0))
    apart = pl.BlockSpec(memory_space=pl.ANY)
    return pl.pallas_call(
        body,
        grid_spec=pltpu.PrefetchScalarGridSpec(
            num_scalar_prefetch=1,
            grid=(count // 2,),
            in_specs=[pl.BlockSpec((2, r, c), lambda j, s: (j, 0, 0)), block, apart, apart],
            out_specs=[block, block, pl.BlockSpec((2, 3, h, h), lambda j, s: (j, 0, 0, 0))],
        ),
        out_shape=[
            jax.ShapeDtypeStruct(momentum.shape, F32),
            jax.ShapeDtypeStruct(momentum.shape, F32),
            jax.ShapeDtypeStruct((count, 3, h, h), F32),
        ],
        input_output_aliases={3: 0, 4: 1},
        compiler_params=params(),
        cost_estimate=pl.CostEstimate(
            flops=6 * count * r * c * c, bytes_accessed=16 * count * r * c, transcendentals=0
        ),
    )(jnp.array(pairs, jnp.int32), grads, momentum, weight_grads, new_momentum)


def renew(weights, momentum, factors, spots, updated):
    _, r, c = weights.shape
    h = c // 2
    steps = len(spots)
    table = jnp.array([spot for spot, _ in spots] + [f for _, places in spots for f in places], jnp.int32)

    def body(s_ref, w_ref, m_ref, *refs):
        factor_refs, o_ref = refs[:TRIO], refs[-1]
        for i in range(TRIO):
            left = m_ref[i, :, :h].astype(BF16)
            right = m_ref[i, :, h:].astype(BF16)
            first, off, last = factor_refs[i][0], factor_refs[i][1], factor_refs[i][2]
            start = mm(left, first, NN) + mm(right, off, NT)
            rest = mm(left, off, NN) + mm(right, last, NN)
            keep = 1.0 - MUON_RATE * MUON_DECAY
            o_ref[i, :, :h] = w_ref[i, :, :h] * keep - MUON_RATE * start
            o_ref[i, :, h:] = w_ref[i, :, h:] * keep - MUON_RATE * rest

    block = pl.BlockSpec((TRIO, r, c), lambda j, s: (s[j], 0, 0))

    def factor_at(i):
        return pl.BlockSpec((None, 3, h, h), lambda j, s: (s[steps + TRIO * j + i], 0, 0, 0))

    apart = [pl.BlockSpec(memory_space=pl.ANY)] * len(updated)
    return pl.pallas_call(
        body,
        grid_spec=pltpu.PrefetchScalarGridSpec(
            num_scalar_prefetch=1,
            grid=(steps,),
            in_specs=[block, block] + [factor_at(i) for i in range(TRIO)] + apart,
            out_specs=block,
        ),
        out_shape=jax.ShapeDtypeStruct(weights.shape, F32),
        input_output_aliases={3 + TRIO: 0} if updated else {},
        compiler_params=params(),
        cost_estimate=pl.CostEstimate(
            flops=2 * TRIO * steps * r * c * c, bytes_accessed=12 * TRIO * steps * r * c, transcendentals=0
        ),
    )(table, weights, momentum, *([factors] * TRIO), *updated)


def top(spec, a, b):
    return jnp.einsum(spec, a, b, precision=NEWTON_PRECISION)


def newton_factor(grams, growth):
    size = grams.shape[-1]
    eye = jnp.eye(size, dtype=F32)
    norm = jnp.sqrt(jnp.sum(grams * eye, axis=(1, 2), keepdims=True))
    inverse = 1.0 / (norm + 1e-07)
    gram = grams * (inverse * inverse)
    factor = None
    for sweep in range(NEWTON_STEPS):
        square = top("bij,bjk->bik", gram, gram)
        poly = NEWTON_LINEAR * eye + NEWTON_SQUARE * gram + NEWTON_CUBIC * square
        factor = poly if sweep == 0 else top("bij,bjk->bik", factor, poly)
        if sweep < NEWTON_STEPS - 1:
            gram = top("bij,bjk->bik", top("bij,bjk->bik", gram, poly), poly)
    return factor * (growth * inverse)


def fold(squares):
    h = squares.shape[1] // 2
    return jnp.stack([squares[:, :h, :h], squares[:, :h, h:], squares[:, h:, h:]], axis=1)


def unfold(parts):
    first, off, last = parts[:, 0], parts[:, 1], parts[:, 2]
    upper = jnp.concatenate([first, off], axis=2)
    lower = jnp.concatenate([jnp.swapaxes(off, 1, 2), last], axis=2)
    return jnp.concatenate([upper, lower], axis=1)


def gram_sums(ring, parts, cap):
    h = parts.shape[2]
    parts = parts.reshape(-1, h, h)
    rows = 3 * cap
    mine = yield from ring.scatter(ring.part(parts, 0, rows), rows // 2 if cap > 1 else None)
    return unfold(mine.reshape(cap, 3, h, h))


def all_factors(ring, factors):
    cap, c, _ = factors.shape
    parts = fold(factors.astype(BF16)).reshape(3 * cap, c // 2, c // 2)
    parts = yield from ring.gather(parts, 3 * cap // 2 if cap > 1 else None)
    return parts.reshape(ring.size * cap, 3, c // 2, c // 2)


def on_device(block_in, cotangent, seq_ids, weights, momentum, gains, gain_first, gain_second):
    tok_rows, model_width = block_in.shape
    rows_dp, group_blocks, head_dim = weights.shape
    head_count = lax.axis_size("head")
    data_count = lax.axis_size("dp")
    group_rows = tok_rows * head_count
    key_heads = KV // head_count
    query_heads = H // head_count
    ffn_blocks = FF // (head_dim * head_count)
    out_mark = query_heads + 2 * key_heads
    gate_mark = out_mark + query_heads
    half_dim = head_dim // 2
    full = ffn_blocks // 2
    scale = head_dim ** (-0.5)
    growth = math.sqrt(max(1.0, model_width / head_dim))
    data_index = lax.axis_index("dp")
    head_index = lax.axis_index("head")
    parity = (data_index >> 2) & 1
    ring = Ring()

    weights = jnp.transpose(weights, (1, 0, 2))
    momentum = jnp.transpose(momentum, (1, 0, 2))
    attn_low = cast_blocks(weights, gate_mark)
    inputs = block_in.astype(F32)
    normed_one, norm_one_back = jax.vjp(rms_scale, inputs, gains[0])
    ids_column = jnp.pad(seq_ids.astype(BF16)[:, None], ((0, 0), (0, 127)))

    early = full - 1
    mine_early, mine_late, other_early, other_late = pack_units(
        jnp.reshape(parity, (1,)), weights, gate_mark, ffn_blocks, early
    )
    spread = [Spread(mine_early, other_early), Spread(mine_late, other_late)]

    group_in = run(head_gather(jnp.concatenate([normed_one.astype(BF16), ids_column], axis=1)))
    qkv_parts = run(ring.gather(attn_low[:out_mark], out_mark // 2))
    qkv_blocks = jnp.transpose(qkv_parts, (1, 0, 2, 3)).reshape(out_mark, model_width, head_dim)
    cot_flow = Flow(wide_gather(cotangent))
    group_in, qkv_blocks, attn_low = stage(
        [spread[0].near(0), spread[0].y(0)], [group_in, qkv_blocks, attn_low], idle=[cot_flow]
    )
    projected = block_project(group_in, qkv_blocks)
    queries = projected[:query_heads].reshape(query_heads * group_rows, head_dim)
    group_ids = group_in[:, model_width]
    kv_rows = 2 * key_heads * group_rows
    out_rows = query_heads * rows_dp
    id_rows = group_rows // head_dim
    packed = jnp.concatenate(
        [
            projected[query_heads:].reshape(kv_rows, head_dim),
            attn_low[out_mark:].reshape(out_rows, head_dim),
            jnp.pad(group_ids.reshape(id_rows, head_dim), ((0, 16 - id_rows), (0, 0))),
        ],
        axis=0,
    )
    keys_values = run(ring.gather(packed, packed.shape[0] // 32 * 16))
    out_blocks = keys_values[:, kv_rows : kv_rows + out_rows].reshape(data_count, query_heads, rows_dp, head_dim)
    out_blocks = jnp.transpose(out_blocks, (1, 0, 2, 3)).reshape(query_heads, model_width, head_dim)
    queries, keys_values, out_blocks = stage(
        [cot_flow, spread[0].y(1), spread[1].near(0)], [queries, keys_values, out_blocks]
    )
    all_ids = keys_values[:, kv_rows + out_rows : kv_rows + out_rows + id_rows].reshape(-1)

    local = in_group(jnp.arange(group_rows, dtype=jnp.int32), group_rows, head_index * tok_rows)
    query_pos = data_index * group_rows + local
    first_pos = jnp.sum((all_ids[None, :] < group_ids[:, None]).astype(jnp.int32), axis=1)
    query_pos = jnp.tile(query_pos, query_heads)
    first_pos = jnp.tile(first_pos, query_heads)
    place = jnp.stack([data_index, head_index * tok_rows]).astype(jnp.int32)
    mixed_low, mixed_full, totals = attend(
        place, queries, keys_values, query_pos[:, None], first_pos[:, None], scale, group_rows
    )
    mixed_heads = mixed_low.reshape(query_heads, group_rows, head_dim)
    mixed_heads, mixed_full, totals, attn_part = stage(
        [spread[0].cross(), spread[1].y(0), spread[1].y(1), cot_flow],
        [mixed_heads, mixed_full, totals, block_back(mixed_heads, out_blocks)],
    )
    attn_flow = Flow(scatter_rows(*attn_part, HEAD_MOVES))
    attn_flow.advance([lax.ppermute(*send) for send in attn_flow.sends])
    stage([attn_flow, spread[0].near(3), spread[0].y(3), spread[1].cross()], idle=[cot_flow])
    residual = inputs + attn_flow.value
    normed_two, norm_two_back = jax.vjp(rms_scale, residual, gains[1])
    wide_flow = Flow(wide_gather(normed_two.astype(BF16)))
    stage([wide_flow, spread[0].y(2), spread[1].near(3), spread[1].y(3)], idle=[cot_flow])
    stage([wide_flow, spread[1].y(2), cot_flow])
    stage([wide_flow])
    finish(wide_flow, cot_flow)

    def whole_rows(pieces):
        if rows_dp % 16 == 0:
            return pieces
        out = jnp.zeros((3, data_count) + pieces[0].shape[1:], BF16)
        for k, piece in enumerate(pieces):
            out = lax.dynamic_update_index_in_dim(out, piece, data_index ^ k, 1)
        return [out.reshape(3, model_width, -1)]

    ffn_sides, ffn_full, *ffn_grads = ffn_front(
        place, wide_flow.value, cot_flow.value, whole_rows(spread[0].value()), whole_rows(spread[1].value())
    )

    def taker(pieces):
        if len(pieces) > 1:
            return lambda k: pieces[k]
        cut = pieces[0].reshape(3, data_count, rows_dp, pieces[0].shape[2])
        return lambda k: lax.dynamic_index_in_dim(cut, data_index ^ k, 1, keepdims=False)

    pieces = len(ffn_grads) // 2
    reduce = [Reduce(taker(ffn_grads[:pieces])), Reduce(taker(ffn_grads[pieces:]))]
    *down_part, dx_kept, dx_sent = stage([reduce[0].y(2)], ffn_back(ffn_sides, ffn_full))
    out_flow = Flow(scatter_rows(*down_part, WIDE_MOVES, 2))
    dx_flow = Flow(scatter_rows(dx_kept, dx_sent, WIDE_MOVES))
    dx_flow.advance([lax.ppermute(*send) for send in dx_flow.sends])
    stage([dx_flow, reduce[0].near(2), reduce[0].y(3), reduce[1].y(2)])
    stage([dx_flow, reduce[1].y(3), reduce[1].y(1), reduce[1].near(2), out_flow])
    grad_residual_norm, grad_gain_two = norm_two_back(dx_flow.value)
    grad_residual = cotangent.astype(F32) + grad_residual_norm
    grad_flow = Flow(head_gather(grad_residual.astype(BF16)))
    stage([grad_flow, reduce[1].cross(), reduce[0].y(1)])
    grad_flow.advance([lax.ppermute(*send) for send in grad_flow.sends])
    group_grad = grad_flow.value

    grad_heads = block_project(group_grad, out_blocks)
    grad_mixed = grad_heads.reshape(query_heads * group_rows, head_dim)
    delta = jnp.sum(grad_mixed.astype(F32) * mixed_full, axis=1)
    grad_queries, grad_keys_values = attend_back(
        place,
        queries,
        grad_mixed,
        keys_values,
        1.0 / totals.reshape(1, -1),
        delta[None, :],
        query_pos[None, :],
        first_pos[None, :],
        scale,
        group_rows,
    )
    late_near = reduce[1].near(1)
    group_grad, grad_queries, grad_keys_values = stage(
        [reduce[0].cross(), reduce[0].near(1), reduce[0].y(0), reduce[1].y(0)],
        [group_grad, grad_queries, grad_keys_values],
        idle=[late_near, out_flow],
    )
    grad_queries = grad_queries.reshape(query_heads, group_rows, head_dim)

    late = 2
    main = 3 * ffn_blocks - late
    cap = -(-main // data_count)
    places = -(-max(cap * data_count, 3 * ffn_blocks) // TRIO) * TRIO
    def weight_sums(outer):
        cut = outer.reshape(outer.shape[0], data_count, rows_dp, head_dim)
        return Flow(ring.scatter(ring.part(cut, 1), outer.shape[0] // 2 if outer.shape[0] > 2 else None))

    key_flow = Flow(ring.scatter(ring.part(grad_keys_values, 0), key_heads))
    (outer,) = stage(
        [key_flow, late_near],
        [block_outer([group_in, group_grad], [grad_queries, mixed_heads], model_width)],
    )
    (own_early, other_early), (own_late, other_late) = (part.value() for part in reduce)
    first_flow = weight_sums(outer)
    weight_grads, new_momentum, grams = stage(
        [key_flow, first_flow, out_flow],
        ffn_moment(
            jnp.reshape(parity, (1,)),
            [own_early, own_late],
            [other_early, other_late],
            momentum,
            gate_mark,
            ffn_blocks,
            places,
        ),
    )
    gram_flow = Flow(gram_sums(ring, grams, cap))
    stage([key_flow, first_flow, gram_flow])
    while key_flow.sends is not None:
        stage([key_flow, first_flow, gram_flow])
    key_value_sums = key_flow.value
    grad_keys = (key_value_sums[:key_heads] * scale).astype(BF16)
    grad_values = key_value_sums[key_heads:].astype(BF16)
    grad_keys_values = jnp.concatenate([grad_keys, grad_values], axis=0)
    (outer,) = stage([first_flow, gram_flow], [block_outer([group_in], [grad_keys_values], model_width)])
    finish(first_flow)
    second_flow = weight_sums(outer)
    pairs = [k for k in range(gate_mark // 2) if not query_heads <= 2 * k < out_mark]
    grad_projected = jnp.concatenate([grad_queries, grad_keys_values], axis=0)
    *attn_dx, weight_grads, new_momentum, first_grams = stage(
        [second_flow, gram_flow],
        [
            *block_back(grad_projected, qkv_blocks),
            *attn_moment(first_flow.value, pairs, momentum, weight_grads, new_momentum),
        ],
    )
    last_flow = Flow(scatter_rows(*attn_dx, HEAD_MOVES))
    finish(gram_flow)
    gram_value = gram_flow.value
    while second_flow.sends is not None:
        (gram_value,) = stage([second_flow, last_flow], [gram_value], idle=[out_flow])
    finish(last_flow)
    grad_input_norm, grad_gain_one = norm_one_back(last_flow.value)
    grad_input = grad_residual + grad_input_norm
    gain_flow = Flow(total_sum(jnp.stack([grad_gain_one, grad_gain_two])))
    weight_grads, new_momentum, second_grams = attn_moment(
        second_flow.value, list(range(query_heads // 2, out_mark // 2)), momentum, weight_grads, new_momentum
    )
    late_count = gate_mark + late
    late_cap = -(-late_count // data_count)
    late_grams = jnp.concatenate([first_grams, second_grams, grams[main : main + late]], axis=0)
    late_grams = jnp.pad(late_grams, ((0, late_cap * data_count - late_count), (0, 0), (0, 0), (0, 0)))
    late_gram_flow = Flow(gram_sums(ring, late_grams, late_cap))
    (gram_value,) = stage([late_gram_flow, gain_flow], [gram_value])
    (factors,) = stage([late_gram_flow, gain_flow, out_flow], [newton_factor(gram_value, growth)])
    factor_flow = Flow(all_factors(ring, factors))
    while late_gram_flow.sends is not None:
        stage([late_gram_flow, factor_flow, gain_flow])
    (late_factors,) = stage([factor_flow, gain_flow, out_flow], [newton_factor(late_gram_flow.value, growth)])
    finish(out_flow)
    block_out = (residual + out_flow.value).astype(BF16)
    late_factor_flow = Flow(all_factors(ring, late_factors))
    while factor_flow.sends is not None:
        stage([factor_flow, late_factor_flow, gain_flow])
    factors = factor_flow.value

    threes = main // TRIO
    early_spots = [(gate_mark // TRIO + k, [TRIO * k + i for i in range(TRIO)]) for k in range(threes)]
    new_weights = []
    for k in range(0, threes, 3):
        new_weights = stage(
            [late_factor_flow, gain_flow],
            [renew(weights, new_momentum, factors, early_spots[k : k + 3], new_weights)],
        )

    finish(late_factor_flow, gain_flow)
    gain_grads = gain_flow.value
    rest = jnp.concatenate([late_factor_flow.value[:late_count], factors[TRIO * threes : main]], axis=0)
    blocks_of = [2 * pair + i for pair in pairs for i in range(2)] + list(range(query_heads, out_mark))
    blocks_of += [gate_mark + main + k for k in range(late)] + [gate_mark + k for k in range(TRIO * threes, main)]
    late_spots = [
        (spot, [blocks_of.index(TRIO * spot + i) for i in range(TRIO)])
        for spot in sorted({block // TRIO for block in blocks_of})
    ]
    new_weights = renew(weights, new_momentum, rest, late_spots, new_weights)

    new_gain_first = BETA_ONE * gain_first + (1.0 - BETA_ONE) * gain_grads
    new_gain_second = BETA_TWO * gain_second + (1.0 - BETA_TWO) * gain_grads * gain_grads
    first_hat = new_gain_first / (1.0 - BETA_ONE**UPDATE_STEP)
    second_hat = new_gain_second / (1.0 - BETA_TWO**UPDATE_STEP)
    new_gains = gains - ADAM_RATE * first_hat / (jnp.sqrt(second_hat) + ADAM_EPS)
    back = lambda array: jnp.transpose(array, (1, 0, 2))
    return (
        block_out,
        grad_input,
        back(weight_grads),
        back(new_momentum),
        back(new_weights),
        gain_grads,
        new_gain_first,
        new_gain_second,
        new_gains,
    )


def solution(mesh):
    return jax.shard_map(
        on_device,
        mesh=mesh,
        in_specs=(
            P(("dp", "head"), None),
            P(("dp", "head"), None),
            P(("dp", "head")),
            P("dp", "head", None),
            P("dp", "head", None),
            P(),
            P(),
            P(),
        ),
        out_specs=(
            P(("dp", "head"), None),
            P(("dp", "head"), None),
            P("dp", "head", None),
            P("dp", "head", None),
            P("dp", "head", None),
            P(),
            P(),
            P(),
            P(),
        ),
        check_vma=False,
    )
```
